32 devices in a mesh: dp: 16 (over z, y, x), tensor: 2 (over core).
Axes of the slice: x: 2, y: 2, z: 4, core: 2. Of those that a mesh axis runs over, the one named last changes fastest.
Arguments:
- hidden_in: bfloat16 [16, 1024, 1536], P('dp', 'tensor'), may hold values from -6 to 6
- text_states: bfloat16 [16, 64, 1536], P('dp'), may hold values from -6 to 6
- norm1_gain: bfloat16 [1536], P('dp'), may hold values from 0.5 to 1.5
- norm1_bias: bfloat16 [1536], P('dp'), may hold values from -3 to 3
- self_query: bfloat16 [1536, 1536], P('tensor', 'dp'), may hold values from -0.15625 to 0.15625
- self_key: bfloat16 [1536, 1536], P('tensor', 'dp'), may hold values from -0.15625 to 0.15625
- self_value: bfloat16 [1536, 1536], P('tensor', 'dp'), may hold values from -0.15625 to 0.15625
- self_out: bfloat16 [1536, 1536], P('dp', 'tensor'), may hold values from -1.25 to 1.25
- norm2_gain: bfloat16 [1536], P('dp'), may hold values from 0.5 to 1.5
- norm2_bias: bfloat16 [1536], P('dp'), may hold values from -3 to 3
- cross_query: bfloat16 [1536, 1536], P('tensor', 'dp'), may hold values from -0.15625 to 0.15625
- cross_key: bfloat16 [1536, 1536], P('tensor', 'dp'), may hold values from -0.15625 to 0.15625
- cross_value: bfloat16 [1536, 1536], P('tensor', 'dp'), may hold values from -0.15625 to 0.15625
- cross_out: bfloat16 [1536, 1536], P('dp', 'tensor'), may hold values from -0.625 to 0.625
- norm3_gain: bfloat16 [1536], P('dp'), may hold values from 0.5 to 1.5
- norm3_bias: bfloat16 [1536], P('dp'), may hold values from -3 to 3
- hidden_up: bfloat16 [6144, 1536], P('tensor', 'dp'), may hold values from -0.15625 to 0.15625
- hidden_down: bfloat16 [1536, 6144], P('dp', 'tensor'), may hold values from -0.15625 to 0.15625
- cotangent: bfloat16 [16, 1024, 1536], P('dp', 'tensor'), may hold values from -6 to 6
Outputs:
- layer_out: bfloat16 [16, 1024, 1536], P('dp', 'tensor')
- grad_input: float32 [16, 1024, 1536], P('dp', 'tensor')
- grad_text: float32 [16, 64, 1536], P('dp', None, 'tensor')
- grad_norm1_gain: float32 [1536], P('dp')
- grad_norm1_bias: float32 [1536], P('dp')
- grad_self_query: float32 [1536, 1536], P('tensor', 'dp')
- grad_self_key: float32 [1536, 1536], P('tensor', 'dp')
- grad_self_value: float32 [1536, 1536], P('tensor', 'dp')
- grad_self_out: float32 [1536, 1536], P('dp', 'tensor')
- grad_norm2_gain: float32 [1536], P('dp')
- grad_norm2_bias: float32 [1536], P('dp')
- grad_cross_query: float32 [1536, 1536], P('tensor', 'dp')
- grad_cross_key: float32 [1536, 1536], P('tensor', 'dp')
- grad_cross_value: float32 [1536, 1536], P('tensor', 'dp')
- grad_cross_out: float32 [1536, 1536], P('dp', 'tensor')
- grad_norm3_gain: float32 [1536], P('dp')
- grad_norm3_bias: float32 [1536], P('dp')
- grad_hidden_up: float32 [6144, 1536], P('tensor', 'dp')
- grad_hidden_down: float32 [1536, 6144], P('dp', 'tensor')
The draws below stay inside these ranges and needn't reach their ends.
All inputs are finite; a program needn't handle non-finite values.
Results may differ from the reference program's by a relative error of at most 0.025.
Values may be sent and summed in bfloat16 or wider, within the bound.
A program may use at most 384 MiB of HBM per device.

```python
import functools
import jax
import jax.numpy as jnp
from jax import lax

D = 1536
HEADS = 24
HEAD_DIM = 64
FF = 6144
FRAMES = 1024
TEXT_LEN = 64
CLIPS = 16


def spiked(values, own_key, source, target, parts, factor):
    owner, partner = [(jnp.arange(values.shape[dim]) // (values.shape[dim] // parts)).reshape([-1 if axis == dim else 1 for axis in range(values.ndim)]) for dim in (source, target)]
    chosen = jax.random.permutation(own_key, parts)[partner]
    strong = (owner == chosen) | (owner == (partner + parts // 2) % parts)
    return jnp.where(strong, factor * values, values)


def shard_levels(rng, dims, split, least, top_value):
    factor_of, own = 1.0, jax.random.fold_in(rng, 6)
    for dim, shards_of in split:
        steps = jnp.exp(jax.random.uniform(jax.random.fold_in(own, dim), (shards_of,), jnp.float32, least / len(split), top_value / len(split)))
        factor_of = factor_of * jnp.repeat(steps, dims[dim] // shards_of).reshape([-1 if axis == dim else 1 for axis in range(len(dims))])
    return factor_of


def centred(stream_key, shape, width, bound, cuts=(), held_as=jnp.bfloat16):
    level = shard_levels(stream_key, shape, cuts, -0.22, 0.18) if cuts else 1.0
    array = jax.random.normal(stream_key, shape, jnp.float32) * width * level
    return jnp.minimum(jnp.maximum(array, -bound), bound).astype(held_as)


def gaussian_with(rng, extent, width, most, shards, heavy, held_as=jnp.bfloat16):
    values = width * jax.random.normal(rng, extent, jnp.float32)
    if shards:
        values = values * shard_levels(rng, extent, shards, -0.22, 0.18)
    return jnp.clip(spiked(values, jax.random.fold_in(rng, 3), *heavy), -most, most).astype(held_as)


def setup_inputs(seed: int = 0) -> dict:
    splits = jax.random.split(jax.random.key(seed), 20)
    hidden_in = centred(splits[0], (CLIPS, FRAMES, D), 1.0, 6.0, ((0, 16), (1, 2)))
    text_states = centred(splits[1], (CLIPS, TEXT_LEN, D), 1.0, 6.0, ((0, 16),))
    norm1_gain = jnp.clip(1.0 + 0.1 * jax.random.normal(splits[2], (D,), jnp.float32), 0.5, 1.5).astype(jnp.bfloat16)
    norm1_bias = centred(splits[3], (D,), 0.5, 3.0, ((0, 16),))
    self_query = centred(splits[4], (D, D), D ** -0.5, 0.15625, ((0, 2), (1, 16)))
    self_key = centred(splits[5], (D, D), D ** -0.5, 0.15625, ((0, 2), (1, 16)))
    self_value = centred(splits[6], (D, D), D ** -0.5, 0.15625, ((0, 2), (1, 16)))
    self_out = centred(splits[7], (D, D), (D // 64) ** -0.5, 1.25, ((0, 16), (1, 2)))
    norm2_gain = jnp.clip(1.0 + 0.1 * jax.random.normal(splits[8], (D,), jnp.float32), 0.5, 1.5).astype(jnp.bfloat16)
    norm2_bias = centred(splits[9], (D,), 0.5, 3.0, ((0, 16),))
    cross_query = centred(splits[10], (D, D), D ** -0.5, 0.15625, ((0, 2), (1, 16)))
    cross_key = centred(splits[11], (D, D), D ** -0.5, 0.15625, ((0, 2), (1, 16)))
    cross_value = centred(splits[12], (D, D), D ** -0.5, 0.15625, ((0, 2), (1, 16)))
    cross_out = centred(splits[13], (D, D), (D // 16) ** -0.5, 0.625, ((0, 16), (1, 2)))
    norm3_gain = jnp.clip(1.0 + 0.1 * jax.random.normal(splits[14], (D,), jnp.float32), 0.5, 1.5).astype(jnp.bfloat16)
    norm3_bias = centred(splits[15], (D,), 0.5, 3.0, ((0, 16),))
    hidden_up = centred(splits[16], (FF, D), D ** -0.5, 0.15625, ((0, 2), (1, 16)))
    hidden_down = centred(splits[17], (D, FF), (FF // 4) ** -0.5, 0.15625, ((0, 16), (1, 2)))
    cotangent = gaussian_with(splits[18], (CLIPS, FRAMES, D), 1.0, 6.0, ((0, 16), (1, 2)), (0, 2, 16, 2.0))
    return {"hidden_in": hidden_in, "text_states": text_states, "norm1_gain": norm1_gain, "norm1_bias": norm1_bias, "self_query": self_query, "self_key": self_key, "self_value": self_value, "self_out": self_out, "norm2_gain": norm2_gain, "norm2_bias": norm2_bias, "cross_query": cross_query, "cross_key": cross_key, "cross_value": cross_value, "cross_out": cross_out, "norm3_gain": norm3_gain, "norm3_bias": norm3_bias, "hidden_up": hidden_up, "hidden_down": hidden_down, "cotangent": cotangent}


@jax.custom_vjp
def low(v):
    return lax.optimization_barrier(v.astype(jnp.bfloat16)).astype(jnp.float32)

@jax.custom_vjp
def low_back(v):
    return v

def low_keep(v):
    return (low(v), None)

def low_pass(kept, grad):
    return (grad,)

def back_keep(v):
    return (v, None)

def back_low(kept, grad):
    return (low(grad),)
low.defvjp(low_keep, low_pass)
low_back.defvjp(back_keep, back_low)
norm_eps = 1e-05
highest = lax.Precision.HIGHEST

def layer_norm(values, gain, shift):
    centre = lax.optimization_barrier(jnp.mean(values, axis=-1, keepdims=True))
    offset = values - centre
    spread = lax.optimization_barrier(jnp.mean(offset * offset, axis=-1, keepdims=True))
    return offset * lax.rsqrt(spread + norm_eps) * gain + shift

def matmul(left, right):
    return jnp.dot(left, right, precision=highest, preferred_element_type=jnp.float32)

def split_heads(values):
    return values.reshape(values.shape[0], HEADS, HEAD_DIM).transpose(1, 0, 2)

def merge_heads(values):
    return values.transpose(1, 0, 2).reshape(values.shape[1], HEADS * HEAD_DIM)

def head_attention(causal, operands):
    queries, key_rows, val_rows = operands
    scores = low_back(matmul(queries, key_rows.T) * 0.125)
    if causal:
        row_ids = lax.broadcasted_iota(jnp.int32, scores.shape, 0)
        col_ids = lax.broadcasted_iota(jnp.int32, scores.shape, 1)
        scores = jnp.where(col_ids <= row_ids, scores, -1e+30)
    row_peak = lax.optimization_barrier(jnp.max(scores, axis=-1, keepdims=True))
    exp_scores = jnp.exp(scores - row_peak)
    soft = exp_scores / lax.optimization_barrier(jnp.sum(exp_scores, axis=-1, keepdims=True))
    return matmul(low(soft), val_rows)

def attention(queries, key_rows, val_rows, causal):
    per_head = jax.checkpoint(functools.partial(head_attention, causal))
    heads_out = lax.map(per_head, (split_heads(queries), split_heads(key_rows), split_heads(val_rows)))
    return merge_heads(heads_out)

def project_round(rows_in, weight):
    return low(low_back(matmul(rows_in, weight.T)))

def clip_forward(rows_in, text_rows, params):
    gain_self, bias_self, query_self, key_self, value_self, out_self, gain_cross, bias_cross, query_cross, key_cross, value_cross, out_cross, gain_ffn, bias_ffn, up_proj, down_proj = params
    normed = low(layer_norm(rows_in, gain_self, bias_self))
    attended = low(low_back(attention(project_round(normed, query_self), project_round(normed, key_self), project_round(normed, value_self), True)))
    stream = rows_in + low_back(matmul(attended, out_self.T))
    normed = low(layer_norm(stream, gain_cross, bias_cross))
    attended = low(low_back(attention(project_round(normed, query_cross), project_round(text_rows, key_cross), project_round(text_rows, value_cross), False)))
    stream = stream + low_back(matmul(attended, out_cross.T))
    normed = low(layer_norm(stream, gain_ffn, bias_ffn))
    upper = low_back(matmul(normed, up_proj.T))
    active = low(jax.nn.gelu(upper, approximate=False))
    return stream + low_back(matmul(active, down_proj.T))

def reference(hidden_in, text_states, norm1_gain, norm1_bias, self_query, self_key, self_value, self_out, norm2_gain, norm2_bias, cross_query, cross_key, cross_value, cross_out, norm3_gain, norm3_bias, hidden_up, hidden_down, cotangent):
    params = tuple((member.astype(jnp.float32) for member in (norm1_gain, norm1_bias, self_query, self_key, self_value, self_out, norm2_gain, norm2_bias, cross_query, cross_key, cross_value, cross_out, norm3_gain, norm3_bias, hidden_up, hidden_down)))

    def clip_step(totals, clip_data):
        rows_in, text_rows, grad_rows = clip_data
        result, pullback = jax.vjp(clip_forward, rows_in.astype(jnp.float32), text_rows.astype(jnp.float32), params)
        grad_in, grad_txt, grad_params = pullback(grad_rows.astype(jnp.float32))
        totals = jax.tree.map(lambda left, right: left + right, totals, grad_params)
        return (totals, (result.astype(jnp.bfloat16), grad_in, grad_txt))
    zeros_init = jax.tree.map(jnp.zeros_like, params)
    totals, outputs = lax.scan(clip_step, zeros_init, (hidden_in, text_states, cotangent))
    layer_out, grad_input, grad_text = outputs
    return (layer_out, grad_input, grad_text, totals[0], totals[1], totals[2], totals[3], totals[4], totals[5], totals[6], totals[7], totals[8], totals[9], totals[10], totals[11], totals[12], totals[13], totals[14], totals[15])
```

```python
import functools

import jax
import jax.numpy as jnp
from jax import lax
from jax.experimental import pallas as pl
from jax.experimental.pallas import tpu as pltpu
from jax.sharding import PartitionSpec as P

HEAD_DIM = 64


norm_eps = 1e-05
score_scale = 0.125


def layer_norm(values, gain, shift):
    centre = jnp.mean(values, axis=-1, keepdims=True)
    offset = values - centre
    spread = jnp.mean(offset * offset, axis=-1, keepdims=True)
    return offset * lax.rsqrt(spread + norm_eps) * gain + shift


def gelu_exact(values):
    return jax.nn.gelu(values, approximate=False)


def project(row_data, weight):
    return jnp.einsum("cli,oi->clo", row_data, weight, preferred_element_type=jnp.float32)


def split_heads(values):
    return values.reshape(values.shape[0], values.shape[1], -1, HEAD_DIM)


def flatten_heads(values):
    return values.reshape(values.shape[0], values.shape[1], -1)


def causal_keep(first_row, count, length):
    row_ids = first_row + lax.broadcasted_iota(jnp.int32, (count, length), 0)
    col_ids = lax.broadcasted_iota(jnp.int32, (count, length), 1)
    return col_ids <= row_ids


def block_scores(queries, key_rows, first_row, block_rows, key_end, causal):
    scores = (
        jnp.einsum(
            "cqhe,ckhe->chqk",
            queries[:, first_row : first_row + block_rows],
            key_rows[:, :key_end],
            preferred_element_type=jnp.float32,
        )
        * score_scale
    )
    if causal:
        scores = jnp.where(causal_keep(first_row, block_rows, key_end), scores, -1e30)
    return scores


def attend(queries, key_rows, val_rows, causal):
    length = queries.shape[1]
    block_rows = min(512, length)
    outputs = []
    log_sums = []
    for block_num in range(length // block_rows):
        first_row = block_num * block_rows
        key_end = first_row + block_rows if causal else key_rows.shape[1]
        scores = block_scores(queries, key_rows, first_row, block_rows, key_end, causal)
        row_peak = jnp.max(scores, axis=-1, keepdims=True)
        exp_scores = jnp.exp(scores - row_peak)
        row_total = jnp.sum(exp_scores, axis=-1, keepdims=True)
        soft_weights = (exp_scores / row_total).astype(jnp.bfloat16)
        outputs.append(
            jnp.einsum(
                "chqk,ckhe->cqhe",
                soft_weights,
                val_rows[:, :key_end],
                preferred_element_type=jnp.float32,
            ).astype(jnp.bfloat16)
        )
        log_sums.append((row_peak + jnp.log(row_total))[..., 0])
    return (jnp.concatenate(outputs, axis=1), jnp.concatenate(log_sums, axis=2))


def attend_back(queries, key_rows, val_rows, grad_out, log_sums, causal):
    length = queries.shape[1]
    block_rows = min(512, length)
    grad_keys = jnp.zeros(key_rows.shape, jnp.float32)
    grad_vals = jnp.zeros(val_rows.shape, jnp.float32)
    grad_queries = []
    for block_num in range(length // block_rows):
        first_row = block_num * block_rows
        key_end = first_row + block_rows if causal else key_rows.shape[1]
        query_blk = queries[:, first_row : first_row + block_rows]
        grad_blk = grad_out[:, first_row : first_row + block_rows]
        scores = block_scores(queries, key_rows, first_row, block_rows, key_end, causal)
        soft = jnp.exp(scores - log_sums[:, :, first_row : first_row + block_rows, None])
        grad_soft = jnp.einsum(
            "cqhe,ckhe->chqk", grad_blk, val_rows[:, :key_end], preferred_element_type=jnp.float32
        )
        grad_vals = grad_vals.at[:, :key_end].add(
            jnp.einsum(
                "chqk,cqhe->ckhe",
                soft.astype(jnp.bfloat16),
                grad_blk,
                preferred_element_type=jnp.float32,
            )
        )
        inner = jnp.sum(soft * grad_soft, axis=-1, keepdims=True)
        grad_scores = (soft * (grad_soft - inner)).astype(jnp.bfloat16)
        grad_queries.append(
            jnp.einsum(
                "chqk,ckhe->cqhe",
                grad_scores,
                key_rows[:, :key_end],
                preferred_element_type=jnp.float32,
            )
            * score_scale
        )
        grad_keys = grad_keys.at[:, :key_end].add(
            jnp.einsum(
                "chqk,cqhe->ckhe", grad_scores, query_blk, preferred_element_type=jnp.float32
            )
            * score_scale
        )
    return (jnp.concatenate(grad_queries, axis=1), grad_keys, grad_vals)


def gather_rows(values):
    return lax.all_gather(values, "tensor", axis=1, tiled=True)


def scatter_rows(values):
    return lax.psum_scatter(values, "tensor", scatter_dimension=1, tiled=True)


def gather_grads(values):
    return lax.all_gather(values, "tensor", axis=1, tiled=True)


def scatter_grads(values):
    return lax.psum_scatter(
        values.astype(jnp.bfloat16), "tensor", scatter_dimension=1, tiled=True
    ).astype(jnp.float32)


def heads_grads(grad_branch, attended, out_weight):
    grad_out_proj = jnp.einsum(
        "clo,cla->oa", grad_branch, flatten_heads(attended), preferred_element_type=jnp.float32
    )
    grad_attended = split_heads(
        jnp.einsum(
            "clo,oa->cla", grad_branch, out_weight, preferred_element_type=jnp.float32
        ).astype(jnp.bfloat16)
    )
    return (grad_out_proj, grad_attended)


def weight_grad(grad_rows, source_rows):
    return jnp.einsum("cla,cli->ai", grad_rows, source_rows, preferred_element_type=jnp.float32)


def input_grad(grad_rows, weight):
    return jnp.einsum("cla,ai->cli", grad_rows, weight, preferred_element_type=jnp.float32)


def local_generic(
    hidden_in,
    text_states,
    norm1_gain,
    norm1_bias,
    self_query,
    self_key,
    self_value,
    self_out,
    norm2_gain,
    norm2_bias,
    cross_query,
    cross_key,
    cross_value,
    cross_out,
    norm3_gain,
    norm3_bias,
    hidden_up,
    hidden_down,
    cotangent,
):
    full_weights = (
        lax.all_gather(norm1_gain, "dp", axis=0, tiled=True),
        lax.all_gather(norm1_bias, "dp", axis=0, tiled=True),
        lax.all_gather(self_query, "dp", axis=1, tiled=True),
        lax.all_gather(self_key, "dp", axis=1, tiled=True),
        lax.all_gather(self_value, "dp", axis=1, tiled=True),
        lax.all_gather(self_out, "dp", axis=0, tiled=True),
        lax.all_gather(norm2_gain, "dp", axis=0, tiled=True),
        lax.all_gather(norm2_bias, "dp", axis=0, tiled=True),
        lax.all_gather(cross_query, "dp", axis=1, tiled=True),
        lax.all_gather(cross_key, "dp", axis=1, tiled=True),
        lax.all_gather(cross_value, "dp", axis=1, tiled=True),
        lax.all_gather(cross_out, "dp", axis=0, tiled=True),
        lax.all_gather(norm3_gain, "dp", axis=0, tiled=True),
        lax.all_gather(norm3_bias, "dp", axis=0, tiled=True),
        lax.all_gather(hidden_up, "dp", axis=1, tiled=True),
        lax.all_gather(hidden_down, "dp", axis=0, tiled=True),
    )
    gain_self = full_weights[0].astype(jnp.float32)
    bias_self = full_weights[1].astype(jnp.float32)
    gain_cross = full_weights[6].astype(jnp.float32)
    bias_cross = full_weights[7].astype(jnp.float32)
    gain_ffn = full_weights[12].astype(jnp.float32)
    bias_ffn = full_weights[13].astype(jnp.float32)
    stream_one = hidden_in.astype(jnp.float32)
    key_two = split_heads(project(text_states, full_weights[9]).astype(jnp.bfloat16))
    value_two = split_heads(project(text_states, full_weights[10]).astype(jnp.bfloat16))
    normed_one = gather_rows(layer_norm(stream_one, gain_self, bias_self).astype(jnp.bfloat16))
    query_one = split_heads(project(normed_one, full_weights[2]).astype(jnp.bfloat16))
    key_one = split_heads(project(normed_one, full_weights[3]).astype(jnp.bfloat16))
    value_one = split_heads(project(normed_one, full_weights[4]).astype(jnp.bfloat16))
    attended_one, logsum_one = attend(query_one, key_one, value_one, True)
    stream_two = stream_one + scatter_rows(project(flatten_heads(attended_one), full_weights[5]))
    normed_two = gather_rows(layer_norm(stream_two, gain_cross, bias_cross).astype(jnp.bfloat16))
    query_two = split_heads(project(normed_two, full_weights[8]).astype(jnp.bfloat16))
    attended_two, logsum_two = attend(query_two, key_two, value_two, False)
    stream_three = stream_two + scatter_rows(project(flatten_heads(attended_two), full_weights[11]))
    normed_three = gather_rows(layer_norm(stream_three, gain_ffn, bias_ffn).astype(jnp.bfloat16))
    upper = project(normed_three, full_weights[14])
    active = gelu_exact(upper).astype(jnp.bfloat16)
    layer_out = (stream_three + scatter_rows(project(active, full_weights[15]))).astype(
        jnp.bfloat16
    )
    grad_three = cotangent.astype(jnp.float32)
    grad_branch = gather_grads(grad_three.astype(jnp.bfloat16))
    grad_down = jnp.einsum("clo,clf->of", grad_branch, active, preferred_element_type=jnp.float32)
    grad_active = jnp.einsum(
        "clo,of->clf", grad_branch, full_weights[15], preferred_element_type=jnp.float32
    )
    grad_upper = jax.vjp(gelu_exact, upper)[1](grad_active)[0].astype(jnp.bfloat16)
    grad_up = weight_grad(grad_upper, normed_three)
    norm_back = jax.vjp(layer_norm, stream_three, gain_ffn, bias_ffn)[1]
    grad_stream, grad_gain_ffn, grad_bias_ffn = norm_back(
        scatter_grads(input_grad(grad_upper, full_weights[14]))
    )
    grad_two = grad_three + grad_stream
    grad_branch = gather_grads(grad_two.astype(jnp.bfloat16))
    grad_out_cross, grad_attended = heads_grads(grad_branch, attended_two, full_weights[11])
    grad_query, grad_key, grad_value = attend_back(
        query_two, key_two, value_two, grad_attended, logsum_two, False
    )
    grad_query = flatten_heads(grad_query).astype(jnp.bfloat16)
    grad_key = flatten_heads(grad_key).astype(jnp.bfloat16)
    grad_value = flatten_heads(grad_value).astype(jnp.bfloat16)
    grad_query_cross = weight_grad(grad_query, normed_two)
    grad_key_cross = weight_grad(grad_key, text_states)
    grad_value_cross = weight_grad(grad_value, text_states)
    text_part = input_grad(grad_key, full_weights[9]) + input_grad(grad_value, full_weights[10])
    grad_text = lax.psum_scatter(
        text_part.astype(jnp.bfloat16), "tensor", scatter_dimension=2, tiled=True
    ).astype(jnp.float32)
    norm_back = jax.vjp(layer_norm, stream_two, gain_cross, bias_cross)[1]
    grad_stream, grad_gain_cross, grad_bias_cross = norm_back(
        scatter_grads(input_grad(grad_query, full_weights[8]))
    )
    grad_one = grad_two + grad_stream
    grad_branch = gather_grads(grad_one.astype(jnp.bfloat16))
    grad_out_self, grad_attended = heads_grads(grad_branch, attended_one, full_weights[5])
    grad_query, grad_key, grad_value = attend_back(
        query_one, key_one, value_one, grad_attended, logsum_one, True
    )
    grad_query = flatten_heads(grad_query).astype(jnp.bfloat16)
    grad_key = flatten_heads(grad_key).astype(jnp.bfloat16)
    grad_value = flatten_heads(grad_value).astype(jnp.bfloat16)
    grad_query_self = weight_grad(grad_query, normed_one)
    grad_key_self = weight_grad(grad_key, normed_one)
    grad_value_self = weight_grad(grad_value, normed_one)
    grad_normed = (
        input_grad(grad_query, full_weights[2])
        + input_grad(grad_key, full_weights[3])
        + input_grad(grad_value, full_weights[4])
    )
    norm_back = jax.vjp(layer_norm, stream_one, gain_self, bias_self)[1]
    grad_stream, grad_gain_self, grad_bias_self = norm_back(scatter_grads(grad_normed))
    grad_input = grad_one + grad_stream
    summed = (
        lax.psum_scatter(
            grad_gain_self.astype(jnp.bfloat16), "dp", scatter_dimension=0, tiled=True
        ).astype(jnp.float32),
        lax.psum_scatter(
            grad_bias_self.astype(jnp.bfloat16), "dp", scatter_dimension=0, tiled=True
        ).astype(jnp.float32),
        lax.psum_scatter(
            grad_query_self.astype(jnp.bfloat16), "dp", scatter_dimension=1, tiled=True
        ).astype(jnp.float32),
        lax.psum_scatter(
            grad_key_self.astype(jnp.bfloat16), "dp", scatter_dimension=1, tiled=True
        ).astype(jnp.float32),
        lax.psum_scatter(
            grad_value_self.astype(jnp.bfloat16), "dp", scatter_dimension=1, tiled=True
        ).astype(jnp.float32),
        lax.psum_scatter(
            grad_out_self.astype(jnp.bfloat16), "dp", scatter_dimension=0, tiled=True
        ).astype(jnp.float32),
        lax.psum_scatter(
            grad_gain_cross.astype(jnp.bfloat16), "dp", scatter_dimension=0, tiled=True
        ).astype(jnp.float32),
        lax.psum_scatter(
            grad_bias_cross.astype(jnp.bfloat16), "dp", scatter_dimension=0, tiled=True
        ).astype(jnp.float32),
        lax.psum_scatter(
            grad_query_cross.astype(jnp.bfloat16), "dp", scatter_dimension=1, tiled=True
        ).astype(jnp.float32),
        lax.psum_scatter(
            grad_key_cross.astype(jnp.bfloat16), "dp", scatter_dimension=1, tiled=True
        ).astype(jnp.float32),
        lax.psum_scatter(
            grad_value_cross.astype(jnp.bfloat16), "dp", scatter_dimension=1, tiled=True
        ).astype(jnp.float32),
        lax.psum_scatter(
            grad_out_cross.astype(jnp.bfloat16), "dp", scatter_dimension=0, tiled=True
        ).astype(jnp.float32),
        lax.psum_scatter(
            grad_gain_ffn.astype(jnp.bfloat16), "dp", scatter_dimension=0, tiled=True
        ).astype(jnp.float32),
        lax.psum_scatter(
            grad_bias_ffn.astype(jnp.bfloat16), "dp", scatter_dimension=0, tiled=True
        ).astype(jnp.float32),
        lax.psum_scatter(
            grad_up.astype(jnp.bfloat16), "dp", scatter_dimension=1, tiled=True
        ).astype(jnp.float32),
        lax.psum_scatter(
            grad_down.astype(jnp.bfloat16), "dp", scatter_dimension=0, tiled=True
        ).astype(jnp.float32),
    )
    norm_sums = lax.psum(
        (summed[0], summed[1], summed[6], summed[7], summed[12], summed[13]), "tensor"
    )
    return (
        layer_out,
        grad_input,
        grad_text,
        norm_sums[0],
        norm_sums[1],
        summed[2],
        summed[3],
        summed[4],
        summed[5],
        norm_sums[2],
        norm_sums[3],
        summed[8],
        summed[9],
        summed[10],
        summed[11],
        norm_sums[4],
        norm_sums[5],
        summed[14],
        summed[15],
    )


MESH_IDS = pl.DeviceIdType.MESH
BF16 = jnp.bfloat16
F32 = jnp.float32
VMEM_LIMIT = 60 * 2**20


def my_place():
    chip = lax.axis_index("dp")
    core = lax.axis_index("tensor")
    return (lax.rem(chip, 2), lax.rem(lax.div(chip, 2), 2), lax.div(chip, 4), core)


def neighbours(x, y, z, core):
    def device(zz, yy, xx):
        return (zz * 4 + yy * 2 + xx, core)

    return (device(z, y, 1 - x), device(z, 1 - y, x), device(z + 1, y, x), device(z - 1, y, x))


def when(cond, fn):
    if cond is None:
        fn()
    else:
        pl.when(cond)(fn)


def signal_neighbours(sems, near, has_up, has_down):
    for sem, device, cond in zip(sems, near, (None, None, has_up, has_down), strict=True):
        when(
            cond,
            functools.partial(
                pl.semaphore_signal, sem, inc=1, device_id=device, device_id_type=MESH_IDS
            ),
        )


def gather_kernel(count, chunks, *refs):
    shards, outs = refs[:count], refs[count : 2 * count]
    local_sem, send_sem, zs, xs, ys, ds = refs[2 * count :]
    x, y, z, core = my_place()
    xn, yn = 1 - x, 1 - y
    near = neighbours(x, y, z, core)
    right, across, up, down = near
    has_up, has_down = z < 3, z > 0
    barrier = pltpu.get_barrier_semaphore()
    signal_neighbours([barrier] * 4, near, has_up, has_down)
    pl.semaphore_wait(barrier, 2 + has_up.astype(jnp.int32) + has_down.astype(jnp.int32))
    total = len(chunks)
    pending = []

    half_rows = shards[0].shape[0] // 2

    def span(c):
        _, first, width, _ = chunks[c]
        return pl.ds(first, width)

    def at(zz, yy, xx, c, half=None):
        lines = slice(None) if half is None else pl.ds(half * half_rows, half_rows)
        return outs[chunks[c][0]].at[zz, yy, xx, lines, span(c)]

    def plane(zz, c):
        return outs[chunks[c][0]].at[zz, :, :, :, span(c)]

    def own(c):
        return shards[chunks[c][0]].at[:, span(c)]

    local = [pltpu.make_async_copy(own(c), at(z, y, x, c), local_sem.at[c]) for c in range(total)]

    def remote(src, dst, sem, device):
        return pltpu.make_async_remote_copy(
            src_ref=src,
            dst_ref=dst,
            send_sem=send_sem,
            recv_sem=sem,
            device_id=device,
            device_id_type=MESH_IDS,
        )

    def send(src, dst, sem, device, cond=None):
        copy = remote(src, dst, sem, device)
        when(cond, copy.start)
        pending.append((cond, copy))

    def wait(ref, sem, cond=None):
        when(cond, remote(ref, ref, sem, right).wait_recv)

    def lines(step):
        for sign, device, more in ((-1, up, has_up), (1, down, has_down)):
            block = z + sign * step
            yield block, (block >= 0) if sign < 0 else (block <= 3), device, more

    def stage_z(c, step):
        if step == 0:
            send(own(c), at(z, y, x, c), zs.at[c, z], up, has_up)
            send(own(c), at(z, y, x, c), zs.at[c, z], down, has_down)
            send(own(c), at(z, y, x, c), xs.at[c, z], right)
            send(own(c), at(z, y, x, c), ys.at[c, z], across)
            local[c].start()
        if 1 <= step <= 3:
            for block, exists, device, more in lines(step):
                ref = at(block, y, x, c)
                wait(ref, zs.at[c, block], exists)
                if step < 3:
                    send(ref, ref, zs.at[c, block], device, exists & more)
                send(ref, ref, xs.at[c, block], right, exists)
                send(ref, ref, ys.at[c, block], across, exists)
        if 1 <= step <= 4:
            for block, exists, _, _ in [(z, None, None, None)] if step == 1 else lines(step - 1):
                wait(at(block, y, xn, c), xs.at[c, block], exists)
                ref = at(block, y, xn, c, 0)
                send(ref, ref, ds.at[c, block, 0], across, exists)
                wait(at(block, yn, x, c), ys.at[c, block], exists)
                ref = at(block, yn, x, c, 1)
                send(ref, ref, ds.at[c, block, 1], right, exists)
        if step == 5:
            for block in range(4):
                for half in range(2):
                    wait(at(block, yn, xn, c, half), ds.at[c, block, half])
            local[c].wait()

    def stage_a(c, step):
        if step == 0:
            send(own(c), at(z, y, x, c), xs.at[c, z], right)
            send(own(c), at(z, y, x, c), ys.at[c, z], across)
            local[c].start()
        if step == 1:
            wait(at(z, y, xn, c), xs.at[c, z])
            ref = at(z, y, xn, c, 0)
            send(ref, ref, ds.at[c, z, 0], across)
            wait(at(z, yn, x, c), ys.at[c, z])
            ref = at(z, yn, x, c, 1)
            send(ref, ref, ds.at[c, z, 1], right)
        if step == 2:
            for half in range(2):
                wait(at(z, yn, xn, c, half), ds.at[c, z, half])
            local[c].wait()
            send(plane(z, c), plane(z, c), zs.at[c, z], up, has_up)
            send(plane(z, c), plane(z, c), zs.at[c, z], down, has_down)
        if step >= 3:
            for block, exists, device, more in lines(step - 2):
                wait(plane(block, c), zs.at[c, block], exists)
                if step < 5:
                    send(plane(block, c), plane(block, c), zs.at[c, block], device, exists & more)

    stages = 6
    for turn in range(total + stages - 1):
        for step in range(stages):
            c = turn - step
            if 0 <= c < total:
                (stage_z if chunks[c][3] == "Z" else stage_a)(c, step)
    for cond, copy in pending:
        when(cond, copy.wait_send)


def gather_all(shards, chunks):
    total, count = len(chunks), len(shards)
    dma = pltpu.SemaphoreType.DMA
    return pl.pallas_call(
        functools.partial(gather_kernel, count, chunks),
        out_shape=[jax.ShapeDtypeStruct((4, 2, 2) + s.shape, s.dtype) for s in shards],
        in_specs=[pl.BlockSpec(memory_space=pl.ANY)] * count,
        out_specs=[pl.BlockSpec(memory_space=pl.ANY)] * count,
        scratch_shapes=[
            dma((total,)),
            dma,
            dma((total, 4)),
            dma((total, 4)),
            dma((total, 4)),
            dma((total, 4, 2)),
        ],
        compiler_params=pltpu.CompilerParams(collective_id=0, has_side_effects=True),
        name="gather_weights",
    )(*shards)


def total_of(*parts):
    value = parts[0].astype(F32)
    for part in parts[1:]:
        value = value + part.astype(F32)
    return value


XD, YD, XA, YA, XB, YB, UP, DOWN = range(8)


def scatter_kernel(places, width_z, width_a, slots, *refs):
    count = 1 + max(place[0] for place in places)
    grads, out = refs[:count], refs[count]
    gz, ga, xdz, ydz, xaz, yaz, xbz, ybz, upz, dnz = refs[count + 1 : count + 11]
    xda, yda, xaa, yaa, xba, yba, upa, dna, oz, oa = refs[count + 11 : count + 21]
    load_sem, out_sem, send_z, send_a, recv_z, recv_a, credit = refs[count + 21 :]
    total, width = len(places), width_z + width_a
    x, y, z, core = my_place()
    xn, yn = 1 - x, 1 - y
    near = neighbours(x, y, z, core)
    right, across, up, down = near
    has_up, has_down = z < 3, z > 0
    degree = 2 + has_up.astype(jnp.int32) + has_down.astype(jnp.int32)
    barrier = pltpu.get_barrier_semaphore()
    signal_neighbours([barrier] * 4, near, has_up, has_down)
    pl.semaphore_wait(barrier, degree)
    rows = gz.shape[4]
    low, high = pl.ds(0, rows // 2), pl.ds(rows // 2, rows // 2)

    def remote(src, dst, send_sem, recv_sem, device):
        return pltpu.make_async_remote_copy(
            src_ref=src,
            dst_ref=dst,
            send_sem=send_sem,
            recv_sem=recv_sem,
            device_id=device,
            device_id_type=MESH_IDS,
        )

    def arrived(ref, sem):
        remote(ref, ref, send_z.at[0], sem, right).wait_recv()

    def sent(ref, sem):
        remote(ref, ref, sem, recv_z.at[0, 0], right).wait_send()

    def load_copies(array, first, k):
        grad = grads[array]
        return (
            pltpu.make_async_copy(
                grad.at[:, :, :, :, pl.ds(first, width_z)], gz.at[k], load_sem.at[k, 0]
            ),
            pltpu.make_async_copy(
                grad.at[:, :, :, :, pl.ds(first + width_z, width_a)], ga.at[k], load_sem.at[k, 1]
            ),
        )

    def out_copies(c):
        o = lax.rem(c, 2)
        first = pl.multiple_of(c * width, 128)
        return (
            pltpu.make_async_copy(oz.at[o], out.at[:, pl.ds(first, width_z)], out_sem.at[o, 0]),
            pltpu.make_async_copy(
                oa.at[o], out.at[:, pl.ds(first + width_z, width_a)], out_sem.at[o, 1]
            ),
        )

    def plane_first(own, k, bufs, send_sem, recv):
        xd, yd, xa, ya = bufs
        remote(own(yn, xn, low), xd.at[k], send_sem.at[k], recv.at[k, XD], right).start()
        remote(own(yn, xn, high), yd.at[k], send_sem.at[k], recv.at[k, YD], across).start()
        remote(own(y, xn, low), xa.at[k], send_sem.at[k], recv.at[k, XA], right).start()
        remote(own(yn, x, high), ya.at[k], send_sem.at[k], recv.at[k, YA], across).start()

    def plane_second(add, k, bufs, send_sem, recv):
        xd, yd, xb, yb = bufs
        arrived(xd.at[k], recv.at[k, XD])
        add(xd, yn, x, low)
        remote(xd.at[k], yb.at[k], send_sem.at[k], recv.at[k, YB], across).start()
        arrived(yd.at[k], recv.at[k, YD])
        add(yd, y, xn, high)
        remote(yd.at[k], xb.at[k], send_sem.at[k], recv.at[k, XB], right).start()

    def line_up(first, buf, add, k, send_sem, recv):
        blocks = 4 - first
        arrived(buf.at[k, pl.ds(first, blocks)], recv.at[k, UP])
        if blocks > 1:
            for block in range(first + 1, 4):
                add(buf, block)
            ref = buf.at[k, pl.ds(first + 1, blocks - 1)]
            remote(ref, ref, send_sem.at[k], recv.at[k, UP], up).start()

    def line_down(last, buf, add, k, send_sem, recv):
        arrived(buf.at[k, pl.ds(0, last + 1)], recv.at[k, DOWN])
        if last > 0:
            for block in range(last):
                add(buf, block)
            ref = buf.at[k, pl.ds(0, last)]
            remote(ref, ref, send_sem.at[k], recv.at[k, DOWN], down).start()

    def add_a(k):
        def add(buf, block):
            for yy in range(2):
                for xx in range(2):
                    buf[k, block, yy, xx] = total_of(
                        buf[k, block, yy, xx], ga[k, block, yy, xx]
                    ).astype(BF16)

        return add

    def add_z(k):
        def add(buf, block):
            buf[k, block] = total_of(buf[k, block], gz[k, block, y, x]).astype(BF16)

        return add

    def start_load(c, k):
        for index, (array, first) in enumerate(places):

            @pl.when(c == index)
            def _():
                for copy in load_copies(array, first, k):
                    copy.start()

    def begin(c, k):
        for copy in load_copies(0, 0, k):
            copy.wait()

        @pl.when(c >= slots)
        def _():
            pl.semaphore_wait(credit.at[0], 1)
            pl.semaphore_wait(credit.at[1], 1)
            pl.when(has_up)(lambda: pl.semaphore_wait(credit.at[2], 1))
            pl.when(has_down)(lambda: pl.semaphore_wait(credit.at[3], 1))

        plane_first(
            lambda yy, xx, half: gz.at[k, :, yy, xx, half, :], k, (xdz, ydz, xaz, yaz), send_z, recv_z
        )

        @pl.when(z == 0)
        def _():
            ref = pl.ds(1, 3)
            remote(ga.at[k, ref], upa.at[k, ref], send_a.at[k], recv_a.at[k, UP], up).start()

        @pl.when(z == 3)
        def _():
            ref = pl.ds(0, 3)
            remote(ga.at[k, ref], dna.at[k, ref], send_a.at[k], recv_a.at[k, DOWN], down).start()

    def second(c, k):
        def add(buf, yy, xx, half):
            for block in range(4):
                buf[k, block] = total_of(buf[k, block], gz[k, block, yy, xx, half, :]).astype(BF16)

        plane_second(add, k, (xdz, ydz, xbz, ybz), send_z, recv_z)
        pl.when(z == 1)(lambda: line_up(1, upa, add_a(k), k, send_a, recv_a))
        pl.when(z == 2)(lambda: line_down(2, dna, add_a(k), k, send_a, recv_a))

    def third(c, k):
        for buf, kind in ((xaz, XA), (yaz, YA), (xbz, XB), (ybz, YB)):
            arrived(buf.at[k], recv_z.at[k, kind])
        for block in range(4):
            for half, one, two in ((low, xaz, ybz), (high, yaz, xbz)):
                gz[k, block, y, x, half, :] = total_of(
                    gz[k, block, y, x, half, :], one[k, block], two[k, block]
                ).astype(BF16)

        @pl.when(z == 0)
        def _():
            ref = pl.ds(1, 3)
            remote(
                gz.at[k, ref, y, x], upz.at[k, ref], send_z.at[k], recv_z.at[k, UP], up
            ).start()

        @pl.when(z == 3)
        def _():
            ref = pl.ds(0, 3)
            remote(
                gz.at[k, ref, y, x], dnz.at[k, ref], send_z.at[k], recv_z.at[k, DOWN], down
            ).start()

        pl.when(z == 2)(lambda: line_up(2, upa, add_a(k), k, send_a, recv_a))
        pl.when(z == 1)(lambda: line_down(1, dna, add_a(k), k, send_a, recv_a))

    def fourth(c, k):
        pl.when(z == 1)(lambda: line_up(1, upz, add_z(k), k, send_z, recv_z))
        pl.when(z == 2)(lambda: line_down(2, dnz, add_z(k), k, send_z, recv_z))
        pl.when(z == 3)(lambda: line_up(3, upa, None, k, send_a, recv_a))
        pl.when(z == 0)(lambda: line_down(0, dna, None, k, send_a, recv_a))
        for buf, exists in ((upa, has_down), (dna, has_up)):

            @pl.when(exists)
            def _():
                for yy in range(2):
                    for xx in range(2):
                        ga[k, z, yy, xx] = total_of(ga[k, z, yy, xx], buf[k, z, yy, xx]).astype(BF16)

        plane_first(
            lambda yy, xx, half: ga.at[k, z, yy, xx, half, :], k, (xda, yda, xaa, yaa), send_a, recv_a
        )

    def fifth(c, k):
        pl.when(z == 2)(lambda: line_up(2, upz, add_z(k), k, send_z, recv_z))
        pl.when(z == 1)(lambda: line_down(1, dnz, add_z(k), k, send_z, recv_z))

        def add(buf, yy, xx, half):
            buf[k] = total_of(buf[k], ga[k, z, yy, xx, half, :]).astype(BF16)

        plane_second(add, k, (xda, yda, xba, yba), send_a, recv_a)

    def finish(c, k):
        pl.when(z == 3)(lambda: line_up(3, upz, None, k, send_z, recv_z))
        pl.when(z == 0)(lambda: line_down(0, dnz, None, k, send_z, recv_z))
        o = lax.rem(c, 2)

        @pl.when(c >= 2)
        def _():
            for copy in out_copies(c - 2):
                copy.wait()

        oz[o] = gz[k, z, y, x].astype(F32)
        for buf, exists in ((upz, has_down), (dnz, has_up)):

            @pl.when(exists)
            def _():
                oz[o] = oz[o] + buf[k, z].astype(F32)

        for buf, kind in ((xaa, XA), (yaa, YA), (xba, XB), (yba, YB)):
            arrived(buf.at[k], recv_a.at[k, kind])
        oa[o, low, :] = total_of(ga[k, z, y, x, low, :], xaa[k], yba[k])
        oa[o, high, :] = total_of(ga[k, z, y, x, high, :], yaa[k], xba[k])
        for copy in out_copies(c):
            copy.start()
        for buf in (xdz, ydz, xaz, yaz, xbz, ybz):
            sent(buf.at[k], send_z.at[k])
        for buf in (xda, yda, xaa, yaa, xba, yba):
            sent(buf.at[k], send_a.at[k])
        for step in range(3):

            @pl.when(z == step)
            def _():
                sent(upz.at[k, pl.ds(step + 1, 3 - step)], send_z.at[k])
                sent(upa.at[k, pl.ds(step + 1, 3 - step)], send_a.at[k])

            @pl.when(z == 3 - step)
            def _():
                sent(dnz.at[k, pl.ds(0, 3 - step)], send_z.at[k])
                sent(dna.at[k, pl.ds(0, 3 - step)], send_a.at[k])

        @pl.when(c < total - slots)
        def _():
            signal_neighbours([credit.at[i] for i in (0, 1, 3, 2)], near, has_up, has_down)

    stages = (start_load, begin, second, third, fourth, fifth, finish)

    def body(turn, carry):
        for step, stage in enumerate(stages):
            c = turn - step

            @pl.when((c >= 0) & (c < total))
            def _():
                stage(c, lax.rem(c, slots))

        return carry

    lax.fori_loop(0, total + len(stages) - 1, body, 0)
    for c in (total - 2, total - 1):
        for copy in out_copies(jnp.int32(c)):
            copy.wait()


def scatter_all(grads, places, width_z, width_a, slots):
    rows = grads[0].shape[3]
    columns = len(places) * (width_z + width_a)
    dma = pltpu.SemaphoreType.DMA

    def buffer(*shape, dtype=BF16):
        return pltpu.VMEM((slots,) + shape, dtype)

    return pl.pallas_call(
        functools.partial(scatter_kernel, places, width_z, width_a, slots),
        out_shape=jax.ShapeDtypeStruct((rows, columns), F32),
        in_specs=[pl.BlockSpec(memory_space=pl.ANY)] * len(grads),
        out_specs=pl.BlockSpec(memory_space=pl.ANY),
        scratch_shapes=[
            buffer(4, 2, 2, rows, width_z),
            buffer(4, 2, 2, rows, width_a),
            *[buffer(4, rows // 2, width_z)] * 6,
            *[buffer(4, rows, width_z)] * 2,
            *[buffer(rows // 2, width_a)] * 6,
            *[buffer(4, 2, 2, rows, width_a)] * 2,
            pltpu.VMEM((2, rows, width_z), F32),
            pltpu.VMEM((2, rows, width_a), F32),
            dma((slots, 2)),
            dma((2, 2)),
            dma((slots,)),
            dma((slots,)),
            dma((slots, 8)),
            dma((slots, 8)),
            pltpu.SemaphoreType.REGULAR((4,)),
        ],
        compiler_params=pltpu.CompilerParams(
            collective_id=1, has_side_effects=True, vmem_limit_bytes=VMEM_LIMIT
        ),
        name="scatter_gradients",
    )(*grads)


def sum_cores(values):
    return values + lax.ppermute(values, "tensor", [(0, 1), (1, 0)])


def weight_grad_t(source_rows, grad_rows):
    return jnp.einsum(
        "cli,cla->ia", source_rows, grad_rows, preferred_element_type=jnp.float32
    ).astype(BF16)


def project_t(row_data, weight):
    return jnp.einsum("cli,io->clo", row_data, weight, preferred_element_type=jnp.float32)


def input_grad_t(grad_rows, weight):
    return jnp.einsum("cla,ia->cli", grad_rows, weight, preferred_element_type=jnp.float32)


def gather_plan(columns):
    chunks, since = [], 0
    for array, width in enumerate(columns):
        size = 768 if width % 768 == 0 else width
        for first in range(0, width, size):
            since += 1
            family = "A" if since % 5 == 3 and size == 768 else "Z"
            chunks.append((array, first, size, family))
    return tuple(chunks)


def scatter_plan(columns, width):
    return tuple((array, first) for array, all_of in enumerate(columns) for first in range(0, all_of, width))


def local_fast(
    hidden_in,
    text_states,
    norm1_gain,
    norm1_bias,
    self_query,
    self_key,
    self_value,
    self_out,
    norm2_gain,
    norm2_bias,
    cross_query,
    cross_key,
    cross_value,
    cross_out,
    norm3_gain,
    norm3_bias,
    hidden_up,
    hidden_down,
    cotangent,
):
    width = norm1_gain.shape[0] * 16
    norms = jnp.stack([norm1_gain, norm1_bias, norm2_gain, norm2_bias, norm3_gain, norm3_bias], axis=1)
    norms = jnp.pad(norms, ((0, 0), (0, 122)))
    shards = (
        norms,
        self_query.T,
        self_key.T,
        self_value.T,
        self_out,
        cross_query.T,
        cross_key.T,
        cross_value.T,
        cross_out,
        hidden_up.T,
        hidden_down,
    )
    gathered = gather_all(shards, gather_plan([s.shape[1] for s in shards]))
    gathered = [g.reshape(width, g.shape[-1]) for g in gathered]
    norms = gathered[0][:, :6].T.astype(jnp.float32)
    gain_self, bias_self, gain_cross, bias_cross, gain_ffn, bias_ffn = [norms[i] for i in range(6)]
    w_q, w_k, w_v, w_o, w_cq, w_ck, w_cv, w_co, w_up, w_down = gathered[1:]
    stream_one = hidden_in.astype(jnp.float32)
    key_two = split_heads(project_t(text_states, w_ck).astype(jnp.bfloat16))
    value_two = split_heads(project_t(text_states, w_cv).astype(jnp.bfloat16))
    normed_one = gather_rows(layer_norm(stream_one, gain_self, bias_self).astype(jnp.bfloat16))
    query_one = split_heads(project_t(normed_one, w_q).astype(jnp.bfloat16))
    key_one = split_heads(project_t(normed_one, w_k).astype(jnp.bfloat16))
    value_one = split_heads(project_t(normed_one, w_v).astype(jnp.bfloat16))
    attended_one, logsum_one = attend(query_one, key_one, value_one, True)
    stream_two = stream_one + scatter_rows(project(flatten_heads(attended_one), w_o))
    normed_two = gather_rows(layer_norm(stream_two, gain_cross, bias_cross).astype(jnp.bfloat16))
    query_two = split_heads(project_t(normed_two, w_cq).astype(jnp.bfloat16))
    attended_two, logsum_two = attend(query_two, key_two, value_two, False)
    stream_three = stream_two + scatter_rows(project(flatten_heads(attended_two), w_co))
    normed_three = gather_rows(layer_norm(stream_three, gain_ffn, bias_ffn).astype(jnp.bfloat16))
    upper = project_t(normed_three, w_up)
    active = gelu_exact(upper).astype(jnp.bfloat16)
    layer_out = (stream_three + scatter_rows(project(active, w_down))).astype(jnp.bfloat16)
    grad_three = cotangent.astype(jnp.float32)
    grad_branch = gather_grads(grad_three.astype(jnp.bfloat16))
    grad_down = weight_grad_t(grad_branch, active)
    grad_active = jnp.einsum("clo,of->clf", grad_branch, w_down, preferred_element_type=jnp.float32)
    grad_upper = jax.vjp(gelu_exact, upper)[1](grad_active)[0].astype(jnp.bfloat16)
    grad_up = weight_grad_t(normed_three, grad_upper)
    norm_back = jax.vjp(layer_norm, stream_three, gain_ffn, bias_ffn)[1]
    grad_stream, grad_gain_ffn, grad_bias_ffn = norm_back(
        scatter_grads(input_grad_t(grad_upper, w_up))
    )
    grad_two = grad_three + grad_stream
    grad_branch = gather_grads(grad_two.astype(jnp.bfloat16))
    grad_out_cross, grad_attended = heads_grads(grad_branch, attended_two, w_co)
    grad_query, grad_key, grad_value = attend_back(
        query_two, key_two, value_two, grad_attended, logsum_two, False
    )
    grad_query = flatten_heads(grad_query).astype(jnp.bfloat16)
    grad_key = flatten_heads(grad_key).astype(jnp.bfloat16)
    grad_value = flatten_heads(grad_value).astype(jnp.bfloat16)
    grad_query_cross = weight_grad_t(normed_two, grad_query)
    grad_key_cross = weight_grad_t(text_states, grad_key)
    grad_value_cross = weight_grad_t(text_states, grad_value)
    text_part = input_grad_t(grad_key, w_ck) + input_grad_t(grad_value, w_cv)
    grad_text = lax.psum_scatter(
        text_part.astype(jnp.bfloat16), "tensor", scatter_dimension=2, tiled=True
    ).astype(jnp.float32)
    norm_back = jax.vjp(layer_norm, stream_two, gain_cross, bias_cross)[1]
    grad_stream, grad_gain_cross, grad_bias_cross = norm_back(
        scatter_grads(input_grad_t(grad_query, w_cq))
    )
    grad_one = grad_two + grad_stream
    grad_branch = gather_grads(grad_one.astype(jnp.bfloat16))
    grad_out_self, grad_attended = heads_grads(grad_branch, attended_one, w_o)
    grad_query, grad_key, grad_value = attend_back(
        query_one, key_one, value_one, grad_attended, logsum_one, True
    )
    grad_query = flatten_heads(grad_query).astype(jnp.bfloat16)
    grad_key = flatten_heads(grad_key).astype(jnp.bfloat16)
    grad_value = flatten_heads(grad_value).astype(jnp.bfloat16)
    grad_query_self = weight_grad_t(normed_one, grad_query)
    grad_key_self = weight_grad_t(normed_one, grad_key)
    grad_value_self = weight_grad_t(normed_one, grad_value)
    grad_normed = (
        input_grad_t(grad_query, w_q) + input_grad_t(grad_key, w_k) + input_grad_t(grad_value, w_v)
    )
    norm_back = jax.vjp(layer_norm, stream_one, gain_self, bias_self)[1]
    grad_stream, grad_gain_self, grad_bias_self = norm_back(scatter_grads(grad_normed))
    grad_input = grad_one + grad_stream
    norm_grads = jnp.stack(
        [
            grad_gain_self,
            grad_bias_self,
            grad_gain_cross,
            grad_bias_cross,
            grad_gain_ffn,
            grad_bias_ffn,
        ],
        axis=1,
    )
    norm_grads = jnp.pad(norm_grads, ((0, 0), (0, 122)))
    norm_sums = sum_cores(lax.psum_scatter(norm_grads, "dp", scatter_dimension=0, tiled=True)).T
    grads = (
        grad_down,
        grad_up,
        grad_out_cross.astype(BF16),
        grad_query_cross,
        grad_key_cross,
        grad_value_cross,
        grad_out_self.astype(BF16),
        grad_query_self,
        grad_key_self,
        grad_value_self,
    )
    columns = [g.shape[1] for g in grads]
    summed = scatter_all(
        [g.reshape(4, 2, 2, width // 16, g.shape[1]) for g in grads],
        scatter_plan(columns, 768),
        640,
        128,
        8,
    )
    pieces, first = [], 0
    for count in columns:
        pieces.append(summed[:, first : first + count])
        first += count
    down, up, out_cross, query_cross, key_cross, value_cross, out_self, query, key, value = pieces
    return (
        layer_out,
        grad_input,
        grad_text,
        norm_sums[0],
        norm_sums[1],
        query.T,
        key.T,
        value.T,
        out_self,
        norm_sums[2],
        norm_sums[3],
        query_cross.T,
        key_cross.T,
        value_cross.T,
        out_cross,
        norm_sums[4],
        norm_sums[5],
        up.T,
        down,
    )


def solution(mesh):
    placed = (
        P("dp", "tensor", None),
        P("dp", None, None),
        P("dp"),
        P("dp"),
        P("tensor", "dp"),
        P("tensor", "dp"),
        P("tensor", "dp"),
        P("dp", "tensor"),
        P("dp"),
        P("dp"),
        P("tensor", "dp"),
        P("tensor", "dp"),
        P("tensor", "dp"),
        P("dp", "tensor"),
        P("dp"),
        P("dp"),
        P("tensor", "dp"),
        P("dp", "tensor"),
        P("dp", "tensor", None),
    )
    fast = dict(mesh.shape) == {"dp": 16, "tensor": 2}
    return jax.shard_map(
        local_fast if fast else local_generic,
        mesh=mesh,
        in_specs=placed,
        out_specs=(
            P("dp", "tensor", None),
            P("dp", "tensor", None),
            P("dp", None, "tensor"),
            P("dp"),
            P("dp"),
            P("tensor", "dp"),
            P("tensor", "dp"),
            P("tensor", "dp"),
            P("dp", "tensor"),
            P("dp"),
            P("dp"),
            P("tensor", "dp"),
            P("tensor", "dp"),
            P("tensor", "dp"),
            P("dp", "tensor"),
            P("dp"),
            P("dp"),
            P("tensor", "dp"),
            P("dp", "tensor"),
        ),
        check_vma=False,
    )
```

```python
import functools

import jax
import jax.numpy as jnp
from jax import lax
from jax.experimental import pallas as pl
from jax.experimental.pallas import tpu as pltpu
from jax.sharding import PartitionSpec as P

HEAD_DIM = 64


norm_eps = 1e-05
score_scale = 0.125


def layer_norm(values, gain, shift):
    centre = jnp.mean(values, axis=-1, keepdims=True)
    offset = values - centre
    spread = jnp.mean(offset * offset, axis=-1, keepdims=True)
    return offset * lax.rsqrt(spread + norm_eps) * gain + shift


def gelu_exact(values):
    return jax.nn.gelu(values, approximate=False)


def project(row_data, weight):
    return jnp.einsum("cli,oi->clo", row_data, weight, preferred_element_type=jnp.float32)


def split_heads(values):
    return values.reshape(values.shape[0], values.shape[1], -1, HEAD_DIM)


def flatten_heads(values):
    return values.reshape(values.shape[0], values.shape[1], -1)


def causal_keep(first_row, count, length):
    row_ids = first_row + lax.broadcasted_iota(jnp.int32, (count, length), 0)
    col_ids = lax.broadcasted_iota(jnp.int32, (count, length), 1)
    return col_ids <= row_ids


def block_scores(queries, key_rows, first_row, block_rows, key_end, causal):
    scores = (
        jnp.einsum(
            "cqhe,ckhe->chqk",
            queries[:, first_row : first_row + block_rows],
            key_rows[:, :key_end],
            preferred_element_type=jnp.float32,
        )
        * score_scale
    )
    if causal:
        scores = jnp.where(causal_keep(first_row, block_rows, key_end), scores, -1e30)
    return scores


def attend(queries, key_rows, val_rows, causal):
    length = queries.shape[1]
    block_rows = min(512, length)
    outputs = []
    log_sums = []
    for block_num in range(length // block_rows):
        first_row = block_num * block_rows
        key_end = first_row + block_rows if causal else key_rows.shape[1]
        scores = block_scores(queries, key_rows, first_row, block_rows, key_end, causal)
        row_peak = jnp.max(scores, axis=-1, keepdims=True)
        exp_scores = jnp.exp(scores - row_peak)
        row_total = jnp.sum(exp_scores, axis=-1, keepdims=True)
        soft_weights = (exp_scores / row_total).astype(jnp.bfloat16)
        outputs.append(
            jnp.einsum(
                "chqk,ckhe->cqhe",
                soft_weights,
                val_rows[:, :key_end],
                preferred_element_type=jnp.float32,
            ).astype(jnp.bfloat16)
        )
        log_sums.append((row_peak + jnp.log(row_total))[..., 0])
    return (jnp.concatenate(outputs, axis=1), jnp.concatenate(log_sums, axis=2))


def attend_back(queries, key_rows, val_rows, grad_out, log_sums, causal):
    length = queries.shape[1]
    block_rows = min(512, length)
    grad_keys = jnp.zeros(key_rows.shape, jnp.float32)
    grad_vals = jnp.zeros(val_rows.shape, jnp.float32)
    grad_queries = []
    for block_num in range(length // block_rows):
        first_row = block_num * block_rows
        key_end = first_row + block_rows if causal else key_rows.shape[1]
        query_blk = queries[:, first_row : first_row + block_rows]
        grad_blk = grad_out[:, first_row : first_row + block_rows]
        scores = block_scores(queries, key_rows, first_row, block_rows, key_end, causal)
        soft = jnp.exp(scores - log_sums[:, :, first_row : first_row + block_rows, None])
        grad_soft = jnp.einsum(
            "cqhe,ckhe->chqk", grad_blk, val_rows[:, :key_end], preferred_element_type=jnp.float32
        )
        grad_vals = grad_vals.at[:, :key_end].add(
            jnp.einsum(
                "chqk,cqhe->ckhe",
                soft.astype(jnp.bfloat16),
                grad_blk,
                preferred_element_type=jnp.float32,
            )
        )
        inner = jnp.sum(soft * grad_soft, axis=-1, keepdims=True)
        grad_scores = (soft * (grad_soft - inner)).astype(jnp.bfloat16)
        grad_queries.append(
            jnp.einsum(
                "chqk,ckhe->cqhe",
                grad_scores,
                key_rows[:, :key_end],
                preferred_element_type=jnp.float32,
            )
            * score_scale
        )
        grad_keys = grad_keys.at[:, :key_end].add(
            jnp.einsum(
                "chqk,cqhe->ckhe", grad_scores, query_blk, preferred_element_type=jnp.float32
            )
            * score_scale
        )
    return (jnp.concatenate(grad_queries, axis=1), grad_keys, grad_vals)


def gather_rows(values):
    return lax.all_gather(values, "tensor", axis=1, tiled=True)


def scatter_rows(values):
    return lax.psum_scatter(values, "tensor", scatter_dimension=1, tiled=True)


def gather_grads(values):
    return lax.all_gather(values, "tensor", axis=1, tiled=True)


def scatter_grads(values):
    return lax.psum_scatter(
        values.astype(jnp.bfloat16), "tensor", scatter_dimension=1, tiled=True
    ).astype(jnp.float32)


def heads_grads(grad_branch, attended, out_weight):
    grad_out_proj = jnp.einsum(
        "clo,cla->oa", grad_branch, flatten_heads(attended), preferred_element_type=jnp.float32
    )
    grad_attended = split_heads(
        jnp.einsum(
            "clo,oa->cla", grad_branch, out_weight, preferred_element_type=jnp.float32
        ).astype(jnp.bfloat16)
    )
    return (grad_out_proj, grad_attended)


def weight_grad(grad_rows, source_rows):
    return jnp.einsum("cla,cli->ai", grad_rows, source_rows, preferred_element_type=jnp.float32)


def input_grad(grad_rows, weight):
    return jnp.einsum("cla,ai->cli", grad_rows, weight, preferred_element_type=jnp.float32)


def local_generic(
    hidden_in,
    text_states,
    norm1_gain,
    norm1_bias,
    self_query,
    self_key,
    self_value,
    self_out,
    norm2_gain,
    norm2_bias,
    cross_query,
    cross_key,
    cross_value,
    cross_out,
    norm3_gain,
    norm3_bias,
    hidden_up,
    hidden_down,
    cotangent,
):
    full_weights = (
        lax.all_gather(norm1_gain, "dp", axis=0, tiled=True),
        lax.all_gather(norm1_bias, "dp", axis=0, tiled=True),
        lax.all_gather(self_query, "dp", axis=1, tiled=True),
        lax.all_gather(self_key, "dp", axis=1, tiled=True),
        lax.all_gather(self_value, "dp", axis=1, tiled=True),
        lax.all_gather(self_out, "dp", axis=0, tiled=True),
        lax.all_gather(norm2_gain, "dp", axis=0, tiled=True),
        lax.all_gather(norm2_bias, "dp", axis=0, tiled=True),
        lax.all_gather(cross_query, "dp", axis=1, tiled=True),
        lax.all_gather(cross_key, "dp", axis=1, tiled=True),
        lax.all_gather(cross_value, "dp", axis=1, tiled=True),
        lax.all_gather(cross_out, "dp", axis=0, tiled=True),
        lax.all_gather(norm3_gain, "dp", axis=0, tiled=True),
        lax.all_gather(norm3_bias, "dp", axis=0, tiled=True),
        lax.all_gather(hidden_up, "dp", axis=1, tiled=True),
        lax.all_gather(hidden_down, "dp", axis=0, tiled=True),
    )
    gain_self = full_weights[0].astype(jnp.float32)
    bias_self = full_weights[1].astype(jnp.float32)
    gain_cross = full_weights[6].astype(jnp.float32)
    bias_cross = full_weights[7].astype(jnp.float32)
    gain_ffn = full_weights[12].astype(jnp.float32)
    bias_ffn = full_weights[13].astype(jnp.float32)
    stream_one = hidden_in.astype(jnp.float32)
    key_two = split_heads(project(text_states, full_weights[9]).astype(jnp.bfloat16))
    value_two = split_heads(project(text_states, full_weights[10]).astype(jnp.bfloat16))
    normed_one = gather_rows(layer_norm(stream_one, gain_self, bias_self).astype(jnp.bfloat16))
    query_one = split_heads(project(normed_one, full_weights[2]).astype(jnp.bfloat16))
    key_one = split_heads(project(normed_one, full_weights[3]).astype(jnp.bfloat16))
    value_one = split_heads(project(normed_one, full_weights[4]).astype(jnp.bfloat16))
    attended_one, logsum_one = attend(query_one, key_one, value_one, True)
    stream_two = stream_one + scatter_rows(project(flatten_heads(attended_one), full_weights[5]))
    normed_two = gather_rows(layer_norm(stream_two, gain_cross, bias_cross).astype(jnp.bfloat16))
    query_two = split_heads(project(normed_two, full_weights[8]).astype(jnp.bfloat16))
    attended_two, logsum_two = attend(query_two, key_two, value_two, False)
    stream_three = stream_two + scatter_rows(project(flatten_heads(attended_two), full_weights[11]))
    normed_three = gather_rows(layer_norm(stream_three, gain_ffn, bias_ffn).astype(jnp.bfloat16))
    upper = project(normed_three, full_weights[14])
    active = gelu_exact(upper).astype(jnp.bfloat16)
    layer_out = (stream_three + scatter_rows(project(active, full_weights[15]))).astype(
        jnp.bfloat16
    )
    grad_three = cotangent.astype(jnp.float32)
    grad_branch = gather_grads(grad_three.astype(jnp.bfloat16))
    grad_down = jnp.einsum("clo,clf->of", grad_branch, active, preferred_element_type=jnp.float32)
    grad_active = jnp.einsum(
        "clo,of->clf", grad_branch, full_weights[15], preferred_element_type=jnp.float32
    )
    grad_upper = jax.vjp(gelu_exact, upper)[1](grad_active)[0].astype(jnp.bfloat16)
    grad_up = weight_grad(grad_upper, normed_three)
    norm_back = jax.vjp(layer_norm, stream_three, gain_ffn, bias_ffn)[1]
    grad_stream, grad_gain_ffn, grad_bias_ffn = norm_back(
        scatter_grads(input_grad(grad_upper, full_weights[14]))
    )
    grad_two = grad_three + grad_stream
    grad_branch = gather_grads(grad_two.astype(jnp.bfloat16))
    grad_out_cross, grad_attended = heads_grads(grad_branch, attended_two, full_weights[11])
    grad_query, grad_key, grad_value = attend_back(
        query_two, key_two, value_two, grad_attended, logsum_two, False
    )
    grad_query = flatten_heads(grad_query).astype(jnp.bfloat16)
    grad_key = flatten_heads(grad_key).astype(jnp.bfloat16)
    grad_value = flatten_heads(grad_value).astype(jnp.bfloat16)
    grad_query_cross = weight_grad(grad_query, normed_two)
    grad_key_cross = weight_grad(grad_key, text_states)
    grad_value_cross = weight_grad(grad_value, text_states)
    text_part = input_grad(grad_key, full_weights[9]) + input_grad(grad_value, full_weights[10])
    grad_text = lax.psum_scatter(
        text_part.astype(jnp.bfloat16), "tensor", scatter_dimension=2, tiled=True
    ).astype(jnp.float32)
    norm_back = jax.vjp(layer_norm, stream_two, gain_cross, bias_cross)[1]
    grad_stream, grad_gain_cross, grad_bias_cross = norm_back(
        scatter_grads(input_grad(grad_query, full_weights[8]))
    )
    grad_one = grad_two + grad_stream
    grad_branch = gather_grads(grad_one.astype(jnp.bfloat16))
    grad_out_self, grad_attended = heads_grads(grad_branch, attended_one, full_weights[5])
    grad_query, grad_key, grad_value = attend_back(
        query_one, key_one, value_one, grad_attended, logsum_one, True
    )
    grad_query = flatten_heads(grad_query).astype(jnp.bfloat16)
    grad_key = flatten_heads(grad_key).astype(jnp.bfloat16)
    grad_value = flatten_heads(grad_value).astype(jnp.bfloat16)
    grad_query_self = weight_grad(grad_query, normed_one)
    grad_key_self = weight_grad(grad_key, normed_one)
    grad_value_self = weight_grad(grad_value, normed_one)
    grad_normed = (
        input_grad(grad_query, full_weights[2])
        + input_grad(grad_key, full_weights[3])
        + input_grad(grad_value, full_weights[4])
    )
    norm_back = jax.vjp(layer_norm, stream_one, gain_self, bias_self)[1]
    grad_stream, grad_gain_self, grad_bias_self = norm_back(scatter_grads(grad_normed))
    grad_input = grad_one + grad_stream
    summed = (
        lax.psum_scatter(
            grad_gain_self.astype(jnp.bfloat16), "dp", scatter_dimension=0, tiled=True
        ).astype(jnp.float32),
        lax.psum_scatter(
            grad_bias_self.astype(jnp.bfloat16), "dp", scatter_dimension=0, tiled=True
        ).astype(jnp.float32),
        lax.psum_scatter(
            grad_query_self.astype(jnp.bfloat16), "dp", scatter_dimension=1, tiled=True
        ).astype(jnp.float32),
        lax.psum_scatter(
            grad_key_self.astype(jnp.bfloat16), "dp", scatter_dimension=1, tiled=True
        ).astype(jnp.float32),
        lax.psum_scatter(
            grad_value_self.astype(jnp.bfloat16), "dp", scatter_dimension=1, tiled=True
        ).astype(jnp.float32),
        lax.psum_scatter(
            grad_out_self.astype(jnp.bfloat16), "dp", scatter_dimension=0, tiled=True
        ).astype(jnp.float32),
        lax.psum_scatter(
            grad_gain_cross.astype(jnp.bfloat16), "dp", scatter_dimension=0, tiled=True
        ).astype(jnp.float32),
        lax.psum_scatter(
            grad_bias_cross.astype(jnp.bfloat16), "dp", scatter_dimension=0, tiled=True
        ).astype(jnp.float32),
        lax.psum_scatter(
            grad_query_cross.astype(jnp.bfloat16), "dp", scatter_dimension=1, tiled=True
        ).astype(jnp.float32),
        lax.psum_scatter(
            grad_key_cross.astype(jnp.bfloat16), "dp", scatter_dimension=1, tiled=True
        ).astype(jnp.float32),
        lax.psum_scatter(
            grad_value_cross.astype(jnp.bfloat16), "dp", scatter_dimension=1, tiled=True
        ).astype(jnp.float32),
        lax.psum_scatter(
            grad_out_cross.astype(jnp.bfloat16), "dp", scatter_dimension=0, tiled=True
        ).astype(jnp.float32),
        lax.psum_scatter(
            grad_gain_ffn.astype(jnp.bfloat16), "dp", scatter_dimension=0, tiled=True
        ).astype(jnp.float32),
        lax.psum_scatter(
            grad_bias_ffn.astype(jnp.bfloat16), "dp", scatter_dimension=0, tiled=True
        ).astype(jnp.float32),
        lax.psum_scatter(
            grad_up.astype(jnp.bfloat16), "dp", scatter_dimension=1, tiled=True
        ).astype(jnp.float32),
        lax.psum_scatter(
            grad_down.astype(jnp.bfloat16), "dp", scatter_dimension=0, tiled=True
        ).astype(jnp.float32),
    )
    norm_sums = lax.psum(
        (summed[0], summed[1], summed[6], summed[7], summed[12], summed[13]), "tensor"
    )
    return (
        layer_out,
        grad_input,
        grad_text,
        norm_sums[0],
        norm_sums[1],
        summed[2],
        summed[3],
        summed[4],
        summed[5],
        norm_sums[2],
        norm_sums[3],
        summed[8],
        summed[9],
        summed[10],
        summed[11],
        norm_sums[4],
        norm_sums[5],
        summed[14],
        summed[15],
    )


MESH_IDS = pl.DeviceIdType.MESH
BF16 = jnp.bfloat16
F32 = jnp.float32
VMEM_LIMIT = 60 * 2**20


def my_place():
    chip = lax.axis_index("dp")
    core = lax.axis_index("tensor")
    return (lax.rem(chip, 2), lax.rem(lax.div(chip, 2), 2), lax.div(chip, 4), core)


def neighbours(x, y, z, core):
    def device(zz, yy, xx):
        return (zz * 4 + yy * 2 + xx, core)

    return (device(z, y, 1 - x), device(z, 1 - y, x), device(z + 1, y, x), device(z - 1, y, x))


def when(cond, fn):
    if cond is None:
        fn()
    else:
        pl.when(cond)(fn)


def signal_neighbours(sems, near, has_up, has_down):
    for sem, device, cond in zip(sems, near, (None, None, has_up, has_down), strict=True):
        when(
            cond,
            functools.partial(
                pl.semaphore_signal, sem, inc=1, device_id=device, device_id_type=MESH_IDS
            ),
        )


def gather_kernel(count, chunks, *refs):
    shards, outs = refs[:count], refs[count : 2 * count]
    local_sem, send_sem, zs, xs, ys, ds = refs[2 * count :]
    x, y, z, core = my_place()
    xn, yn = 1 - x, 1 - y
    near = neighbours(x, y, z, core)
    right, across, up, down = near
    has_up, has_down = z < 3, z > 0
    barrier = pltpu.get_barrier_semaphore()
    signal_neighbours([barrier] * 4, near, has_up, has_down)
    pl.semaphore_wait(barrier, 2 + has_up.astype(jnp.int32) + has_down.astype(jnp.int32))
    total = len(chunks)
    pending = []

    half_rows = shards[0].shape[0] // 2

    def span(c):
        _, first, width, _ = chunks[c]
        return pl.ds(first, width)

    def at(zz, yy, xx, c, half=None):
        lines = slice(None) if half is None else pl.ds(half * half_rows, half_rows)
        return outs[chunks[c][0]].at[zz, yy, xx, lines, span(c)]

    def plane(zz, c):
        return outs[chunks[c][0]].at[zz, :, :, :, span(c)]

    def own(c):
        return shards[chunks[c][0]].at[:, span(c)]

    local = [pltpu.make_async_copy(own(c), at(z, y, x, c), local_sem.at[c]) for c in range(total)]

    def remote(src, dst, sem, device):
        return pltpu.make_async_remote_copy(
            src_ref=src,
            dst_ref=dst,
            send_sem=send_sem,
            recv_sem=sem,
            device_id=device,
            device_id_type=MESH_IDS,
        )

    def send(src, dst, sem, device, cond=None):
        copy = remote(src, dst, sem, device)
        when(cond, copy.start)
        pending.append((cond, copy))

    def wait(ref, sem, cond=None):
        when(cond, remote(ref, ref, sem, right).wait_recv)

    def lines(step):
        for sign, device, more in ((-1, up, has_up), (1, down, has_down)):
            block = z + sign * step
            yield block, (block >= 0) if sign < 0 else (block <= 3), device, more

    def stage_z(c, step):
        if step == 0:
            send(own(c), at(z, y, x, c), zs.at[c, z], up, has_up)
            send(own(c), at(z, y, x, c), zs.at[c, z], down, has_down)
            send(own(c), at(z, y, x, c), xs.at[c, z], right)
            send(own(c), at(z, y, x, c), ys.at[c, z], across)
            local[c].start()
        if 1 <= step <= 3:
            for block, exists, device, more in lines(step):
                ref = at(block, y, x, c)
                wait(ref, zs.at[c, block], exists)
                if step < 3:
                    send(ref, ref, zs.at[c, block], device, exists & more)
                send(ref, ref, xs.at[c, block], right, exists)
                send(ref, ref, ys.at[c, block], across, exists)
        if 1 <= step <= 4:
            for block, exists, _, _ in [(z, None, None, None)] if step == 1 else lines(step - 1):
                wait(at(block, y, xn, c), xs.at[c, block], exists)
                ref = at(block, y, xn, c, 0)
                send(ref, ref, ds.at[c, block, 0], across, exists)
                wait(at(block, yn, x, c), ys.at[c, block], exists)
                ref = at(block, yn, x, c, 1)
                send(ref, ref, ds.at[c, block, 1], right, exists)
        if step == 5:
            for block in range(4):
                for half in range(2):
                    wait(at(block, yn, xn, c, half), ds.at[c, block, half])
            local[c].wait()

    def stage_a(c, step):
        if step == 0:
            send(own(c), at(z, y, x, c), xs.at[c, z], right)
            send(own(c), at(z, y, x, c), ys.at[c, z], across)
            local[c].start()
        if step == 1:
            wait(at(z, y, xn, c), xs.at[c, z])
            ref = at(z, y, xn, c, 0)
            send(ref, ref, ds.at[c, z, 0], across)
            wait(at(z, yn, x, c), ys.at[c, z])
            ref = at(z, yn, x, c, 1)
            send(ref, ref, ds.at[c, z, 1], right)
        if step == 2:
            for half in range(2):
                wait(at(z, yn, xn, c, half), ds.at[c, z, half])
            local[c].wait()
            send(plane(z, c), plane(z, c), zs.at[c, z], up, has_up)
            send(plane(z, c), plane(z, c), zs.at[c, z], down, has_down)
        if step >= 3:
            for block, exists, device, more in lines(step - 2):
                wait(plane(block, c), zs.at[c, block], exists)
                if step < 5:
                    send(plane(block, c), plane(block, c), zs.at[c, block], device, exists & more)

    stages = 6
    for turn in range(total + stages - 1):
        for step in range(stages):
            c = turn - step
            if 0 <= c < total:
                (stage_z if chunks[c][3] == "Z" else stage_a)(c, step)
    for cond, copy in pending:
        when(cond, copy.wait_send)


def gather_all(shards, chunks):
    total, count = len(chunks), len(shards)
    dma = pltpu.SemaphoreType.DMA
    return pl.pallas_call(
        functools.partial(gather_kernel, count, chunks),
        out_shape=[jax.ShapeDtypeStruct((4, 2, 2) + s.shape, s.dtype) for s in shards],
        in_specs=[pl.BlockSpec(memory_space=pl.ANY)] * count,
        out_specs=[pl.BlockSpec(memory_space=pl.ANY)] * count,
        scratch_shapes=[
            dma((total,)),
            dma,
            dma((total, 4)),
            dma((total, 4)),
            dma((total, 4)),
            dma((total, 4, 2)),
        ],
        compiler_params=pltpu.CompilerParams(collective_id=0, has_side_effects=True),
        name="gather_weights",
    )(*shards)


def total_of(*parts):
    value = parts[0].astype(F32)
    for part in parts[1:]:
        value = value + part.astype(F32)
    return value


XD, YD, XA, YA, XB, YB, UP, DOWN = range(8)


UNIT = 256
WIDTH_Z, WIDTH_A, SLOTS = 384, 128, 8
ROWS_L = 6
FIRST_L = (0, 12, 24, 27, 36, 39)
FIRST_R = ((0, 12), (12, 24), (24, 27), (27, 30), (36, 39))
TEXT_UNITS = (30, 36)
SELF_UNITS = (39, 48)
UNITS = 48


def dot_nt(left, right):
    return lax.dot_general(left, right, (((1,), (1,)), ((), ())), preferred_element_type=F32)


def dot_tn(left, right):
    return lax.dot_general(left, right, (((0,), (0,)), ((), ())), preferred_element_type=F32)


def dot_nn(left, right):
    return jnp.dot(left, right, preferred_element_type=F32)


def head_back(head, q_ref, k_ref, v_ref, do_ref, lse_ref, dqkv, acc_k, acc_v):
    width = q_ref.shape[1]
    pair, half = lax.div(head, 2), lax.rem(head, 2)
    lanes = [pl.ds(pl.multiple_of(pair * 128 + n * width, 128), 128) for n in range(3)]
    cols = lanes[0]
    mine = lax.div(lax.broadcasted_iota(jnp.int32, (1, 128), 1), 64) == half
    acc_k[...] = jnp.zeros_like(acc_k)
    acc_v[...] = jnp.zeros_like(acc_v)
    block = 256
    keep = lax.broadcasted_iota(jnp.int32, (block, block), 0) <= lax.broadcasted_iota(
        jnp.int32, (block, block), 1
    )

    def merged(rows, lane, value):
        before = jnp.where(half == 0, 0.0, dqkv[rows, lane].astype(F32))
        dqkv[rows, lane] = (before + value).astype(BF16)

    for i in range(q_ref.shape[0] // block):
        rows = pl.ds(i * block, block)
        q = jnp.where(mine, q_ref[rows, cols].astype(F32), 0.0).astype(BF16)
        do = jnp.where(mine, do_ref[rows, cols].astype(F32), 0.0).astype(BF16)
        lse = lse_ref[pl.ds(head, 1), rows]
        parts = [(i * block, block, True)]
        if i:
            parts.insert(0, (0, i * block, False))
        held, inner = [], 0.0
        for first, count, diagonal in parts:
            keys = pl.ds(first, count)
            soft = jnp.exp(dot_nt(k_ref[keys, cols], q) * score_scale - lse)
            if diagonal:
                soft = jnp.where(keep, soft, 0.0)
            slope = dot_nt(v_ref[keys, cols], do)
            inner = inner + jnp.sum(soft * slope, axis=0, keepdims=True)
            held.append((keys, soft, slope))
        grad_q = 0.0
        for keys, soft, slope in held:
            ds = (soft * (slope - inner)).astype(BF16)
            acc_v[keys, :] += dot_nn(soft.astype(BF16), do)
            acc_k[keys, :] += dot_nn(ds, q)
            grad_q = grad_q + dot_tn(ds, k_ref[keys, cols])
        merged(rows, lanes[0], jnp.where(mine, grad_q * score_scale, 0.0))
    merged(slice(None), lanes[1], acc_k[...] * score_scale)
    merged(slice(None), lanes[2], acc_v[...])


def backward_kernel(*refs):
    lefts, refs = refs[:ROWS_L], refs[ROWS_L:]
    rights, refs = refs[:5], refs[5:]
    text_h, dkv_h, q_h, k_h, v_h, do_h, lse_ref, out, dqkv_h = refs[:9]
    refs = refs[9:]
    gz, ga, xdz, ydz, xaz, yaz, xbz, ybz, upz, dnz = refs[:10]
    xda, yda, xaa, yaa, xba, yba, upa, dna, oz, oa = refs[10:20]
    lbuf, rbuf, text_v, dkv_v, q_v, k_v, v_v, do_v, dqkv, acc_k, acc_v = refs[20:31]
    first_sem, l_sem, r_sem, dqkv_sem, out_sem, send_z, send_a, recv_z, recv_a, credit = refs[31:]
    width_z, width_a, slots = WIDTH_Z, WIDTH_A, SLOTS
    total, width = UNITS // 2, WIDTH_Z + WIDTH_A
    heads = q_v.shape[1] // HEAD_DIM
    x, y, z, core = my_place()
    xn, yn = 1 - x, 1 - y
    near = neighbours(x, y, z, core)
    right, across, up, down = near
    has_up, has_down = z < 3, z > 0
    degree = 2 + has_up.astype(jnp.int32) + has_down.astype(jnp.int32)
    barrier = pltpu.get_barrier_semaphore()
    signal_neighbours([barrier] * 4, near, has_up, has_down)
    pl.semaphore_wait(barrier, degree)
    rows = gz.shape[4]
    low, high = pl.ds(0, rows // 2), pl.ds(rows // 2, rows // 2)

    def remote(src, dst, send_sem, recv_sem, device):
        return pltpu.make_async_remote_copy(
            src_ref=src,
            dst_ref=dst,
            send_sem=send_sem,
            recv_sem=recv_sem,
            device_id=device,
            device_id_type=MESH_IDS,
        )

    def arrived(ref, sem):
        remote(ref, ref, send_z.at[0], sem, right).wait_recv()

    def sent(ref, sem):
        remote(ref, ref, sem, recv_z.at[0, 0], right).wait_send()

    firsts = [
        pltpu.make_async_copy(src, dst, first_sem.at[n])
        for n, (src, dst) in enumerate(
            (
                (text_h, text_v),
                (dkv_h, dkv_v),
                (q_h, q_v),
                (k_h, k_v),
                (v_h, v_v),
                (do_h, do_v),
            )
        )
    ]

    def left_copy(n):
        return pltpu.make_async_copy(lefts[n], lbuf.at[n % 2], l_sem.at[n % 2])

    def right_copies(c, which):
        unit = 2 * c + which
        place, sem = rbuf.at[lax.rem(c, 2), which], r_sem.at[lax.rem(c, 2), which]
        for source, (lo, hi) in zip((*rights, dqkv), (*FIRST_R, SELF_UNITS), strict=True):
            first = pl.multiple_of((unit - lo) * UNIT, UNIT)
            yield (
                (unit >= lo) & (unit < hi),
                pltpu.make_async_copy(source.at[:, pl.ds(first, UNIT)], place, sem),
            )

    def start_rights(c):
        for which in range(2):
            for cond, copy in right_copies(c, which):
                pl.when(cond)(copy.start)

    def store_unit(which, k, i, value):
        for yy in range(2):
            for xx in range(2):
                first = (yy * 2 + xx) * rows
                block = value[first : first + rows, :].astype(BF16)
                if which == 0:
                    gz[k, i, yy, xx, :, pl.ds(0, UNIT)] = block
                else:
                    gz[k, i, yy, xx, :, pl.ds(UNIT, width_z - UNIT)] = block[:, : width_z - UNIT]
                    ga[k, i, yy, xx] = block[:, width_z - UNIT :]

    def compute(c, k):
        for n in range(1, ROWS_L):
            pl.when(c == FIRST_L[n] // 2)(left_copy(n).wait)
        for which in range(2):
            unit = 2 * c + which
            text = (unit >= TEXT_UNITS[0]) & (unit < TEXT_UNITS[1])
            slot = lax.rem(sum((unit >= first).astype(jnp.int32) for first in FIRST_L) + 1, 2)

            @pl.when(text)
            def _():
                first = pl.multiple_of((unit - TEXT_UNITS[0]) * UNIT, UNIT)
                right_part = dkv_v[:, pl.ds(first, UNIT)]
                for i in range(4):
                    store_unit(which, k, i, dot_tn(text_v[:, pl.ds(i * 4 * rows, 4 * rows)], right_part))

            @pl.when(jnp.logical_not(text))
            def _():
                par = lax.rem(c, 2)
                pltpu.make_async_copy(rbuf.at[par, which], rbuf.at[par, which], r_sem.at[par, which]).wait()
                right_part = rbuf[par, which]
                for i in range(4):
                    left_part = lbuf[slot, :, pl.ds(i * 4 * rows, 4 * rows)]
                    store_unit(which, k, i, dot_tn(left_part, right_part))

        for n in range(2, ROWS_L):
            pl.when(c == FIRST_L[n - 1] // 2)(left_copy(n).start)
        pl.when(c + 1 < total)(lambda: start_rights(c + 1))

    def out_copies(c):
        o = lax.rem(c, 2)
        first = pl.multiple_of(c * width, 128)
        return (
            pltpu.make_async_copy(oz.at[o], out.at[:, pl.ds(first, width_z)], out_sem.at[o, 0]),
            pltpu.make_async_copy(
                oa.at[o], out.at[:, pl.ds(first + width_z, width_a)], out_sem.at[o, 1]
            ),
        )

    def plane_first(own, k, bufs, send_sem, recv):
        xd, yd, xa, ya = bufs
        remote(own(yn, xn, low), xd.at[k], send_sem.at[k], recv.at[k, XD], right).start()
        remote(own(yn, xn, high), yd.at[k], send_sem.at[k], recv.at[k, YD], across).start()
        remote(own(y, xn, low), xa.at[k], send_sem.at[k], recv.at[k, XA], right).start()
        remote(own(yn, x, high), ya.at[k], send_sem.at[k], recv.at[k, YA], across).start()

    def plane_second(add, k, bufs, send_sem, recv):
        xd, yd, xb, yb = bufs
        arrived(xd.at[k], recv.at[k, XD])
        add(xd, yn, x, low)
        remote(xd.at[k], yb.at[k], send_sem.at[k], recv.at[k, YB], across).start()
        arrived(yd.at[k], recv.at[k, YD])
        add(yd, y, xn, high)
        remote(yd.at[k], xb.at[k], send_sem.at[k], recv.at[k, XB], right).start()

    def line_up(first, buf, add, k, send_sem, recv):
        blocks = 4 - first
        arrived(buf.at[k, pl.ds(first, blocks)], recv.at[k, UP])
        if blocks > 1:
            for block in range(first + 1, 4):
                add(buf, block)
            ref = buf.at[k, pl.ds(first + 1, blocks - 1)]
            remote(ref, ref, send_sem.at[k], recv.at[k, UP], up).start()

    def line_down(last, buf, add, k, send_sem, recv):
        arrived(buf.at[k, pl.ds(0, last + 1)], recv.at[k, DOWN])
        if last > 0:
            for block in range(last):
                add(buf, block)
            ref = buf.at[k, pl.ds(0, last)]
            remote(ref, ref, send_sem.at[k], recv.at[k, DOWN], down).start()

    def add_a(k):
        def add(buf, block):
            for yy in range(2):
                for xx in range(2):
                    buf[k, block, yy, xx] = total_of(
                        buf[k, block, yy, xx], ga[k, block, yy, xx]
                    ).astype(BF16)

        return add

    def add_z(k):
        def add(buf, block):
            buf[k, block] = total_of(buf[k, block], gz[k, block, y, x]).astype(BF16)

        return add

    def begin(c, k):
        @pl.when(c >= slots)
        def _():
            pl.semaphore_wait(credit.at[0], 1)
            pl.semaphore_wait(credit.at[1], 1)
            pl.when(has_up)(lambda: pl.semaphore_wait(credit.at[2], 1))
            pl.when(has_down)(lambda: pl.semaphore_wait(credit.at[3], 1))

        plane_first(
            lambda yy, xx, half: gz.at[k, :, yy, xx, half, :], k, (xdz, ydz, xaz, yaz), send_z, recv_z
        )

        @pl.when(z == 0)
        def _():
            ref = pl.ds(1, 3)
            remote(ga.at[k, ref], upa.at[k, ref], send_a.at[k], recv_a.at[k, UP], up).start()

        @pl.when(z == 3)
        def _():
            ref = pl.ds(0, 3)
            remote(ga.at[k, ref], dna.at[k, ref], send_a.at[k], recv_a.at[k, DOWN], down).start()

    def second(c, k):
        def add(buf, yy, xx, half):
            for block in range(4):
                buf[k, block] = total_of(buf[k, block], gz[k, block, yy, xx, half, :]).astype(BF16)

        plane_second(add, k, (xdz, ydz, xbz, ybz), send_z, recv_z)
        pl.when(z == 1)(lambda: line_up(1, upa, add_a(k), k, send_a, recv_a))
        pl.when(z == 2)(lambda: line_down(2, dna, add_a(k), k, send_a, recv_a))

    def third(c, k):
        for buf, kind in ((xaz, XA), (yaz, YA), (xbz, XB), (ybz, YB)):
            arrived(buf.at[k], recv_z.at[k, kind])
        for block in range(4):
            for half, one, two in ((low, xaz, ybz), (high, yaz, xbz)):
                gz[k, block, y, x, half, :] = total_of(
                    gz[k, block, y, x, half, :], one[k, block], two[k, block]
                ).astype(BF16)

        @pl.when(z == 0)
        def _():
            ref = pl.ds(1, 3)
            remote(
                gz.at[k, ref, y, x], upz.at[k, ref], send_z.at[k], recv_z.at[k, UP], up
            ).start()

        @pl.when(z == 3)
        def _():
            ref = pl.ds(0, 3)
            remote(
                gz.at[k, ref, y, x], dnz.at[k, ref], send_z.at[k], recv_z.at[k, DOWN], down
            ).start()

        pl.when(z == 2)(lambda: line_up(2, upa, add_a(k), k, send_a, recv_a))
        pl.when(z == 1)(lambda: line_down(1, dna, add_a(k), k, send_a, recv_a))

    def fourth(c, k):
        pl.when(z == 1)(lambda: line_up(1, upz, add_z(k), k, send_z, recv_z))
        pl.when(z == 2)(lambda: line_down(2, dnz, add_z(k), k, send_z, recv_z))
        pl.when(z == 3)(lambda: line_up(3, upa, None, k, send_a, recv_a))
        pl.when(z == 0)(lambda: line_down(0, dna, None, k, send_a, recv_a))
        for buf, exists in ((upa, has_down), (dna, has_up)):

            @pl.when(exists)
            def _():
                for yy in range(2):
                    for xx in range(2):
                        ga[k, z, yy, xx] = total_of(ga[k, z, yy, xx], buf[k, z, yy, xx]).astype(BF16)

        plane_first(
            lambda yy, xx, half: ga.at[k, z, yy, xx, half, :], k, (xda, yda, xaa, yaa), send_a, recv_a
        )

    def fifth(c, k):
        pl.when(z == 2)(lambda: line_up(2, upz, add_z(k), k, send_z, recv_z))
        pl.when(z == 1)(lambda: line_down(1, dnz, add_z(k), k, send_z, recv_z))

        def add(buf, yy, xx, half):
            buf[k] = total_of(buf[k], ga[k, z, yy, xx, half, :]).astype(BF16)

        plane_second(add, k, (xda, yda, xba, yba), send_a, recv_a)

    def finish(c, k):
        pl.when(z == 3)(lambda: line_up(3, upz, None, k, send_z, recv_z))
        pl.when(z == 0)(lambda: line_down(0, dnz, None, k, send_z, recv_z))
        o = lax.rem(c, 2)

        @pl.when(c >= 2)
        def _():
            for copy in out_copies(c - 2):
                copy.wait()

        oz[o] = gz[k, z, y, x].astype(F32)
        for buf, exists in ((upz, has_down), (dnz, has_up)):

            @pl.when(exists)
            def _():
                oz[o] = oz[o] + buf[k, z].astype(F32)

        for buf, kind in ((xaa, XA), (yaa, YA), (xba, XB), (yba, YB)):
            arrived(buf.at[k], recv_a.at[k, kind])
        oa[o, low, :] = total_of(ga[k, z, y, x, low, :], xaa[k], yba[k])
        oa[o, high, :] = total_of(ga[k, z, y, x, high, :], yaa[k], xba[k])
        for copy in out_copies(c):
            copy.start()
        for buf in (xdz, ydz, xaz, yaz, xbz, ybz):
            sent(buf.at[k], send_z.at[k])
        for buf in (xda, yda, xaa, yaa, xba, yba):
            sent(buf.at[k], send_a.at[k])
        for step in range(3):

            @pl.when(z == step)
            def _():
                sent(upz.at[k, pl.ds(step + 1, 3 - step)], send_z.at[k])
                sent(upa.at[k, pl.ds(step + 1, 3 - step)], send_a.at[k])

            @pl.when(z == 3 - step)
            def _():
                sent(dnz.at[k, pl.ds(0, 3 - step)], send_z.at[k])
                sent(dna.at[k, pl.ds(0, 3 - step)], send_a.at[k])

        @pl.when(c < total - slots)
        def _():
            signal_neighbours([credit.at[i] for i in (0, 1, 3, 2)], near, has_up, has_down)

    stages = (begin, second, third, fourth, fifth, finish)
    left_copy(0).start()
    start_rights(jnp.int32(0))
    left_copy(1).start()
    for copy in firsts:
        copy.start()
    left_copy(0).wait()
    for copy in firsts:
        copy.wait()
    dqkv_copy = pltpu.make_async_copy(dqkv, dqkv_h, dqkv_sem)

    def body(turn, carry):
        for step, stage in enumerate(stages):
            c = turn - step - 1

            @pl.when((c >= 0) & (c < total))
            def _():
                stage(c, lax.rem(c, slots))

        pl.when(turn < total)(lambda: compute(turn, lax.rem(turn, slots)))

        @pl.when((turn >= 1) & (turn <= heads))
        def _():
            head_back(turn - 1, q_v, k_v, v_v, do_v, lse_ref, dqkv, acc_k, acc_v)

        pl.when(turn == heads + 1)(dqkv_copy.start)
        return carry

    lax.fori_loop(0, total + len(stages), body, 0)
    for c in (total - 2, total - 1):
        for copy in out_copies(jnp.int32(c)):
            copy.wait()
    dqkv_copy.wait()


def backward_all(lefts, rights, text, grad_text_rows, heads_in, log_sums):
    frames, width = lefts[0].shape
    rows = width // 16
    part = heads_in[0].shape[1]
    dma = pltpu.SemaphoreType.DMA
    vmem = pltpu.VMEM

    def buffer(*shape):
        return vmem((SLOTS,) + shape, BF16)

    anywhere = pl.BlockSpec(memory_space=pl.ANY)
    inputs = (*lefts, *rights, text, grad_text_rows, *heads_in, log_sums)
    return pl.pallas_call(
        backward_kernel,
        out_shape=[
            jax.ShapeDtypeStruct((rows, UNITS * UNIT), F32),
            jax.ShapeDtypeStruct((frames, 3 * part), BF16),
        ],
        in_specs=[anywhere] * (len(inputs) - 1) + [pl.BlockSpec(memory_space=vmem)],
        out_specs=[anywhere] * 2,
        scratch_shapes=[
            buffer(4, 2, 2, rows, WIDTH_Z),
            buffer(4, 2, 2, rows, WIDTH_A),
            *[buffer(4, rows // 2, WIDTH_Z)] * 6,
            *[buffer(4, rows, WIDTH_Z)] * 2,
            *[buffer(rows // 2, WIDTH_A)] * 6,
            *[buffer(4, 2, 2, rows, WIDTH_A)] * 2,
            vmem((2, rows, WIDTH_Z), F32),
            vmem((2, rows, WIDTH_A), F32),
            vmem((2, frames, width), BF16),
            vmem((2, 2, frames, UNIT), BF16),
            vmem(text.shape, BF16),
            vmem(grad_text_rows.shape, BF16),
            *[vmem((frames, part), BF16)] * 4,
            vmem((frames, 3 * part), BF16),
            *[vmem((frames, 128), F32)] * 2,
            dma((6,)),
            dma((2,)),
            dma((2, 2)),
            dma,
            dma((2, 2)),
            dma((SLOTS,)),
            dma((SLOTS,)),
            dma((SLOTS, 8)),
            dma((SLOTS, 8)),
            pltpu.SemaphoreType.REGULAR((4,)),
        ],
        compiler_params=pltpu.CompilerParams(
            collective_id=1, has_side_effects=True, vmem_limit_bytes=VMEM_LIMIT
        ),
        name="backward",
    )(*inputs)


def sum_everywhere_kernel(values, out, got, send_sem, recv_sem):
    chip, core = lax.axis_index("dp"), lax.axis_index("tensor")
    partners = [(chip, 1 - core)]
    for bit in (1, 2, 4, 8):
        partners.append((chip + bit * (1 - 2 * lax.rem(lax.div(chip, bit), 2)), core))
    barrier = pltpu.get_barrier_semaphore()
    for device in partners:
        pl.semaphore_signal(barrier, inc=1, device_id=device, device_id_type=MESH_IDS)
    pl.semaphore_wait(barrier, len(partners))
    got[0] = values[...]
    for step, device in enumerate(partners):
        copy = pltpu.make_async_remote_copy(
            src_ref=got.at[2 * step],
            dst_ref=got.at[2 * step + 1],
            send_sem=send_sem.at[step],
            recv_sem=recv_sem.at[step],
            device_id=device,
            device_id_type=MESH_IDS,
        )
        copy.start()
        copy.wait()
        got[2 * step + 2] = got[2 * step] + got[2 * step + 1]
    out[...] = got[2 * len(partners)]


def sum_everywhere(values):
    dma = pltpu.SemaphoreType.DMA
    vmem = pl.BlockSpec(memory_space=pltpu.VMEM)
    return pl.pallas_call(
        sum_everywhere_kernel,
        out_shape=jax.ShapeDtypeStruct(values.shape, F32),
        in_specs=[vmem],
        out_specs=vmem,
        scratch_shapes=[pltpu.VMEM((11,) + values.shape, F32), dma((5,)), dma((5,))],
        compiler_params=pltpu.CompilerParams(collective_id=2, has_side_effects=True),
        name="sum_norm_gradients",
    )(values)


def project_t(row_data, weight):
    return jnp.einsum("cli,io->clo", row_data, weight, preferred_element_type=jnp.float32)


def input_grad_t(grad_rows, weight):
    return jnp.einsum("cla,ia->cli", grad_rows, weight, preferred_element_type=jnp.float32)


def other_core(values):
    return lax.ppermute(values, "tensor", [(0, 1), (1, 0)])


def share_rows(values):
    other = other_core(values)
    first = lax.axis_index("tensor") == 0
    return jnp.concatenate(
        [jnp.where(first, values, other), jnp.where(first, other, values)], axis=1
    )


def sum_rows(rows, product):
    core, half = lax.axis_index("tensor"), rows[0].shape[1] // 2
    theirs = product(*[lax.dynamic_slice_in_dim(r, (1 - core) * half, half, 1) for r in rows])
    arriving = other_core(theirs.astype(BF16))
    mine = product(*[lax.dynamic_slice_in_dim(r, core * half, half, 1) for r in rows])
    return mine + arriving.astype(F32)


def gelu_parts(values):
    below = 0.5 * (1.0 + lax.erf(values * (0.5**0.5)))
    density = jnp.exp(-0.5 * values * values) * 0.3989422804014327
    return (values * below).astype(BF16), (below + values * density).astype(BF16)


def gather_plan(columns):
    chunks, since = [], 0
    for array, width in enumerate(columns):
        size = 768 if width % 768 == 0 else width
        for first in range(0, width, size):
            since += 1
            family = "A" if since % 5 == 3 and size == 768 else "Z"
            chunks.append((array, first, size, family))
    return tuple(chunks)


def local_fast(
    hidden_in,
    text_states,
    norm1_gain,
    norm1_bias,
    self_query,
    self_key,
    self_value,
    self_out,
    norm2_gain,
    norm2_bias,
    cross_query,
    cross_key,
    cross_value,
    cross_out,
    norm3_gain,
    norm3_bias,
    hidden_up,
    hidden_down,
    cotangent,
):
    width = norm1_gain.shape[0] * 16
    norms = jnp.stack([norm1_gain, norm1_bias, norm2_gain, norm2_bias, norm3_gain, norm3_bias], axis=1)
    norms = jnp.pad(norms, ((0, 0), (0, 122)))
    shards = (
        norms,
        self_query.T,
        self_key.T,
        self_value.T,
        self_out,
        cross_query.T,
        cross_key.T,
        cross_value.T,
        cross_out,
        hidden_up.T,
    )
    w_down = lax.all_gather(hidden_down, "dp", axis=0, tiled=True)
    gathered = gather_all(shards, gather_plan([s.shape[1] for s in shards]))
    gathered = [g.reshape(width, g.shape[-1]) for g in gathered]
    norms = gathered[0][:, :6].T.astype(jnp.float32)
    gain_self, bias_self, gain_cross, bias_cross, gain_ffn, bias_ffn = [norms[i] for i in range(6)]
    w_q, w_k, w_v, w_o, w_cq, w_ck, w_cv, w_co, w_up = gathered[1:]
    stream_one = hidden_in.astype(jnp.float32)
    key_two = split_heads(project_t(text_states, w_ck).astype(jnp.bfloat16))
    value_two = split_heads(project_t(text_states, w_cv).astype(jnp.bfloat16))
    normed_one = share_rows(layer_norm(stream_one, gain_self, bias_self).astype(jnp.bfloat16))
    query_one = split_heads(project_t(normed_one, w_q).astype(jnp.bfloat16))
    key_one = split_heads(project_t(normed_one, w_k).astype(jnp.bfloat16))
    value_one = split_heads(project_t(normed_one, w_v).astype(jnp.bfloat16))
    attended_one, logsum_one = attend(query_one, key_one, value_one, True)
    stream_two = stream_one + sum_rows([flatten_heads(attended_one)], lambda r: project(r, w_o))
    normed_two = share_rows(layer_norm(stream_two, gain_cross, bias_cross).astype(jnp.bfloat16))
    query_two = split_heads(project_t(normed_two, w_cq).astype(jnp.bfloat16))
    attended_two, logsum_two = attend(query_two, key_two, value_two, False)
    stream_three = stream_two + sum_rows([flatten_heads(attended_two)], lambda r: project(r, w_co))
    normed_three = share_rows(layer_norm(stream_three, gain_ffn, bias_ffn).astype(jnp.bfloat16))
    upper = project_t(normed_three, w_up)
    active, slope = gelu_parts(upper)
    layer_out = (stream_three + sum_rows([active], lambda r: project(r, w_down))).astype(jnp.bfloat16)
    grad_three = cotangent.astype(jnp.float32)
    grad_branch = share_rows(grad_three.astype(jnp.bfloat16))
    branch_three = grad_branch
    grad_active = jnp.einsum("clo,of->clf", grad_branch, w_down, preferred_element_type=jnp.float32)
    grad_upper = (grad_active * slope.astype(F32)).astype(jnp.bfloat16)
    norm_back = jax.vjp(layer_norm, stream_three, gain_ffn, bias_ffn)[1]
    grad_stream, grad_gain_ffn, grad_bias_ffn = norm_back(
        sum_rows([grad_upper], lambda r: input_grad_t(r, w_up))
    )
    grad_two = grad_three + grad_stream
    grad_branch = share_rows(grad_two.astype(jnp.bfloat16))
    branch_two = grad_branch
    grad_attended = split_heads(
        jnp.einsum("clo,oa->cla", grad_branch, w_co, preferred_element_type=F32).astype(BF16)
    )
    grad_query, grad_key, grad_value = attend_back(
        query_two, key_two, value_two, grad_attended, logsum_two, False
    )
    grad_query = flatten_heads(grad_query).astype(jnp.bfloat16)
    grad_key = flatten_heads(grad_key).astype(jnp.bfloat16)
    grad_value = flatten_heads(grad_value).astype(jnp.bfloat16)
    grad_query_two = grad_query
    text_part = input_grad_t(grad_key, w_ck) + input_grad_t(grad_value, w_cv)
    core, half = lax.axis_index("tensor"), width // 2
    arriving = other_core(
        lax.dynamic_slice_in_dim(text_part, (1 - core) * half, half, 2).astype(BF16)
    )
    grad_text = lax.dynamic_slice_in_dim(text_part, core * half, half, 2) + arriving.astype(F32)
    norm_back = jax.vjp(layer_norm, stream_two, gain_cross, bias_cross)[1]
    grad_stream, grad_gain_cross, grad_bias_cross = norm_back(
        sum_rows([grad_query], lambda r: input_grad_t(r, w_cq))
    )
    grad_one = grad_two + grad_stream
    grad_branch = share_rows(grad_one.astype(jnp.bfloat16))
    grad_attended = jnp.einsum(
        "clo,oa->cla", grad_branch, w_o, preferred_element_type=F32
    ).astype(BF16)
    part = grad_attended.shape[2]
    summed, grad_heads = backward_all(
        [
            r[0]
            for r in (branch_three, normed_three, branch_two, normed_two, grad_branch, normed_one)
        ],
        [
            r[0]
            for r in (
                active,
                grad_upper,
                flatten_heads(attended_two),
                grad_query_two,
                flatten_heads(attended_one),
            )
        ],
        text_states[0],
        jnp.concatenate([grad_key[0], grad_value[0]], axis=1),
        [flatten_heads(query_one)[0], flatten_heads(key_one)[0], flatten_heads(value_one)[0], grad_attended[0]],
        jnp.pad(logsum_one[0], ((0, 4), (0, 0))),
    )
    grad_query, grad_key, grad_value = [
        grad_heads[None, :, n * part : (n + 1) * part] for n in range(3)
    ]
    grad_normed = sum_rows(
        [grad_query, grad_key, grad_value],
        lambda q, k, v: input_grad_t(q, w_q) + input_grad_t(k, w_k) + input_grad_t(v, w_v),
    )
    norm_back = jax.vjp(layer_norm, stream_one, gain_self, bias_self)[1]
    grad_stream, grad_gain_self, grad_bias_self = norm_back(grad_normed)
    grad_input = grad_one + grad_stream
    norm_grads = jnp.stack(
        [
            grad_gain_self,
            grad_bias_self,
            grad_gain_cross,
            grad_bias_cross,
            grad_gain_ffn,
            grad_bias_ffn,
        ]
    )
    rows = width // 16
    norm_sums = lax.dynamic_slice_in_dim(
        sum_everywhere(jnp.pad(norm_grads, ((0, 2), (0, 0)))), lax.axis_index("dp") * rows, rows, 1
    )
    columns = [hidden_down.shape[1]] * 2 + [part] * 8
    pieces, first = [], 0
    for count in columns:
        pieces.append(summed[:, first : first + count])
        first += count
    down, up, out_cross, query_cross, key_cross, value_cross, out_self, query, key, value = pieces
    return (
        layer_out,
        grad_input,
        grad_text,
        norm_sums[0],
        norm_sums[1],
        query.T,
        key.T,
        value.T,
        out_self,
        norm_sums[2],
        norm_sums[3],
        query_cross.T,
        key_cross.T,
        value_cross.T,
        out_cross,
        norm_sums[4],
        norm_sums[5],
        up.T,
        down,
    )


def solution(mesh):
    placed = (
        P("dp", "tensor", None),
        P("dp", None, None),
        P("dp"),
        P("dp"),
        P("tensor", "dp"),
        P("tensor", "dp"),
        P("tensor", "dp"),
        P("dp", "tensor"),
        P("dp"),
        P("dp"),
        P("tensor", "dp"),
        P("tensor", "dp"),
        P("tensor", "dp"),
        P("dp", "tensor"),
        P("dp"),
        P("dp"),
        P("tensor", "dp"),
        P("dp", "tensor"),
        P("dp", "tensor", None),
    )
    fast = dict(mesh.shape) == {"dp": 16, "tensor": 2}
    return jax.shard_map(
        local_fast if fast else local_generic,
        mesh=mesh,
        in_specs=placed,
        out_specs=(
            P("dp", "tensor", None),
            P("dp", "tensor", None),
            P("dp", None, "tensor"),
            P("dp"),
            P("dp"),
            P("tensor", "dp"),
            P("tensor", "dp"),
            P("tensor", "dp"),
            P("dp", "tensor"),
            P("dp"),
            P("dp"),
            P("tensor", "dp"),
            P("tensor", "dp"),
            P("tensor", "dp"),
            P("dp", "tensor"),
            P("dp"),
            P("dp"),
            P("tensor", "dp"),
            P("dp", "tensor"),
        ),
        check_vma=False,
    )
```

```python
import functools

import jax
import jax.numpy as jnp
from jax import lax
from jax.experimental import pallas as pl
from jax.experimental.pallas import tpu as pltpu
from jax.sharding import PartitionSpec as P

HEAD_DIM = 64


norm_eps = 1e-05
score_scale = 0.125


def layer_norm(values, gain, shift):
    centre = jnp.mean(values, axis=-1, keepdims=True)
    offset = values - centre
    spread = jnp.mean(offset * offset, axis=-1, keepdims=True)
    return offset * lax.rsqrt(spread + norm_eps) * gain + shift


def gelu_exact(values):
    return jax.nn.gelu(values, approximate=False)


def project(row_data, weight):
    return jnp.einsum("cli,oi->clo", row_data, weight, preferred_element_type=jnp.float32)


def split_heads(values):
    return values.reshape(values.shape[0], values.shape[1], -1, HEAD_DIM)


def flatten_heads(values):
    return values.reshape(values.shape[0], values.shape[1], -1)


def causal_keep(first_row, count, length):
    row_ids = first_row + lax.broadcasted_iota(jnp.int32, (count, length), 0)
    col_ids = lax.broadcasted_iota(jnp.int32, (count, length), 1)
    return col_ids <= row_ids


def block_scores(queries, key_rows, first_row, block_rows, key_end, causal):
    scores = (
        jnp.einsum(
            "cqhe,ckhe->chqk",
            queries[:, first_row : first_row + block_rows],
            key_rows[:, :key_end],
            preferred_element_type=jnp.float32,
        )
        * score_scale
    )
    if causal:
        scores = jnp.where(causal_keep(first_row, block_rows, key_end), scores, -1e30)
    return scores


def attend(queries, key_rows, val_rows, causal):
    length = queries.shape[1]
    block_rows = min(512, length)
    outputs = []
    log_sums = []
    for block_num in range(length // block_rows):
        first_row = block_num * block_rows
        key_end = first_row + block_rows if causal else key_rows.shape[1]
        scores = block_scores(queries, key_rows, first_row, block_rows, key_end, causal)
        row_peak = jnp.max(scores, axis=-1, keepdims=True)
        exp_scores = jnp.exp(scores - row_peak)
        row_total = jnp.sum(exp_scores, axis=-1, keepdims=True)
        soft_weights = (exp_scores / row_total).astype(jnp.bfloat16)
        outputs.append(
            jnp.einsum(
                "chqk,ckhe->cqhe",
                soft_weights,
                val_rows[:, :key_end],
                preferred_element_type=jnp.float32,
            ).astype(jnp.bfloat16)
        )
        log_sums.append((row_peak + jnp.log(row_total))[..., 0])
    return (jnp.concatenate(outputs, axis=1), jnp.concatenate(log_sums, axis=2))


def attend_back(queries, key_rows, val_rows, grad_out, log_sums, causal):
    length = queries.shape[1]
    block_rows = min(512, length)
    grad_keys = jnp.zeros(key_rows.shape, jnp.float32)
    grad_vals = jnp.zeros(val_rows.shape, jnp.float32)
    grad_queries = []
    for block_num in range(length // block_rows):
        first_row = block_num * block_rows
        key_end = first_row + block_rows if causal else key_rows.shape[1]
        query_blk = queries[:, first_row : first_row + block_rows]
        grad_blk = grad_out[:, first_row : first_row + block_rows]
        scores = block_scores(queries, key_rows, first_row, block_rows, key_end, causal)
        soft = jnp.exp(scores - log_sums[:, :, first_row : first_row + block_rows, None])
        grad_soft = jnp.einsum(
            "cqhe,ckhe->chqk", grad_blk, val_rows[:, :key_end], preferred_element_type=jnp.float32
        )
        grad_vals = grad_vals.at[:, :key_end].add(
            jnp.einsum(
                "chqk,cqhe->ckhe",
                soft.astype(jnp.bfloat16),
                grad_blk,
                preferred_element_type=jnp.float32,
            )
        )
        inner = jnp.sum(soft * grad_soft, axis=-1, keepdims=True)
        grad_scores = (soft * (grad_soft - inner)).astype(jnp.bfloat16)
        grad_queries.append(
            jnp.einsum(
                "chqk,ckhe->cqhe",
                grad_scores,
                key_rows[:, :key_end],
                preferred_element_type=jnp.float32,
            )
            * score_scale
        )
        grad_keys = grad_keys.at[:, :key_end].add(
            jnp.einsum(
                "chqk,cqhe->ckhe", grad_scores, query_blk, preferred_element_type=jnp.float32
            )
            * score_scale
        )
    return (jnp.concatenate(grad_queries, axis=1), grad_keys, grad_vals)


def gather_rows(values):
    return lax.all_gather(values, "tensor", axis=1, tiled=True)


def scatter_rows(values):
    return lax.psum_scatter(values, "tensor", scatter_dimension=1, tiled=True)


def gather_grads(values):
    return lax.all_gather(values, "tensor", axis=1, tiled=True)


def scatter_grads(values):
    return lax.psum_scatter(
        values.astype(jnp.bfloat16), "tensor", scatter_dimension=1, tiled=True
    ).astype(jnp.float32)


def heads_grads(grad_branch, attended, out_weight):
    grad_out_proj = jnp.einsum(
        "clo,cla->oa", grad_branch, flatten_heads(attended), preferred_element_type=jnp.float32
    )
    grad_attended = split_heads(
        jnp.einsum(
            "clo,oa->cla", grad_branch, out_weight, preferred_element_type=jnp.float32
        ).astype(jnp.bfloat16)
    )
    return (grad_out_proj, grad_attended)


def weight_grad(grad_rows, source_rows):
    return jnp.einsum("cla,cli->ai", grad_rows, source_rows, preferred_element_type=jnp.float32)


def input_grad(grad_rows, weight):
    return jnp.einsum("cla,ai->cli", grad_rows, weight, preferred_element_type=jnp.float32)


def local_generic(
    hidden_in,
    text_states,
    norm1_gain,
    norm1_bias,
    self_query,
    self_key,
    self_value,
    self_out,
    norm2_gain,
    norm2_bias,
    cross_query,
    cross_key,
    cross_value,
    cross_out,
    norm3_gain,
    norm3_bias,
    hidden_up,
    hidden_down,
    cotangent,
):
    full_weights = (
        lax.all_gather(norm1_gain, "dp", axis=0, tiled=True),
        lax.all_gather(norm1_bias, "dp", axis=0, tiled=True),
        lax.all_gather(self_query, "dp", axis=1, tiled=True),
        lax.all_gather(self_key, "dp", axis=1, tiled=True),
        lax.all_gather(self_value, "dp", axis=1, tiled=True),
        lax.all_gather(self_out, "dp", axis=0, tiled=True),
        lax.all_gather(norm2_gain, "dp", axis=0, tiled=True),
        lax.all_gather(norm2_bias, "dp", axis=0, tiled=True),
        lax.all_gather(cross_query, "dp", axis=1, tiled=True),
        lax.all_gather(cross_key, "dp", axis=1, tiled=True),
        lax.all_gather(cross_value, "dp", axis=1, tiled=True),
        lax.all_gather(cross_out, "dp", axis=0, tiled=True),
        lax.all_gather(norm3_gain, "dp", axis=0, tiled=True),
        lax.all_gather(norm3_bias, "dp", axis=0, tiled=True),
        lax.all_gather(hidden_up, "dp", axis=1, tiled=True),
        lax.all_gather(hidden_down, "dp", axis=0, tiled=True),
    )
    gain_self = full_weights[0].astype(jnp.float32)
    bias_self = full_weights[1].astype(jnp.float32)
    gain_cross = full_weights[6].astype(jnp.float32)
    bias_cross = full_weights[7].astype(jnp.float32)
    gain_ffn = full_weights[12].astype(jnp.float32)
    bias_ffn = full_weights[13].astype(jnp.float32)
    stream_one = hidden_in.astype(jnp.float32)
    key_two = split_heads(project(text_states, full_weights[9]).astype(jnp.bfloat16))
    value_two = split_heads(project(text_states, full_weights[10]).astype(jnp.bfloat16))
    normed_one = gather_rows(layer_norm(stream_one, gain_self, bias_self).astype(jnp.bfloat16))
    query_one = split_heads(project(normed_one, full_weights[2]).astype(jnp.bfloat16))
    key_one = split_heads(project(normed_one, full_weights[3]).astype(jnp.bfloat16))
    value_one = split_heads(project(normed_one, full_weights[4]).astype(jnp.bfloat16))
    attended_one, logsum_one = attend(query_one, key_one, value_one, True)
    stream_two = stream_one + scatter_rows(project(flatten_heads(attended_one), full_weights[5]))
    normed_two = gather_rows(layer_norm(stream_two, gain_cross, bias_cross).astype(jnp.bfloat16))
    query_two = split_heads(project(normed_two, full_weights[8]).astype(jnp.bfloat16))
    attended_two, logsum_two = attend(query_two, key_two, value_two, False)
    stream_three = stream_two + scatter_rows(project(flatten_heads(attended_two), full_weights[11]))
    normed_three = gather_rows(layer_norm(stream_three, gain_ffn, bias_ffn).astype(jnp.bfloat16))
    upper = project(normed_three, full_weights[14])
    active = gelu_exact(upper).astype(jnp.bfloat16)
    layer_out = (stream_three + scatter_rows(project(active, full_weights[15]))).astype(
        jnp.bfloat16
    )
    grad_three = cotangent.astype(jnp.float32)
    grad_branch = gather_grads(grad_three.astype(jnp.bfloat16))
    grad_down = jnp.einsum("clo,clf->of", grad_branch, active, preferred_element_type=jnp.float32)
    grad_active = jnp.einsum(
        "clo,of->clf", grad_branch, full_weights[15], preferred_element_type=jnp.float32
    )
    grad_upper = jax.vjp(gelu_exact, upper)[1](grad_active)[0].astype(jnp.bfloat16)
    grad_up = weight_grad(grad_upper, normed_three)
    norm_back = jax.vjp(layer_norm, stream_three, gain_ffn, bias_ffn)[1]
    grad_stream, grad_gain_ffn, grad_bias_ffn = norm_back(
        scatter_grads(input_grad(grad_upper, full_weights[14]))
    )
    grad_two = grad_three + grad_stream
    grad_branch = gather_grads(grad_two.astype(jnp.bfloat16))
    grad_out_cross, grad_attended = heads_grads(grad_branch, attended_two, full_weights[11])
    grad_query, grad_key, grad_value = attend_back(
        query_two, key_two, value_two, grad_attended, logsum_two, False
    )
    grad_query = flatten_heads(grad_query).astype(jnp.bfloat16)
    grad_key = flatten_heads(grad_key).astype(jnp.bfloat16)
    grad_value = flatten_heads(grad_value).astype(jnp.bfloat16)
    grad_query_cross = weight_grad(grad_query, normed_two)
    grad_key_cross = weight_grad(grad_key, text_states)
    grad_value_cross = weight_grad(grad_value, text_states)
    text_part = input_grad(grad_key, full_weights[9]) + input_grad(grad_value, full_weights[10])
    grad_text = lax.psum_scatter(
        text_part.astype(jnp.bfloat16), "tensor", scatter_dimension=2, tiled=True
    ).astype(jnp.float32)
    norm_back = jax.vjp(layer_norm, stream_two, gain_cross, bias_cross)[1]
    grad_stream, grad_gain_cross, grad_bias_cross = norm_back(
        scatter_grads(input_grad(grad_query, full_weights[8]))
    )
    grad_one = grad_two + grad_stream
    grad_branch = gather_grads(grad_one.astype(jnp.bfloat16))
    grad_out_self, grad_attended = heads_grads(grad_branch, attended_one, full_weights[5])
    grad_query, grad_key, grad_value = attend_back(
        query_one, key_one, value_one, grad_attended, logsum_one, True
    )
    grad_query = flatten_heads(grad_query).astype(jnp.bfloat16)
    grad_key = flatten_heads(grad_key).astype(jnp.bfloat16)
    grad_value = flatten_heads(grad_value).astype(jnp.bfloat16)
    grad_query_self = weight_grad(grad_query, normed_one)
    grad_key_self = weight_grad(grad_key, normed_one)
    grad_value_self = weight_grad(grad_value, normed_one)
    grad_normed = (
        input_grad(grad_query, full_weights[2])
        + input_grad(grad_key, full_weights[3])
        + input_grad(grad_value, full_weights[4])
    )
    norm_back = jax.vjp(layer_norm, stream_one, gain_self, bias_self)[1]
    grad_stream, grad_gain_self, grad_bias_self = norm_back(scatter_grads(grad_normed))
    grad_input = grad_one + grad_stream
    summed = (
        lax.psum_scatter(
            grad_gain_self.astype(jnp.bfloat16), "dp", scatter_dimension=0, tiled=True
        ).astype(jnp.float32),
        lax.psum_scatter(
            grad_bias_self.astype(jnp.bfloat16), "dp", scatter_dimension=0, tiled=True
        ).astype(jnp.float32),
        lax.psum_scatter(
            grad_query_self.astype(jnp.bfloat16), "dp", scatter_dimension=1, tiled=True
        ).astype(jnp.float32),
        lax.psum_scatter(
            grad_key_self.astype(jnp.bfloat16), "dp", scatter_dimension=1, tiled=True
        ).astype(jnp.float32),
        lax.psum_scatter(
            grad_value_self.astype(jnp.bfloat16), "dp", scatter_dimension=1, tiled=True
        ).astype(jnp.float32),
        lax.psum_scatter(
            grad_out_self.astype(jnp.bfloat16), "dp", scatter_dimension=0, tiled=True
        ).astype(jnp.float32),
        lax.psum_scatter(
            grad_gain_cross.astype(jnp.bfloat16), "dp", scatter_dimension=0, tiled=True
        ).astype(jnp.float32),
        lax.psum_scatter(
            grad_bias_cross.astype(jnp.bfloat16), "dp", scatter_dimension=0, tiled=True
        ).astype(jnp.float32),
        lax.psum_scatter(
            grad_query_cross.astype(jnp.bfloat16), "dp", scatter_dimension=1, tiled=True
        ).astype(jnp.float32),
        lax.psum_scatter(
            grad_key_cross.astype(jnp.bfloat16), "dp", scatter_dimension=1, tiled=True
        ).astype(jnp.float32),
        lax.psum_scatter(
            grad_value_cross.astype(jnp.bfloat16), "dp", scatter_dimension=1, tiled=True
        ).astype(jnp.float32),
        lax.psum_scatter(
            grad_out_cross.astype(jnp.bfloat16), "dp", scatter_dimension=0, tiled=True
        ).astype(jnp.float32),
        lax.psum_scatter(
            grad_gain_ffn.astype(jnp.bfloat16), "dp", scatter_dimension=0, tiled=True
        ).astype(jnp.float32),
        lax.psum_scatter(
            grad_bias_ffn.astype(jnp.bfloat16), "dp", scatter_dimension=0, tiled=True
        ).astype(jnp.float32),
        lax.psum_scatter(
            grad_up.astype(jnp.bfloat16), "dp", scatter_dimension=1, tiled=True
        ).astype(jnp.float32),
        lax.psum_scatter(
            grad_down.astype(jnp.bfloat16), "dp", scatter_dimension=0, tiled=True
        ).astype(jnp.float32),
    )
    norm_sums = lax.psum(
        (summed[0], summed[1], summed[6], summed[7], summed[12], summed[13]), "tensor"
    )
    return (
        layer_out,
        grad_input,
        grad_text,
        norm_sums[0],
        norm_sums[1],
        summed[2],
        summed[3],
        summed[4],
        summed[5],
        norm_sums[2],
        norm_sums[3],
        summed[8],
        summed[9],
        summed[10],
        summed[11],
        norm_sums[4],
        norm_sums[5],
        summed[14],
        summed[15],
    )


MESH_IDS = pl.DeviceIdType.MESH
BF16 = jnp.bfloat16
F32 = jnp.float32
VMEM_LIMIT = 60 * 2**20


def my_place():
    chip = lax.axis_index("dp")
    core = lax.axis_index("tensor")
    return (lax.rem(chip, 2), lax.rem(lax.div(chip, 2), 2), lax.div(chip, 4), core)


def neighbours(x, y, z, core):
    def device(zz, yy, xx):
        return (zz * 4 + yy * 2 + xx, core)

    return (device(z, y, 1 - x), device(z, 1 - y, x), device(z + 1, y, x), device(z - 1, y, x))


def when(cond, fn):
    if cond is None:
        fn()
    else:
        pl.when(cond)(fn)


def signal_neighbours(sems, near, has_up, has_down):
    for sem, device, cond in zip(sems, near, (None, None, has_up, has_down), strict=True):
        when(
            cond,
            functools.partial(
                pl.semaphore_signal, sem, inc=1, device_id=device, device_id_type=MESH_IDS
            ),
        )


def gather_engine(chunks, shards, outs, sems):
    local_sem, send_sem, zs, xs, ys, ds = sems
    x, y, z, core = my_place()
    xn, yn = 1 - x, 1 - y
    near = neighbours(x, y, z, core)
    right, across, up, down = near
    has_up, has_down = z < 3, z > 0
    barrier = pltpu.get_barrier_semaphore()
    signal_neighbours([barrier] * 4, near, has_up, has_down)
    pl.semaphore_signal(barrier, inc=1, device_id=(lax.axis_index("dp"), 1 - core), device_id_type=MESH_IDS)
    pl.semaphore_wait(barrier, 3 + has_up.astype(jnp.int32) + has_down.astype(jnp.int32))
    total = len(chunks)
    pending = []


    def span(c):
        _, first, width, _ = chunks[c]
        return pl.ds(first, width)

    def at(zz, yy, xx, c, half=None):
        ref = outs[chunks[c][0]]
        half_rows = ref.shape[3] // 2
        lines = slice(None) if half is None else pl.ds(half * half_rows, half_rows)
        return ref.at[zz, yy, xx, lines, span(c)]

    def plane(zz, c):
        return outs[chunks[c][0]].at[zz, :, :, :, span(c)]

    def own(c):
        return shards[chunks[c][0]].at[:, span(c)]

    local = [pltpu.make_async_copy(own(c), at(z, y, x, c), local_sem.at[c]) for c in range(total)]

    def remote(src, dst, sem, device):
        return pltpu.make_async_remote_copy(
            src_ref=src,
            dst_ref=dst,
            send_sem=send_sem,
            recv_sem=sem,
            device_id=device,
            device_id_type=MESH_IDS,
        )

    def send(src, dst, sem, device, cond=None):
        copy = remote(src, dst, sem, device)
        when(cond, copy.start)
        pending.append((cond, copy))

    def wait(ref, sem, cond=None):
        when(cond, remote(ref, ref, sem, right).wait_recv)

    def lines(step):
        for sign, device, more in ((-1, up, has_up), (1, down, has_down)):
            block = z + sign * step
            yield block, (block >= 0) if sign < 0 else (block <= 3), device, more

    def stage_z(c, step):
        if step == 0:
            send(own(c), at(z, y, x, c), zs.at[c, z], up, has_up)
            send(own(c), at(z, y, x, c), zs.at[c, z], down, has_down)
            send(own(c), at(z, y, x, c), xs.at[c, z], right)
            send(own(c), at(z, y, x, c), ys.at[c, z], across)
            local[c].start()
        if 1 <= step <= 3:
            for block, exists, device, more in lines(step):
                ref = at(block, y, x, c)
                wait(ref, zs.at[c, block], exists)
                if step < 3:
                    send(ref, ref, zs.at[c, block], device, exists & more)
                send(ref, ref, xs.at[c, block], right, exists)
                send(ref, ref, ys.at[c, block], across, exists)
        if 1 <= step <= 4:
            for block, exists, _, _ in [(z, None, None, None)] if step == 1 else lines(step - 1):
                wait(at(block, y, xn, c), xs.at[c, block], exists)
                ref = at(block, y, xn, c, 0)
                send(ref, ref, ds.at[c, block, 0], across, exists)
                wait(at(block, yn, x, c), ys.at[c, block], exists)
                ref = at(block, yn, x, c, 1)
                send(ref, ref, ds.at[c, block, 1], right, exists)
        if step == 5:
            for block in range(4):
                for half in range(2):
                    wait(at(block, yn, xn, c, half), ds.at[c, block, half])
            local[c].wait()

    def stage_a(c, step):
        if step == 0:
            send(own(c), at(z, y, x, c), xs.at[c, z], right)
            send(own(c), at(z, y, x, c), ys.at[c, z], across)
            local[c].start()
        if step == 1:
            wait(at(z, y, xn, c), xs.at[c, z])
            ref = at(z, y, xn, c, 0)
            send(ref, ref, ds.at[c, z, 0], across)
            wait(at(z, yn, x, c), ys.at[c, z])
            ref = at(z, yn, x, c, 1)
            send(ref, ref, ds.at[c, z, 1], right)
        if step == 2:
            for half in range(2):
                wait(at(z, yn, xn, c, half), ds.at[c, z, half])
            local[c].wait()
            send(plane(z, c), plane(z, c), zs.at[c, z], up, has_up)
            send(plane(z, c), plane(z, c), zs.at[c, z], down, has_down)
        if step >= 3:
            for block, exists, device, more in lines(step - 2):
                wait(plane(block, c), zs.at[c, block], exists)
                if step < 5:
                    send(plane(block, c), plane(block, c), zs.at[c, block], device, exists & more)

    stages = 6

    def turn(number):
        for step in range(stages):
            c = number - step
            if 0 <= c < total:
                (stage_z if chunks[c][3] == "Z" else stage_a)(c, step)

    def finish():
        for cond, copy in pending:
            when(cond, copy.wait_send)

    return turn, finish


def total_of(*parts):
    value = parts[0].astype(F32)
    for part in parts[1:]:
        value = value + part.astype(F32)
    return value


def dot_nt(left, right):
    return lax.dot_general(left, right, (((1,), (1,)), ((), ())), preferred_element_type=F32)


def dot_tn(left, right):
    return lax.dot_general(left, right, (((0,), (0,)), ((), ())), preferred_element_type=F32)


def dot_nn(left, right):
    return jnp.dot(left, right, preferred_element_type=F32)


def project_rows(source, weight, store, rows=256, transposed=False):
    def body(n, carry):
        first = pl.multiple_of(n * rows, rows)
        part = source[pl.ds(first, rows), :]
        store(first, dot_nt(part, weight[...]) if transposed else dot_nn(part, weight[...]))
        return carry

    lax.fori_loop(0, source.shape[0] // rows, body, 0)


def normalize(values, gain, shift):
    offset = values - jnp.mean(values, axis=-1, keepdims=True)
    spread = jnp.mean(offset * offset, axis=-1, keepdims=True)
    return offset * lax.rsqrt(spread + norm_eps) * gain + shift


def head_lanes(half):
    return lax.div(lax.broadcasted_iota(jnp.int32, (1, 128), 1), 64) == half


def only(mask, value):
    return jnp.where(mask, value.astype(F32), 0.0).astype(BF16)


def pair_forward(pair, q_ref, k_ref, v_ref, o_ref, lse_ref, causal):
    cols = pl.ds(pl.multiple_of(pair * 128, 128), 128)
    block = 256
    keep = lax.broadcasted_iota(jnp.int32, (block, block), 0) <= lax.broadcasted_iota(
        jnp.int32, (block, block), 1
    )
    for i in range(q_ref.shape[0] // block):
        rows = pl.ds(i * block, block)
        parts = [(0, k_ref.shape[0], False)]
        if causal:
            parts = [(0, i * block, False)] * (i > 0) + [(i * block, block, True)]
        total = 0.0
        for half in range(2):
            mine = head_lanes(half)
            q = only(mine, q_ref[rows, cols])
            scores = []
            for first, count, diagonal in parts:
                part = dot_nt(k_ref[pl.ds(first, count), cols], q) * score_scale
                scores.append(jnp.where(keep, part, -1e30) if diagonal else part)
            peak = functools.reduce(
                jnp.maximum, [jnp.max(part, axis=0, keepdims=True) for part in scores]
            )
            scores = [jnp.exp(part - peak) for part in scores]
            weight = sum(jnp.sum(part, axis=0, keepdims=True) for part in scores)
            lse_ref[pl.ds(2 * pair + half, 1), rows] = peak + jnp.log(weight)
            share = 1.0 / weight
            for (first, count, _), part in zip(parts, scores, strict=True):
                v = only(mine, v_ref[pl.ds(first, count), cols])
                total = total + dot_tn((part * share).astype(BF16), v)
        o_ref[rows, cols] = total.astype(BF16)


def forward_kernel(chunks, count, *refs):
    shards, refs = refs[:count], refs[count:]
    hidden_h, text_h, refs = refs[0], refs[1], refs[2:]
    outs, refs = refs[:count], refs[count:]
    results, refs = refs[:16], refs[16:]
    sems, refs = refs[:6], refs[6:]
    (h1, h2, h3, q1, k1, v1, o1, q2, k2, v2, o2, lse1, lse2, x2, x3), refs = refs[:15], refs[15:]
    gathered_norms, norms, weights, hidden, text, mine, theirs, arrived = refs[:8]
    norm_sem, weight_sem, load_sem, share_send, share_recv, result_sem = refs[8:]
    names = dict(norms=0, q=1, k=2, v=3, o=4, ck=5, cv=6, cq=7, co=8, up=9, down=10)
    turn, finish = gather_engine(chunks, shards, outs, sems)
    chip, core = lax.axis_index("dp"), lax.axis_index("tensor")
    frames, width = h1.shape
    half = frames // 2
    own = pl.ds(pl.multiple_of(core * half, half), half)
    loads = [
        pltpu.make_async_copy(hidden_h, hidden, load_sem.at[0]),
        pltpu.make_async_copy(text_h, text, load_sem.at[1]),
    ]
    for copy in loads:
        copy.start()
    pending = []

    def weight_copy(name, slot, first=0):
        return [
            pltpu.make_async_copy(
                outs[names[name]].at[zz, yy, xx, :, pl.ds(first, weights.shape[2])],
                weights.at[slot, pl.ds(((zz * 2 + yy) * 2 + xx) * rows, rows), :],
                weight_sem.at[slot, (zz * 2 + yy) * 2 + xx],
            )
            for zz in range(4)
            for yy in range(2)
            for xx in range(2)
        ]

    rows = width // 16

    def load_weight(name, slot, first=0):
        for copy in weight_copy(name, slot, first):
            copy.start()

    def wait_weight(slot):
        for copy in weight_copy("q", slot):
            copy.wait()

    def share(n, src, dst):
        return pltpu.make_async_remote_copy(
            src_ref=src,
            dst_ref=dst,
            send_sem=share_send.at[n],
            recv_sem=share_recv.at[n],
            device_id=(chip, 1 - core),
            device_id_type=MESH_IDS,
        )

    def give(n, ref):
        copy = pltpu.make_async_copy(ref, results[n], result_sem.at[n])
        copy.start()
        pending.append(copy)

    def norm_share(n, values, kind, h):
        step = 64

        def body(i, carry):
            first = pl.multiple_of(i * step, step)
            h[pl.ds(pl.multiple_of(core * half + first, step), step), :] = normalize(
                values(first, step), norms[2 * kind : 2 * kind + 1], norms[2 * kind + 1 : 2 * kind + 2]
            ).astype(BF16)
            return carry

        lax.fori_loop(0, half // step, body, 0)
        share(n, h.at[own], h.at[own]).start()

    def get_share(n, h):
        share(n, h.at[own], h.at[own]).wait()

    def to(ref):
        def store(first, value):
            ref[pl.ds(first, value.shape[0]), :] = value.astype(BF16)

        return store

    def out_project(n, o, slot):
        step = 256
        for whose, ref in ((1 - core, theirs.at[n]), (core, mine)):
            for first in range(0, half, step):
                part = o[pl.ds(pl.multiple_of(whose * half + first, step), step), :]
                ref[pl.ds(first, step), :] = dot_nt(part, weights[slot]).astype(ref.dtype)
            if whose is not core:
                share(3 + n, theirs.at[n], arrived.at[n]).start()

    def add_stream(n, before, after):
        def values(first, step):
            lines = pl.ds(first, step)
            total = before[lines, :].astype(F32) + (mine[lines, :] + arrived[n, lines, :].astype(F32))
            after[lines, :] = total
            return total

        return values

    def work(number):
        if number == 5:
            copy = pltpu.make_async_copy(outs[0], gathered_norms, norm_sem)
            copy.start()
            copy.wait()
            for copy in loads:
                copy.wait()
            total = 0.0
            lane = lax.broadcasted_iota(jnp.int32, (128, width), 0)
            place = lax.broadcasted_iota(jnp.int32, (128, width), 1)
            for n in range(16):
                pick = (place == lane + n * rows) & (lane < rows)
                total = total + dot_nn(
                    gathered_norms[n // 4, n // 2 % 2, n % 2],
                    jnp.where(pick, 1.0, 0.0).astype(BF16),
                )
            norms[...] = total
            give(13, norms)
            norm_share(0, lambda first, step: hidden[pl.ds(first, step), :].astype(F32), 0, h1)
        if number == 6:
            load_weight("q", 0)
            get_share(0, h1)
            give(0, h1)
            wait_weight(0)
            project_rows(h1, weights.at[0], to(q1))
            give(3, q1)
        if number == 7:
            load_weight("k", 1)
            wait_weight(1)
            project_rows(h1, weights.at[1], to(k1))
            give(4, k1)
        if number == 8:
            load_weight("v", 0)
            wait_weight(0)
            project_rows(h1, weights.at[0], to(v1))
            give(5, v1)
        if number in (9, 10, 11):
            if number == 9:
                load_weight("o", 1)
            pairs = q1.shape[1] // 128
            first = pairs * (number - 9) // 3
            last = pairs * (number - 8) // 3

            def body(pair, carry):
                pair_forward(pair, q1, k1, v1, o1, lse1, True)
                return carry

            lax.fori_loop(first, last, body, 0)
            if number == 11:
                load_weight("cv", 0)
        if number == 12:
            give(6, o1)
            give(11, lse1)
            wait_weight(1)
            out_project(0, o1, 1)
            load_weight("ck", 1)
            wait_weight(0)
            v2[...] = dot_nn(text[...], weights[0]).astype(BF16)
            give(9, v2)
            load_weight("cq", 0)
        if number == 13:
            share(3, theirs.at[0], arrived.at[0]).wait()
            norm_share(1, add_stream(0, hidden, x2), 1, h2)
            give(14, x2)
            wait_weight(1)
            k2[...] = dot_nn(text[...], weights[1]).astype(BF16)
            give(8, k2)
            load_weight("co", 1)
        if number == 14:
            get_share(1, h2)
            give(1, h2)
            wait_weight(0)
            project_rows(h2, weights.at[0], to(q2))
            give(7, q2)
        if number == 15:

            def body(pair, carry):
                pair_forward(pair, q2, k2, v2, o2, lse2, False)
                return carry

            lax.fori_loop(0, q2.shape[1] // 128, body, 0)
            give(10, o2)
            give(12, lse2)
        if number == 16:
            wait_weight(1)
            out_project(1, o2, 1)
        if number == 17:
            share(4, theirs.at[1], arrived.at[1]).wait()
            norm_share(2, add_stream(1, x2, x3), 2, h3)
            give(15, x3)
        if number == 18:
            get_share(2, h3)
            give(2, h3)

    for number in range(len(chunks) + 5):
        turn(number)
        work(number)
    finish()
    for copy in pending:
        copy.wait()


def forward_all(shards, chunks, hidden, text):
    total, count = len(chunks), len(shards)
    dma, vmem = pltpu.SemaphoreType.DMA, pltpu.VMEM
    half, width = hidden.shape
    frames, part = 2 * half, shards[1].shape[1]
    anywhere = pl.BlockSpec(memory_space=pl.ANY)
    shape = jax.ShapeDtypeStruct
    kept = [
        *[((frames, width), BF16)] * 3,
        *[((frames, part), BF16)] * 4,
        ((frames, part), BF16),
        *[((text.shape[0], part), BF16)] * 2,
        ((frames, part), BF16),
        *[((16, frames), F32)] * 2,
    ]
    given = [*kept, ((shards[0].shape[0], width), F32), ((half, width), F32), ((half, width), F32)]
    held = [*kept, ((half, width), F32), ((half, width), F32)]
    outs = pl.pallas_call(
        functools.partial(forward_kernel, chunks, count),
        out_shape=[shape((4, 2, 2) + s.shape, s.dtype) for s in shards] + [shape(*g) for g in given],
        in_specs=[anywhere] * (count + 2),
        out_specs=[anywhere] * (count + len(given)),
        scratch_shapes=[
            dma((total,)),
            dma,
            dma((total, 4)),
            dma((total, 4)),
            dma((total, 4)),
            dma((total, 4, 2)),
            *[vmem(*h) for h in held],
            vmem((4, 2, 2) + shards[0].shape, BF16),
            vmem((shards[0].shape[0], width), F32),
            vmem((2, width, part), BF16),
            vmem((half, width), BF16),
            vmem(text.shape, BF16),
            vmem((half, width), F32),
            vmem((2, half, width), BF16),
            vmem((2, half, width), BF16),
            dma,
            dma((2, 16)),
            dma((2,)),
            dma((5,)),
            dma((5,)),
            dma((16,)),
        ],
        compiler_params=pltpu.CompilerParams(
            collective_id=0, has_side_effects=True, vmem_limit_bytes=VMEM_LIMIT
        ),
        name="forward",
    )(*shards, hidden, text)
    return outs[:count], outs[count:]


XD, YD, XA, YA, XB, YB, UP, DOWN = range(8)


UNIT = 256
WIDTH_Z, WIDTH_A, SLOTS = 384, 128, 8
ROWS_L = 6
FIRST_L = (0, 12, 24, 27, 36, 39)
FIRST_R = ((0, 12), (12, 24), (24, 27), (27, 30), (36, 39))
TEXT_UNITS = (30, 36)
SELF_UNITS = (39, 48)
UNITS = 48


def head_back(head, q_ref, k_ref, v_ref, do_ref, lse_ref, dqkv, acc_k, acc_v):
    width = q_ref.shape[1]
    pair, half = lax.div(head, 2), lax.rem(head, 2)
    lanes = [pl.ds(pl.multiple_of(pair * 128 + n * width, 128), 128) for n in range(3)]
    cols = lanes[0]
    mine = lax.div(lax.broadcasted_iota(jnp.int32, (1, 128), 1), 64) == half
    acc_k[...] = jnp.zeros_like(acc_k)
    acc_v[...] = jnp.zeros_like(acc_v)
    block = 256
    keep = lax.broadcasted_iota(jnp.int32, (block, block), 0) <= lax.broadcasted_iota(
        jnp.int32, (block, block), 1
    )

    def merged(rows, lane, value):
        before = jnp.where(half == 0, 0.0, dqkv[rows, lane].astype(F32))
        dqkv[rows, lane] = (before + value).astype(BF16)

    for i in range(q_ref.shape[0] // block):
        rows = pl.ds(i * block, block)
        q = jnp.where(mine, q_ref[rows, cols].astype(F32), 0.0).astype(BF16)
        do = jnp.where(mine, do_ref[rows, cols].astype(F32), 0.0).astype(BF16)
        lse = lse_ref[pl.ds(head, 1), rows]
        parts = [(i * block, block, True)]
        if i:
            parts.insert(0, (0, i * block, False))
        held, inner = [], 0.0
        for first, count, diagonal in parts:
            keys = pl.ds(first, count)
            soft = jnp.exp(dot_nt(k_ref[keys, cols], q) * score_scale - lse)
            if diagonal:
                soft = jnp.where(keep, soft, 0.0)
            slope = dot_nt(v_ref[keys, cols], do)
            inner = inner + jnp.sum(soft * slope, axis=0, keepdims=True)
            held.append((keys, soft, slope))
        grad_q = 0.0
        for keys, soft, slope in held:
            ds = (soft * (slope - inner)).astype(BF16)
            acc_v[keys, :] += dot_nn(soft.astype(BF16), do)
            acc_k[keys, :] += dot_nn(ds, q)
            grad_q = grad_q + dot_tn(ds, k_ref[keys, cols])
        merged(rows, lanes[0], jnp.where(mine, grad_q * score_scale, 0.0))
    merged(slice(None), lanes[1], acc_k[...] * score_scale)
    merged(slice(None), lanes[2], acc_v[...])


def backward_kernel(*refs):
    lefts, refs = refs[:ROWS_L], refs[ROWS_L:]
    rights, refs = refs[:5], refs[5:]
    text_h, dkv_h, q_h, k_h, v_h, do_h, lse_ref, out, dqkv_h = refs[:9]
    refs = refs[9:]
    gz, ga, xdz, ydz, xaz, yaz, xbz, ybz, upz, dnz = refs[:10]
    xda, yda, xaa, yaa, xba, yba, upa, dna, oz, oa = refs[10:20]
    lbuf, rbuf, text_v, dkv_v, q_v, k_v, v_v, do_v, dqkv, acc_k, acc_v = refs[20:31]
    first_sem, l_sem, r_sem, dqkv_sem, out_sem, send_z, send_a, recv_z, recv_a, credit = refs[31:]
    width_z, width_a, slots = WIDTH_Z, WIDTH_A, SLOTS
    total, width = UNITS // 2, WIDTH_Z + WIDTH_A
    heads = q_v.shape[1] // HEAD_DIM
    x, y, z, core = my_place()
    xn, yn = 1 - x, 1 - y
    near = neighbours(x, y, z, core)
    right, across, up, down = near
    has_up, has_down = z < 3, z > 0
    degree = 2 + has_up.astype(jnp.int32) + has_down.astype(jnp.int32)
    barrier = pltpu.get_barrier_semaphore()
    signal_neighbours([barrier] * 4, near, has_up, has_down)
    pl.semaphore_wait(barrier, degree)
    rows = gz.shape[4]
    low, high = pl.ds(0, rows // 2), pl.ds(rows // 2, rows // 2)

    def remote(src, dst, send_sem, recv_sem, device):
        return pltpu.make_async_remote_copy(
            src_ref=src,
            dst_ref=dst,
            send_sem=send_sem,
            recv_sem=recv_sem,
            device_id=device,
            device_id_type=MESH_IDS,
        )

    def arrived(ref, sem):
        remote(ref, ref, send_z.at[0], sem, right).wait_recv()

    def sent(ref, sem):
        remote(ref, ref, sem, recv_z.at[0, 0], right).wait_send()

    firsts = [
        pltpu.make_async_copy(src, dst, first_sem.at[n])
        for n, (src, dst) in enumerate(
            (
                (text_h, text_v),
                (dkv_h, dkv_v),
                (q_h, q_v),
                (k_h, k_v),
                (v_h, v_v),
                (do_h, do_v),
            )
        )
    ]

    def left_copy(n):
        return pltpu.make_async_copy(lefts[n], lbuf.at[n % 2], l_sem.at[n % 2])

    def right_copies(c, which):
        unit = 2 * c + which
        place, sem = rbuf.at[lax.rem(c, 2), which], r_sem.at[lax.rem(c, 2), which]
        for source, (lo, hi) in zip((*rights, dqkv), (*FIRST_R, SELF_UNITS), strict=True):
            first = pl.multiple_of((unit - lo) * UNIT, UNIT)
            yield (
                (unit >= lo) & (unit < hi),
                pltpu.make_async_copy(source.at[:, pl.ds(first, UNIT)], place, sem),
            )

    def start_rights(c):
        for which in range(2):
            for cond, copy in right_copies(c, which):
                pl.when(cond)(copy.start)

    def store_unit(which, k, i, value):
        for yy in range(2):
            for xx in range(2):
                first = (yy * 2 + xx) * rows
                block = value[first : first + rows, :].astype(BF16)
                if which == 0:
                    gz[k, i, yy, xx, :, pl.ds(0, UNIT)] = block
                else:
                    gz[k, i, yy, xx, :, pl.ds(UNIT, width_z - UNIT)] = block[:, : width_z - UNIT]
                    ga[k, i, yy, xx] = block[:, width_z - UNIT :]

    def compute(c, k):
        for n in range(1, ROWS_L):
            pl.when(c == FIRST_L[n] // 2)(left_copy(n).wait)
        for which in range(2):
            unit = 2 * c + which
            text = (unit >= TEXT_UNITS[0]) & (unit < TEXT_UNITS[1])
            slot = lax.rem(sum((unit >= first).astype(jnp.int32) for first in FIRST_L) + 1, 2)

            @pl.when(text)
            def _():
                first = pl.multiple_of((unit - TEXT_UNITS[0]) * UNIT, UNIT)
                right_part = dkv_v[:, pl.ds(first, UNIT)]
                for i in range(4):
                    store_unit(which, k, i, dot_tn(text_v[:, pl.ds(i * 4 * rows, 4 * rows)], right_part))

            @pl.when(jnp.logical_not(text))
            def _():
                par = lax.rem(c, 2)
                pltpu.make_async_copy(rbuf.at[par, which], rbuf.at[par, which], r_sem.at[par, which]).wait()
                right_part = rbuf[par, which]
                for i in range(4):
                    left_part = lbuf[slot, :, pl.ds(i * 4 * rows, 4 * rows)]
                    store_unit(which, k, i, dot_tn(left_part, right_part))

        for n in range(2, ROWS_L):
            pl.when(c == FIRST_L[n - 1] // 2)(left_copy(n).start)
        pl.when(c + 1 < total)(lambda: start_rights(c + 1))

    def out_copies(c):
        o = lax.rem(c, 2)
        first = pl.multiple_of(c * width, 128)
        return (
            pltpu.make_async_copy(oz.at[o], out.at[:, pl.ds(first, width_z)], out_sem.at[o, 0]),
            pltpu.make_async_copy(
                oa.at[o], out.at[:, pl.ds(first + width_z, width_a)], out_sem.at[o, 1]
            ),
        )

    def plane_first(own, k, bufs, send_sem, recv):
        xd, yd, xa, ya = bufs
        remote(own(yn, xn, low), xd.at[k], send_sem.at[k], recv.at[k, XD], right).start()
        remote(own(yn, xn, high), yd.at[k], send_sem.at[k], recv.at[k, YD], across).start()
        remote(own(y, xn, low), xa.at[k], send_sem.at[k], recv.at[k, XA], right).start()
        remote(own(yn, x, high), ya.at[k], send_sem.at[k], recv.at[k, YA], across).start()

    def plane_second(add, k, bufs, send_sem, recv):
        xd, yd, xb, yb = bufs
        arrived(xd.at[k], recv.at[k, XD])
        add(xd, yn, x, low)
        remote(xd.at[k], yb.at[k], send_sem.at[k], recv.at[k, YB], across).start()
        arrived(yd.at[k], recv.at[k, YD])
        add(yd, y, xn, high)
        remote(yd.at[k], xb.at[k], send_sem.at[k], recv.at[k, XB], right).start()

    def line_up(first, buf, add, k, send_sem, recv):
        blocks = 4 - first
        arrived(buf.at[k, pl.ds(first, blocks)], recv.at[k, UP])
        if blocks > 1:
            for block in range(first + 1, 4):
                add(buf, block)
            ref = buf.at[k, pl.ds(first + 1, blocks - 1)]
            remote(ref, ref, send_sem.at[k], recv.at[k, UP], up).start()

    def line_down(last, buf, add, k, send_sem, recv):
        arrived(buf.at[k, pl.ds(0, last + 1)], recv.at[k, DOWN])
        if last > 0:
            for block in range(last):
                add(buf, block)
            ref = buf.at[k, pl.ds(0, last)]
            remote(ref, ref, send_sem.at[k], recv.at[k, DOWN], down).start()

    def add_a(k):
        def add(buf, block):
            for yy in range(2):
                for xx in range(2):
                    buf[k, block, yy, xx] = total_of(
                        buf[k, block, yy, xx], ga[k, block, yy, xx]
                    ).astype(BF16)

        return add

    def add_z(k):
        def add(buf, block):
            buf[k, block] = total_of(buf[k, block], gz[k, block, y, x]).astype(BF16)

        return add

    def begin(c, k):
        @pl.when(c >= slots)
        def _():
            pl.semaphore_wait(credit.at[0], 1)
            pl.semaphore_wait(credit.at[1], 1)
            pl.when(has_up)(lambda: pl.semaphore_wait(credit.at[2], 1))
            pl.when(has_down)(lambda: pl.semaphore_wait(credit.at[3], 1))

        plane_first(
            lambda yy, xx, half: gz.at[k, :, yy, xx, half, :], k, (xdz, ydz, xaz, yaz), send_z, recv_z
        )

        @pl.when(z == 0)
        def _():
            ref = pl.ds(1, 3)
            remote(ga.at[k, ref], upa.at[k, ref], send_a.at[k], recv_a.at[k, UP], up).start()

        @pl.when(z == 3)
        def _():
            ref = pl.ds(0, 3)
            remote(ga.at[k, ref], dna.at[k, ref], send_a.at[k], recv_a.at[k, DOWN], down).start()

    def second(c, k):
        def add(buf, yy, xx, half):
            for block in range(4):
                buf[k, block] = total_of(buf[k, block], gz[k, block, yy, xx, half, :]).astype(BF16)

        plane_second(add, k, (xdz, ydz, xbz, ybz), send_z, recv_z)
        pl.when(z == 1)(lambda: line_up(1, upa, add_a(k), k, send_a, recv_a))
        pl.when(z == 2)(lambda: line_down(2, dna, add_a(k), k, send_a, recv_a))

    def third(c, k):
        for buf, kind in ((xaz, XA), (yaz, YA), (xbz, XB), (ybz, YB)):
            arrived(buf.at[k], recv_z.at[k, kind])
        for block in range(4):
            for half, one, two in ((low, xaz, ybz), (high, yaz, xbz)):
                gz[k, block, y, x, half, :] = total_of(
                    gz[k, block, y, x, half, :], one[k, block], two[k, block]
                ).astype(BF16)

        @pl.when(z == 0)
        def _():
            ref = pl.ds(1, 3)
            remote(
                gz.at[k, ref, y, x], upz.at[k, ref], send_z.at[k], recv_z.at[k, UP], up
            ).start()

        @pl.when(z == 3)
        def _():
            ref = pl.ds(0, 3)
            remote(
                gz.at[k, ref, y, x], dnz.at[k, ref], send_z.at[k], recv_z.at[k, DOWN], down
            ).start()

        pl.when(z == 2)(lambda: line_up(2, upa, add_a(k), k, send_a, recv_a))
        pl.when(z == 1)(lambda: line_down(1, dna, add_a(k), k, send_a, recv_a))

    def fourth(c, k):
        pl.when(z == 1)(lambda: line_up(1, upz, add_z(k), k, send_z, recv_z))
        pl.when(z == 2)(lambda: line_down(2, dnz, add_z(k), k, send_z, recv_z))
        pl.when(z == 3)(lambda: line_up(3, upa, None, k, send_a, recv_a))
        pl.when(z == 0)(lambda: line_down(0, dna, None, k, send_a, recv_a))
        for buf, exists in ((upa, has_down), (dna, has_up)):

            @pl.when(exists)
            def _():
                for yy in range(2):
                    for xx in range(2):
                        ga[k, z, yy, xx] = total_of(ga[k, z, yy, xx], buf[k, z, yy, xx]).astype(BF16)

        plane_first(
            lambda yy, xx, half: ga.at[k, z, yy, xx, half, :], k, (xda, yda, xaa, yaa), send_a, recv_a
        )

    def fifth(c, k):
        pl.when(z == 2)(lambda: line_up(2, upz, add_z(k), k, send_z, recv_z))
        pl.when(z == 1)(lambda: line_down(1, dnz, add_z(k), k, send_z, recv_z))

        def add(buf, yy, xx, half):
            buf[k] = total_of(buf[k], ga[k, z, yy, xx, half, :]).astype(BF16)

        plane_second(add, k, (xda, yda, xba, yba), send_a, recv_a)

    def finish(c, k):
        pl.when(z == 3)(lambda: line_up(3, upz, None, k, send_z, recv_z))
        pl.when(z == 0)(lambda: line_down(0, dnz, None, k, send_z, recv_z))
        o = lax.rem(c, 2)

        @pl.when(c >= 2)
        def _():
            for copy in out_copies(c - 2):
                copy.wait()

        oz[o] = gz[k, z, y, x].astype(F32)
        for buf, exists in ((upz, has_down), (dnz, has_up)):

            @pl.when(exists)
            def _():
                oz[o] = oz[o] + buf[k, z].astype(F32)

        for buf, kind in ((xaa, XA), (yaa, YA), (xba, XB), (yba, YB)):
            arrived(buf.at[k], recv_a.at[k, kind])
        oa[o, low, :] = total_of(ga[k, z, y, x, low, :], xaa[k], yba[k])
        oa[o, high, :] = total_of(ga[k, z, y, x, high, :], yaa[k], xba[k])
        for copy in out_copies(c):
            copy.start()
        for buf in (xdz, ydz, xaz, yaz, xbz, ybz):
            sent(buf.at[k], send_z.at[k])
        for buf in (xda, yda, xaa, yaa, xba, yba):
            sent(buf.at[k], send_a.at[k])
        for step in range(3):

            @pl.when(z == step)
            def _():
                sent(upz.at[k, pl.ds(step + 1, 3 - step)], send_z.at[k])
                sent(upa.at[k, pl.ds(step + 1, 3 - step)], send_a.at[k])

            @pl.when(z == 3 - step)
            def _():
                sent(dnz.at[k, pl.ds(0, 3 - step)], send_z.at[k])
                sent(dna.at[k, pl.ds(0, 3 - step)], send_a.at[k])

        @pl.when(c < total - slots)
        def _():
            signal_neighbours([credit.at[i] for i in (0, 1, 3, 2)], near, has_up, has_down)

    stages = (begin, second, third, fourth, fifth, finish)
    left_copy(0).start()
    start_rights(jnp.int32(0))
    left_copy(1).start()
    for copy in firsts:
        copy.start()
    left_copy(0).wait()
    for copy in firsts:
        copy.wait()
    dqkv_copy = pltpu.make_async_copy(dqkv, dqkv_h, dqkv_sem)

    def body(turn, carry):
        for step, stage in enumerate(stages):
            c = turn - step - 1

            @pl.when((c >= 0) & (c < total))
            def _():
                stage(c, lax.rem(c, slots))

        pl.when(turn < total)(lambda: compute(turn, lax.rem(turn, slots)))

        @pl.when((turn >= 1) & (turn <= heads))
        def _():
            head_back(turn - 1, q_v, k_v, v_v, do_v, lse_ref, dqkv, acc_k, acc_v)

        pl.when(turn == heads + 1)(dqkv_copy.start)
        return carry

    lax.fori_loop(0, total + len(stages), body, 0)
    for c in (total - 2, total - 1):
        for copy in out_copies(jnp.int32(c)):
            copy.wait()
    dqkv_copy.wait()


def backward_all(lefts, rights, text, grad_text_rows, heads_in, log_sums):
    frames, width = lefts[0].shape
    rows = width // 16
    part = heads_in[0].shape[1]
    dma = pltpu.SemaphoreType.DMA
    vmem = pltpu.VMEM

    def buffer(*shape):
        return vmem((SLOTS,) + shape, BF16)

    anywhere = pl.BlockSpec(memory_space=pl.ANY)
    inputs = (*lefts, *rights, text, grad_text_rows, *heads_in, log_sums)
    return pl.pallas_call(
        backward_kernel,
        out_shape=[
            jax.ShapeDtypeStruct((rows, UNITS * UNIT), F32),
            jax.ShapeDtypeStruct((frames, 3 * part), BF16),
        ],
        in_specs=[anywhere] * (len(inputs) - 1) + [pl.BlockSpec(memory_space=vmem)],
        out_specs=[anywhere] * 2,
        scratch_shapes=[
            buffer(4, 2, 2, rows, WIDTH_Z),
            buffer(4, 2, 2, rows, WIDTH_A),
            *[buffer(4, rows // 2, WIDTH_Z)] * 6,
            *[buffer(4, rows, WIDTH_Z)] * 2,
            *[buffer(rows // 2, WIDTH_A)] * 6,
            *[buffer(4, 2, 2, rows, WIDTH_A)] * 2,
            vmem((2, rows, WIDTH_Z), F32),
            vmem((2, rows, WIDTH_A), F32),
            vmem((2, frames, width), BF16),
            vmem((2, 2, frames, UNIT), BF16),
            vmem(text.shape, BF16),
            vmem(grad_text_rows.shape, BF16),
            *[vmem((frames, part), BF16)] * 4,
            vmem((frames, 3 * part), BF16),
            *[vmem((frames, 128), F32)] * 2,
            dma((6,)),
            dma((2,)),
            dma((2, 2)),
            dma,
            dma((2, 2)),
            dma((SLOTS,)),
            dma((SLOTS,)),
            dma((SLOTS, 8)),
            dma((SLOTS, 8)),
            pltpu.SemaphoreType.REGULAR((4,)),
        ],
        compiler_params=pltpu.CompilerParams(
            collective_id=1, has_side_effects=True, vmem_limit_bytes=VMEM_LIMIT
        ),
        name="backward",
    )(*inputs)


def sum_everywhere_kernel(values, out, got, send_sem, recv_sem):
    chip, core = lax.axis_index("dp"), lax.axis_index("tensor")
    partners = [(chip, 1 - core)]
    for bit in (1, 2, 4, 8):
        partners.append((chip + bit * (1 - 2 * lax.rem(lax.div(chip, bit), 2)), core))
    barrier = pltpu.get_barrier_semaphore()
    for device in partners:
        pl.semaphore_signal(barrier, inc=1, device_id=device, device_id_type=MESH_IDS)
    pl.semaphore_wait(barrier, len(partners))
    got[0] = values[...]
    for step, device in enumerate(partners):
        copy = pltpu.make_async_remote_copy(
            src_ref=got.at[2 * step],
            dst_ref=got.at[2 * step + 1],
            send_sem=send_sem.at[step],
            recv_sem=recv_sem.at[step],
            device_id=device,
            device_id_type=MESH_IDS,
        )
        copy.start()
        copy.wait()
        got[2 * step + 2] = got[2 * step] + got[2 * step + 1]
    out[...] = got[2 * len(partners)]


def sum_everywhere(values):
    dma = pltpu.SemaphoreType.DMA
    vmem = pl.BlockSpec(memory_space=pltpu.VMEM)
    return pl.pallas_call(
        sum_everywhere_kernel,
        out_shape=jax.ShapeDtypeStruct(values.shape, F32),
        in_specs=[vmem],
        out_specs=vmem,
        scratch_shapes=[pltpu.VMEM((11,) + values.shape, F32), dma((5,)), dma((5,))],
        compiler_params=pltpu.CompilerParams(collective_id=2, has_side_effects=True),
        name="sum_norm_gradients",
    )(values)


def project_t(row_data, weight):
    return jnp.einsum("cli,io->clo", row_data, weight, preferred_element_type=jnp.float32)


def input_grad_t(grad_rows, weight):
    return jnp.einsum("cla,ia->cli", grad_rows, weight, preferred_element_type=jnp.float32)


def other_core(values):
    return lax.ppermute(values, "tensor", [(0, 1), (1, 0)])


def share_rows(values):
    other = other_core(values)
    first = lax.axis_index("tensor") == 0
    return jnp.concatenate(
        [jnp.where(first, values, other), jnp.where(first, other, values)], axis=1
    )


def sum_rows(rows, product):
    core, half = lax.axis_index("tensor"), rows[0].shape[1] // 2
    theirs = product(*[lax.dynamic_slice_in_dim(r, (1 - core) * half, half, 1) for r in rows])
    arriving = other_core(theirs.astype(BF16))
    mine = product(*[lax.dynamic_slice_in_dim(r, core * half, half, 1) for r in rows])
    return mine + arriving.astype(F32)


def gelu_parts(values):
    below = 0.5 * (1.0 + lax.erf(values * (0.5**0.5)))
    density = jnp.exp(-0.5 * values * values) * 0.3989422804014327
    return (values * below).astype(BF16), (below + values * density).astype(BF16)


def gather_plan(columns):
    chunks, since = [], 0
    for array, width in enumerate(columns):
        size = 768 if width % 768 == 0 else width
        for first in range(0, width, size):
            since += 1
            family = "A" if since % 5 == 3 and size == 768 else "Z"
            chunks.append((array, first, size, family))
    return tuple(chunks)


def local_fast(
    hidden_in,
    text_states,
    norm1_gain,
    norm1_bias,
    self_query,
    self_key,
    self_value,
    self_out,
    norm2_gain,
    norm2_bias,
    cross_query,
    cross_key,
    cross_value,
    cross_out,
    norm3_gain,
    norm3_bias,
    hidden_up,
    hidden_down,
    cotangent,
):
    width = norm1_gain.shape[0] * 16
    norms = jnp.stack([norm1_gain, norm1_bias, norm2_gain, norm2_bias, norm3_gain, norm3_bias])
    norms = jnp.pad(norms, ((0, 26), (0, 128 - norms.shape[1])))
    shards = (
        norms,
        self_query.T,
        self_key.T,
        self_value.T,
        self_out,
        cross_key.T,
        cross_value.T,
        cross_query.T,
        cross_out,
        hidden_up.T,
        hidden_down,
    )
    gathered, kept = forward_all(
        shards, gather_plan([s.shape[1] for s in shards]), hidden_in[0], text_states[0]
    )
    w_q, w_k, w_v, w_o, w_ck, w_cv, w_cq, w_co, w_up, w_down = [
        g.reshape(width, g.shape[-1]) for g in gathered[1:]
    ]
    normed_one, normed_two, normed_three = [k[None] for k in kept[:3]]
    query_one, key_one, value_one, attended_one = kept[3:7]
    query_two, key_two, value_two, attended_two = [split_heads(k[None]) for k in kept[7:11]]
    logsum_one, logsum_two = kept[11], kept[12][None, :12]
    gain_self, bias_self, gain_cross, bias_cross, gain_ffn, bias_ffn = [kept[13][i] for i in range(6)]
    stream_one, stream_two, stream_three = hidden_in.astype(F32), kept[14][None], kept[15][None]
    upper = project_t(normed_three, w_up)
    active, slope = gelu_parts(upper)
    layer_out = (stream_three + sum_rows([active], lambda r: project(r, w_down))).astype(jnp.bfloat16)
    grad_three = cotangent.astype(jnp.float32)
    grad_branch = share_rows(grad_three.astype(jnp.bfloat16))
    branch_three = grad_branch
    grad_active = jnp.einsum("clo,of->clf", grad_branch, w_down, preferred_element_type=jnp.float32)
    grad_upper = (grad_active * slope.astype(F32)).astype(jnp.bfloat16)
    norm_back = jax.vjp(layer_norm, stream_three, gain_ffn, bias_ffn)[1]
    grad_stream, grad_gain_ffn, grad_bias_ffn = norm_back(
        sum_rows([grad_upper], lambda r: input_grad_t(r, w_up))
    )
    grad_two = grad_three + grad_stream
    grad_branch = share_rows(grad_two.astype(jnp.bfloat16))
    branch_two = grad_branch
    grad_attended = split_heads(
        jnp.einsum("clo,oa->cla", grad_branch, w_co, preferred_element_type=F32).astype(BF16)
    )
    grad_query, grad_key, grad_value = attend_back(
        query_two, key_two, value_two, grad_attended, logsum_two, False
    )
    grad_query = flatten_heads(grad_query).astype(jnp.bfloat16)
    grad_key = flatten_heads(grad_key).astype(jnp.bfloat16)
    grad_value = flatten_heads(grad_value).astype(jnp.bfloat16)
    grad_query_two = grad_query
    text_part = input_grad_t(grad_key, w_ck) + input_grad_t(grad_value, w_cv)
    core, half = lax.axis_index("tensor"), width // 2
    arriving = other_core(
        lax.dynamic_slice_in_dim(text_part, (1 - core) * half, half, 2).astype(BF16)
    )
    grad_text = lax.dynamic_slice_in_dim(text_part, core * half, half, 2) + arriving.astype(F32)
    norm_back = jax.vjp(layer_norm, stream_two, gain_cross, bias_cross)[1]
    grad_stream, grad_gain_cross, grad_bias_cross = norm_back(
        sum_rows([grad_query], lambda r: input_grad_t(r, w_cq))
    )
    grad_one = grad_two + grad_stream
    grad_branch = share_rows(grad_one.astype(jnp.bfloat16))
    grad_attended = jnp.einsum(
        "clo,oa->cla", grad_branch, w_o, preferred_element_type=F32
    ).astype(BF16)
    part = grad_attended.shape[2]
    summed, grad_heads = backward_all(
        [
            r[0]
            for r in (branch_three, normed_three, branch_two, normed_two, grad_branch, normed_one)
        ],
        [
            r[0]
            for r in (
                active,
                grad_upper,
                flatten_heads(attended_two),
                grad_query_two,
                attended_one[None],
            )
        ],
        text_states[0],
        jnp.concatenate([grad_key[0], grad_value[0]], axis=1),
        [query_one, key_one, value_one, grad_attended[0]],
        logsum_one,
    )
    grad_query, grad_key, grad_value = [
        grad_heads[None, :, n * part : (n + 1) * part] for n in range(3)
    ]
    grad_normed = sum_rows(
        [grad_query, grad_key, grad_value],
        lambda q, k, v: input_grad_t(q, w_q) + input_grad_t(k, w_k) + input_grad_t(v, w_v),
    )
    norm_back = jax.vjp(layer_norm, stream_one, gain_self, bias_self)[1]
    grad_stream, grad_gain_self, grad_bias_self = norm_back(grad_normed)
    grad_input = grad_one + grad_stream
    norm_grads = jnp.stack(
        [
            grad_gain_self,
            grad_bias_self,
            grad_gain_cross,
            grad_bias_cross,
            grad_gain_ffn,
            grad_bias_ffn,
        ]
    )
    rows = width // 16
    norm_sums = lax.dynamic_slice_in_dim(
        sum_everywhere(jnp.pad(norm_grads, ((0, 2), (0, 0)))), lax.axis_index("dp") * rows, rows, 1
    )
    columns = [hidden_down.shape[1]] * 2 + [part] * 8
    pieces, first = [], 0
    for count in columns:
        pieces.append(summed[:, first : first + count])
        first += count
    down, up, out_cross, query_cross, key_cross, value_cross, out_self, query, key, value = pieces
    return (
        layer_out,
        grad_input,
        grad_text,
        norm_sums[0],
        norm_sums[1],
        query.T,
        key.T,
        value.T,
        out_self,
        norm_sums[2],
        norm_sums[3],
        query_cross.T,
        key_cross.T,
        value_cross.T,
        out_cross,
        norm_sums[4],
        norm_sums[5],
        up.T,
        down,
    )


def solution(mesh):
    placed = (
        P("dp", "tensor", None),
        P("dp", None, None),
        P("dp"),
        P("dp"),
        P("tensor", "dp"),
        P("tensor", "dp"),
        P("tensor", "dp"),
        P("dp", "tensor"),
        P("dp"),
        P("dp"),
        P("tensor", "dp"),
        P("tensor", "dp"),
        P("tensor", "dp"),
        P("dp", "tensor"),
        P("dp"),
        P("dp"),
        P("tensor", "dp"),
        P("dp", "tensor"),
        P("dp", "tensor", None),
    )
    fast = dict(mesh.shape) == {"dp": 16, "tensor": 2}
    return jax.shard_map(
        local_fast if fast else local_generic,
        mesh=mesh,
        in_specs=placed,
        out_specs=(
            P("dp", "tensor", None),
            P("dp", "tensor", None),
            P("dp", None, "tensor"),
            P("dp"),
            P("dp"),
            P("tensor", "dp"),
            P("tensor", "dp"),
            P("tensor", "dp"),
            P("dp", "tensor"),
            P("dp"),
            P("dp"),
            P("tensor", "dp"),
            P("tensor", "dp"),
            P("tensor", "dp"),
            P("dp", "tensor"),
            P("dp"),
            P("dp"),
            P("tensor", "dp"),
            P("dp", "tensor"),
        ),
        check_vma=False,
    )
```

```python
import functools

import jax
import jax.numpy as jnp
from jax import lax
from jax.experimental import pallas as pl
from jax.experimental.pallas import tpu as pltpu
from jax.sharding import PartitionSpec as P

HEAD_DIM = 64


norm_eps = 1e-05
score_scale = 0.125


def layer_norm(values, gain, shift):
    centre = jnp.mean(values, axis=-1, keepdims=True)
    offset = values - centre
    spread = jnp.mean(offset * offset, axis=-1, keepdims=True)
    return offset * lax.rsqrt(spread + norm_eps) * gain + shift


def gelu_exact(values):
    return jax.nn.gelu(values, approximate=False)


def project(row_data, weight):
    return jnp.einsum("cli,oi->clo", row_data, weight, preferred_element_type=jnp.float32)


def split_heads(values):
    return values.reshape(values.shape[0], values.shape[1], -1, HEAD_DIM)


def flatten_heads(values):
    return values.reshape(values.shape[0], values.shape[1], -1)


def causal_keep(first_row, count, length):
    row_ids = first_row + lax.broadcasted_iota(jnp.int32, (count, length), 0)
    col_ids = lax.broadcasted_iota(jnp.int32, (count, length), 1)
    return col_ids <= row_ids


def block_scores(queries, key_rows, first_row, block_rows, key_end, causal):
    scores = (
        jnp.einsum(
            "cqhe,ckhe->chqk",
            queries[:, first_row : first_row + block_rows],
            key_rows[:, :key_end],
            preferred_element_type=jnp.float32,
        )
        * score_scale
    )
    if causal:
        scores = jnp.where(causal_keep(first_row, block_rows, key_end), scores, -1e30)
    return scores


def attend(queries, key_rows, val_rows, causal):
    length = queries.shape[1]
    block_rows = min(512, length)
    outputs = []
    log_sums = []
    for block_num in range(length // block_rows):
        first_row = block_num * block_rows
        key_end = first_row + block_rows if causal else key_rows.shape[1]
        scores = block_scores(queries, key_rows, first_row, block_rows, key_end, causal)
        row_peak = jnp.max(scores, axis=-1, keepdims=True)
        exp_scores = jnp.exp(scores - row_peak)
        row_total = jnp.sum(exp_scores, axis=-1, keepdims=True)
        soft_weights = (exp_scores / row_total).astype(jnp.bfloat16)
        outputs.append(
            jnp.einsum(
                "chqk,ckhe->cqhe",
                soft_weights,
                val_rows[:, :key_end],
                preferred_element_type=jnp.float32,
            ).astype(jnp.bfloat16)
        )
        log_sums.append((row_peak + jnp.log(row_total))[..., 0])
    return (jnp.concatenate(outputs, axis=1), jnp.concatenate(log_sums, axis=2))


def attend_back(queries, key_rows, val_rows, grad_out, log_sums, causal):
    length = queries.shape[1]
    block_rows = min(512, length)
    grad_keys = jnp.zeros(key_rows.shape, jnp.float32)
    grad_vals = jnp.zeros(val_rows.shape, jnp.float32)
    grad_queries = []
    for block_num in range(length // block_rows):
        first_row = block_num * block_rows
        key_end = first_row + block_rows if causal else key_rows.shape[1]
        query_blk = queries[:, first_row : first_row + block_rows]
        grad_blk = grad_out[:, first_row : first_row + block_rows]
        scores = block_scores(queries, key_rows, first_row, block_rows, key_end, causal)
        soft = jnp.exp(scores - log_sums[:, :, first_row : first_row + block_rows, None])
        grad_soft = jnp.einsum(
            "cqhe,ckhe->chqk", grad_blk, val_rows[:, :key_end], preferred_element_type=jnp.float32
        )
        grad_vals = grad_vals.at[:, :key_end].add(
            jnp.einsum(
                "chqk,cqhe->ckhe",
                soft.astype(jnp.bfloat16),
                grad_blk,
                preferred_element_type=jnp.float32,
            )
        )
        inner = jnp.sum(soft * grad_soft, axis=-1, keepdims=True)
        grad_scores = (soft * (grad_soft - inner)).astype(jnp.bfloat16)
        grad_queries.append(
            jnp.einsum(
                "chqk,ckhe->cqhe",
                grad_scores,
                key_rows[:, :key_end],
                preferred_element_type=jnp.float32,
            )
            * score_scale
        )
        grad_keys = grad_keys.at[:, :key_end].add(
            jnp.einsum(
                "chqk,cqhe->ckhe", grad_scores, query_blk, preferred_element_type=jnp.float32
            )
            * score_scale
        )
    return (jnp.concatenate(grad_queries, axis=1), grad_keys, grad_vals)


def gather_rows(values):
    return lax.all_gather(values, "tensor", axis=1, tiled=True)


def scatter_rows(values):
    return lax.psum_scatter(values, "tensor", scatter_dimension=1, tiled=True)


def gather_grads(values):
    return lax.all_gather(values, "tensor", axis=1, tiled=True)


def scatter_grads(values):
    return lax.psum_scatter(
        values.astype(jnp.bfloat16), "tensor", scatter_dimension=1, tiled=True
    ).astype(jnp.float32)


def heads_grads(grad_branch, attended, out_weight):
    grad_out_proj = jnp.einsum(
        "clo,cla->oa", grad_branch, flatten_heads(attended), preferred_element_type=jnp.float32
    )
    grad_attended = split_heads(
        jnp.einsum(
            "clo,oa->cla", grad_branch, out_weight, preferred_element_type=jnp.float32
        ).astype(jnp.bfloat16)
    )
    return (grad_out_proj, grad_attended)


def weight_grad(grad_rows, source_rows):
    return jnp.einsum("cla,cli->ai", grad_rows, source_rows, preferred_element_type=jnp.float32)


def input_grad(grad_rows, weight):
    return jnp.einsum("cla,ai->cli", grad_rows, weight, preferred_element_type=jnp.float32)


def local_generic(
    hidden_in,
    text_states,
    norm1_gain,
    norm1_bias,
    self_query,
    self_key,
    self_value,
    self_out,
    norm2_gain,
    norm2_bias,
    cross_query,
    cross_key,
    cross_value,
    cross_out,
    norm3_gain,
    norm3_bias,
    hidden_up,
    hidden_down,
    cotangent,
):
    full_weights = (
        lax.all_gather(norm1_gain, "dp", axis=0, tiled=True),
        lax.all_gather(norm1_bias, "dp", axis=0, tiled=True),
        lax.all_gather(self_query, "dp", axis=1, tiled=True),
        lax.all_gather(self_key, "dp", axis=1, tiled=True),
        lax.all_gather(self_value, "dp", axis=1, tiled=True),
        lax.all_gather(self_out, "dp", axis=0, tiled=True),
        lax.all_gather(norm2_gain, "dp", axis=0, tiled=True),
        lax.all_gather(norm2_bias, "dp", axis=0, tiled=True),
        lax.all_gather(cross_query, "dp", axis=1, tiled=True),
        lax.all_gather(cross_key, "dp", axis=1, tiled=True),
        lax.all_gather(cross_value, "dp", axis=1, tiled=True),
        lax.all_gather(cross_out, "dp", axis=0, tiled=True),
        lax.all_gather(norm3_gain, "dp", axis=0, tiled=True),
        lax.all_gather(norm3_bias, "dp", axis=0, tiled=True),
        lax.all_gather(hidden_up, "dp", axis=1, tiled=True),
        lax.all_gather(hidden_down, "dp", axis=0, tiled=True),
    )
    gain_self = full_weights[0].astype(jnp.float32)
    bias_self = full_weights[1].astype(jnp.float32)
    gain_cross = full_weights[6].astype(jnp.float32)
    bias_cross = full_weights[7].astype(jnp.float32)
    gain_ffn = full_weights[12].astype(jnp.float32)
    bias_ffn = full_weights[13].astype(jnp.float32)
    stream_one = hidden_in.astype(jnp.float32)
    key_two = split_heads(project(text_states, full_weights[9]).astype(jnp.bfloat16))
    value_two = split_heads(project(text_states, full_weights[10]).astype(jnp.bfloat16))
    normed_one = gather_rows(layer_norm(stream_one, gain_self, bias_self).astype(jnp.bfloat16))
    query_one = split_heads(project(normed_one, full_weights[2]).astype(jnp.bfloat16))
    key_one = split_heads(project(normed_one, full_weights[3]).astype(jnp.bfloat16))
    value_one = split_heads(project(normed_one, full_weights[4]).astype(jnp.bfloat16))
    attended_one, logsum_one = attend(query_one, key_one, value_one, True)
    stream_two = stream_one + scatter_rows(project(flatten_heads(attended_one), full_weights[5]))
    normed_two = gather_rows(layer_norm(stream_two, gain_cross, bias_cross).astype(jnp.bfloat16))
    query_two = split_heads(project(normed_two, full_weights[8]).astype(jnp.bfloat16))
    attended_two, logsum_two = attend(query_two, key_two, value_two, False)
    stream_three = stream_two + scatter_rows(project(flatten_heads(attended_two), full_weights[11]))
    normed_three = gather_rows(layer_norm(stream_three, gain_ffn, bias_ffn).astype(jnp.bfloat16))
    upper = project(normed_three, full_weights[14])
    active = gelu_exact(upper).astype(jnp.bfloat16)
    layer_out = (stream_three + scatter_rows(project(active, full_weights[15]))).astype(
        jnp.bfloat16
    )
    grad_three = cotangent.astype(jnp.float32)
    grad_branch = gather_grads(grad_three.astype(jnp.bfloat16))
    grad_down = jnp.einsum("clo,clf->of", grad_branch, active, preferred_element_type=jnp.float32)
    grad_active = jnp.einsum(
        "clo,of->clf", grad_branch, full_weights[15], preferred_element_type=jnp.float32
    )
    grad_upper = jax.vjp(gelu_exact, upper)[1](grad_active)[0].astype(jnp.bfloat16)
    grad_up = weight_grad(grad_upper, normed_three)
    norm_back = jax.vjp(layer_norm, stream_three, gain_ffn, bias_ffn)[1]
    grad_stream, grad_gain_ffn, grad_bias_ffn = norm_back(
        scatter_grads(input_grad(grad_upper, full_weights[14]))
    )
    grad_two = grad_three + grad_stream
    grad_branch = gather_grads(grad_two.astype(jnp.bfloat16))
    grad_out_cross, grad_attended = heads_grads(grad_branch, attended_two, full_weights[11])
    grad_query, grad_key, grad_value = attend_back(
        query_two, key_two, value_two, grad_attended, logsum_two, False
    )
    grad_query = flatten_heads(grad_query).astype(jnp.bfloat16)
    grad_key = flatten_heads(grad_key).astype(jnp.bfloat16)
    grad_value = flatten_heads(grad_value).astype(jnp.bfloat16)
    grad_query_cross = weight_grad(grad_query, normed_two)
    grad_key_cross = weight_grad(grad_key, text_states)
    grad_value_cross = weight_grad(grad_value, text_states)
    text_part = input_grad(grad_key, full_weights[9]) + input_grad(grad_value, full_weights[10])
    grad_text = lax.psum_scatter(
        text_part.astype(jnp.bfloat16), "tensor", scatter_dimension=2, tiled=True
    ).astype(jnp.float32)
    norm_back = jax.vjp(layer_norm, stream_two, gain_cross, bias_cross)[1]
    grad_stream, grad_gain_cross, grad_bias_cross = norm_back(
        scatter_grads(input_grad(grad_query, full_weights[8]))
    )
    grad_one = grad_two + grad_stream
    grad_branch = gather_grads(grad_one.astype(jnp.bfloat16))
    grad_out_self, grad_attended = heads_grads(grad_branch, attended_one, full_weights[5])
    grad_query, grad_key, grad_value = attend_back(
        query_one, key_one, value_one, grad_attended, logsum_one, True
    )
    grad_query = flatten_heads(grad_query).astype(jnp.bfloat16)
    grad_key = flatten_heads(grad_key).astype(jnp.bfloat16)
    grad_value = flatten_heads(grad_value).astype(jnp.bfloat16)
    grad_query_self = weight_grad(grad_query, normed_one)
    grad_key_self = weight_grad(grad_key, normed_one)
    grad_value_self = weight_grad(grad_value, normed_one)
    grad_normed = (
        input_grad(grad_query, full_weights[2])
        + input_grad(grad_key, full_weights[3])
        + input_grad(grad_value, full_weights[4])
    )
    norm_back = jax.vjp(layer_norm, stream_one, gain_self, bias_self)[1]
    grad_stream, grad_gain_self, grad_bias_self = norm_back(scatter_grads(grad_normed))
    grad_input = grad_one + grad_stream
    summed = (
        lax.psum_scatter(
            grad_gain_self.astype(jnp.bfloat16), "dp", scatter_dimension=0, tiled=True
        ).astype(jnp.float32),
        lax.psum_scatter(
            grad_bias_self.astype(jnp.bfloat16), "dp", scatter_dimension=0, tiled=True
        ).astype(jnp.float32),
        lax.psum_scatter(
            grad_query_self.astype(jnp.bfloat16), "dp", scatter_dimension=1, tiled=True
        ).astype(jnp.float32),
        lax.psum_scatter(
            grad_key_self.astype(jnp.bfloat16), "dp", scatter_dimension=1, tiled=True
        ).astype(jnp.float32),
        lax.psum_scatter(
            grad_value_self.astype(jnp.bfloat16), "dp", scatter_dimension=1, tiled=True
        ).astype(jnp.float32),
        lax.psum_scatter(
            grad_out_self.astype(jnp.bfloat16), "dp", scatter_dimension=0, tiled=True
        ).astype(jnp.float32),
        lax.psum_scatter(
            grad_gain_cross.astype(jnp.bfloat16), "dp", scatter_dimension=0, tiled=True
        ).astype(jnp.float32),
        lax.psum_scatter(
            grad_bias_cross.astype(jnp.bfloat16), "dp", scatter_dimension=0, tiled=True
        ).astype(jnp.float32),
        lax.psum_scatter(
            grad_query_cross.astype(jnp.bfloat16), "dp", scatter_dimension=1, tiled=True
        ).astype(jnp.float32),
        lax.psum_scatter(
            grad_key_cross.astype(jnp.bfloat16), "dp", scatter_dimension=1, tiled=True
        ).astype(jnp.float32),
        lax.psum_scatter(
            grad_value_cross.astype(jnp.bfloat16), "dp", scatter_dimension=1, tiled=True
        ).astype(jnp.float32),
        lax.psum_scatter(
            grad_out_cross.astype(jnp.bfloat16), "dp", scatter_dimension=0, tiled=True
        ).astype(jnp.float32),
        lax.psum_scatter(
            grad_gain_ffn.astype(jnp.bfloat16), "dp", scatter_dimension=0, tiled=True
        ).astype(jnp.float32),
        lax.psum_scatter(
            grad_bias_ffn.astype(jnp.bfloat16), "dp", scatter_dimension=0, tiled=True
        ).astype(jnp.float32),
        lax.psum_scatter(
            grad_up.astype(jnp.bfloat16), "dp", scatter_dimension=1, tiled=True
        ).astype(jnp.float32),
        lax.psum_scatter(
            grad_down.astype(jnp.bfloat16), "dp", scatter_dimension=0, tiled=True
        ).astype(jnp.float32),
    )
    norm_sums = lax.psum(
        (summed[0], summed[1], summed[6], summed[7], summed[12], summed[13]), "tensor"
    )
    return (
        layer_out,
        grad_input,
        grad_text,
        norm_sums[0],
        norm_sums[1],
        summed[2],
        summed[3],
        summed[4],
        summed[5],
        norm_sums[2],
        norm_sums[3],
        summed[8],
        summed[9],
        summed[10],
        summed[11],
        norm_sums[4],
        norm_sums[5],
        summed[14],
        summed[15],
    )


MESH_IDS = pl.DeviceIdType.MESH
BF16 = jnp.bfloat16
F32 = jnp.float32
VMEM_LIMIT = 63 * 2**20


def my_place():
    chip = lax.axis_index("dp")
    core = lax.axis_index("tensor")
    return (lax.rem(chip, 2), lax.rem(lax.div(chip, 2), 2), lax.div(chip, 4), core)


def neighbours(x, y, z, core):
    def device(zz, yy, xx):
        return (zz * 4 + yy * 2 + xx, core)

    return (device(z, y, 1 - x), device(z, 1 - y, x), device(z + 1, y, x), device(z - 1, y, x))


def when(cond, fn):
    if cond is None:
        fn()
    else:
        pl.when(cond)(fn)


def signal_neighbours(sems, near, has_up, has_down):
    for sem, device, cond in zip(sems, near, (None, None, has_up, has_down), strict=True):
        when(
            cond,
            functools.partial(
                pl.semaphore_signal, sem, inc=1, device_id=device, device_id_type=MESH_IDS
            ),
        )


def gather_engine(chunks, shards, outs, sems):
    local_sem, send_sem, zs, xs, ys, ds = sems
    x, y, z, core = my_place()
    xn, yn = 1 - x, 1 - y
    near = neighbours(x, y, z, core)
    right, across, up, down = near
    has_up, has_down = z < 3, z > 0
    barrier = pltpu.get_barrier_semaphore()
    signal_neighbours([barrier] * 4, near, has_up, has_down)
    pl.semaphore_signal(barrier, inc=1, device_id=(lax.axis_index("dp"), 1 - core), device_id_type=MESH_IDS)
    pl.semaphore_wait(barrier, 3 + has_up.astype(jnp.int32) + has_down.astype(jnp.int32))
    total = len(chunks)
    pending = []


    def span(c):
        _, first, width, _ = chunks[c]
        return pl.ds(first, width)

    def at(zz, yy, xx, c, half=None):
        ref = outs[chunks[c][0]]
        half_rows = ref.shape[3] // 2
        lines = slice(None) if half is None else pl.ds(half * half_rows, half_rows)
        return ref.at[zz, yy, xx, lines, span(c)]

    def plane(zz, c):
        return outs[chunks[c][0]].at[zz, :, :, :, span(c)]

    def own(c):
        return shards[chunks[c][0]].at[:, span(c)]

    local = [pltpu.make_async_copy(own(c), at(z, y, x, c), local_sem.at[c]) for c in range(total)]

    def remote(src, dst, sem, device):
        return pltpu.make_async_remote_copy(
            src_ref=src,
            dst_ref=dst,
            send_sem=send_sem,
            recv_sem=sem,
            device_id=device,
            device_id_type=MESH_IDS,
        )

    def send(src, dst, sem, device, cond=None):
        copy = remote(src, dst, sem, device)
        when(cond, copy.start)
        pending.append((cond, copy))

    def wait(ref, sem, cond=None):
        when(cond, remote(ref, ref, sem, right).wait_recv)

    def lines(step):
        for sign, device, more in ((-1, up, has_up), (1, down, has_down)):
            block = z + sign * step
            yield block, (block >= 0) if sign < 0 else (block <= 3), device, more

    def stage_z(c, step):
        if step == 0:
            send(own(c), at(z, y, x, c), zs.at[c, z], up, has_up)
            send(own(c), at(z, y, x, c), zs.at[c, z], down, has_down)
            send(own(c), at(z, y, x, c), xs.at[c, z], right)
            send(own(c), at(z, y, x, c), ys.at[c, z], across)
            local[c].start()
        if 1 <= step <= 3:
            for block, exists, device, more in lines(step):
                ref = at(block, y, x, c)
                wait(ref, zs.at[c, block], exists)
                if step < 3:
                    send(ref, ref, zs.at[c, block], device, exists & more)
                send(ref, ref, xs.at[c, block], right, exists)
                send(ref, ref, ys.at[c, block], across, exists)
        if 1 <= step <= 4:
            for block, exists, _, _ in [(z, None, None, None)] if step == 1 else lines(step - 1):
                wait(at(block, y, xn, c), xs.at[c, block], exists)
                ref = at(block, y, xn, c, 0)
                send(ref, ref, ds.at[c, block, 0], across, exists)
                wait(at(block, yn, x, c), ys.at[c, block], exists)
                ref = at(block, yn, x, c, 1)
                send(ref, ref, ds.at[c, block, 1], right, exists)
        if step == 5:
            for block in range(4):
                for half in range(2):
                    wait(at(block, yn, xn, c, half), ds.at[c, block, half])
            local[c].wait()

    def stage_a(c, step):
        if step == 0:
            send(own(c), at(z, y, x, c), xs.at[c, z], right)
            send(own(c), at(z, y, x, c), ys.at[c, z], across)
            local[c].start()
        if step == 1:
            wait(at(z, y, xn, c), xs.at[c, z])
            ref = at(z, y, xn, c, 0)
            send(ref, ref, ds.at[c, z, 0], across)
            wait(at(z, yn, x, c), ys.at[c, z])
            ref = at(z, yn, x, c, 1)
            send(ref, ref, ds.at[c, z, 1], right)
        if step == 2:
            for half in range(2):
                wait(at(z, yn, xn, c, half), ds.at[c, z, half])
            local[c].wait()
            send(plane(z, c), plane(z, c), zs.at[c, z], up, has_up)
            send(plane(z, c), plane(z, c), zs.at[c, z], down, has_down)
        if step >= 3:
            for block, exists, device, more in lines(step - 2):
                wait(plane(block, c), zs.at[c, block], exists)
                if step < 5:
                    send(plane(block, c), plane(block, c), zs.at[c, block], device, exists & more)

    stages = 6

    def turn(number):
        for step in range(stages):
            c = number - step
            if 0 <= c < total:
                (stage_z if chunks[c][3] == "Z" else stage_a)(c, step)

    def finish():
        for cond, copy in pending:
            when(cond, copy.wait_send)

    return turn, finish


def total_of(*parts):
    value = parts[0].astype(F32)
    for part in parts[1:]:
        value = value + part.astype(F32)
    return value


def dot_nt(left, right):
    return lax.dot_general(left, right, (((1,), (1,)), ((), ())), preferred_element_type=F32)


def dot_tn(left, right):
    return lax.dot_general(left, right, (((0,), (0,)), ((), ())), preferred_element_type=F32)


def dot_nn(left, right):
    return jnp.dot(left, right, preferred_element_type=F32)


def project_rows(source, weight, store, rows=256, transposed=False):
    def body(n, carry):
        first = pl.multiple_of(n * rows, rows)
        part = source[pl.ds(first, rows), :]
        store(first, dot_nt(part, weight[...]) if transposed else dot_nn(part, weight[...]))
        return carry

    lax.fori_loop(0, source.shape[0] // rows, body, 0)


def normalize(values, gain, shift):
    offset = values - jnp.mean(values, axis=-1, keepdims=True)
    spread = jnp.mean(offset * offset, axis=-1, keepdims=True)
    return offset * lax.rsqrt(spread + norm_eps) * gain + shift


def head_lanes(half):
    return lax.div(lax.broadcasted_iota(jnp.int32, (1, 128), 1), 64) == half


def only(mask, value):
    return jnp.where(mask, value.astype(F32), 0.0).astype(BF16)


def pair_forward(pair, q_ref, k_ref, v_ref, o_ref, lse_ref, causal):
    cols = pl.ds(pl.multiple_of(pair * 128, 128), 128)
    block = 256
    keep = lax.broadcasted_iota(jnp.int32, (block, block), 0) <= lax.broadcasted_iota(
        jnp.int32, (block, block), 1
    )
    for i in range(q_ref.shape[0] // block):
        rows = pl.ds(i * block, block)
        parts = [(0, k_ref.shape[0], False)]
        if causal:
            parts = [(0, i * block, False)] * (i > 0) + [(i * block, block, True)]
        total = 0.0
        for half in range(2):
            mine = head_lanes(half)
            q = only(mine, q_ref[rows, cols])
            scores = []
            for first, count, diagonal in parts:
                part = dot_nt(k_ref[pl.ds(first, count), cols], q) * score_scale
                scores.append(jnp.where(keep, part, -1e30) if diagonal else part)
            peak = functools.reduce(
                jnp.maximum, [jnp.max(part, axis=0, keepdims=True) for part in scores]
            )
            scores = [jnp.exp(part - peak) for part in scores]
            weight = sum(jnp.sum(part, axis=0, keepdims=True) for part in scores)
            lse_ref[pl.ds(2 * pair + half, 1), rows] = peak + jnp.log(weight)
            share = 1.0 / weight
            for (first, count, _), part in zip(parts, scores, strict=True):
                v = only(mine, v_ref[pl.ds(first, count), cols])
                total = total + dot_tn((part * share).astype(BF16), v)
        o_ref[rows, cols] = total.astype(BF16)


def forward_kernel(chunks, count, *refs):
    shards, refs = refs[:count], refs[count:]
    hidden_h, text_h, cotangent_h, refs = refs[0], refs[1], refs[2], refs[3:]
    outs, refs = refs[:count], refs[count:]
    results, refs = refs[:19], refs[19:]
    sems, refs = refs[:6], refs[6:]
    (h1, h2, h3, q1, k1, v1, o1, q2, k2, v2, o2, lse1, lse2, x2, x3), refs = refs[:15], refs[15:]
    gathered_norms, norms, weights, hidden, text, mine, theirs, arrived, active, slopes = refs[:10]
    norm_sem, weight_sem, load_sem, share_send, share_recv, result_sem = refs[10:]
    names = dict(norms=0, q=1, k=2, v=3, o=4, ck=5, cv=6, cq=7, co=8, up=9, down=10)
    turn, finish = gather_engine(chunks, shards, outs, sems)
    chip, core = lax.axis_index("dp"), lax.axis_index("tensor")
    frames, width = h1.shape
    half = frames // 2
    own = pl.ds(pl.multiple_of(core * half, half), half)
    loads = [
        pltpu.make_async_copy(hidden_h, hidden, load_sem.at[0]),
        pltpu.make_async_copy(text_h, text, load_sem.at[1]),
    ]
    for copy in loads:
        copy.start()
    pending = []

    def weight_copy(name, slot, first=0):
        return [
            pltpu.make_async_copy(
                outs[names[name]].at[zz, yy, xx, :, pl.ds(first, weights.shape[2])],
                weights.at[slot, pl.ds(((zz * 2 + yy) * 2 + xx) * rows, rows), :],
                weight_sem.at[slot, (zz * 2 + yy) * 2 + xx],
            )
            for zz in range(4)
            for yy in range(2)
            for xx in range(2)
        ]

    rows = width // 16

    def load_weight(name, slot, first=0):
        for copy in weight_copy(name, slot, first):
            copy.start()

    def wait_weight(slot):
        for copy in weight_copy("q", slot):
            copy.wait()

    def share(n, src, dst):
        return pltpu.make_async_remote_copy(
            src_ref=src,
            dst_ref=dst,
            send_sem=share_send.at[n],
            recv_sem=share_recv.at[n],
            device_id=(chip, 1 - core),
            device_id_type=MESH_IDS,
        )

    def give(n, ref):
        copy = pltpu.make_async_copy(ref, results[n], result_sem.at[n])
        copy.start()
        pending.append(copy)

    def norm_share(n, values, kind, h):
        step = 64

        def body(i, carry):
            first = pl.multiple_of(i * step, step)
            h[pl.ds(pl.multiple_of(core * half + first, step), step), :] = normalize(
                values(first, step), norms[2 * kind : 2 * kind + 1], norms[2 * kind + 1 : 2 * kind + 2]
            ).astype(BF16)
            return carry

        lax.fori_loop(0, half // step, body, 0)
        share(n, h.at[own], h.at[own]).start()

    def get_share(n, h):
        share(n, h.at[own], h.at[own]).wait()

    def to(ref):
        def store(first, value):
            ref[pl.ds(first, value.shape[0]), :] = value.astype(BF16)

        return store

    def out_project(n, o, slot):
        step = 256
        for whose, ref in ((1 - core, theirs.at[n]), (core, mine)):
            for first in range(0, half, step):
                part = o[pl.ds(pl.multiple_of(whose * half + first, step), step), :]
                ref[pl.ds(first, step), :] = dot_nt(part, weights[slot]).astype(ref.dtype)
            if whose is not core:
                share(3 + n, theirs.at[n], arrived.at[n]).start()

    def add_stream(n, before, after):
        def values(first, step):
            lines = pl.ds(first, step)
            total = before[lines, :].astype(F32) + (mine[lines, :] + arrived[n, lines, :].astype(F32))
            after[lines, :] = total
            return total

        return values

    branch = results[16].at[own]
    branch_copy = pltpu.make_async_copy(cotangent_h, branch, result_sem.at[16])

    def active_copies(j):
        lanes = pl.ds(j * active.shape[1], active.shape[1])
        return (
            pltpu.make_async_copy(active, results[17].at[:, lanes], result_sem.at[17]),
            pltpu.make_async_copy(slopes, results[18].at[:, lanes], result_sem.at[18]),
        )

    def hidden_units(j):
        wait_weight(j % 2)
        if j < 3:
            load_weight("up", (j + 1) % 2, (j + 1) * active.shape[1])
        if j:
            for copy in active_copies(j - 1):
                copy.wait()

        def store(first, value):
            lines = pl.ds(first, value.shape[0])
            below = 0.5 * (1.0 + lax.erf(value * (0.5**0.5)))
            density = jnp.exp(-0.5 * value * value) * 0.3989422804014327
            active[lines, :] = (value * below).astype(BF16)
            slopes[lines, :] = (below + value * density).astype(BF16)

        project_rows(h3, weights.at[j % 2], store)
        for copy in active_copies(j):
            copy.start()

    def work(number):
        if number == 0:
            share(5, cotangent_h, branch).start()
            branch_copy.start()
        if number == 5:
            copy = pltpu.make_async_copy(outs[0], gathered_norms, norm_sem)
            copy.start()
            copy.wait()
            for copy in loads:
                copy.wait()
            total = 0.0
            lane = lax.broadcasted_iota(jnp.int32, (128, width), 0)
            place = lax.broadcasted_iota(jnp.int32, (128, width), 1)
            for n in range(16):
                pick = (place == lane + n * rows) & (lane < rows)
                total = total + dot_nn(
                    gathered_norms[n // 4, n // 2 % 2, n % 2],
                    jnp.where(pick, 1.0, 0.0).astype(BF16),
                )
            norms[...] = total
            give(13, norms)
            norm_share(0, lambda first, step: hidden[pl.ds(first, step), :].astype(F32), 0, h1)
        if number == 6:
            load_weight("q", 0)
            get_share(0, h1)
            give(0, h1)
            wait_weight(0)
            project_rows(h1, weights.at[0], to(q1))
            give(3, q1)
        if number == 7:
            load_weight("k", 1)
            wait_weight(1)
            project_rows(h1, weights.at[1], to(k1))
            give(4, k1)
        if number == 8:
            load_weight("v", 0)
            wait_weight(0)
            project_rows(h1, weights.at[0], to(v1))
            give(5, v1)
        if number in (9, 10, 11):
            if number == 9:
                load_weight("o", 1)
            pairs = q1.shape[1] // 128
            first = pairs * (number - 9) // 3
            last = pairs * (number - 8) // 3

            def body(pair, carry):
                pair_forward(pair, q1, k1, v1, o1, lse1, True)
                return carry

            lax.fori_loop(first, last, body, 0)
            if number == 11:
                load_weight("cv", 0)
        if number == 12:
            give(6, o1)
            give(11, lse1)
            wait_weight(1)
            out_project(0, o1, 1)
            load_weight("ck", 1)
            wait_weight(0)
            v2[...] = dot_nn(text[...], weights[0]).astype(BF16)
            give(9, v2)
            load_weight("cq", 0)
        if number == 13:
            share(3, theirs.at[0], arrived.at[0]).wait()
            norm_share(1, add_stream(0, hidden, x2), 1, h2)
            give(14, x2)
            wait_weight(1)
            k2[...] = dot_nn(text[...], weights[1]).astype(BF16)
            give(8, k2)
            load_weight("co", 1)
        if number == 14:
            get_share(1, h2)
            give(1, h2)
            wait_weight(0)
            project_rows(h2, weights.at[0], to(q2))
            give(7, q2)
        if number == 15:

            def body(pair, carry):
                pair_forward(pair, q2, k2, v2, o2, lse2, False)
                return carry

            lax.fori_loop(0, q2.shape[1] // 128, body, 0)
            give(10, o2)
            give(12, lse2)
        if number == 16:
            wait_weight(1)
            out_project(1, o2, 1)
        if number == 17:
            share(4, theirs.at[1], arrived.at[1]).wait()
            norm_share(2, add_stream(1, x2, x3), 2, h3)
            give(15, x3)
            load_weight("up", 0)
        if number == 18:
            get_share(2, h3)
            give(2, h3)
            share(5, cotangent_h, branch).wait()
            branch_copy.wait()
        if 18 <= number < 22:
            hidden_units(number - 18)

    for number in range(len(chunks) + 5):
        turn(number)
        work(number)
    finish()
    for copy in (*pending, *active_copies(3)):
        copy.wait()


def forward_all(shards, chunks, hidden, text, cotangent):
    total, count = len(chunks), len(shards)
    dma, vmem = pltpu.SemaphoreType.DMA, pltpu.VMEM
    half, width = hidden.shape
    frames, part = 2 * half, shards[1].shape[1]
    anywhere = pl.BlockSpec(memory_space=pl.ANY)
    shape = jax.ShapeDtypeStruct
    kept = [
        *[((frames, width), BF16)] * 3,
        *[((frames, part), BF16)] * 4,
        ((frames, part), BF16),
        *[((text.shape[0], part), BF16)] * 2,
        ((frames, part), BF16),
        *[((16, frames), F32)] * 2,
    ]
    given = [*kept, ((shards[0].shape[0], width), F32), ((half, width), F32), ((half, width), F32)]
    given += [((frames, width), BF16), ((frames, 4 * part), BF16), ((frames, 4 * part), BF16)]
    held = [*kept, ((half, width), F32), ((half, width), F32)]
    outs = pl.pallas_call(
        functools.partial(forward_kernel, chunks, count),
        out_shape=[shape((4, 2, 2) + s.shape, s.dtype) for s in shards] + [shape(*g) for g in given],
        in_specs=[anywhere] * (count + 3),
        out_specs=[anywhere] * (count + len(given)),
        scratch_shapes=[
            dma((total,)),
            dma,
            dma((total, 4)),
            dma((total, 4)),
            dma((total, 4)),
            dma((total, 4, 2)),
            *[vmem(*h) for h in held],
            vmem((4, 2, 2) + shards[0].shape, BF16),
            vmem((shards[0].shape[0], width), F32),
            vmem((2, width, part), BF16),
            vmem((half, width), BF16),
            vmem(text.shape, BF16),
            vmem((half, width), F32),
            vmem((2, half, width), BF16),
            vmem((2, half, width), BF16),
            vmem((frames, part), BF16),
            vmem((frames, part), BF16),
            dma,
            dma((2, 16)),
            dma((2,)),
            dma((6,)),
            dma((6,)),
            dma((19,)),
        ],
        compiler_params=pltpu.CompilerParams(
            collective_id=0, has_side_effects=True, vmem_limit_bytes=VMEM_LIMIT
        ),
        name="forward",
    )(*shards, hidden, text, cotangent)
    return outs[:count], outs[count:]


XD, YD, XA, YA, XB, YB, UP, DOWN = range(8)


UNIT = 256
WIDTH_Z, WIDTH_A, SLOTS = 384, 128, 7
ROWS_L = 6
FIRST_L = (0, 12, 24, 27, 36, 39)
LOAD_L = ((2, 10), (3, 11), (4, 14), (5, 15))
FIRST_R = ((0, 12), (12, 24), (24, 27), (27, 30), (36, 39))
TEXT_UNITS = (30, 36)
SELF_UNITS = (39, 48)
UNITS = 48


def head_back(head, q_ref, k_ref, v_ref, do_ref, lse_ref, dq_ref, dkv_ref, bases, acc_k, acc_v, causal):
    pair, half = lax.div(head, 2), lax.rem(head, 2)
    cols = pl.ds(pl.multiple_of(pair * 128, 128), 128)
    lanes = [pl.ds(pl.multiple_of(pair * 128 + base, 128), 128) for base in bases]
    mine = head_lanes(half)
    length = k_ref.shape[0]
    acc_k[pl.ds(0, length), :] = jnp.zeros((length, 128), F32)
    acc_v[pl.ds(0, length), :] = jnp.zeros((length, 128), F32)
    block = 256
    keep = lax.broadcasted_iota(jnp.int32, (block, block), 0) <= lax.broadcasted_iota(
        jnp.int32, (block, block), 1
    )

    def merged(ref, rows, lane, value):
        before = jnp.where(half == 0, 0.0, ref[rows, lane].astype(F32))
        ref[rows, lane] = (before + value).astype(BF16)

    for i in range(q_ref.shape[0] // block):
        rows = pl.ds(i * block, block)
        q = only(mine, q_ref[rows, cols])
        do = only(mine, do_ref[rows, cols])
        lse = lse_ref[pl.ds(head, 1), rows]
        parts = [(0, length, False)]
        if causal:
            parts = [(0, i * block, False)] * (i > 0) + [(i * block, block, True)]
        held, inner = [], 0.0
        for first, count, diagonal in parts:
            keys = pl.ds(first, count)
            soft = jnp.exp(dot_nt(k_ref[keys, cols], q) * score_scale - lse)
            if diagonal:
                soft = jnp.where(keep, soft, 0.0)
            slope = dot_nt(v_ref[keys, cols], do)
            inner = inner + jnp.sum(soft * slope, axis=0, keepdims=True)
            held.append((keys, soft, slope))
        grad_q = 0.0
        for keys, soft, slope in held:
            ds = (soft * (slope - inner)).astype(BF16)
            acc_v[keys, :] += dot_nn(soft.astype(BF16), do)
            acc_k[keys, :] += dot_nn(ds, q)
            grad_q = grad_q + dot_tn(ds, k_ref[keys, cols])
        merged(dq_ref, rows, lanes[0], jnp.where(mine, grad_q * score_scale, 0.0))
    everything = pl.ds(0, length)
    merged(dkv_ref, everything, lanes[1], acc_k[everything, :] * score_scale)
    merged(dkv_ref, everything, lanes[2], acc_v[everything, :])


def backward_kernel(*refs):
    (e3_h, h3_h, h2_h, h1_h, a_h, slope_h, o2_h, o1_h, text_h), refs = refs[:9], refs[9:]
    (q2_h, k2_h, v2_h, q1_h, k1_h, v1_h, x3_h, x2_h, x1_h), refs = refs[:9], refs[9:]
    (w_q, w_k, w_v, w_o, w_ck, w_cv, w_cq, w_co, w_up, w_down), refs = refs[:10], refs[10:]
    (lse2_ref, lse1_ref, norms), refs = refs[:3], refs[3:]
    (out, layer_out, grad_input, grad_text, norm_out), refs = refs[:5], refs[5:]
    (du_h, dq2_h, e2_h, e1_h), refs = refs[:4], refs[4:]
    (gz, ga, xdz, ydz, xaz, yaz, xbz, ybz, lnz), refs = refs[:9], refs[9:]
    (xda, yda, xaa, yaa, xba, yba, lna, oz, oa), refs = refs[:9], refs[9:]
    (lbuf, rbuf, text_v, dkv_v, k2_v, v2_v, pool, dqkv, acc_k, acc_v), refs = refs[:10], refs[10:]
    (acc, grad, xbuf, theirs, arrived, weights, text_part, text_send, text_got), refs = refs[:9], refs[9:]
    (norm_grads, got), refs = refs[:2], refs[2:]
    (first_sem, l_sem, r_sem, out_sem, send_z, send_a, recv_z, recv_a), refs = refs[:8], refs[8:]
    (pool_sem, slope_sem, weight_sem, x_sem, keep_sem, share_send, share_recv, norm_send), refs = refs[:8], refs[8:]
    norm_recv, credit = refs
    lefts = (e3_h, h3_h, e2_h, h2_h, e1_h, h1_h)
    rights = (a_h, du_h, o2_h, dq2_h, o1_h)
    width_z, width_a, slots = WIDTH_Z, WIDTH_A, SLOTS
    total, width = UNITS // 2, WIDTH_Z + WIDTH_A
    x, y, z, core = my_place()
    xn, yn = 1 - x, 1 - y
    near = neighbours(x, y, z, core)
    right, across, up, down = near
    has_up, has_down = z < 3, z > 0
    degree = 2 + has_up.astype(jnp.int32) + has_down.astype(jnp.int32)
    chip = lax.axis_index("dp")
    other = (chip, 1 - core)
    partners = [other]
    for bit in (1, 2, 4, 8):
        partners.append((chip + bit * (1 - 2 * lax.rem(lax.div(chip, bit), 2)), core))
    barrier = pltpu.get_barrier_semaphore()
    signal_neighbours([barrier] * 4, near, has_up, has_down)
    for device in (other, partners[4]):
        pl.semaphore_signal(barrier, inc=1, device_id=device, device_id_type=MESH_IDS)
    pl.semaphore_wait(barrier, degree + 2)
    rows = gz.shape[4]
    low, high = pl.ds(0, rows // 2), pl.ds(rows // 2, rows // 2)

    def remote(src, dst, send_sem, recv_sem, device):
        return pltpu.make_async_remote_copy(
            src_ref=src,
            dst_ref=dst,
            send_sem=send_sem,
            recv_sem=recv_sem,
            device_id=device,
            device_id_type=MESH_IDS,
        )

    def arrived_at(ref, sem):
        remote(ref, ref, send_z.at[0], sem, right).wait_recv()

    def sent(ref, sem):
        remote(ref, ref, sem, recv_z.at[0, 0], right).wait_send()

    firsts = [
        pltpu.make_async_copy(src, dst, first_sem.at[n])
        for n, (src, dst) in enumerate(((text_h, text_v), (k2_h, k2_v), (v2_h, v2_v)))
    ]

    def left_copy(n):
        return pltpu.make_async_copy(lefts[n], lbuf.at[n % 2], l_sem.at[n % 2])

    def right_copies(c, which):
        unit = 2 * c + which
        place, sem = rbuf.at[lax.rem(c, 2), which], r_sem.at[lax.rem(c, 2), which]
        for source, (lo, hi) in zip((*rights, dqkv), (*FIRST_R, SELF_UNITS), strict=True):
            first = pl.multiple_of((unit - lo) * UNIT, UNIT)
            yield (
                (unit >= lo) & (unit < hi),
                pltpu.make_async_copy(source.at[:, pl.ds(first, UNIT)], place, sem),
            )

    def start_rights(c):
        for which in range(2):
            for cond, copy in right_copies(c, which):
                pl.when(cond)(copy.start)

    def store_unit(which, k, i, value):
        for yy in range(2):
            for xx in range(2):
                first = (yy * 2 + xx) * rows
                block = value[first : first + rows, :].astype(BF16)
                if which == 0:
                    gz[k, i, yy, xx, :, pl.ds(0, UNIT)] = block
                else:
                    gz[k, i, yy, xx, :, pl.ds(UNIT, width_z - UNIT)] = block[:, : width_z - UNIT]
                    ga[k, i, yy, xx] = block[:, width_z - UNIT :]

    def compute(c, k):
        for n in range(1, ROWS_L):
            pl.when(c == FIRST_L[n] // 2)(left_copy(n).wait)
        for which in range(2):
            unit = 2 * c + which
            text = (unit >= TEXT_UNITS[0]) & (unit < TEXT_UNITS[1])
            slot = lax.rem(sum((unit >= first).astype(jnp.int32) for first in FIRST_L) + 1, 2)

            @pl.when(text)
            def _():
                first = pl.multiple_of((unit - TEXT_UNITS[0]) * UNIT, UNIT)
                right_part = dkv_v[:, pl.ds(first, UNIT)]
                for i in range(4):
                    store_unit(which, k, i, dot_tn(text_v[:, pl.ds(i * 4 * rows, 4 * rows)], right_part))

            @pl.when(jnp.logical_not(text))
            def _():
                par = lax.rem(c, 2)
                pltpu.make_async_copy(rbuf.at[par, which], rbuf.at[par, which], r_sem.at[par, which]).wait()
                right_part = rbuf[par, which]
                for i in range(4):
                    left_part = lbuf[slot, :, pl.ds(i * 4 * rows, 4 * rows)]
                    store_unit(which, k, i, dot_tn(left_part, right_part))

        for n, at in LOAD_L:
            pl.when(c == at)(left_copy(n).start)
        pl.when(c + 1 < total)(lambda: start_rights(c + 1))

    def out_copies(c):
        o = lax.rem(c, 2)
        first = pl.multiple_of(c * width, 128)
        return (
            pltpu.make_async_copy(oz.at[o], out.at[:, pl.ds(first, width_z)], out_sem.at[o, 0]),
            pltpu.make_async_copy(
                oa.at[o], out.at[:, pl.ds(first + width_z, width_a)], out_sem.at[o, 1]
            ),
        )

    def plane_first(own, k, bufs, send_sem, recv):
        xd, yd, xa, ya = bufs
        remote(own(yn, xn, low), xd.at[k], send_sem.at[k], recv.at[k, XD], right).start()
        remote(own(yn, xn, high), yd.at[k], send_sem.at[k], recv.at[k, YD], across).start()
        remote(own(y, xn, low), xa.at[k], send_sem.at[k], recv.at[k, XA], right).start()
        remote(own(yn, x, high), ya.at[k], send_sem.at[k], recv.at[k, YA], across).start()

    def plane_second(add, k, bufs, send_sem, recv):
        xd, yd, xb, yb = bufs
        arrived_at(xd.at[k], recv.at[k, XD])
        add(xd, yn, x, low)
        remote(xd.at[k], yb.at[k], send_sem.at[k], recv.at[k, YB], across).start()
        arrived_at(yd.at[k], recv.at[k, YD])
        add(yd, y, xn, high)
        remote(yd.at[k], xb.at[k], send_sem.at[k], recv.at[k, XB], right).start()

    def above(buf, k, first, blocks):
        return buf.at[k, pl.ds(first + 1, blocks)]

    def below(buf, k, blocks):
        return buf.at[k, pl.ds(0, blocks)]

    def line_up(first, buf, add, k, send_sem, recv):
        blocks = 4 - first
        arrived_at(above(buf, k, first, blocks), recv.at[k, UP])
        if blocks > 1:
            for block in range(first + 1, 4):
                add(buf, block, block + 1)
            ref = above(buf, k, first + 1, blocks - 1)
            remote(ref, ref, send_sem.at[k], recv.at[k, UP], up).start()

    def line_down(last, buf, add, k, send_sem, recv):
        arrived_at(below(buf, k, last + 1), recv.at[k, DOWN])
        if last > 0:
            for block in range(last):
                add(buf, block, block)
            ref = below(buf, k, last)
            remote(ref, ref, send_sem.at[k], recv.at[k, DOWN], down).start()

    def add_a(k):
        def add(buf, block, at):
            for yy in range(2):
                for xx in range(2):
                    buf[k, at, yy, xx] = total_of(
                        buf[k, at, yy, xx], ga[k, block, yy, xx]
                    ).astype(BF16)

        return add

    def add_z(k):
        def add(buf, block, at):
            buf[k, at] = total_of(buf[k, at], gz[k, block, y, x]).astype(BF16)

        return add

    def begin(c, k):
        @pl.when(c >= slots)
        def _():
            pl.semaphore_wait(credit.at[0], 1)
            pl.semaphore_wait(credit.at[1], 1)
            pl.when(has_up)(lambda: pl.semaphore_wait(credit.at[2], 1))
            pl.when(has_down)(lambda: pl.semaphore_wait(credit.at[3], 1))

        plane_first(
            lambda yy, xx, half: gz.at[k, :, yy, xx, half, :], k, (xdz, ydz, xaz, yaz), send_z, recv_z
        )

        @pl.when(z == 0)
        def _():
            ref = pl.ds(1, 3)
            remote(ga.at[k, ref], above(lna, k, 1, 3), send_a.at[k], recv_a.at[k, UP], up).start()

        @pl.when(z == 3)
        def _():
            ref = pl.ds(0, 3)
            remote(ga.at[k, ref], below(lna, k, 3), send_a.at[k], recv_a.at[k, DOWN], down).start()

    def second(c, k):
        def add(buf, yy, xx, half):
            for block in range(4):
                buf[k, block] = total_of(buf[k, block], gz[k, block, yy, xx, half, :]).astype(BF16)

        plane_second(add, k, (xdz, ydz, xbz, ybz), send_z, recv_z)
        pl.when(z == 1)(lambda: line_up(1, lna, add_a(k), k, send_a, recv_a))
        pl.when(z == 2)(lambda: line_down(2, lna, add_a(k), k, send_a, recv_a))

    def third(c, k):
        for buf, kind in ((xaz, XA), (yaz, YA), (xbz, XB), (ybz, YB)):
            arrived_at(buf.at[k], recv_z.at[k, kind])
        for block in range(4):
            for half, one, two in ((low, xaz, ybz), (high, yaz, xbz)):
                gz[k, block, y, x, half, :] = total_of(
                    gz[k, block, y, x, half, :], one[k, block], two[k, block]
                ).astype(BF16)

        @pl.when(z == 0)
        def _():
            ref = pl.ds(1, 3)
            remote(
                gz.at[k, ref, y, x], above(lnz, k, 1, 3), send_z.at[k], recv_z.at[k, UP], up
            ).start()

        @pl.when(z == 3)
        def _():
            ref = pl.ds(0, 3)
            remote(
                gz.at[k, ref, y, x], below(lnz, k, 3), send_z.at[k], recv_z.at[k, DOWN], down
            ).start()

        pl.when(z == 2)(lambda: line_up(2, lna, add_a(k), k, send_a, recv_a))
        pl.when(z == 1)(lambda: line_down(1, lna, add_a(k), k, send_a, recv_a))

    def fourth(c, k):
        pl.when(z == 1)(lambda: line_up(1, lnz, add_z(k), k, send_z, recv_z))
        pl.when(z == 2)(lambda: line_down(2, lnz, add_z(k), k, send_z, recv_z))
        pl.when(z == 3)(lambda: line_up(3, lna, None, k, send_a, recv_a))
        pl.when(z == 0)(lambda: line_down(0, lna, None, k, send_a, recv_a))
        for shift, exists in ((1, has_down), (0, has_up)):

            @pl.when(exists)
            def _():
                for yy in range(2):
                    for xx in range(2):
                        ga[k, z, yy, xx] = total_of(
                            ga[k, z, yy, xx], lna[k, z + shift, yy, xx]
                        ).astype(BF16)

        plane_first(
            lambda yy, xx, half: ga.at[k, z, yy, xx, half, :], k, (xda, yda, xaa, yaa), send_a, recv_a
        )

    def fifth(c, k):
        pl.when(z == 2)(lambda: line_up(2, lnz, add_z(k), k, send_z, recv_z))
        pl.when(z == 1)(lambda: line_down(1, lnz, add_z(k), k, send_z, recv_z))

        def add(buf, yy, xx, half):
            buf[k] = total_of(buf[k], ga[k, z, yy, xx, half, :]).astype(BF16)

        plane_second(add, k, (xda, yda, xba, yba), send_a, recv_a)

    def finish(c, k):
        pl.when(z == 3)(lambda: line_up(3, lnz, None, k, send_z, recv_z))
        pl.when(z == 0)(lambda: line_down(0, lnz, None, k, send_z, recv_z))
        o = lax.rem(c, 2)

        @pl.when(c >= 2)
        def _():
            for copy in out_copies(c - 2):
                copy.wait()

        oz[o] = gz[k, z, y, x].astype(F32)
        for shift, exists in ((1, has_down), (0, has_up)):

            @pl.when(exists)
            def _():
                oz[o] = oz[o] + lnz[k, z + shift].astype(F32)

        for buf, kind in ((xaa, XA), (yaa, YA), (xba, XB), (yba, YB)):
            arrived_at(buf.at[k], recv_a.at[k, kind])
        oa[o, low, :] = total_of(ga[k, z, y, x, low, :], xaa[k], yba[k])
        oa[o, high, :] = total_of(ga[k, z, y, x, high, :], yaa[k], xba[k])
        for copy in out_copies(c):
            copy.start()
        for buf in (xdz, ydz, xaz, yaz, xbz, ybz):
            sent(buf.at[k], send_z.at[k])
        for buf in (xda, yda, xaa, yaa, xba, yba):
            sent(buf.at[k], send_a.at[k])
        for step in range(3):

            @pl.when(z == step)
            def _():
                sent(above(lnz, k, step + 1, 3 - step), send_z.at[k])
                sent(above(lna, k, step + 1, 3 - step), send_a.at[k])

            @pl.when(z == 3 - step)
            def _():
                sent(below(lnz, k, 3 - step), send_z.at[k])
                sent(below(lna, k, 3 - step), send_a.at[k])

        @pl.when(c < total - slots)
        def _():
            signal_neighbours([credit.at[i] for i in (0, 1, 3, 2)], near, has_up, has_down)

    frames, features = e3_h.shape
    part, half_rows = pool.shape[2], frames // 2
    heads = part // HEAD_DIM
    own_rows = pl.ds(pl.multiple_of(core * half_rows, half_rows), half_rows)
    wide = pl.ds(0, features)
    slope = dqkv.at[:, pl.ds(features, part)]
    block = 256

    def columns(n):
        return pl.ds(pl.multiple_of(n * part, part), part)

    def weight_copy(slot, ref, n=0):
        return pltpu.make_async_copy(ref.at[:, columns(n)], weights.at[slot], weight_sem.at[slot])

    def use(slot):
        weight_copy(slot, w_q).wait()

    def pool_copy(n, ref, m=0):
        return pltpu.make_async_copy(ref.at[:, columns(m)], pool.at[n], pool_sem.at[n])

    def slope_copy(n):
        return pltpu.make_async_copy(slope_h.at[:, columns(n)], slope, slope_sem)

    def keep_copy(n, src, dst):
        return pltpu.make_async_copy(src, dst, keep_sem.at[n])

    def du_copy(n):
        return keep_copy(0, pool.at[n], du_h.at[:, columns(n)])

    def to_other(n, src, dst):
        return remote(src, dst, share_send.at[n], share_recv.at[n], other)

    def share_sum(n):
        return to_other(n, theirs, arrived.at[n % 2])

    def share_branch(n):
        ref = dqkv.at[own_rows, wide]
        return to_other(4 + n, ref, ref)

    def multiply(whose, source, slot, fresh):
        for first in range(0, half_rows, block):
            rows_of = pl.ds(pl.multiple_of(whose * half_rows + first, block), block)
            value = dot_nt(source(rows_of), weights[slot])
            lines = pl.ds(first, block)
            acc[lines, :] = value if fresh else acc[lines, :] + value

    def pooled(n):
        return lambda rows_of: pool[n, rows_of, :]

    def headed(n):
        return lambda rows_of: dqkv[rows_of, pl.ds(n * part, part)]

    def send_sum(n):
        for first in range(0, half_rows, block):
            lines = pl.ds(first, block)
            theirs[lines, :] = acc[lines, :].astype(BF16)
        share_sum(n).start()

    def norm_back(kind, n, load, before, store):
        step = 64
        gain = norms[2 * kind : 2 * kind + 1, :]

        def body(i, sums):
            first = pl.multiple_of(i * step, step)
            lines = pl.ds(first, step)
            value = load(i, lines)
            offset = value - jnp.mean(value, axis=-1, keepdims=True)
            scale = lax.rsqrt(jnp.mean(offset * offset, axis=-1, keepdims=True) + norm_eps)
            unit = offset * scale
            slope_in = acc[lines, :] + arrived[n % 2, lines, :].astype(F32)
            scaled = slope_in * gain
            inner = jnp.mean(scaled * unit, axis=-1, keepdims=True)
            change = scale * (scaled - jnp.mean(scaled, axis=-1, keepdims=True) - unit * inner)
            store(first, lines, before(first, lines) + change)
            return (
                sums[0] + jnp.sum(slope_in * unit, axis=0, keepdims=True),
                sums[1] + jnp.sum(slope_in, axis=0, keepdims=True),
            )

        zero = jnp.zeros((1, features), F32)
        gains, shifts = lax.fori_loop(0, half_rows // step, body, (zero, zero))
        norm_grads[2 * kind : 2 * kind + 1, :] = gains
        norm_grads[2 * kind + 1 : 2 * kind + 2, :] = shifts

    def streamed(ref):
        step = xbuf.shape[1]

        def copy(i):
            first = pl.multiple_of(i * step, step)
            return pltpu.make_async_copy(
                ref.at[pl.ds(first, step), :], xbuf.at[lax.rem(i, 2)], x_sem.at[lax.rem(i, 2)]
            )

        copy(jnp.int32(0)).start()

        def load(i, lines):
            copy(i).wait()
            pl.when(i + 1 < half_rows // step)(copy(i + 1).start)
            return xbuf[lax.rem(i, 2)]

        return load

    def store_branch(first, lines, value):
        grad[lines, :] = value
        dqkv[pl.ds(pl.multiple_of(core * half_rows + first, 64), 64), wide] = value.astype(BF16)

    def project_to(n, slot):
        for first in range(0, frames, block):
            lines = pl.ds(first, block)
            pool[n, lines, :] = dot_nn(dqkv[lines, wide], weights[slot]).astype(BF16)

    def feed_forward(j):
        use(0)
        slope_copy(j).wait()
        for first in range(0, frames, block):
            lines = pl.ds(first, block)
            value = dot_nn(lbuf[0, lines, :], weights[0])
            pool[j, lines, :] = (
                value * dqkv[lines, pl.ds(features, part)].astype(F32)
            ).astype(BF16)

        @pl.when(j > 0)
        def _():
            du_copy(j - 1).wait()

        du_copy(j).start()

        @pl.when(j < 3)
        def _():
            weight_copy(0, w_down, j + 1).start()
            slope_copy(j + 1).start()

        pl.when(j == 3)(lambda: weight_copy(0, w_up, 0).start())
        use(1)
        multiply(1 - core, pooled(j), 1, False)
        pl.when(j < 3)(lambda: weight_copy(1, w_up, j + 1).start())
        pl.when(j == 3)(lambda: send_sum(0))

    def turn_4():
        du_copy(3).wait()
        multiply(core, pooled(3), 1, True)
        weight_copy(1, w_up, 1).start()
        use(0)
        multiply(core, pooled(0), 0, False)
        weight_copy(0, w_up, 2).start()

    def turn_5():
        use(1)
        multiply(core, pooled(1), 1, False)
        weight_copy(1, w_cq).start()
        use(0)
        multiply(core, pooled(2), 0, False)
        weight_copy(0, w_co).start()

    def turn_6():
        pool_copy(0, q2_h).start()
        share_sum(0).wait()
        norm_back(
            2,
            0,
            streamed(x3_h),
            lambda first, lines: lbuf[
                0, pl.ds(pl.multiple_of(core * half_rows + first, 64), 64), :
            ].astype(F32),
            store_branch,
        )
        share_branch(0).start()

    def turn_7():
        share_branch(0).wait()
        keep_copy(1, dqkv.at[:, wide], e2_h).start()
        use(0)
        project_to(1, 0)
        weight_copy(0, w_ck).start()

    def turn_8():
        pool_copy(0, q2_h).wait()
        for copy in firsts:
            copy.wait()

        def body(head, carry):
            head_back(
                head,
                pool.at[0],
                k2_v,
                v2_v,
                pool.at[1],
                lse2_ref,
                pool.at[2],
                dkv_v,
                (0, 0, part),
                acc_k,
                acc_v,
                False,
            )
            return carry

        lax.fori_loop(0, heads, body, 0)
        keep_copy(1, dqkv.at[:, wide], e2_h).wait()
        keep_copy(0, pool.at[2], dq2_h).start()
        use(0)
        text_part[...] = dot_nt(dkv_v[:, pl.ds(0, part)], weights[0])
        weight_copy(0, w_cv).start()

    def text_columns(whose):
        count = features // 2
        return pl.ds(pl.multiple_of(whose * count, count), count)

    def text_share():
        return to_other(6, text_send, text_got)

    def turn_9():
        keep_copy(0, pool.at[2], dq2_h).wait()
        use(0)
        text_part[...] += dot_nt(dkv_v[:, pl.ds(part, part)], weights[0])
        text_send[...] = text_part[:, text_columns(1 - core)].astype(BF16)
        text_share().start()
        weight_copy(0, w_o).start()
        use(1)
        multiply(1 - core, pooled(2), 1, True)
        send_sum(1)

    def turn_10():
        multiply(core, pooled(2), 1, True)
        for n, ref in enumerate((q1_h, k1_h, v1_h)):
            pool_copy(n, ref).start()
        share_sum(1).wait()
        norm_back(1, 1, streamed(x2_h), lambda first, lines: grad[lines, :], store_branch)
        share_branch(1).start()
        text_share().wait()
        text_part[:, pl.ds(0, features // 2)] = text_part[:, text_columns(core)] + text_got[
            ...
        ].astype(F32)
        keep_copy(2, text_part.at[:, pl.ds(0, features // 2)], grad_text).start()

    def turn_11():
        share_branch(1).wait()
        keep_copy(1, dqkv.at[:, wide], e1_h).start()
        use(0)
        project_to(3, 0)
        weight_copy(0, w_q).start()
        weight_copy(1, w_k).start()

    def turn_12():
        keep_copy(1, dqkv.at[:, wide], e1_h).wait()
        for n, ref in enumerate((q1_h, k1_h, v1_h)):
            pool_copy(n, ref).wait()

    def self_head(head):
        head_back(
            head,
            pool.at[0],
            pool.at[1],
            pool.at[2],
            pool.at[3],
            lse1_ref,
            dqkv,
            dqkv,
            (0, part, 2 * part),
            acc_k,
            acc_v,
            True,
        )

    def turn_18():
        for n in range(4):
            pool_copy(n, a_h, n).start()
        use(0)
        multiply(1 - core, headed(0), 0, True)
        weight_copy(0, w_v).start()
        use(1)
        multiply(1 - core, headed(1), 1, False)

    def turn_19():
        use(0)
        multiply(1 - core, headed(2), 0, False)
        send_sum(2)
        multiply(core, headed(2), 0, True)
        weight_copy(0, w_down, 0).start()
        multiply(core, headed(1), 1, False)
        weight_copy(1, w_q).start()

    def turn_20():
        use(1)
        multiply(core, headed(0), 1, False)
        weight_copy(1, w_down, 1).start()

    def turn_21():
        share_sum(2).wait()
        hidden = keep_copy(1, x1_h, theirs)
        hidden.start()
        hidden.wait()

        def store(first, lines, value):
            grad[lines, :] = value

        norm_back(
            0,
            2,
            lambda i, lines: theirs[lines, :].astype(F32),
            lambda first, lines: grad[lines, :],
            store,
        )
        keep_copy(3, grad, grad_input).start()

    def turn_22():
        for n in range(4):
            pool_copy(n, a_h, n).wait()
        use(0)
        multiply(1 - core, pooled(0), 0, True)
        weight_copy(0, w_down, 2).start()
        use(1)
        multiply(1 - core, pooled(1), 1, False)
        weight_copy(1, w_down, 3).start()

    def turn_23():
        keep_copy(3, grad, grad_input).wait()
        keep_copy(1, x3_h, grad).start()
        use(0)
        multiply(1 - core, pooled(2), 0, False)
        use(1)
        multiply(1 - core, pooled(3), 1, False)
        send_sum(3)
        multiply(core, pooled(2), 0, True)
        weight_copy(0, w_down, 0).start()
        multiply(core, pooled(3), 1, False)
        weight_copy(1, w_down, 1).start()

    def turn_24():
        use(0)
        multiply(core, pooled(0), 0, False)
        use(1)
        multiply(core, pooled(1), 1, False)

    def turn_25():
        share_sum(3).wait()
        keep_copy(1, x3_h, grad).wait()
        for first in range(0, half_rows, 64):
            lines = pl.ds(first, 64)
            theirs[lines, :] = (
                grad[lines, :] + (acc[lines, :] + arrived[1, lines, :].astype(F32))
            ).astype(BF16)
        keep_copy(0, theirs, layer_out).start()

    def norm_copy(step):
        return remote(
            got.at[2 * step],
            got.at[2 * step + 1],
            norm_send.at[step],
            norm_recv.at[step],
            partners[step],
        )

    def norm_sum(step):
        if step == 0:
            got[0] = norm_grads[...]
        else:
            norm_copy(step - 1).wait()
            got[2 * step] = got[2 * step - 2] + got[2 * step - 1]
        if step < len(partners):
            norm_copy(step).start()
        else:
            keep_copy(1, got.at[2 * step], norm_out).start()

    chain = {
        4: turn_4,
        5: turn_5,
        6: turn_6,
        7: turn_7,
        8: turn_8,
        9: turn_9,
        10: turn_10,
        11: turn_11,
        18: turn_18,
        19: turn_19,
        20: turn_20,
        21: turn_21,
        22: turn_22,
        23: turn_23,
        24: turn_24,
        25: turn_25,
    }
    stages = (begin, second, third, fourth, fifth, finish)
    left_copy(0).start()
    weight_copy(0, w_down, 0).start()
    slope_copy(0).start()
    start_rights(jnp.int32(0))
    weight_copy(1, w_up, 0).start()
    left_copy(1).start()
    for copy in firsts:
        copy.start()
    for first in range(0, half_rows, block):
        acc[pl.ds(first, block), :] = jnp.zeros((block, features), F32)
    norm_grads[...] = jnp.zeros_like(norm_grads)
    left_copy(0).wait()

    def body(turn, carry):
        for step, stage in enumerate(stages):
            c = turn - step - 1

            @pl.when((c >= 0) & (c < total))
            def _():
                stage(c, lax.rem(c, slots))

        pl.when(turn < total)(lambda: compute(turn, lax.rem(turn, slots)))
        pl.when(turn < 4)(lambda: feed_forward(turn))
        for number, fn in chain.items():
            pl.when(turn == number)(fn)
        pl.when(turn == 12)(turn_12)

        @pl.when((turn >= 12) & (turn < 18))
        def _():
            def both(head, carry):
                self_head(head)
                return carry

            first = lax.div(heads, 6) * (turn - 12)
            lax.fori_loop(first, first + heads // 6, both, 0)

        for step in range(len(partners) + 1):
            pl.when(turn == 22 + step)(functools.partial(norm_sum, step))
        return carry

    lax.fori_loop(0, total + len(stages), body, 0)
    for c in (total - 2, total - 1):
        for copy in out_copies(jnp.int32(c)):
            copy.wait()
    keep_copy(0, theirs, layer_out).wait()
    keep_copy(1, got.at[2 * len(partners)], norm_out).wait()
    keep_copy(2, text_part.at[:, pl.ds(0, features // 2)], grad_text).wait()


def backward_all(arrays, small):
    frames, width = arrays[0].shape
    text = arrays[8]
    rows, half, part = width // 16, frames // 2, arrays[9].shape[1]
    dma, vmem, shape = pltpu.SemaphoreType.DMA, pltpu.VMEM, jax.ShapeDtypeStruct

    def buffer(*dims):
        return vmem((SLOTS,) + dims, BF16)

    anywhere = pl.BlockSpec(memory_space=pl.ANY)
    return pl.pallas_call(
        backward_kernel,
        out_shape=[
            shape((rows, UNITS * UNIT), F32),
            shape((half, width), BF16),
            shape((half, width), F32),
            shape((text.shape[0], width // 2), F32),
            shape((8, width), F32),
            shape((frames, 4 * part), BF16),
            shape((frames, part), BF16),
            shape((frames, width), BF16),
            shape((frames, width), BF16),
        ],
        in_specs=[anywhere] * len(arrays) + [pl.BlockSpec(memory_space=vmem)] * len(small),
        out_specs=[anywhere] * 9,
        scratch_shapes=[
            buffer(4, 2, 2, rows, WIDTH_Z),
            buffer(4, 2, 2, rows, WIDTH_A),
            *[buffer(4, rows // 2, WIDTH_Z)] * 6,
            buffer(5, rows, WIDTH_Z),
            *[buffer(rows // 2, WIDTH_A)] * 6,
            buffer(5, 2, 2, rows, WIDTH_A),
            vmem((2, rows, WIDTH_Z), F32),
            vmem((2, rows, WIDTH_A), F32),
            vmem((2, frames, width), BF16),
            vmem((2, 2, frames, UNIT), BF16),
            vmem(text.shape, BF16),
            vmem((text.shape[0], 2 * part), BF16),
            *[vmem((text.shape[0], part), BF16)] * 2,
            vmem((4, frames, part), BF16),
            vmem((frames, 3 * part), BF16),
            *[vmem((frames, 128), F32)] * 2,
            *[vmem((half, width), F32)] * 2,
            vmem((2, 64, width), F32),
            vmem((half, width), BF16),
            vmem((2, half, width), BF16),
            vmem((2, width, part), BF16),
            vmem((text.shape[0], width), F32),
            *[vmem((text.shape[0], width // 2), BF16)] * 2,
            vmem((8, width), F32),
            vmem((11, 8, width), F32),
            dma((3,)),
            dma((2,)),
            dma((2, 2)),
            dma((2, 2)),
            dma((SLOTS,)),
            dma((SLOTS,)),
            dma((SLOTS, 8)),
            dma((SLOTS, 8)),
            dma((4,)),
            dma,
            dma((2,)),
            dma((2,)),
            dma((4,)),
            dma((7,)),
            dma((7,)),
            dma((5,)),
            dma((5,)),
            pltpu.SemaphoreType.REGULAR((4,)),
        ],
        compiler_params=pltpu.CompilerParams(
            collective_id=1, has_side_effects=True, vmem_limit_bytes=VMEM_LIMIT
        ),
        name="backward",
    )(*arrays, *small)


def gather_plan(columns):
    chunks, since = [], 0
    for array, width in enumerate(columns):
        size = 768 if width % 768 == 0 else width
        for first in range(0, width, size):
            since += 1
            family = "A" if since % 5 == 3 and size == 768 else "Z"
            chunks.append((array, first, size, family))
    return tuple(chunks)


def local_fast(
    hidden_in,
    text_states,
    norm1_gain,
    norm1_bias,
    self_query,
    self_key,
    self_value,
    self_out,
    norm2_gain,
    norm2_bias,
    cross_query,
    cross_key,
    cross_value,
    cross_out,
    norm3_gain,
    norm3_bias,
    hidden_up,
    hidden_down,
    cotangent,
):
    width = norm1_gain.shape[0] * 16
    norms = jnp.stack([norm1_gain, norm1_bias, norm2_gain, norm2_bias, norm3_gain, norm3_bias])
    norms = jnp.pad(norms, ((0, 26), (0, 128 - norms.shape[1])))
    shards = (
        norms,
        self_query.T,
        self_key.T,
        self_value.T,
        self_out,
        cross_key.T,
        cross_value.T,
        cross_query.T,
        cross_out,
        hidden_up.T,
        hidden_down,
    )
    gathered, kept = forward_all(
        shards,
        gather_plan([s.shape[1] for s in shards]),
        hidden_in[0],
        text_states[0],
        cotangent[0],
    )
    w_q, w_k, w_v, w_o, w_ck, w_cv, w_cq, w_co, w_up, w_down = [
        g.reshape(width, g.shape[-1]) for g in gathered[1:]
    ]
    normed_one, normed_two, normed_three = kept[:3]
    query_one, key_one, value_one, attended_one = kept[3:7]
    query_two, key_two, value_two, attended_two = kept[7:11]
    logsum_one, logsum_two, norms, stream_two, stream_three, branch, active, slope = kept[11:]
    summed, layer_out, grad_input, grad_text, norm_sums, *_ = backward_all(
        (
            *(branch, normed_three, normed_two, normed_one),
            *(active, slope, attended_two, attended_one, text_states[0]),
            *(query_two, key_two, value_two, query_one, key_one, value_one),
            *(stream_three, stream_two, hidden_in[0]),
            *(w_q, w_k, w_v, w_o, w_ck, w_cv, w_cq, w_co, w_up, w_down),
        ),
        (logsum_two, logsum_one, norms),
    )
    rows, part = width // 16, query_one.shape[1]
    norm_sums = lax.dynamic_slice_in_dim(norm_sums, lax.axis_index("dp") * rows, rows, 1)
    columns = [hidden_down.shape[1]] * 2 + [part] * 8
    pieces, first = [], 0
    for count in columns:
        pieces.append(summed[:, first : first + count])
        first += count
    down, up, out_cross, query_cross, key_cross, value_cross, out_self, query, key, value = pieces
    return (
        layer_out[None],
        grad_input[None],
        grad_text[None],
        norm_sums[0],
        norm_sums[1],
        query.T,
        key.T,
        value.T,
        out_self,
        norm_sums[2],
        norm_sums[3],
        query_cross.T,
        key_cross.T,
        value_cross.T,
        out_cross,
        norm_sums[4],
        norm_sums[5],
        up.T,
        down,
    )


def solution(mesh):
    placed = (
        P("dp", "tensor", None),
        P("dp", None, None),
        P("dp"),
        P("dp"),
        P("tensor", "dp"),
        P("tensor", "dp"),
        P("tensor", "dp"),
        P("dp", "tensor"),
        P("dp"),
        P("dp"),
        P("tensor", "dp"),
        P("tensor", "dp"),
        P("tensor", "dp"),
        P("dp", "tensor"),
        P("dp"),
        P("dp"),
        P("tensor", "dp"),
        P("dp", "tensor"),
        P("dp", "tensor", None),
    )
    fast = dict(mesh.shape) == {"dp": 16, "tensor": 2}
    return jax.shard_map(
        local_fast if fast else local_generic,
        mesh=mesh,
        in_specs=placed,
        out_specs=(
            P("dp", "tensor", None),
            P("dp", "tensor", None),
            P("dp", None, "tensor"),
            P("dp"),
            P("dp"),
            P("tensor", "dp"),
            P("tensor", "dp"),
            P("tensor", "dp"),
            P("dp", "tensor"),
            P("dp"),
            P("dp"),
            P("tensor", "dp"),
            P("tensor", "dp"),
            P("tensor", "dp"),
            P("dp", "tensor"),
            P("dp"),
            P("dp"),
            P("tensor", "dp"),
            P("dp", "tensor"),
        ),
        check_vma=False,
    )
```

```python
import functools

import jax
import jax.numpy as jnp
from jax import lax
from jax.experimental import pallas as pl
from jax.experimental.pallas import tpu as pltpu
from jax.sharding import PartitionSpec as P

HEAD_DIM = 64


norm_eps = 1e-05
score_scale = 0.125


def layer_norm(values, gain, shift):
    centre = jnp.mean(values, axis=-1, keepdims=True)
    offset = values - centre
    spread = jnp.mean(offset * offset, axis=-1, keepdims=True)
    return offset * lax.rsqrt(spread + norm_eps) * gain + shift


def gelu_exact(values):
    return jax.nn.gelu(values, approximate=False)


def project(row_data, weight):
    return jnp.einsum("cli,oi->clo", row_data, weight, preferred_element_type=jnp.float32)


def split_heads(values):
    return values.reshape(values.shape[0], values.shape[1], -1, HEAD_DIM)


def flatten_heads(values):
    return values.reshape(values.shape[0], values.shape[1], -1)


def causal_keep(first_row, count, length):
    row_ids = first_row + lax.broadcasted_iota(jnp.int32, (count, length), 0)
    col_ids = lax.broadcasted_iota(jnp.int32, (count, length), 1)
    return col_ids <= row_ids


def block_scores(queries, key_rows, first_row, block_rows, key_end, causal):
    scores = (
        jnp.einsum(
            "cqhe,ckhe->chqk",
            queries[:, first_row : first_row + block_rows],
            key_rows[:, :key_end],
            preferred_element_type=jnp.float32,
        )
        * score_scale
    )
    if causal:
        scores = jnp.where(causal_keep(first_row, block_rows, key_end), scores, -1e30)
    return scores


def attend(queries, key_rows, val_rows, causal):
    length = queries.shape[1]
    block_rows = min(512, length)
    outputs = []
    log_sums = []
    for block_num in range(length // block_rows):
        first_row = block_num * block_rows
        key_end = first_row + block_rows if causal else key_rows.shape[1]
        scores = block_scores(queries, key_rows, first_row, block_rows, key_end, causal)
        row_peak = jnp.max(scores, axis=-1, keepdims=True)
        exp_scores = jnp.exp(scores - row_peak)
        row_total = jnp.sum(exp_scores, axis=-1, keepdims=True)
        soft_weights = (exp_scores / row_total).astype(jnp.bfloat16)
        outputs.append(
            jnp.einsum(
                "chqk,ckhe->cqhe",
                soft_weights,
                val_rows[:, :key_end],
                preferred_element_type=jnp.float32,
            ).astype(jnp.bfloat16)
        )
        log_sums.append((row_peak + jnp.log(row_total))[..., 0])
    return (jnp.concatenate(outputs, axis=1), jnp.concatenate(log_sums, axis=2))


def attend_back(queries, key_rows, val_rows, grad_out, log_sums, causal):
    length = queries.shape[1]
    block_rows = min(512, length)
    grad_keys = jnp.zeros(key_rows.shape, jnp.float32)
    grad_vals = jnp.zeros(val_rows.shape, jnp.float32)
    grad_queries = []
    for block_num in range(length // block_rows):
        first_row = block_num * block_rows
        key_end = first_row + block_rows if causal else key_rows.shape[1]
        query_blk = queries[:, first_row : first_row + block_rows]
        grad_blk = grad_out[:, first_row : first_row + block_rows]
        scores = block_scores(queries, key_rows, first_row, block_rows, key_end, causal)
        soft = jnp.exp(scores - log_sums[:, :, first_row : first_row + block_rows, None])
        grad_soft = jnp.einsum(
            "cqhe,ckhe->chqk", grad_blk, val_rows[:, :key_end], preferred_element_type=jnp.float32
        )
        grad_vals = grad_vals.at[:, :key_end].add(
            jnp.einsum(
                "chqk,cqhe->ckhe",
                soft.astype(jnp.bfloat16),
                grad_blk,
                preferred_element_type=jnp.float32,
            )
        )
        inner = jnp.sum(soft * grad_soft, axis=-1, keepdims=True)
        grad_scores = (soft * (grad_soft - inner)).astype(jnp.bfloat16)
        grad_queries.append(
            jnp.einsum(
                "chqk,ckhe->cqhe",
                grad_scores,
                key_rows[:, :key_end],
                preferred_element_type=jnp.float32,
            )
            * score_scale
        )
        grad_keys = grad_keys.at[:, :key_end].add(
            jnp.einsum(
                "chqk,cqhe->ckhe", grad_scores, query_blk, preferred_element_type=jnp.float32
            )
            * score_scale
        )
    return (jnp.concatenate(grad_queries, axis=1), grad_keys, grad_vals)


def gather_rows(values):
    return lax.all_gather(values, "tensor", axis=1, tiled=True)


def scatter_rows(values):
    return lax.psum_scatter(values, "tensor", scatter_dimension=1, tiled=True)


def gather_grads(values):
    return lax.all_gather(values, "tensor", axis=1, tiled=True)


def scatter_grads(values):
    return lax.psum_scatter(
        values.astype(jnp.bfloat16), "tensor", scatter_dimension=1, tiled=True
    ).astype(jnp.float32)


def heads_grads(grad_branch, attended, out_weight):
    grad_out_proj = jnp.einsum(
        "clo,cla->oa", grad_branch, flatten_heads(attended), preferred_element_type=jnp.float32
    )
    grad_attended = split_heads(
        jnp.einsum(
            "clo,oa->cla", grad_branch, out_weight, preferred_element_type=jnp.float32
        ).astype(jnp.bfloat16)
    )
    return (grad_out_proj, grad_attended)


def weight_grad(grad_rows, source_rows):
    return jnp.einsum("cla,cli->ai", grad_rows, source_rows, preferred_element_type=jnp.float32)


def input_grad(grad_rows, weight):
    return jnp.einsum("cla,ai->cli", grad_rows, weight, preferred_element_type=jnp.float32)


def local_generic(
    hidden_in,
    text_states,
    norm1_gain,
    norm1_bias,
    self_query,
    self_key,
    self_value,
    self_out,
    norm2_gain,
    norm2_bias,
    cross_query,
    cross_key,
    cross_value,
    cross_out,
    norm3_gain,
    norm3_bias,
    hidden_up,
    hidden_down,
    cotangent,
):
    full_weights = (
        lax.all_gather(norm1_gain, "dp", axis=0, tiled=True),
        lax.all_gather(norm1_bias, "dp", axis=0, tiled=True),
        lax.all_gather(self_query, "dp", axis=1, tiled=True),
        lax.all_gather(self_key, "dp", axis=1, tiled=True),
        lax.all_gather(self_value, "dp", axis=1, tiled=True),
        lax.all_gather(self_out, "dp", axis=0, tiled=True),
        lax.all_gather(norm2_gain, "dp", axis=0, tiled=True),
        lax.all_gather(norm2_bias, "dp", axis=0, tiled=True),
        lax.all_gather(cross_query, "dp", axis=1, tiled=True),
        lax.all_gather(cross_key, "dp", axis=1, tiled=True),
        lax.all_gather(cross_value, "dp", axis=1, tiled=True),
        lax.all_gather(cross_out, "dp", axis=0, tiled=True),
        lax.all_gather(norm3_gain, "dp", axis=0, tiled=True),
        lax.all_gather(norm3_bias, "dp", axis=0, tiled=True),
        lax.all_gather(hidden_up, "dp", axis=1, tiled=True),
        lax.all_gather(hidden_down, "dp", axis=0, tiled=True),
    )
    gain_self = full_weights[0].astype(jnp.float32)
    bias_self = full_weights[1].astype(jnp.float32)
    gain_cross = full_weights[6].astype(jnp.float32)
    bias_cross = full_weights[7].astype(jnp.float32)
    gain_ffn = full_weights[12].astype(jnp.float32)
    bias_ffn = full_weights[13].astype(jnp.float32)
    stream_one = hidden_in.astype(jnp.float32)
    key_two = split_heads(project(text_states, full_weights[9]).astype(jnp.bfloat16))
    value_two = split_heads(project(text_states, full_weights[10]).astype(jnp.bfloat16))
    normed_one = gather_rows(layer_norm(stream_one, gain_self, bias_self).astype(jnp.bfloat16))
    query_one = split_heads(project(normed_one, full_weights[2]).astype(jnp.bfloat16))
    key_one = split_heads(project(normed_one, full_weights[3]).astype(jnp.bfloat16))
    value_one = split_heads(project(normed_one, full_weights[4]).astype(jnp.bfloat16))
    attended_one, logsum_one = attend(query_one, key_one, value_one, True)
    stream_two = stream_one + scatter_rows(project(flatten_heads(attended_one), full_weights[5]))
    normed_two = gather_rows(layer_norm(stream_two, gain_cross, bias_cross).astype(jnp.bfloat16))
    query_two = split_heads(project(normed_two, full_weights[8]).astype(jnp.bfloat16))
    attended_two, logsum_two = attend(query_two, key_two, value_two, False)
    stream_three = stream_two + scatter_rows(project(flatten_heads(attended_two), full_weights[11]))
    normed_three = gather_rows(layer_norm(stream_three, gain_ffn, bias_ffn).astype(jnp.bfloat16))
    upper = project(normed_three, full_weights[14])
    active = gelu_exact(upper).astype(jnp.bfloat16)
    layer_out = (stream_three + scatter_rows(project(active, full_weights[15]))).astype(
        jnp.bfloat16
    )
    grad_three = cotangent.astype(jnp.float32)
    grad_branch = gather_grads(grad_three.astype(jnp.bfloat16))
    grad_down = jnp.einsum("clo,clf->of", grad_branch, active, preferred_element_type=jnp.float32)
    grad_active = jnp.einsum(
        "clo,of->clf", grad_branch, full_weights[15], preferred_element_type=jnp.float32
    )
    grad_upper = jax.vjp(gelu_exact, upper)[1](grad_active)[0].astype(jnp.bfloat16)
    grad_up = weight_grad(grad_upper, normed_three)
    norm_back = jax.vjp(layer_norm, stream_three, gain_ffn, bias_ffn)[1]
    grad_stream, grad_gain_ffn, grad_bias_ffn = norm_back(
        scatter_grads(input_grad(grad_upper, full_weights[14]))
    )
    grad_two = grad_three + grad_stream
    grad_branch = gather_grads(grad_two.astype(jnp.bfloat16))
    grad_out_cross, grad_attended = heads_grads(grad_branch, attended_two, full_weights[11])
    grad_query, grad_key, grad_value = attend_back(
        query_two, key_two, value_two, grad_attended, logsum_two, False
    )
    grad_query = flatten_heads(grad_query).astype(jnp.bfloat16)
    grad_key = flatten_heads(grad_key).astype(jnp.bfloat16)
    grad_value = flatten_heads(grad_value).astype(jnp.bfloat16)
    grad_query_cross = weight_grad(grad_query, normed_two)
    grad_key_cross = weight_grad(grad_key, text_states)
    grad_value_cross = weight_grad(grad_value, text_states)
    text_part = input_grad(grad_key, full_weights[9]) + input_grad(grad_value, full_weights[10])
    grad_text = lax.psum_scatter(
        text_part.astype(jnp.bfloat16), "tensor", scatter_dimension=2, tiled=True
    ).astype(jnp.float32)
    norm_back = jax.vjp(layer_norm, stream_two, gain_cross, bias_cross)[1]
    grad_stream, grad_gain_cross, grad_bias_cross = norm_back(
        scatter_grads(input_grad(grad_query, full_weights[8]))
    )
    grad_one = grad_two + grad_stream
    grad_branch = gather_grads(grad_one.astype(jnp.bfloat16))
    grad_out_self, grad_attended = heads_grads(grad_branch, attended_one, full_weights[5])
    grad_query, grad_key, grad_value = attend_back(
        query_one, key_one, value_one, grad_attended, logsum_one, True
    )
    grad_query = flatten_heads(grad_query).astype(jnp.bfloat16)
    grad_key = flatten_heads(grad_key).astype(jnp.bfloat16)
    grad_value = flatten_heads(grad_value).astype(jnp.bfloat16)
    grad_query_self = weight_grad(grad_query, normed_one)
    grad_key_self = weight_grad(grad_key, normed_one)
    grad_value_self = weight_grad(grad_value, normed_one)
    grad_normed = (
        input_grad(grad_query, full_weights[2])
        + input_grad(grad_key, full_weights[3])
        + input_grad(grad_value, full_weights[4])
    )
    norm_back = jax.vjp(layer_norm, stream_one, gain_self, bias_self)[1]
    grad_stream, grad_gain_self, grad_bias_self = norm_back(scatter_grads(grad_normed))
    grad_input = grad_one + grad_stream
    summed = (
        lax.psum_scatter(
            grad_gain_self.astype(jnp.bfloat16), "dp", scatter_dimension=0, tiled=True
        ).astype(jnp.float32),
        lax.psum_scatter(
            grad_bias_self.astype(jnp.bfloat16), "dp", scatter_dimension=0, tiled=True
        ).astype(jnp.float32),
        lax.psum_scatter(
            grad_query_self.astype(jnp.bfloat16), "dp", scatter_dimension=1, tiled=True
        ).astype(jnp.float32),
        lax.psum_scatter(
            grad_key_self.astype(jnp.bfloat16), "dp", scatter_dimension=1, tiled=True
        ).astype(jnp.float32),
        lax.psum_scatter(
            grad_value_self.astype(jnp.bfloat16), "dp", scatter_dimension=1, tiled=True
        ).astype(jnp.float32),
        lax.psum_scatter(
            grad_out_self.astype(jnp.bfloat16), "dp", scatter_dimension=0, tiled=True
        ).astype(jnp.float32),
        lax.psum_scatter(
            grad_gain_cross.astype(jnp.bfloat16), "dp", scatter_dimension=0, tiled=True
        ).astype(jnp.float32),
        lax.psum_scatter(
            grad_bias_cross.astype(jnp.bfloat16), "dp", scatter_dimension=0, tiled=True
        ).astype(jnp.float32),
        lax.psum_scatter(
            grad_query_cross.astype(jnp.bfloat16), "dp", scatter_dimension=1, tiled=True
        ).astype(jnp.float32),
        lax.psum_scatter(
            grad_key_cross.astype(jnp.bfloat16), "dp", scatter_dimension=1, tiled=True
        ).astype(jnp.float32),
        lax.psum_scatter(
            grad_value_cross.astype(jnp.bfloat16), "dp", scatter_dimension=1, tiled=True
        ).astype(jnp.float32),
        lax.psum_scatter(
            grad_out_cross.astype(jnp.bfloat16), "dp", scatter_dimension=0, tiled=True
        ).astype(jnp.float32),
        lax.psum_scatter(
            grad_gain_ffn.astype(jnp.bfloat16), "dp", scatter_dimension=0, tiled=True
        ).astype(jnp.float32),
        lax.psum_scatter(
            grad_bias_ffn.astype(jnp.bfloat16), "dp", scatter_dimension=0, tiled=True
        ).astype(jnp.float32),
        lax.psum_scatter(
            grad_up.astype(jnp.bfloat16), "dp", scatter_dimension=1, tiled=True
        ).astype(jnp.float32),
        lax.psum_scatter(
            grad_down.astype(jnp.bfloat16), "dp", scatter_dimension=0, tiled=True
        ).astype(jnp.float32),
    )
    norm_sums = lax.psum(
        (summed[0], summed[1], summed[6], summed[7], summed[12], summed[13]), "tensor"
    )
    return (
        layer_out,
        grad_input,
        grad_text,
        norm_sums[0],
        norm_sums[1],
        summed[2],
        summed[3],
        summed[4],
        summed[5],
        norm_sums[2],
        norm_sums[3],
        summed[8],
        summed[9],
        summed[10],
        summed[11],
        norm_sums[4],
        norm_sums[5],
        summed[14],
        summed[15],
    )


MESH_IDS = pl.DeviceIdType.MESH
BF16 = jnp.bfloat16
F32 = jnp.float32
VMEM_LIMIT = 63 * 2**20


def my_place():
    chip = lax.axis_index("dp")
    core = lax.axis_index("tensor")
    return (lax.rem(chip, 2), lax.rem(lax.div(chip, 2), 2), lax.div(chip, 4), core)


def neighbours(x, y, z, core):
    def device(zz, yy, xx):
        return (zz * 4 + yy * 2 + xx, core)

    return (device(z, y, 1 - x), device(z, 1 - y, x), device(z + 1, y, x), device(z - 1, y, x))


def when(cond, fn):
    if cond is None:
        fn()
    else:
        pl.when(cond)(fn)


def signal_neighbours(sems, near, has_up, has_down):
    for sem, device, cond in zip(sems, near, (None, None, has_up, has_down), strict=True):
        when(
            cond,
            functools.partial(
                pl.semaphore_signal, sem, inc=1, device_id=device, device_id_type=MESH_IDS
            ),
        )


def gather_engine(chunks, shards, outs, sems):
    local_sem, send_sem, zs, xs, ys, ds = sems
    x, y, z, core = my_place()
    xn, yn = 1 - x, 1 - y
    near = neighbours(x, y, z, core)
    right, across, up, down = near
    has_up, has_down = z < 3, z > 0
    barrier = pltpu.get_barrier_semaphore()
    signal_neighbours([barrier] * 4, near, has_up, has_down)
    pl.semaphore_signal(barrier, inc=1, device_id=(lax.axis_index("dp"), 1 - core), device_id_type=MESH_IDS)
    pl.semaphore_wait(barrier, 3 + has_up.astype(jnp.int32) + has_down.astype(jnp.int32))
    total = len(chunks)
    pending = []


    def span(c):
        _, first, width, _ = chunks[c]
        return pl.ds(first, width)

    def at(zz, yy, xx, c, half=None):
        ref = outs[chunks[c][0]]
        half_rows = ref.shape[3] // 2
        lines = slice(None) if half is None else pl.ds(half * half_rows, half_rows)
        return ref.at[zz, yy, xx, lines, span(c)]

    def plane(zz, c):
        return outs[chunks[c][0]].at[zz, :, :, :, span(c)]

    def own(c):
        return shards[chunks[c][0]].at[:, span(c)]

    local = [pltpu.make_async_copy(own(c), at(z, y, x, c), local_sem.at[c]) for c in range(total)]

    def remote(src, dst, sem, device):
        return pltpu.make_async_remote_copy(
            src_ref=src,
            dst_ref=dst,
            send_sem=send_sem,
            recv_sem=sem,
            device_id=device,
            device_id_type=MESH_IDS,
        )

    def send(src, dst, sem, device, cond=None):
        copy = remote(src, dst, sem, device)
        when(cond, copy.start)
        pending.append((cond, copy))

    def wait(ref, sem, cond=None):
        when(cond, remote(ref, ref, sem, right).wait_recv)

    def lines(step):
        for sign, device, more in ((-1, up, has_up), (1, down, has_down)):
            block = z + sign * step
            yield block, (block >= 0) if sign < 0 else (block <= 3), device, more

    def stage_z(c, step):
        if step == 0:
            send(own(c), at(z, y, x, c), zs.at[c, z], up, has_up)
            send(own(c), at(z, y, x, c), zs.at[c, z], down, has_down)
            send(own(c), at(z, y, x, c), xs.at[c, z], right)
            send(own(c), at(z, y, x, c), ys.at[c, z], across)
            local[c].start()
        if 1 <= step <= 3:
            for block, exists, device, more in lines(step):
                ref = at(block, y, x, c)
                wait(ref, zs.at[c, block], exists)
                if step < 3:
                    send(ref, ref, zs.at[c, block], device, exists & more)
                send(ref, ref, xs.at[c, block], right, exists)
                send(ref, ref, ys.at[c, block], across, exists)
        if 1 <= step <= 4:
            for block, exists, _, _ in [(z, None, None, None)] if step == 1 else lines(step - 1):
                wait(at(block, y, xn, c), xs.at[c, block], exists)
                ref = at(block, y, xn, c, 0)
                send(ref, ref, ds.at[c, block, 0], across, exists)
                wait(at(block, yn, x, c), ys.at[c, block], exists)
                ref = at(block, yn, x, c, 1)
                send(ref, ref, ds.at[c, block, 1], right, exists)
        if step == 5:
            for block in range(4):
                for half in range(2):
                    wait(at(block, yn, xn, c, half), ds.at[c, block, half])
            local[c].wait()

    def stage_a(c, step):
        if step == 0:
            send(own(c), at(z, y, x, c), xs.at[c, z], right)
            send(own(c), at(z, y, x, c), ys.at[c, z], across)
            local[c].start()
        if step == 1:
            wait(at(z, y, xn, c), xs.at[c, z])
            ref = at(z, y, xn, c, 0)
            send(ref, ref, ds.at[c, z, 0], across)
            wait(at(z, yn, x, c), ys.at[c, z])
            ref = at(z, yn, x, c, 1)
            send(ref, ref, ds.at[c, z, 1], right)
        if step == 2:
            for half in range(2):
                wait(at(z, yn, xn, c, half), ds.at[c, z, half])
            local[c].wait()
            send(plane(z, c), plane(z, c), zs.at[c, z], up, has_up)
            send(plane(z, c), plane(z, c), zs.at[c, z], down, has_down)
        if step >= 3:
            for block, exists, device, more in lines(step - 2):
                wait(plane(block, c), zs.at[c, block], exists)
                if step < 5:
                    send(plane(block, c), plane(block, c), zs.at[c, block], device, exists & more)

    stages = 6

    def turn(number):
        for step in range(stages):
            c = number - step
            if 0 <= c < total:
                (stage_z if chunks[c][3] == "Z" else stage_a)(c, step)

    def finish():
        for cond, copy in pending:
            when(cond, copy.wait_send)

    return turn, finish


def total_of(*parts):
    value = parts[0].astype(F32)
    for part in parts[1:]:
        value = value + part.astype(F32)
    return value


def dot_nt(left, right):
    return lax.dot_general(left, right, (((1,), (1,)), ((), ())), preferred_element_type=F32)


def dot_tn(left, right):
    return lax.dot_general(left, right, (((0,), (0,)), ((), ())), preferred_element_type=F32)


def dot_nn(left, right):
    return jnp.dot(left, right, preferred_element_type=F32)


def project_rows(source, weight, store, rows=256, transposed=False):
    def body(n, carry):
        first = pl.multiple_of(n * rows, rows)
        part = source[pl.ds(first, rows), :]
        store(first, dot_nt(part, weight[...]) if transposed else dot_nn(part, weight[...]))
        return carry

    lax.fori_loop(0, source.shape[0] // rows, body, 0)


def normalize(values, gain, shift):
    offset = values - jnp.mean(values, axis=-1, keepdims=True)
    spread = jnp.mean(offset * offset, axis=-1, keepdims=True)
    return offset * lax.rsqrt(spread + norm_eps) * gain + shift


def head_lanes(half):
    return lax.div(lax.broadcasted_iota(jnp.int32, (1, 128), 1), 64) == half


def only(mask, value):
    return jnp.where(mask, value.astype(F32), 0.0).astype(BF16)


def pair_forward(pair, q_ref, k_ref, v_ref, o_ref, lse_ref, causal):
    cols = pl.ds(pl.multiple_of(pair * 128, 128), 128)
    block = 256
    keep = lax.broadcasted_iota(jnp.int32, (block, block), 0) <= lax.broadcasted_iota(
        jnp.int32, (block, block), 1
    )
    for i in range(q_ref.shape[0] // block):
        rows = pl.ds(i * block, block)
        parts = [(0, k_ref.shape[0], False)]
        if causal:
            parts = [(0, i * block, False)] * (i > 0) + [(i * block, block, True)]
        total = 0.0
        for half in range(2):
            mine = head_lanes(half)
            q = only(mine, q_ref[rows, cols])
            scores = []
            for first, count, diagonal in parts:
                part = dot_nt(k_ref[pl.ds(first, count), cols], q) * score_scale
                scores.append(jnp.where(keep, part, -1e30) if diagonal else part)
            peak = functools.reduce(
                jnp.maximum, [jnp.max(part, axis=0, keepdims=True) for part in scores]
            )
            scores = [jnp.exp(part - peak) for part in scores]
            weight = sum(jnp.sum(part, axis=0, keepdims=True) for part in scores)
            lse_ref[pl.ds(2 * pair + half, 1), rows] = peak + jnp.log(weight)
            share = 1.0 / weight
            for (first, count, _), part in zip(parts, scores, strict=True):
                v = only(mine, v_ref[pl.ds(first, count), cols])
                total = total + dot_tn((part * share).astype(BF16), v)
        o_ref[rows, cols] = total.astype(BF16)


def forward_kernel(chunks, count, *refs):
    shards, refs = refs[:count], refs[count:]
    hidden_h, text_h, cotangent_h, refs = refs[0], refs[1], refs[2], refs[3:]
    outs, refs = refs[:count], refs[count:]
    results, refs = refs[:19], refs[19:]
    sems, refs = refs[:6], refs[6:]
    (h1, h2, h3, q1, k1, v1, o1, q2, k2, v2, o2, lse1, lse2, x2, x3), refs = refs[:15], refs[15:]
    gathered_norms, norms, weights, hidden, text, mine, theirs, arrived, active, slopes = refs[:10]
    norm_sem, weight_sem, load_sem, share_send, share_recv, result_sem = refs[10:]
    names = dict(norms=0, q=1, k=2, v=3, o=4, ck=5, cv=6, cq=7, co=8, up=9, down=10)
    turn, finish = gather_engine(chunks, shards, outs, sems)
    chip, core = lax.axis_index("dp"), lax.axis_index("tensor")
    frames, width = h1.shape
    half = frames // 2
    own = pl.ds(pl.multiple_of(core * half, half), half)
    loads = [
        pltpu.make_async_copy(hidden_h, hidden, load_sem.at[0]),
        pltpu.make_async_copy(text_h, text, load_sem.at[1]),
        pltpu.make_async_copy(cotangent_h, theirs.at[1], load_sem.at[2]),
    ]
    for copy in loads:
        copy.start()
    pending = []

    def weight_copy(name, slot, first=0):
        return [
            pltpu.make_async_copy(
                outs[names[name]].at[zz, yy, xx, :, pl.ds(first, weights.shape[2])],
                weights.at[slot, pl.ds(((zz * 2 + yy) * 2 + xx) * rows, rows), :],
                weight_sem.at[slot, (zz * 2 + yy) * 2 + xx],
            )
            for zz in range(4)
            for yy in range(2)
            for xx in range(2)
        ]

    rows = width // 16

    def load_weight(name, slot, first=0):
        for copy in weight_copy(name, slot, first):
            copy.start()

    def wait_weight(slot):
        for copy in weight_copy("q", slot):
            copy.wait()

    def share(n, src, dst):
        return pltpu.make_async_remote_copy(
            src_ref=src,
            dst_ref=dst,
            send_sem=share_send.at[n],
            recv_sem=share_recv.at[n],
            device_id=(chip, 1 - core),
            device_id_type=MESH_IDS,
        )

    def give(n, ref):
        copy = pltpu.make_async_copy(ref, results[n], result_sem.at[n])
        copy.start()
        pending.append(copy)

    def norm_share(n, values, kind, h):
        step = 64

        def body(i, carry):
            first = pl.multiple_of(i * step, step)
            h[pl.ds(pl.multiple_of(core * half + first, step), step), :] = normalize(
                values(first, step), norms[2 * kind : 2 * kind + 1], norms[2 * kind + 1 : 2 * kind + 2]
            ).astype(BF16)
            return carry

        lax.fori_loop(0, half // step, body, 0)
        share(n, h.at[own], h.at[own]).start()

    def get_share(n, h):
        share(n, h.at[own], h.at[own]).wait()

    def to(ref):
        def store(first, value):
            ref[pl.ds(first, value.shape[0]), :] = value.astype(BF16)

        return store

    def out_project(n, o, slot):
        step = 256
        for whose, ref in ((1 - core, theirs.at[n]), (core, mine)):
            for first in range(0, half, step):
                part = o[pl.ds(pl.multiple_of(whose * half + first, step), step), :]
                ref[pl.ds(first, step), :] = dot_nt(part, weights[slot]).astype(ref.dtype)
            if whose is not core:
                share(3 + n, theirs.at[n], arrived.at[n]).start()

    def add_stream(n, before, after):
        def values(first, step):
            lines = pl.ds(first, step)
            total = before[lines, :].astype(F32) + (mine[lines, :] + arrived[n, lines, :].astype(F32))
            after[lines, :] = total
            return total

        return values

    branch = results[16].at[own]
    branch_copy = pltpu.make_async_copy(theirs.at[1], branch, result_sem.at[16])

    def active_copies(j):
        lanes = pl.ds(j * active.shape[1], active.shape[1])
        return (
            pltpu.make_async_copy(active, results[17].at[:, lanes], result_sem.at[17]),
            pltpu.make_async_copy(slopes, results[18].at[:, lanes], result_sem.at[18]),
        )

    def hidden_units(j):
        wait_weight(j % 2)
        if j < 3:
            load_weight("up", (j + 1) % 2, (j + 1) * active.shape[1])
        if j:
            for copy in active_copies(j - 1):
                copy.wait()

        def store(first, value):
            lines = pl.ds(first, value.shape[0])
            below = 0.5 * (1.0 + lax.erf(value * (0.5**0.5)))
            density = jnp.exp(-0.5 * value * value) * 0.3989422804014327
            active[lines, :] = (value * below).astype(BF16)
            slopes[lines, :] = (below + value * density).astype(BF16)

        project_rows(h3, weights.at[j % 2], store)
        for copy in active_copies(j):
            copy.start()

    def work(number):
        if number == 5:
            copy = pltpu.make_async_copy(outs[0], gathered_norms, norm_sem)
            copy.start()
            copy.wait()
            for copy in loads:
                copy.wait()
            share(5, theirs.at[1], branch).start()
            branch_copy.start()
            total = 0.0
            lane = lax.broadcasted_iota(jnp.int32, (128, width), 0)
            place = lax.broadcasted_iota(jnp.int32, (128, width), 1)
            for n in range(16):
                pick = (place == lane + n * rows) & (lane < rows)
                total = total + dot_nn(
                    gathered_norms[n // 4, n // 2 % 2, n % 2],
                    jnp.where(pick, 1.0, 0.0).astype(BF16),
                )
            norms[...] = total
            give(13, norms)
            norm_share(0, lambda first, step: hidden[pl.ds(first, step), :].astype(F32), 0, h1)
        if number == 6:
            load_weight("q", 0)
            get_share(0, h1)
            give(0, h1)
            wait_weight(0)
            project_rows(h1, weights.at[0], to(q1))
            give(3, q1)
        if number == 7:
            load_weight("k", 1)
            wait_weight(1)
            project_rows(h1, weights.at[1], to(k1))
            give(4, k1)
        if number == 8:
            load_weight("v", 0)
            wait_weight(0)
            project_rows(h1, weights.at[0], to(v1))
            give(5, v1)
        if number in (9, 10, 11):
            if number == 9:
                load_weight("o", 1)
            pairs = q1.shape[1] // 128
            first = pairs * (number - 9) // 3
            last = pairs * (number - 8) // 3

            def body(pair, carry):
                pair_forward(pair, q1, k1, v1, o1, lse1, True)
                return carry

            lax.fori_loop(first, last, body, 0)
            if number == 11:
                load_weight("cv", 0)
        if number == 12:
            share(5, theirs.at[1], branch).wait()
            branch_copy.wait()
            give(6, o1)
            give(11, lse1)
            wait_weight(1)
            out_project(0, o1, 1)
            load_weight("ck", 1)
            wait_weight(0)
            v2[...] = dot_nn(text[...], weights[0]).astype(BF16)
            give(9, v2)
            load_weight("cq", 0)
        if number == 13:
            share(3, theirs.at[0], arrived.at[0]).wait()
            norm_share(1, add_stream(0, hidden, x2), 1, h2)
            give(14, x2)
            wait_weight(1)
            k2[...] = dot_nn(text[...], weights[1]).astype(BF16)
            give(8, k2)
            load_weight("co", 1)
        if number == 14:
            get_share(1, h2)
            give(1, h2)
            wait_weight(0)
            project_rows(h2, weights.at[0], to(q2))
            give(7, q2)
        if number == 15:

            def body(pair, carry):
                pair_forward(pair, q2, k2, v2, o2, lse2, False)
                return carry

            lax.fori_loop(0, q2.shape[1] // 128, body, 0)
            give(10, o2)
            give(12, lse2)
        if number == 16:
            wait_weight(1)
            out_project(1, o2, 1)
        if number == 17:
            share(4, theirs.at[1], arrived.at[1]).wait()
            norm_share(2, add_stream(1, x2, x3), 2, h3)
            give(15, x3)
            load_weight("up", 0)
        if number == 18:
            get_share(2, h3)
            give(2, h3)
        if 18 <= number < 22:
            hidden_units(number - 18)

    for number in range(len(chunks) + 5):
        turn(number)
        work(number)
    finish()
    for copy in (*pending, *active_copies(3)):
        copy.wait()


def forward_all(shards, chunks, hidden, text, cotangent):
    total, count = len(chunks), len(shards)
    dma, vmem = pltpu.SemaphoreType.DMA, pltpu.VMEM
    half, width = hidden.shape
    frames, part = 2 * half, shards[1].shape[1]
    anywhere = pl.BlockSpec(memory_space=pl.ANY)
    shape = jax.ShapeDtypeStruct
    kept = [
        *[((frames, width), BF16)] * 3,
        *[((frames, part), BF16)] * 4,
        ((frames, part), BF16),
        *[((text.shape[0], part), BF16)] * 2,
        ((frames, part), BF16),
        *[((16, frames), F32)] * 2,
    ]
    given = [*kept, ((shards[0].shape[0], width), F32), ((half, width), F32), ((half, width), F32)]
    given += [((frames, width), BF16), ((frames, 4 * part), BF16), ((frames, 4 * part), BF16)]
    held = [*kept, ((half, width), F32), ((half, width), F32)]
    outs = pl.pallas_call(
        functools.partial(forward_kernel, chunks, count),
        out_shape=[shape((4, 2, 2) + s.shape, s.dtype) for s in shards] + [shape(*g) for g in given],
        in_specs=[pl.BlockSpec(memory_space=vmem)] * count + [anywhere] * 3,
        out_specs=[anywhere] * (count + len(given)),
        scratch_shapes=[
            dma((total,)),
            dma,
            dma((total, 4)),
            dma((total, 4)),
            dma((total, 4)),
            dma((total, 4, 2)),
            *[vmem(*h) for h in held],
            vmem((4, 2, 2) + shards[0].shape, BF16),
            vmem((shards[0].shape[0], width), F32),
            vmem((2, width, part), BF16),
            vmem((half, width), BF16),
            vmem(text.shape, BF16),
            vmem((half, width), F32),
            vmem((2, half, width), BF16),
            vmem((2, half, width), BF16),
            vmem((frames, part), BF16),
            vmem((frames, part), BF16),
            dma,
            dma((2, 16)),
            dma((3,)),
            dma((6,)),
            dma((6,)),
            dma((19,)),
        ],
        compiler_params=pltpu.CompilerParams(
            collective_id=0, has_side_effects=True, vmem_limit_bytes=VMEM_LIMIT
        ),
        name="forward",
    )(*shards, hidden, text, cotangent)
    return outs[:count], outs[count:]


XD, YD, XA, YA, XB, YB, UP, DOWN = range(8)


UNIT = 256
WIDTH_Z, WIDTH_A, SLOTS = 384, 128, 7
ROWS_L = 6
FIRST_L = (0, 12, 24, 27, 36, 39)
LOAD_L = ((2, 10), (3, 11), (4, 14), (5, 15))
FIRST_R = ((0, 12), (12, 24), (24, 27), (27, 30), (36, 39))
TEXT_UNITS = (30, 36)
SELF_UNITS = (39, 48)
UNITS = 48


def head_back(head, q_ref, k_ref, v_ref, do_ref, lse_ref, dq_ref, dkv_ref, bases, acc_k, acc_v, causal):
    pair, half = lax.div(head, 2), lax.rem(head, 2)
    cols = pl.ds(pl.multiple_of(pair * 128, 128), 128)
    lanes = [pl.ds(pl.multiple_of(pair * 128 + base, 128), 128) for base in bases]
    mine = head_lanes(half)
    length = k_ref.shape[0]
    acc_k[pl.ds(0, length), :] = jnp.zeros((length, 128), F32)
    acc_v[pl.ds(0, length), :] = jnp.zeros((length, 128), F32)
    block = 256
    keep = lax.broadcasted_iota(jnp.int32, (block, block), 0) <= lax.broadcasted_iota(
        jnp.int32, (block, block), 1
    )

    def merged(ref, rows, lane, value):
        before = jnp.where(half == 0, 0.0, ref[rows, lane].astype(F32))
        ref[rows, lane] = (before + value).astype(BF16)

    for i in range(q_ref.shape[0] // block):
        rows = pl.ds(i * block, block)
        q = only(mine, q_ref[rows, cols])
        do = only(mine, do_ref[rows, cols])
        lse = lse_ref[pl.ds(head, 1), rows]
        parts = [(0, length, False)]
        if causal:
            parts = [(0, i * block, False)] * (i > 0) + [(i * block, block, True)]
        held, inner = [], 0.0
        for first, count, diagonal in parts:
            keys = pl.ds(first, count)
            soft = jnp.exp(dot_nt(k_ref[keys, cols], q) * score_scale - lse)
            if diagonal:
                soft = jnp.where(keep, soft, 0.0)
            slope = dot_nt(v_ref[keys, cols], do)
            inner = inner + jnp.sum(soft * slope, axis=0, keepdims=True)
            held.append((keys, soft, slope))
        grad_q = 0.0
        for keys, soft, slope in held:
            ds = (soft * (slope - inner)).astype(BF16)
            acc_v[keys, :] += dot_nn(soft.astype(BF16), do)
            acc_k[keys, :] += dot_nn(ds, q)
            grad_q = grad_q + dot_tn(ds, k_ref[keys, cols])
        merged(dq_ref, rows, lanes[0], jnp.where(mine, grad_q * score_scale, 0.0))
    everything = pl.ds(0, length)
    merged(dkv_ref, everything, lanes[1], acc_k[everything, :] * score_scale)
    merged(dkv_ref, everything, lanes[2], acc_v[everything, :])


def backward_kernel(*refs):
    (e3_h, h3_h, h2_h, h1_h, a_h, slope_h, o2_h, o1_h, text_h), refs = refs[:9], refs[9:]
    (q2_h, k2_h, v2_h, q1_h, k1_h, v1_h, x3_h, x2_h, x1_h), refs = refs[:9], refs[9:]
    (w_q, w_k, w_v, w_o, w_ck, w_cv, w_cq, w_co, w_up, w_down), refs = refs[:10], refs[10:]
    (lse2_ref, lse1_ref, norms), refs = refs[:3], refs[3:]
    (out, layer_out, grad_input, grad_text, norm_out), refs = refs[:5], refs[5:]
    (du_h, dq2_h, e2_h, e1_h), refs = refs[:4], refs[4:]
    (gz, ga, xdz, ydz, xaz, yaz, xbz, ybz, lnz), refs = refs[:9], refs[9:]
    (xda, yda, xaa, yaa, xba, yba, lna, oz, oa), refs = refs[:9], refs[9:]
    (lbuf, rbuf, text_v, dkv_v, k2_v, v2_v, pool, dqkv, acc_k, acc_v), refs = refs[:10], refs[10:]
    (acc, grad, xbuf, theirs, arrived, weights, text_part, text_send, text_got), refs = refs[:9], refs[9:]
    (norm_grads, got), refs = refs[:2], refs[2:]
    (first_sem, l_sem, r_sem, out_sem, send_z, send_a, recv_z, recv_a), refs = refs[:8], refs[8:]
    (pool_sem, slope_sem, weight_sem, x_sem, keep_sem, share_send, share_recv, norm_send), refs = refs[:8], refs[8:]
    norm_recv, credit = refs
    lefts = (e3_h, h3_h, e2_h, h2_h, e1_h, h1_h)
    rights = (a_h, du_h, o2_h, dq2_h, o1_h)
    width_z, width_a, slots = WIDTH_Z, WIDTH_A, SLOTS
    total, width = UNITS // 2, WIDTH_Z + WIDTH_A
    x, y, z, core = my_place()
    xn, yn = 1 - x, 1 - y
    near = neighbours(x, y, z, core)
    right, across, up, down = near
    has_up, has_down = z < 3, z > 0
    degree = 2 + has_up.astype(jnp.int32) + has_down.astype(jnp.int32)
    chip = lax.axis_index("dp")
    other = (chip, 1 - core)
    partners = [other]
    for bit in (1, 2, 4, 8):
        partners.append((chip + bit * (1 - 2 * lax.rem(lax.div(chip, bit), 2)), core))
    barrier = pltpu.get_barrier_semaphore()
    signal_neighbours([barrier] * 4, near, has_up, has_down)
    for device in (other, partners[4]):
        pl.semaphore_signal(barrier, inc=1, device_id=device, device_id_type=MESH_IDS)
    pl.semaphore_wait(barrier, degree + 2)
    rows = gz.shape[4]
    low, high = pl.ds(0, rows // 2), pl.ds(rows // 2, rows // 2)

    def remote(src, dst, send_sem, recv_sem, device):
        return pltpu.make_async_remote_copy(
            src_ref=src,
            dst_ref=dst,
            send_sem=send_sem,
            recv_sem=recv_sem,
            device_id=device,
            device_id_type=MESH_IDS,
        )

    def arrived_at(ref, sem):
        remote(ref, ref, send_z.at[0], sem, right).wait_recv()

    def sent(ref, sem):
        remote(ref, ref, sem, recv_z.at[0, 0], right).wait_send()

    firsts = [
        pltpu.make_async_copy(src, dst, first_sem.at[n])
        for n, (src, dst) in enumerate(((text_h, text_v), (k2_h, k2_v), (v2_h, v2_v)))
    ]

    def left_copy(n):
        return pltpu.make_async_copy(lefts[n], lbuf.at[n % 2], l_sem.at[n % 2])

    def right_copies(c, which):
        unit = 2 * c + which
        place, sem = rbuf.at[lax.rem(c, 2), which], r_sem.at[lax.rem(c, 2), which]
        for source, (lo, hi) in zip((*rights, dqkv), (*FIRST_R, SELF_UNITS), strict=True):
            first = pl.multiple_of((unit - lo) * UNIT, UNIT)
            yield (
                (unit >= lo) & (unit < hi),
                pltpu.make_async_copy(source.at[:, pl.ds(first, UNIT)], place, sem),
            )

    def start_rights(c):
        for which in range(2):
            for cond, copy in right_copies(c, which):
                pl.when(cond)(copy.start)

    def store_unit(which, k, i, value):
        for yy in range(2):
            for xx in range(2):
                first = (yy * 2 + xx) * rows
                block = value[first : first + rows, :].astype(BF16)
                if which == 0:
                    gz[k, i, yy, xx, :, pl.ds(0, UNIT)] = block
                else:
                    gz[k, i, yy, xx, :, pl.ds(UNIT, width_z - UNIT)] = block[:, : width_z - UNIT]
                    ga[k, i, yy, xx] = block[:, width_z - UNIT :]

    def compute(c, k):
        for n in range(1, ROWS_L):
            pl.when(c == FIRST_L[n] // 2)(left_copy(n).wait)
        for which in range(2):
            unit = 2 * c + which
            text = (unit >= TEXT_UNITS[0]) & (unit < TEXT_UNITS[1])
            slot = lax.rem(sum((unit >= first).astype(jnp.int32) for first in FIRST_L) + 1, 2)

            @pl.when(text)
            def _():
                first = pl.multiple_of((unit - TEXT_UNITS[0]) * UNIT, UNIT)
                right_part = dkv_v[:, pl.ds(first, UNIT)]
                for i in range(4):
                    store_unit(which, k, i, dot_tn(text_v[:, pl.ds(i * 4 * rows, 4 * rows)], right_part))

            @pl.when(jnp.logical_not(text))
            def _():
                par = lax.rem(c, 2)
                pltpu.make_async_copy(rbuf.at[par, which], rbuf.at[par, which], r_sem.at[par, which]).wait()
                right_part = rbuf[par, which]
                for i in range(4):
                    left_part = lbuf[slot, :, pl.ds(i * 4 * rows, 4 * rows)]
                    store_unit(which, k, i, dot_tn(left_part, right_part))

        for n, at in LOAD_L:
            pl.when(c == at)(left_copy(n).start)
        pl.when(c + 1 < total)(lambda: start_rights(c + 1))

    def out_copies(c):
        o = lax.rem(c, 2)
        first = pl.multiple_of(c * width, 128)
        return (
            pltpu.make_async_copy(oz.at[o], out.at[:, pl.ds(first, width_z)], out_sem.at[o, 0]),
            pltpu.make_async_copy(
                oa.at[o], out.at[:, pl.ds(first + width_z, width_a)], out_sem.at[o, 1]
            ),
        )

    def plane_first(own, k, bufs, send_sem, recv):
        xd, yd, xa, ya = bufs
        remote(own(yn, xn, low), xd.at[k], send_sem.at[k], recv.at[k, XD], right).start()
        remote(own(yn, xn, high), yd.at[k], send_sem.at[k], recv.at[k, YD], across).start()
        remote(own(y, xn, low), xa.at[k], send_sem.at[k], recv.at[k, XA], right).start()
        remote(own(yn, x, high), ya.at[k], send_sem.at[k], recv.at[k, YA], across).start()

    def plane_second(add, k, bufs, send_sem, recv):
        xd, yd, xb, yb = bufs
        arrived_at(xd.at[k], recv.at[k, XD])
        add(xd, yn, x, low)
        remote(xd.at[k], yb.at[k], send_sem.at[k], recv.at[k, YB], across).start()
        arrived_at(yd.at[k], recv.at[k, YD])
        add(yd, y, xn, high)
        remote(yd.at[k], xb.at[k], send_sem.at[k], recv.at[k, XB], right).start()

    def above(buf, k, first, blocks):
        return buf.at[k, pl.ds(first + 1, blocks)]

    def below(buf, k, blocks):
        return buf.at[k, pl.ds(0, blocks)]

    def line_up(first, buf, add, k, send_sem, recv):
        blocks = 4 - first
        arrived_at(above(buf, k, first, blocks), recv.at[k, UP])
        if blocks > 1:
            for block in range(first + 1, 4):
                add(buf, block, block + 1)
            ref = above(buf, k, first + 1, blocks - 1)
            remote(ref, ref, send_sem.at[k], recv.at[k, UP], up).start()

    def line_down(last, buf, add, k, send_sem, recv):
        arrived_at(below(buf, k, last + 1), recv.at[k, DOWN])
        if last > 0:
            for block in range(last):
                add(buf, block, block)
            ref = below(buf, k, last)
            remote(ref, ref, send_sem.at[k], recv.at[k, DOWN], down).start()

    def add_a(k):
        def add(buf, block, at):
            for yy in range(2):
                for xx in range(2):
                    buf[k, at, yy, xx] = total_of(
                        buf[k, at, yy, xx], ga[k, block, yy, xx]
                    ).astype(BF16)

        return add

    def add_z(k):
        def add(buf, block, at):
            buf[k, at] = total_of(buf[k, at], gz[k, block, y, x]).astype(BF16)

        return add

    def begin(c, k):
        @pl.when(c >= slots)
        def _():
            pl.semaphore_wait(credit.at[0], 1)
            pl.semaphore_wait(credit.at[1], 1)
            pl.when(has_up)(lambda: pl.semaphore_wait(credit.at[2], 1))
            pl.when(has_down)(lambda: pl.semaphore_wait(credit.at[3], 1))

        plane_first(
            lambda yy, xx, half: gz.at[k, :, yy, xx, half, :], k, (xdz, ydz, xaz, yaz), send_z, recv_z
        )

        @pl.when(z == 0)
        def _():
            ref = pl.ds(1, 3)
            remote(ga.at[k, ref], above(lna, k, 1, 3), send_a.at[k], recv_a.at[k, UP], up).start()

        @pl.when(z == 3)
        def _():
            ref = pl.ds(0, 3)
            remote(ga.at[k, ref], below(lna, k, 3), send_a.at[k], recv_a.at[k, DOWN], down).start()

    def second(c, k):
        def add(buf, yy, xx, half):
            for block in range(4):
                buf[k, block] = total_of(buf[k, block], gz[k, block, yy, xx, half, :]).astype(BF16)

        plane_second(add, k, (xdz, ydz, xbz, ybz), send_z, recv_z)
        pl.when(z == 1)(lambda: line_up(1, lna, add_a(k), k, send_a, recv_a))
        pl.when(z == 2)(lambda: line_down(2, lna, add_a(k), k, send_a, recv_a))

    def third(c, k):
        for buf, kind in ((xaz, XA), (yaz, YA), (xbz, XB), (ybz, YB)):
            arrived_at(buf.at[k], recv_z.at[k, kind])
        for block in range(4):
            for half, one, two in ((low, xaz, ybz), (high, yaz, xbz)):
                gz[k, block, y, x, half, :] = total_of(
                    gz[k, block, y, x, half, :], one[k, block], two[k, block]
                ).astype(BF16)

        @pl.when(z == 0)
        def _():
            ref = pl.ds(1, 3)
            remote(
                gz.at[k, ref, y, x], above(lnz, k, 1, 3), send_z.at[k], recv_z.at[k, UP], up
            ).start()

        @pl.when(z == 3)
        def _():
            ref = pl.ds(0, 3)
            remote(
                gz.at[k, ref, y, x], below(lnz, k, 3), send_z.at[k], recv_z.at[k, DOWN], down
            ).start()

        pl.when(z == 2)(lambda: line_up(2, lna, add_a(k), k, send_a, recv_a))
        pl.when(z == 1)(lambda: line_down(1, lna, add_a(k), k, send_a, recv_a))

    def fourth(c, k):
        pl.when(z == 1)(lambda: line_up(1, lnz, add_z(k), k, send_z, recv_z))
        pl.when(z == 2)(lambda: line_down(2, lnz, add_z(k), k, send_z, recv_z))
        pl.when(z == 3)(lambda: line_up(3, lna, None, k, send_a, recv_a))
        pl.when(z == 0)(lambda: line_down(0, lna, None, k, send_a, recv_a))
        for shift, exists in ((1, has_down), (0, has_up)):

            @pl.when(exists)
            def _():
                for yy in range(2):
                    for xx in range(2):
                        ga[k, z, yy, xx] = total_of(
                            ga[k, z, yy, xx], lna[k, z + shift, yy, xx]
                        ).astype(BF16)

        plane_first(
            lambda yy, xx, half: ga.at[k, z, yy, xx, half, :], k, (xda, yda, xaa, yaa), send_a, recv_a
        )

    def fifth(c, k):
        pl.when(z == 2)(lambda: line_up(2, lnz, add_z(k), k, send_z, recv_z))
        pl.when(z == 1)(lambda: line_down(1, lnz, add_z(k), k, send_z, recv_z))

        def add(buf, yy, xx, half):
            buf[k] = total_of(buf[k], ga[k, z, yy, xx, half, :]).astype(BF16)

        plane_second(add, k, (xda, yda, xba, yba), send_a, recv_a)

    def finish(c, k):
        pl.when(z == 3)(lambda: line_up(3, lnz, None, k, send_z, recv_z))
        pl.when(z == 0)(lambda: line_down(0, lnz, None, k, send_z, recv_z))
        o = lax.rem(c, 2)

        @pl.when(c >= 2)
        def _():
            for copy in out_copies(c - 2):
                copy.wait()

        oz[o] = gz[k, z, y, x].astype(F32)
        for shift, exists in ((1, has_down), (0, has_up)):

            @pl.when(exists)
            def _():
                oz[o] = oz[o] + lnz[k, z + shift].astype(F32)

        for buf, kind in ((xaa, XA), (yaa, YA), (xba, XB), (yba, YB)):
            arrived_at(buf.at[k], recv_a.at[k, kind])
        oa[o, low, :] = total_of(ga[k, z, y, x, low, :], xaa[k], yba[k])
        oa[o, high, :] = total_of(ga[k, z, y, x, high, :], yaa[k], xba[k])
        for copy in out_copies(c):
            copy.start()
        for buf in (xdz, ydz, xaz, yaz, xbz, ybz):
            sent(buf.at[k], send_z.at[k])
        for buf in (xda, yda, xaa, yaa, xba, yba):
            sent(buf.at[k], send_a.at[k])
        for step in range(3):

            @pl.when(z == step)
            def _():
                sent(above(lnz, k, step + 1, 3 - step), send_z.at[k])
                sent(above(lna, k, step + 1, 3 - step), send_a.at[k])

            @pl.when(z == 3 - step)
            def _():
                sent(below(lnz, k, 3 - step), send_z.at[k])
                sent(below(lna, k, 3 - step), send_a.at[k])

        @pl.when(c < total - slots)
        def _():
            signal_neighbours([credit.at[i] for i in (0, 1, 3, 2)], near, has_up, has_down)

    frames, features = e3_h.shape
    part, half_rows = pool.shape[2], frames // 2
    heads = part // HEAD_DIM
    own_rows = pl.ds(pl.multiple_of(core * half_rows, half_rows), half_rows)
    wide = pl.ds(0, features)
    slope = dqkv.at[:, pl.ds(features, part)]
    block = 256

    def columns(n):
        return pl.ds(pl.multiple_of(n * part, part), part)

    def weight_copy(slot, ref, n=0):
        return pltpu.make_async_copy(ref.at[:, columns(n)], weights.at[slot], weight_sem.at[slot])

    def use(slot):
        weight_copy(slot, w_q).wait()

    def pool_copy(n, ref, m=0):
        return pltpu.make_async_copy(ref.at[:, columns(m)], pool.at[n], pool_sem.at[n])

    def slope_copy(n):
        return pltpu.make_async_copy(slope_h.at[:, columns(n)], slope, slope_sem)

    def keep_copy(n, src, dst):
        return pltpu.make_async_copy(src, dst, keep_sem.at[n])

    def du_copy(n):
        return keep_copy(0, pool.at[n], du_h.at[:, columns(n)])

    def to_other(n, src, dst):
        return remote(src, dst, share_send.at[n], share_recv.at[n], other)

    def share_sum(n):
        return to_other(n, theirs, arrived.at[n % 2])

    def share_branch(n):
        ref = dqkv.at[own_rows, wide]
        return to_other(4 + n, ref, ref)

    def multiply(whose, source, slot, fresh):
        for first in range(0, half_rows, block):
            rows_of = pl.ds(pl.multiple_of(whose * half_rows + first, block), block)
            value = dot_nt(source(rows_of), weights[slot])
            lines = pl.ds(first, block)
            acc[lines, :] = value if fresh else acc[lines, :] + value

    def pooled(n):
        return lambda rows_of: pool[n, rows_of, :]

    def headed(n):
        return lambda rows_of: dqkv[rows_of, pl.ds(n * part, part)]

    def send_sum(n):
        for first in range(0, half_rows, block):
            lines = pl.ds(first, block)
            theirs[lines, :] = acc[lines, :].astype(BF16)
        share_sum(n).start()

    def norm_back(kind, n, load, before, store):
        step = 64
        gain = norms[2 * kind : 2 * kind + 1, :]

        def body(i, sums):
            first = pl.multiple_of(i * step, step)
            lines = pl.ds(first, step)
            value = load(i, lines)
            offset = value - jnp.mean(value, axis=-1, keepdims=True)
            scale = lax.rsqrt(jnp.mean(offset * offset, axis=-1, keepdims=True) + norm_eps)
            unit = offset * scale
            slope_in = acc[lines, :] + arrived[n % 2, lines, :].astype(F32)
            scaled = slope_in * gain
            inner = jnp.mean(scaled * unit, axis=-1, keepdims=True)
            change = scale * (scaled - jnp.mean(scaled, axis=-1, keepdims=True) - unit * inner)
            store(first, lines, before(first, lines) + change)
            return (
                sums[0] + jnp.sum(slope_in * unit, axis=0, keepdims=True),
                sums[1] + jnp.sum(slope_in, axis=0, keepdims=True),
            )

        zero = jnp.zeros((1, features), F32)
        gains, shifts = lax.fori_loop(0, half_rows // step, body, (zero, zero))
        norm_grads[2 * kind : 2 * kind + 1, :] = gains
        norm_grads[2 * kind + 1 : 2 * kind + 2, :] = shifts

    def streamed(ref):
        step = xbuf.shape[1]

        def copy(i):
            first = pl.multiple_of(i * step, step)
            return pltpu.make_async_copy(
                ref.at[pl.ds(first, step), :], xbuf.at[lax.rem(i, 2)], x_sem.at[lax.rem(i, 2)]
            )

        copy(jnp.int32(0)).start()

        def load(i, lines):
            copy(i).wait()
            pl.when(i + 1 < half_rows // step)(copy(i + 1).start)
            return xbuf[lax.rem(i, 2)]

        return load

    def store_branch(first, lines, value):
        grad[lines, :] = value
        dqkv[pl.ds(pl.multiple_of(core * half_rows + first, 64), 64), wide] = value.astype(BF16)

    def project_to(n, slot):
        for first in range(0, frames, block):
            lines = pl.ds(first, block)
            pool[n, lines, :] = dot_nn(dqkv[lines, wide], weights[slot]).astype(BF16)

    def feed_forward(j):
        use(0)
        slope_copy(j).wait()
        for first in range(0, frames, block):
            lines = pl.ds(first, block)
            value = dot_nn(lbuf[0, lines, :], weights[0])
            pool[j, lines, :] = (
                value * dqkv[lines, pl.ds(features, part)].astype(F32)
            ).astype(BF16)

        @pl.when(j > 0)
        def _():
            du_copy(j - 1).wait()

        du_copy(j).start()

        @pl.when(j < 3)
        def _():
            weight_copy(0, w_down, j + 1).start()
            slope_copy(j + 1).start()

        pl.when(j == 3)(lambda: weight_copy(0, w_up, 0).start())
        use(1)
        multiply(1 - core, pooled(j), 1, False)
        pl.when(j < 3)(lambda: weight_copy(1, w_up, j + 1).start())
        pl.when(j == 3)(lambda: send_sum(0))

    def turn_4():
        du_copy(3).wait()
        multiply(core, pooled(3), 1, True)
        weight_copy(1, w_up, 1).start()
        use(0)
        multiply(core, pooled(0), 0, False)
        weight_copy(0, w_up, 2).start()

    def turn_5():
        use(1)
        multiply(core, pooled(1), 1, False)
        weight_copy(1, w_cq).start()
        use(0)
        multiply(core, pooled(2), 0, False)
        weight_copy(0, w_co).start()

    def turn_6():
        pool_copy(0, q2_h).start()
        share_sum(0).wait()
        norm_back(
            2,
            0,
            streamed(x3_h),
            lambda first, lines: lbuf[
                0, pl.ds(pl.multiple_of(core * half_rows + first, 64), 64), :
            ].astype(F32),
            store_branch,
        )
        share_branch(0).start()

    def turn_7():
        share_branch(0).wait()
        keep_copy(1, dqkv.at[:, wide], e2_h).start()
        use(0)
        project_to(1, 0)
        weight_copy(0, w_ck).start()

    def turn_8():
        pool_copy(0, q2_h).wait()
        for copy in firsts:
            copy.wait()

        def body(head, carry):
            head_back(
                head,
                pool.at[0],
                k2_v,
                v2_v,
                pool.at[1],
                lse2_ref,
                pool.at[2],
                dkv_v,
                (0, 0, part),
                acc_k,
                acc_v,
                False,
            )
            return carry

        lax.fori_loop(0, heads, body, 0)
        keep_copy(1, dqkv.at[:, wide], e2_h).wait()
        keep_copy(0, pool.at[2], dq2_h).start()
        use(0)
        text_part[...] = dot_nt(dkv_v[:, pl.ds(0, part)], weights[0])
        weight_copy(0, w_cv).start()

    def text_columns(whose):
        count = features // 2
        return pl.ds(pl.multiple_of(whose * count, count), count)

    def text_share():
        return to_other(6, text_send, text_got)

    def turn_9():
        keep_copy(0, pool.at[2], dq2_h).wait()
        use(0)
        text_part[...] += dot_nt(dkv_v[:, pl.ds(part, part)], weights[0])
        text_send[...] = text_part[:, text_columns(1 - core)].astype(BF16)
        text_share().start()
        weight_copy(0, w_o).start()
        use(1)
        multiply(1 - core, pooled(2), 1, True)
        send_sum(1)

    def turn_10():
        multiply(core, pooled(2), 1, True)
        for n, ref in enumerate((q1_h, k1_h, v1_h)):
            pool_copy(n, ref).start()
        share_sum(1).wait()
        norm_back(1, 1, streamed(x2_h), lambda first, lines: grad[lines, :], store_branch)
        share_branch(1).start()
        text_share().wait()
        text_part[:, pl.ds(0, features // 2)] = text_part[:, text_columns(core)] + text_got[
            ...
        ].astype(F32)
        keep_copy(2, text_part.at[:, pl.ds(0, features // 2)], grad_text).start()

    def turn_11():
        share_branch(1).wait()
        keep_copy(1, dqkv.at[:, wide], e1_h).start()
        use(0)
        project_to(3, 0)
        weight_copy(0, w_q).start()
        weight_copy(1, w_k).start()

    def turn_12():
        keep_copy(1, dqkv.at[:, wide], e1_h).wait()
        for n, ref in enumerate((q1_h, k1_h, v1_h)):
            pool_copy(n, ref).wait()

    def self_head(head):
        head_back(
            head,
            pool.at[0],
            pool.at[1],
            pool.at[2],
            pool.at[3],
            lse1_ref,
            dqkv,
            dqkv,
            (0, part, 2 * part),
            acc_k,
            acc_v,
            True,
        )

    def turn_18():
        for n in range(4):
            pool_copy(n, a_h, n).start()
        use(0)
        multiply(1 - core, headed(0), 0, True)
        weight_copy(0, w_v).start()
        use(1)
        multiply(1 - core, headed(1), 1, False)

    def turn_19():
        use(0)
        multiply(1 - core, headed(2), 0, False)
        send_sum(2)
        multiply(core, headed(2), 0, True)
        weight_copy(0, w_down, 0).start()
        multiply(core, headed(1), 1, False)
        weight_copy(1, w_q).start()

    def turn_20():
        use(1)
        multiply(core, headed(0), 1, False)
        weight_copy(1, w_down, 1).start()

    def turn_21():
        share_sum(2).wait()
        hidden = keep_copy(1, x1_h, theirs)
        hidden.start()
        hidden.wait()

        def store(first, lines, value):
            grad[lines, :] = value

        norm_back(
            0,
            2,
            lambda i, lines: theirs[lines, :].astype(F32),
            lambda first, lines: grad[lines, :],
            store,
        )
        keep_copy(3, grad, grad_input).start()

    def turn_22():
        for n in range(4):
            pool_copy(n, a_h, n).wait()
        use(0)
        multiply(1 - core, pooled(0), 0, True)
        weight_copy(0, w_down, 2).start()
        use(1)
        multiply(1 - core, pooled(1), 1, False)
        weight_copy(1, w_down, 3).start()

    def turn_23():
        keep_copy(3, grad, grad_input).wait()
        keep_copy(1, x3_h, grad).start()
        use(0)
        multiply(1 - core, pooled(2), 0, False)
        use(1)
        multiply(1 - core, pooled(3), 1, False)
        send_sum(3)
        multiply(core, pooled(2), 0, True)
        weight_copy(0, w_down, 0).start()
        multiply(core, pooled(3), 1, False)
        weight_copy(1, w_down, 1).start()

    def turn_24():
        use(0)
        multiply(core, pooled(0), 0, False)
        use(1)
        multiply(core, pooled(1), 1, False)

    def turn_25():
        share_sum(3).wait()
        keep_copy(1, x3_h, grad).wait()
        for first in range(0, half_rows, 64):
            lines = pl.ds(first, 64)
            theirs[lines, :] = (
                grad[lines, :] + (acc[lines, :] + arrived[1, lines, :].astype(F32))
            ).astype(BF16)
        keep_copy(0, theirs, layer_out).start()

    def norm_copy(step):
        return remote(
            got.at[2 * step],
            got.at[2 * step + 1],
            norm_send.at[step],
            norm_recv.at[step],
            partners[step],
        )

    def norm_sum(step):
        if step == 0:
            got[0] = norm_grads[...]
        else:
            norm_copy(step - 1).wait()
            got[2 * step] = got[2 * step - 2] + got[2 * step - 1]
        if step < len(partners):
            norm_copy(step).start()
        else:
            keep_copy(1, got.at[2 * step], norm_out).start()

    chain = {
        4: turn_4,
        5: turn_5,
        6: turn_6,
        7: turn_7,
        8: turn_8,
        9: turn_9,
        10: turn_10,
        11: turn_11,
        18: turn_18,
        19: turn_19,
        20: turn_20,
        21: turn_21,
        22: turn_22,
        23: turn_23,
        24: turn_24,
        25: turn_25,
    }
    stages = (begin, second, third, fourth, fifth, finish)
    left_copy(0).start()
    weight_copy(0, w_down, 0).start()
    slope_copy(0).start()
    start_rights(jnp.int32(0))
    weight_copy(1, w_up, 0).start()
    left_copy(1).start()
    for copy in firsts:
        copy.start()
    for first in range(0, half_rows, block):
        acc[pl.ds(first, block), :] = jnp.zeros((block, features), F32)
    norm_grads[...] = jnp.zeros_like(norm_grads)
    left_copy(0).wait()

    def body(turn, carry):
        for step, stage in enumerate(stages):
            c = turn - step - 1

            @pl.when((c >= 0) & (c < total))
            def _():
                stage(c, lax.rem(c, slots))

        pl.when(turn < total)(lambda: compute(turn, lax.rem(turn, slots)))
        pl.when(turn < 4)(lambda: feed_forward(turn))
        for number, fn in chain.items():
            pl.when(turn == number)(fn)
        pl.when(turn == 12)(turn_12)

        @pl.when((turn >= 12) & (turn < 18))
        def _():
            def both(head, carry):
                self_head(head)
                return carry

            first = lax.div(heads, 6) * (turn - 12)
            lax.fori_loop(first, first + heads // 6, both, 0)

        for step in range(len(partners) + 1):
            pl.when(turn == 22 + step)(functools.partial(norm_sum, step))
        return carry

    lax.fori_loop(0, total + len(stages), body, 0)
    for c in (total - 2, total - 1):
        for copy in out_copies(jnp.int32(c)):
            copy.wait()
    keep_copy(0, theirs, layer_out).wait()
    keep_copy(1, got.at[2 * len(partners)], norm_out).wait()
    keep_copy(2, text_part.at[:, pl.ds(0, features // 2)], grad_text).wait()


def backward_all(arrays, small):
    frames, width = arrays[0].shape
    text = arrays[8]
    rows, half, part = width // 16, frames // 2, arrays[9].shape[1]
    dma, vmem, shape = pltpu.SemaphoreType.DMA, pltpu.VMEM, jax.ShapeDtypeStruct

    def buffer(*dims):
        return vmem((SLOTS,) + dims, BF16)

    anywhere = pl.BlockSpec(memory_space=pl.ANY)
    return pl.pallas_call(
        backward_kernel,
        out_shape=[
            shape((rows, UNITS * UNIT), F32),
            shape((half, width), BF16),
            shape((half, width), F32),
            shape((text.shape[0], width // 2), F32),
            shape((8, width), F32),
            shape((frames, 4 * part), BF16),
            shape((frames, part), BF16),
            shape((frames, width), BF16),
            shape((frames, width), BF16),
        ],
        in_specs=[anywhere] * len(arrays) + [pl.BlockSpec(memory_space=vmem)] * len(small),
        out_specs=[anywhere] * 9,
        scratch_shapes=[
            buffer(4, 2, 2, rows, WIDTH_Z),
            buffer(4, 2, 2, rows, WIDTH_A),
            *[buffer(4, rows // 2, WIDTH_Z)] * 6,
            buffer(5, rows, WIDTH_Z),
            *[buffer(rows // 2, WIDTH_A)] * 6,
            buffer(5, 2, 2, rows, WIDTH_A),
            vmem((2, rows, WIDTH_Z), F32),
            vmem((2, rows, WIDTH_A), F32),
            vmem((2, frames, width), BF16),
            vmem((2, 2, frames, UNIT), BF16),
            vmem(text.shape, BF16),
            vmem((text.shape[0], 2 * part), BF16),
            *[vmem((text.shape[0], part), BF16)] * 2,
            vmem((4, frames, part), BF16),
            vmem((frames, 3 * part), BF16),
            *[vmem((frames, 128), F32)] * 2,
            *[vmem((half, width), F32)] * 2,
            vmem((2, 64, width), F32),
            vmem((half, width), BF16),
            vmem((2, half, width), BF16),
            vmem((2, width, part), BF16),
            vmem((text.shape[0], width), F32),
            *[vmem((text.shape[0], width // 2), BF16)] * 2,
            vmem((8, width), F32),
            vmem((11, 8, width), F32),
            dma((3,)),
            dma((2,)),
            dma((2, 2)),
            dma((2, 2)),
            dma((SLOTS,)),
            dma((SLOTS,)),
            dma((SLOTS, 8)),
            dma((SLOTS, 8)),
            dma((4,)),
            dma,
            dma((2,)),
            dma((2,)),
            dma((4,)),
            dma((7,)),
            dma((7,)),
            dma((5,)),
            dma((5,)),
            pltpu.SemaphoreType.REGULAR((4,)),
        ],
        compiler_params=pltpu.CompilerParams(
            collective_id=1, has_side_effects=True, vmem_limit_bytes=VMEM_LIMIT
        ),
        name="backward",
    )(*arrays, *small)


def gather_plan(columns):
    chunks, since = [], 0
    for array, width in enumerate(columns):
        size = 768 if width % 768 == 0 else width
        for first in range(0, width, size):
            since += 1
            family = "A" if since % 5 == 3 and size == 768 else "Z"
            chunks.append((array, first, size, family))
    return tuple(chunks)


def local_fast(
    hidden_in,
    text_states,
    norm1_gain,
    norm1_bias,
    self_query,
    self_key,
    self_value,
    self_out,
    norm2_gain,
    norm2_bias,
    cross_query,
    cross_key,
    cross_value,
    cross_out,
    norm3_gain,
    norm3_bias,
    hidden_up,
    hidden_down,
    cotangent,
):
    width = norm1_gain.shape[0] * 16
    norms = jnp.stack([norm1_gain, norm1_bias, norm2_gain, norm2_bias, norm3_gain, norm3_bias])
    norms = jnp.pad(norms, ((0, 26), (0, 128 - norms.shape[1])))
    shards = (
        norms,
        self_query.T,
        self_key.T,
        self_value.T,
        self_out,
        cross_key.T,
        cross_value.T,
        cross_query.T,
        cross_out,
        hidden_up.T,
        hidden_down,
    )
    gathered, kept = forward_all(
        shards,
        gather_plan([s.shape[1] for s in shards]),
        hidden_in[0],
        text_states[0],
        cotangent[0],
    )
    w_q, w_k, w_v, w_o, w_ck, w_cv, w_cq, w_co, w_up, w_down = [
        g.reshape(width, g.shape[-1]) for g in gathered[1:]
    ]
    normed_one, normed_two, normed_three = kept[:3]
    query_one, key_one, value_one, attended_one = kept[3:7]
    query_two, key_two, value_two, attended_two = kept[7:11]
    logsum_one, logsum_two, norms, stream_two, stream_three, branch, active, slope = kept[11:]
    summed, layer_out, grad_input, grad_text, norm_sums, *_ = backward_all(
        (
            *(branch, normed_three, normed_two, normed_one),
            *(active, slope, attended_two, attended_one, text_states[0]),
            *(query_two, key_two, value_two, query_one, key_one, value_one),
            *(stream_three, stream_two, hidden_in[0]),
            *(w_q, w_k, w_v, w_o, w_ck, w_cv, w_cq, w_co, w_up, w_down),
        ),
        (logsum_two, logsum_one, norms),
    )
    rows, part = width // 16, query_one.shape[1]
    norm_sums = lax.dynamic_slice_in_dim(norm_sums, lax.axis_index("dp") * rows, rows, 1)
    columns = [hidden_down.shape[1]] * 2 + [part] * 8
    pieces, first = [], 0
    for count in columns:
        pieces.append(summed[:, first : first + count])
        first += count
    down, up, out_cross, query_cross, key_cross, value_cross, out_self, query, key, value = pieces
    return (
        layer_out[None],
        grad_input[None],
        grad_text[None],
        norm_sums[0],
        norm_sums[1],
        query.T,
        key.T,
        value.T,
        out_self,
        norm_sums[2],
        norm_sums[3],
        query_cross.T,
        key_cross.T,
        value_cross.T,
        out_cross,
        norm_sums[4],
        norm_sums[5],
        up.T,
        down,
    )


def solution(mesh):
    placed = (
        P("dp", "tensor", None),
        P("dp", None, None),
        P("dp"),
        P("dp"),
        P("tensor", "dp"),
        P("tensor", "dp"),
        P("tensor", "dp"),
        P("dp", "tensor"),
        P("dp"),
        P("dp"),
        P("tensor", "dp"),
        P("tensor", "dp"),
        P("tensor", "dp"),
        P("dp", "tensor"),
        P("dp"),
        P("dp"),
        P("tensor", "dp"),
        P("dp", "tensor"),
        P("dp", "tensor", None),
    )
    fast = dict(mesh.shape) == {"dp": 16, "tensor": 2}
    return jax.shard_map(
        local_fast if fast else local_generic,
        mesh=mesh,
        in_specs=placed,
        out_specs=(
            P("dp", "tensor", None),
            P("dp", "tensor", None),
            P("dp", None, "tensor"),
            P("dp"),
            P("dp"),
            P("tensor", "dp"),
            P("tensor", "dp"),
            P("tensor", "dp"),
            P("dp", "tensor"),
            P("dp"),
            P("dp"),
            P("tensor", "dp"),
            P("tensor", "dp"),
            P("tensor", "dp"),
            P("dp", "tensor"),
            P("dp"),
            P("dp"),
            P("tensor", "dp"),
            P("dp", "tensor"),
        ),
        check_vma=False,
    )
```

```python
import functools

import jax
import jax.numpy as jnp
from jax import lax
from jax.experimental import pallas as pl
from jax.experimental.pallas import tpu as pltpu
from jax.sharding import PartitionSpec as P

HEAD_DIM = 64


norm_eps = 1e-05
score_scale = 0.125


def layer_norm(values, gain, shift):
    centre = jnp.mean(values, axis=-1, keepdims=True)
    offset = values - centre
    spread = jnp.mean(offset * offset, axis=-1, keepdims=True)
    return offset * lax.rsqrt(spread + norm_eps) * gain + shift


def gelu_exact(values):
    return jax.nn.gelu(values, approximate=False)


def project(row_data, weight):
    return jnp.einsum("cli,oi->clo", row_data, weight, preferred_element_type=jnp.float32)


def split_heads(values):
    return values.reshape(values.shape[0], values.shape[1], -1, HEAD_DIM)


def flatten_heads(values):
    return values.reshape(values.shape[0], values.shape[1], -1)


def causal_keep(first_row, count, length):
    row_ids = first_row + lax.broadcasted_iota(jnp.int32, (count, length), 0)
    col_ids = lax.broadcasted_iota(jnp.int32, (count, length), 1)
    return col_ids <= row_ids


def block_scores(queries, key_rows, first_row, block_rows, key_end, causal):
    scores = (
        jnp.einsum(
            "cqhe,ckhe->chqk",
            queries[:, first_row : first_row + block_rows],
            key_rows[:, :key_end],
            preferred_element_type=jnp.float32,
        )
        * score_scale
    )
    if causal:
        scores = jnp.where(causal_keep(first_row, block_rows, key_end), scores, -1e30)
    return scores


def attend(queries, key_rows, val_rows, causal):
    length = queries.shape[1]
    block_rows = min(512, length)
    outputs = []
    log_sums = []
    for block_num in range(length // block_rows):
        first_row = block_num * block_rows
        key_end = first_row + block_rows if causal else key_rows.shape[1]
        scores = block_scores(queries, key_rows, first_row, block_rows, key_end, causal)
        row_peak = jnp.max(scores, axis=-1, keepdims=True)
        exp_scores = jnp.exp(scores - row_peak)
        row_total = jnp.sum(exp_scores, axis=-1, keepdims=True)
        soft_weights = (exp_scores / row_total).astype(jnp.bfloat16)
        outputs.append(
            jnp.einsum(
                "chqk,ckhe->cqhe",
                soft_weights,
                val_rows[:, :key_end],
                preferred_element_type=jnp.float32,
            ).astype(jnp.bfloat16)
        )
        log_sums.append((row_peak + jnp.log(row_total))[..., 0])
    return (jnp.concatenate(outputs, axis=1), jnp.concatenate(log_sums, axis=2))


def attend_back(queries, key_rows, val_rows, grad_out, log_sums, causal):
    length = queries.shape[1]
    block_rows = min(512, length)
    grad_keys = jnp.zeros(key_rows.shape, jnp.float32)
    grad_vals = jnp.zeros(val_rows.shape, jnp.float32)
    grad_queries = []
    for block_num in range(length // block_rows):
        first_row = block_num * block_rows
        key_end = first_row + block_rows if causal else key_rows.shape[1]
        query_blk = queries[:, first_row : first_row + block_rows]
        grad_blk = grad_out[:, first_row : first_row + block_rows]
        scores = block_scores(queries, key_rows, first_row, block_rows, key_end, causal)
        soft = jnp.exp(scores - log_sums[:, :, first_row : first_row + block_rows, None])
        grad_soft = jnp.einsum(
            "cqhe,ckhe->chqk", grad_blk, val_rows[:, :key_end], preferred_element_type=jnp.float32
        )
        grad_vals = grad_vals.at[:, :key_end].add(
            jnp.einsum(
                "chqk,cqhe->ckhe",
                soft.astype(jnp.bfloat16),
                grad_blk,
                preferred_element_type=jnp.float32,
            )
        )
        inner = jnp.sum(soft * grad_soft, axis=-1, keepdims=True)
        grad_scores = (soft * (grad_soft - inner)).astype(jnp.bfloat16)
        grad_queries.append(
            jnp.einsum(
                "chqk,ckhe->cqhe",
                grad_scores,
                key_rows[:, :key_end],
                preferred_element_type=jnp.float32,
            )
            * score_scale
        )
        grad_keys = grad_keys.at[:, :key_end].add(
            jnp.einsum(
                "chqk,cqhe->ckhe", grad_scores, query_blk, preferred_element_type=jnp.float32
            )
            * score_scale
        )
    return (jnp.concatenate(grad_queries, axis=1), grad_keys, grad_vals)


def gather_rows(values):
    return lax.all_gather(values, "tensor", axis=1, tiled=True)


def scatter_rows(values):
    return lax.psum_scatter(values, "tensor", scatter_dimension=1, tiled=True)


def gather_grads(values):
    return lax.all_gather(values, "tensor", axis=1, tiled=True)


def scatter_grads(values):
    return lax.psum_scatter(
        values.astype(jnp.bfloat16), "tensor", scatter_dimension=1, tiled=True
    ).astype(jnp.float32)


def heads_grads(grad_branch, attended, out_weight):
    grad_out_proj = jnp.einsum(
        "clo,cla->oa", grad_branch, flatten_heads(attended), preferred_element_type=jnp.float32
    )
    grad_attended = split_heads(
        jnp.einsum(
            "clo,oa->cla", grad_branch, out_weight, preferred_element_type=jnp.float32
        ).astype(jnp.bfloat16)
    )
    return (grad_out_proj, grad_attended)


def weight_grad(grad_rows, source_rows):
    return jnp.einsum("cla,cli->ai", grad_rows, source_rows, preferred_element_type=jnp.float32)


def input_grad(grad_rows, weight):
    return jnp.einsum("cla,ai->cli", grad_rows, weight, preferred_element_type=jnp.float32)


def local_generic(
    hidden_in,
    text_states,
    norm1_gain,
    norm1_bias,
    self_query,
    self_key,
    self_value,
    self_out,
    norm2_gain,
    norm2_bias,
    cross_query,
    cross_key,
    cross_value,
    cross_out,
    norm3_gain,
    norm3_bias,
    hidden_up,
    hidden_down,
    cotangent,
):
    full_weights = (
        lax.all_gather(norm1_gain, "dp", axis=0, tiled=True),
        lax.all_gather(norm1_bias, "dp", axis=0, tiled=True),
        lax.all_gather(self_query, "dp", axis=1, tiled=True),
        lax.all_gather(self_key, "dp", axis=1, tiled=True),
        lax.all_gather(self_value, "dp", axis=1, tiled=True),
        lax.all_gather(self_out, "dp", axis=0, tiled=True),
        lax.all_gather(norm2_gain, "dp", axis=0, tiled=True),
        lax.all_gather(norm2_bias, "dp", axis=0, tiled=True),
        lax.all_gather(cross_query, "dp", axis=1, tiled=True),
        lax.all_gather(cross_key, "dp", axis=1, tiled=True),
        lax.all_gather(cross_value, "dp", axis=1, tiled=True),
        lax.all_gather(cross_out, "dp", axis=0, tiled=True),
        lax.all_gather(norm3_gain, "dp", axis=0, tiled=True),
        lax.all_gather(norm3_bias, "dp", axis=0, tiled=True),
        lax.all_gather(hidden_up, "dp", axis=1, tiled=True),
        lax.all_gather(hidden_down, "dp", axis=0, tiled=True),
    )
    gain_self = full_weights[0].astype(jnp.float32)
    bias_self = full_weights[1].astype(jnp.float32)
    gain_cross = full_weights[6].astype(jnp.float32)
    bias_cross = full_weights[7].astype(jnp.float32)
    gain_ffn = full_weights[12].astype(jnp.float32)
    bias_ffn = full_weights[13].astype(jnp.float32)
    stream_one = hidden_in.astype(jnp.float32)
    key_two = split_heads(project(text_states, full_weights[9]).astype(jnp.bfloat16))
    value_two = split_heads(project(text_states, full_weights[10]).astype(jnp.bfloat16))
    normed_one = gather_rows(layer_norm(stream_one, gain_self, bias_self).astype(jnp.bfloat16))
    query_one = split_heads(project(normed_one, full_weights[2]).astype(jnp.bfloat16))
    key_one = split_heads(project(normed_one, full_weights[3]).astype(jnp.bfloat16))
    value_one = split_heads(project(normed_one, full_weights[4]).astype(jnp.bfloat16))
    attended_one, logsum_one = attend(query_one, key_one, value_one, True)
    stream_two = stream_one + scatter_rows(project(flatten_heads(attended_one), full_weights[5]))
    normed_two = gather_rows(layer_norm(stream_two, gain_cross, bias_cross).astype(jnp.bfloat16))
    query_two = split_heads(project(normed_two, full_weights[8]).astype(jnp.bfloat16))
    attended_two, logsum_two = attend(query_two, key_two, value_two, False)
    stream_three = stream_two + scatter_rows(project(flatten_heads(attended_two), full_weights[11]))
    normed_three = gather_rows(layer_norm(stream_three, gain_ffn, bias_ffn).astype(jnp.bfloat16))
    upper = project(normed_three, full_weights[14])
    active = gelu_exact(upper).astype(jnp.bfloat16)
    layer_out = (stream_three + scatter_rows(project(active, full_weights[15]))).astype(
        jnp.bfloat16
    )
    grad_three = cotangent.astype(jnp.float32)
    grad_branch = gather_grads(grad_three.astype(jnp.bfloat16))
    grad_down = jnp.einsum("clo,clf->of", grad_branch, active, preferred_element_type=jnp.float32)
    grad_active = jnp.einsum(
        "clo,of->clf", grad_branch, full_weights[15], preferred_element_type=jnp.float32
    )
    grad_upper = jax.vjp(gelu_exact, upper)[1](grad_active)[0].astype(jnp.bfloat16)
    grad_up = weight_grad(grad_upper, normed_three)
    norm_back = jax.vjp(layer_norm, stream_three, gain_ffn, bias_ffn)[1]
    grad_stream, grad_gain_ffn, grad_bias_ffn = norm_back(
        scatter_grads(input_grad(grad_upper, full_weights[14]))
    )
    grad_two = grad_three + grad_stream
    grad_branch = gather_grads(grad_two.astype(jnp.bfloat16))
    grad_out_cross, grad_attended = heads_grads(grad_branch, attended_two, full_weights[11])
    grad_query, grad_key, grad_value = attend_back(
        query_two, key_two, value_two, grad_attended, logsum_two, False
    )
    grad_query = flatten_heads(grad_query).astype(jnp.bfloat16)
    grad_key = flatten_heads(grad_key).astype(jnp.bfloat16)
    grad_value = flatten_heads(grad_value).astype(jnp.bfloat16)
    grad_query_cross = weight_grad(grad_query, normed_two)
    grad_key_cross = weight_grad(grad_key, text_states)
    grad_value_cross = weight_grad(grad_value, text_states)
    text_part = input_grad(grad_key, full_weights[9]) + input_grad(grad_value, full_weights[10])
    grad_text = lax.psum_scatter(
        text_part.astype(jnp.bfloat16), "tensor", scatter_dimension=2, tiled=True
    ).astype(jnp.float32)
    norm_back = jax.vjp(layer_norm, stream_two, gain_cross, bias_cross)[1]
    grad_stream, grad_gain_cross, grad_bias_cross = norm_back(
        scatter_grads(input_grad(grad_query, full_weights[8]))
    )
    grad_one = grad_two + grad_stream
    grad_branch = gather_grads(grad_one.astype(jnp.bfloat16))
    grad_out_self, grad_attended = heads_grads(grad_branch, attended_one, full_weights[5])
    grad_query, grad_key, grad_value = attend_back(
        query_one, key_one, value_one, grad_attended, logsum_one, True
    )
    grad_query = flatten_heads(grad_query).astype(jnp.bfloat16)
    grad_key = flatten_heads(grad_key).astype(jnp.bfloat16)
    grad_value = flatten_heads(grad_value).astype(jnp.bfloat16)
    grad_query_self = weight_grad(grad_query, normed_one)
    grad_key_self = weight_grad(grad_key, normed_one)
    grad_value_self = weight_grad(grad_value, normed_one)
    grad_normed = (
        input_grad(grad_query, full_weights[2])
        + input_grad(grad_key, full_weights[3])
        + input_grad(grad_value, full_weights[4])
    )
    norm_back = jax.vjp(layer_norm, stream_one, gain_self, bias_self)[1]
    grad_stream, grad_gain_self, grad_bias_self = norm_back(scatter_grads(grad_normed))
    grad_input = grad_one + grad_stream
    summed = (
        lax.psum_scatter(
            grad_gain_self.astype(jnp.bfloat16), "dp", scatter_dimension=0, tiled=True
        ).astype(jnp.float32),
        lax.psum_scatter(
            grad_bias_self.astype(jnp.bfloat16), "dp", scatter_dimension=0, tiled=True
        ).astype(jnp.float32),
        lax.psum_scatter(
            grad_query_self.astype(jnp.bfloat16), "dp", scatter_dimension=1, tiled=True
        ).astype(jnp.float32),
        lax.psum_scatter(
            grad_key_self.astype(jnp.bfloat16), "dp", scatter_dimension=1, tiled=True
        ).astype(jnp.float32),
        lax.psum_scatter(
            grad_value_self.astype(jnp.bfloat16), "dp", scatter_dimension=1, tiled=True
        ).astype(jnp.float32),
        lax.psum_scatter(
            grad_out_self.astype(jnp.bfloat16), "dp", scatter_dimension=0, tiled=True
        ).astype(jnp.float32),
        lax.psum_scatter(
            grad_gain_cross.astype(jnp.bfloat16), "dp", scatter_dimension=0, tiled=True
        ).astype(jnp.float32),
        lax.psum_scatter(
            grad_bias_cross.astype(jnp.bfloat16), "dp", scatter_dimension=0, tiled=True
        ).astype(jnp.float32),
        lax.psum_scatter(
            grad_query_cross.astype(jnp.bfloat16), "dp", scatter_dimension=1, tiled=True
        ).astype(jnp.float32),
        lax.psum_scatter(
            grad_key_cross.astype(jnp.bfloat16), "dp", scatter_dimension=1, tiled=True
        ).astype(jnp.float32),
        lax.psum_scatter(
            grad_value_cross.astype(jnp.bfloat16), "dp", scatter_dimension=1, tiled=True
        ).astype(jnp.float32),
        lax.psum_scatter(
            grad_out_cross.astype(jnp.bfloat16), "dp", scatter_dimension=0, tiled=True
        ).astype(jnp.float32),
        lax.psum_scatter(
            grad_gain_ffn.astype(jnp.bfloat16), "dp", scatter_dimension=0, tiled=True
        ).astype(jnp.float32),
        lax.psum_scatter(
            grad_bias_ffn.astype(jnp.bfloat16), "dp", scatter_dimension=0, tiled=True
        ).astype(jnp.float32),
        lax.psum_scatter(
            grad_up.astype(jnp.bfloat16), "dp", scatter_dimension=1, tiled=True
        ).astype(jnp.float32),
        lax.psum_scatter(
            grad_down.astype(jnp.bfloat16), "dp", scatter_dimension=0, tiled=True
        ).astype(jnp.float32),
    )
    norm_sums = lax.psum(
        (summed[0], summed[1], summed[6], summed[7], summed[12], summed[13]), "tensor"
    )
    return (
        layer_out,
        grad_input,
        grad_text,
        norm_sums[0],
        norm_sums[1],
        summed[2],
        summed[3],
        summed[4],
        summed[5],
        norm_sums[2],
        norm_sums[3],
        summed[8],
        summed[9],
        summed[10],
        summed[11],
        norm_sums[4],
        norm_sums[5],
        summed[14],
        summed[15],
    )


MESH_IDS = pl.DeviceIdType.MESH
BF16 = jnp.bfloat16
F32 = jnp.float32
VMEM_LIMIT = 63 * 2**20


def my_place():
    chip = lax.axis_index("dp")
    core = lax.axis_index("tensor")
    return (lax.rem(chip, 2), lax.rem(lax.div(chip, 2), 2), lax.div(chip, 4), core)


def neighbours(x, y, z, core):
    def device(zz, yy, xx):
        return (zz * 4 + yy * 2 + xx, core)

    return (device(z, y, 1 - x), device(z, 1 - y, x), device(z + 1, y, x), device(z - 1, y, x))


def when(cond, fn):
    if cond is None:
        fn()
    else:
        pl.when(cond)(fn)


def signal_neighbours(sems, near, has_up, has_down):
    for sem, device, cond in zip(sems, near, (None, None, has_up, has_down), strict=True):
        when(
            cond,
            functools.partial(
                pl.semaphore_signal, sem, inc=1, device_id=device, device_id_type=MESH_IDS
            ),
        )


def gather_engine(chunks, shards, outs, sems):
    local_sem, send_sem, zs, xs, ys, ds = sems
    x, y, z, core = my_place()
    xn, yn = 1 - x, 1 - y
    near = neighbours(x, y, z, core)
    right, across, up, down = near
    has_up, has_down = z < 3, z > 0
    barrier = pltpu.get_barrier_semaphore()
    signal_neighbours([barrier] * 4, near, has_up, has_down)
    pl.semaphore_signal(barrier, inc=1, device_id=(lax.axis_index("dp"), 1 - core), device_id_type=MESH_IDS)
    pl.semaphore_wait(barrier, 3 + has_up.astype(jnp.int32) + has_down.astype(jnp.int32))
    total = len(chunks)
    pending = []


    def span(c):
        _, first, width, _ = chunks[c]
        return pl.ds(first, width)

    def at(zz, yy, xx, c, half=None):
        ref = outs[chunks[c][0]]
        half_rows = ref.shape[3] // 2
        lines = slice(None) if half is None else pl.ds(half * half_rows, half_rows)
        return ref.at[zz, yy, xx, lines, span(c)]

    def plane(zz, c):
        return outs[chunks[c][0]].at[zz, :, :, :, span(c)]

    def own(c):
        return shards[chunks[c][0]].at[:, span(c)]

    local = [pltpu.make_async_copy(own(c), at(z, y, x, c), local_sem.at[c]) for c in range(total)]

    def remote(src, dst, sem, device):
        return pltpu.make_async_remote_copy(
            src_ref=src,
            dst_ref=dst,
            send_sem=send_sem,
            recv_sem=sem,
            device_id=device,
            device_id_type=MESH_IDS,
        )

    def send(src, dst, sem, device, cond=None):
        copy = remote(src, dst, sem, device)
        when(cond, copy.start)
        pending.append((cond, copy))

    def wait(ref, sem, cond=None):
        when(cond, remote(ref, ref, sem, right).wait_recv)

    def lines(step):
        for sign, device, more in ((-1, up, has_up), (1, down, has_down)):
            block = z + sign * step
            yield block, (block >= 0) if sign < 0 else (block <= 3), device, more

    def stage_z(c, step):
        if step == 0:
            send(own(c), at(z, y, x, c), zs.at[c, z], up, has_up)
            send(own(c), at(z, y, x, c), zs.at[c, z], down, has_down)
            send(own(c), at(z, y, x, c), xs.at[c, z], right)
            send(own(c), at(z, y, x, c), ys.at[c, z], across)
            local[c].start()
        if 1 <= step <= 3:
            for block, exists, device, more in lines(step):
                ref = at(block, y, x, c)
                wait(ref, zs.at[c, block], exists)
                if step < 3:
                    send(ref, ref, zs.at[c, block], device, exists & more)
                send(ref, ref, xs.at[c, block], right, exists)
                send(ref, ref, ys.at[c, block], across, exists)
        if 1 <= step <= 4:
            for block, exists, _, _ in [(z, None, None, None)] if step == 1 else lines(step - 1):
                wait(at(block, y, xn, c), xs.at[c, block], exists)
                ref = at(block, y, xn, c, 0)
                send(ref, ref, ds.at[c, block, 0], across, exists)
                wait(at(block, yn, x, c), ys.at[c, block], exists)
                ref = at(block, yn, x, c, 1)
                send(ref, ref, ds.at[c, block, 1], right, exists)
        if step == 5:
            for block in range(4):
                for half in range(2):
                    wait(at(block, yn, xn, c, half), ds.at[c, block, half])
            local[c].wait()

    def stage_a(c, step):
        if step == 0:
            send(own(c), at(z, y, x, c), xs.at[c, z], right)
            send(own(c), at(z, y, x, c), ys.at[c, z], across)
            local[c].start()
        if step == 1:
            wait(at(z, y, xn, c), xs.at[c, z])
            ref = at(z, y, xn, c, 0)
            send(ref, ref, ds.at[c, z, 0], across)
            wait(at(z, yn, x, c), ys.at[c, z])
            ref = at(z, yn, x, c, 1)
            send(ref, ref, ds.at[c, z, 1], right)
        if step == 2:
            for half in range(2):
                wait(at(z, yn, xn, c, half), ds.at[c, z, half])
            local[c].wait()
            send(plane(z, c), plane(z, c), zs.at[c, z], up, has_up)
            send(plane(z, c), plane(z, c), zs.at[c, z], down, has_down)
        if step >= 3:
            for block, exists, device, more in lines(step - 2):
                wait(plane(block, c), zs.at[c, block], exists)
                if step < 5:
                    send(plane(block, c), plane(block, c), zs.at[c, block], device, exists & more)

    stages = 6

    def turn(number):
        for step in range(stages):
            c = number - step
            if 0 <= c < total:
                (stage_z if chunks[c][3] == "Z" else stage_a)(c, step)

    def finish():
        for cond, copy in pending:
            when(cond, copy.wait_send)

    return turn, finish


def total_of(*parts):
    value = parts[0].astype(F32)
    for part in parts[1:]:
        value = value + part.astype(F32)
    return value


def dot_nt(left, right):
    return lax.dot_general(left, right, (((1,), (1,)), ((), ())), preferred_element_type=F32)


def dot_tn(left, right):
    return lax.dot_general(left, right, (((0,), (0,)), ((), ())), preferred_element_type=F32)


def dot_nn(left, right):
    return jnp.dot(left, right, preferred_element_type=F32)


def project_rows(source, weight, store, rows=256, transposed=False):
    def body(n, carry):
        first = pl.multiple_of(n * rows, rows)
        part = source[pl.ds(first, rows), :]
        store(first, dot_nt(part, weight[...]) if transposed else dot_nn(part, weight[...]))
        return carry

    lax.fori_loop(0, source.shape[0] // rows, body, 0)


def normalize(values, gain, shift):
    offset = values - jnp.mean(values, axis=-1, keepdims=True)
    spread = jnp.mean(offset * offset, axis=-1, keepdims=True)
    return offset * lax.rsqrt(spread + norm_eps) * gain + shift


def head_lanes(half):
    return lax.div(lax.broadcasted_iota(jnp.int32, (1, 128), 1), 64) == half


def only(mask, value):
    return jnp.where(mask, value.astype(F32), 0.0).astype(BF16)


def pair_forward(pair, q_ref, k_ref, v_ref, o_ref, lse_ref, causal):
    cols = pl.ds(pl.multiple_of(pair * 128, 128), 128)
    block = 256
    keep = lax.broadcasted_iota(jnp.int32, (block, block), 0) <= lax.broadcasted_iota(
        jnp.int32, (block, block), 1
    )
    for i in range(q_ref.shape[0] // block):
        rows = pl.ds(i * block, block)
        parts = [(0, k_ref.shape[0], False)]
        if causal:
            parts = [(0, i * block, False)] * (i > 0) + [(i * block, block, True)]
        total = 0.0
        for half in range(2):
            mine = head_lanes(half)
            q = only(mine, q_ref[rows, cols])
            scores = []
            for first, count, diagonal in parts:
                part = dot_nt(k_ref[pl.ds(first, count), cols], q) * score_scale
                scores.append(jnp.where(keep, part, -1e30) if diagonal else part)
            peak = functools.reduce(
                jnp.maximum, [jnp.max(part, axis=0, keepdims=True) for part in scores]
            )
            scores = [jnp.exp(part - peak) for part in scores]
            weight = sum(jnp.sum(part, axis=0, keepdims=True) for part in scores)
            lse_ref[pl.ds(2 * pair + half, 1), rows] = peak + jnp.log(weight)
            share = 1.0 / weight
            for (first, count, _), part in zip(parts, scores, strict=True):
                v = only(mine, v_ref[pl.ds(first, count), cols])
                total = total + dot_tn((part * share).astype(BF16), v)
        o_ref[rows, cols] = total.astype(BF16)


def forward_kernel(chunks, count, *refs):
    shards, refs = refs[:count], refs[count:]
    hidden_h, text_h, cotangent_h, refs = refs[0], refs[1], refs[2], refs[3:]
    outs, refs = refs[:count], refs[count:]
    results, refs = refs[:19], refs[19:]
    sems, refs = refs[:6], refs[6:]
    (h1, h2, h3, q1, k1, v1, o1, q2, k2, v2, o2, lse1, lse2, x2, x3), refs = refs[:15], refs[15:]
    gathered_norms, norms, weights, hidden, text, mine, theirs, arrived, active, slopes, x2_parts = refs[:11]
    norm_sem, weight_sem, load_sem, share_send, share_recv, result_sem = refs[11:]
    names = dict(norms=0, q=1, k=2, v=3, o=4, ck=5, cv=6, cq=7, co=8, up=9, down=10)
    turn, finish = gather_engine(chunks, shards, outs, sems)
    chip, core = lax.axis_index("dp"), lax.axis_index("tensor")
    frames, width = h1.shape
    half = frames // 2
    own = pl.ds(pl.multiple_of(core * half, half), half)
    loads = [
        pltpu.make_async_copy(hidden_h, hidden, load_sem.at[0]),
        pltpu.make_async_copy(text_h, text, load_sem.at[1]),
        pltpu.make_async_copy(cotangent_h, theirs.at[1], load_sem.at[2]),
    ]
    for copy in loads:
        copy.start()
    pending = []

    def weight_copy(name, slot, first=0):
        return [
            pltpu.make_async_copy(
                outs[names[name]].at[zz, yy, xx, :, pl.ds(first, weights.shape[2])],
                weights.at[slot, pl.ds(((zz * 2 + yy) * 2 + xx) * rows, rows), :],
                weight_sem.at[slot, (zz * 2 + yy) * 2 + xx],
            )
            for zz in range(4)
            for yy in range(2)
            for xx in range(2)
        ]

    rows = width // 16

    def load_weight(name, slot, first=0):
        for copy in weight_copy(name, slot, first):
            copy.start()

    def wait_weight(slot):
        for copy in weight_copy("q", slot):
            copy.wait()

    def share(n, src, dst):
        return pltpu.make_async_remote_copy(
            src_ref=src,
            dst_ref=dst,
            send_sem=share_send.at[n],
            recv_sem=share_recv.at[n],
            device_id=(chip, 1 - core),
            device_id_type=MESH_IDS,
        )

    def give(n, ref):
        copy = pltpu.make_async_copy(ref, results[n], result_sem.at[n])
        copy.start()
        pending.append(copy)

    def norm_share(n, values, kind, h):
        step = 64

        def body(i, carry):
            first = pl.multiple_of(i * step, step)
            h[pl.ds(pl.multiple_of(core * half + first, step), step), :] = normalize(
                values(first, step), norms[2 * kind : 2 * kind + 1], norms[2 * kind + 1 : 2 * kind + 2]
            ).astype(BF16)
            return carry

        lax.fori_loop(0, half // step, body, 0)
        share(n, h.at[own], h.at[own]).start()

    def get_share(n, h):
        share(n, h.at[own], h.at[own]).wait()

    def to(ref):
        def store(first, value):
            ref[pl.ds(first, value.shape[0]), :] = value.astype(BF16)

        return store

    def out_project(n, o, slot):
        step = 256
        for whose, ref in ((1 - core, theirs.at[n]), (core, mine)):
            for first in range(0, half, step):
                part = o[pl.ds(pl.multiple_of(whose * half + first, step), step), :]
                ref[pl.ds(first, step), :] = dot_nt(part, weights[slot]).astype(ref.dtype)
            if whose is not core:
                share(3 + n, theirs.at[n], arrived.at[n]).start()

    def add_stream(n, before, after, parts=None):
        def values(first, step):
            lines = pl.ds(first, step)
            total = before[lines, :].astype(F32) + (mine[lines, :] + arrived[n, lines, :].astype(F32))
            after[lines, :] = total
            if parts is not None:
                high = total.astype(BF16)
                parts[lines, :] = high
                low = total - high.astype(F32)
                parts[pl.ds(pl.multiple_of(half + first, step), step), :] = low.astype(BF16)
            return total

        return values

    branch = results[16].at[own]
    branch_copy = pltpu.make_async_copy(theirs.at[1], branch, result_sem.at[16])

    def active_copies(j):
        lanes = pl.ds(j * active.shape[1], active.shape[1])
        return (
            pltpu.make_async_copy(active, results[17].at[:, lanes], result_sem.at[17]),
            pltpu.make_async_copy(slopes, results[18].at[:, lanes], result_sem.at[18]),
        )

    def hidden_units(j):
        wait_weight(j % 2)
        if j < 3:
            load_weight("up", (j + 1) % 2, (j + 1) * active.shape[1])
        if j:
            for copy in active_copies(j - 1):
                copy.wait()

        def store(first, value):
            lines = pl.ds(first, value.shape[0])
            below = 0.5 * (1.0 + lax.erf(value * (0.5**0.5)))
            density = jnp.exp(-0.5 * value * value) * 0.3989422804014327
            active[lines, :] = (value * below).astype(BF16)
            slopes[lines, :] = (below + value * density).astype(BF16)

        project_rows(h3, weights.at[j % 2], store)
        for copy in active_copies(j):
            copy.start()

    def work(number):
        if number == 5:
            copy = pltpu.make_async_copy(outs[0], gathered_norms, norm_sem)
            copy.start()
            copy.wait()
            for copy in loads:
                copy.wait()
            share(5, theirs.at[1], branch).start()
            branch_copy.start()
            total = 0.0
            lane = lax.broadcasted_iota(jnp.int32, (128, width), 0)
            place = lax.broadcasted_iota(jnp.int32, (128, width), 1)
            for n in range(16):
                pick = (place == lane + n * rows) & (lane < rows)
                total = total + dot_nn(
                    gathered_norms[n // 4, n // 2 % 2, n % 2],
                    jnp.where(pick, 1.0, 0.0).astype(BF16),
                )
            norms[...] = total
            give(13, norms)
            norm_share(0, lambda first, step: hidden[pl.ds(first, step), :].astype(F32), 0, h1)
        if number == 6:
            load_weight("q", 0)
            get_share(0, h1)
            give(0, h1)
            wait_weight(0)
            project_rows(h1, weights.at[0], to(q1))
            give(3, q1)
        if number == 7:
            load_weight("k", 1)
            wait_weight(1)
            project_rows(h1, weights.at[1], to(k1))
            give(4, k1)
        if number == 8:
            load_weight("v", 0)
            wait_weight(0)
            project_rows(h1, weights.at[0], to(v1))
            give(5, v1)
        if number in (9, 10, 11):
            if number == 9:
                load_weight("o", 1)
            pairs = q1.shape[1] // 128
            first = pairs * (number - 9) // 3
            last = pairs * (number - 8) // 3

            def body(pair, carry):
                pair_forward(pair, q1, k1, v1, o1, lse1, True)
                return carry

            lax.fori_loop(first, last, body, 0)
            if number == 11:
                load_weight("cv", 0)
        if number == 12:
            share(5, theirs.at[1], branch).wait()
            branch_copy.wait()
            give(6, o1)
            give(11, lse1)
            wait_weight(1)
            out_project(0, o1, 1)
            load_weight("ck", 1)
            wait_weight(0)
            v2[...] = dot_nn(text[...], weights[0]).astype(BF16)
            give(9, v2)
            load_weight("cq", 0)
        if number == 13:
            share(3, theirs.at[0], arrived.at[0]).wait()
            norm_share(1, add_stream(0, hidden, x2, x2_parts), 1, h2)
            give(14, x2_parts)
            wait_weight(1)
            k2[...] = dot_nn(text[...], weights[1]).astype(BF16)
            give(8, k2)
            load_weight("co", 1)
        if number == 14:
            get_share(1, h2)
            give(1, h2)
            wait_weight(0)
            project_rows(h2, weights.at[0], to(q2))
            give(7, q2)
        if number == 15:

            def body(pair, carry):
                pair_forward(pair, q2, k2, v2, o2, lse2, False)
                return carry

            lax.fori_loop(0, q2.shape[1] // 128, body, 0)
            give(10, o2)
            give(12, lse2)
        if number == 16:
            wait_weight(1)
            out_project(1, o2, 1)
        if number == 17:
            share(4, theirs.at[1], arrived.at[1]).wait()
            norm_share(2, add_stream(1, x2, x3), 2, h3)
            give(15, x3)
            load_weight("up", 0)
        if number == 18:
            get_share(2, h3)
            give(2, h3)
        if 18 <= number < 22:
            hidden_units(number - 18)

    for number in range(len(chunks) + 5):
        turn(number)
        work(number)
    finish()
    for copy in (*pending, *active_copies(3)):
        copy.wait()


def forward_all(shards, chunks, hidden, text, cotangent):
    total, count = len(chunks), len(shards)
    dma, vmem = pltpu.SemaphoreType.DMA, pltpu.VMEM
    half, width = hidden.shape
    frames, part = 2 * half, shards[1].shape[1]
    anywhere = pl.BlockSpec(memory_space=pl.ANY)
    shape = jax.ShapeDtypeStruct
    kept = [
        *[((frames, width), BF16)] * 3,
        *[((frames, part), BF16)] * 4,
        ((frames, part), BF16),
        *[((text.shape[0], part), BF16)] * 2,
        ((frames, part), BF16),
        *[((16, frames), F32)] * 2,
    ]
    given = [*kept, ((shards[0].shape[0], width), F32), ((frames, width), BF16), ((half, width), F32)]
    given += [((frames, width), BF16), ((frames, 4 * part), BF16), ((frames, 4 * part), BF16)]
    held = [*kept, ((half, width), F32), ((half, width), F32)]
    outs = pl.pallas_call(
        functools.partial(forward_kernel, chunks, count),
        out_shape=[shape((4, 2, 2) + s.shape, s.dtype) for s in shards] + [shape(*g) for g in given],
        in_specs=[pl.BlockSpec(memory_space=vmem)] * count + [anywhere] * 3,
        out_specs=[anywhere] * (count + len(given)),
        scratch_shapes=[
            dma((total,)),
            dma,
            dma((total, 4)),
            dma((total, 4)),
            dma((total, 4)),
            dma((total, 4, 2)),
            *[vmem(*h) for h in held],
            vmem((4, 2, 2) + shards[0].shape, BF16),
            vmem((shards[0].shape[0], width), F32),
            vmem((2, width, part), BF16),
            vmem((half, width), BF16),
            vmem(text.shape, BF16),
            vmem((half, width), F32),
            vmem((2, half, width), BF16),
            vmem((2, half, width), BF16),
            vmem((frames, part), BF16),
            vmem((frames, part), BF16),
            vmem((frames, width), BF16),
            dma,
            dma((2, 16)),
            dma((3,)),
            dma((6,)),
            dma((6,)),
            dma((19,)),
        ],
        compiler_params=pltpu.CompilerParams(
            collective_id=0, has_side_effects=True, vmem_limit_bytes=VMEM_LIMIT
        ),
        name="forward",
    )(*shards, hidden, text, cotangent)
    return outs[:count], outs[count:]


XD, YD, XA, YA, XB, YB, UP, DOWN = range(8)


UNIT = 256
WIDTH_Z, WIDTH_A, SLOTS = 384, 128, 7
ROWS_L = 6
FIRST_L = (0, 12, 24, 27, 36, 39)
LOAD_L = ((2, 11), (3, 11), (4, 14), (5, 15))
FIRST_R = ((0, 12), (12, 24), (24, 27), (27, 30), (36, 39))
TEXT_UNITS = (30, 36)
SELF_UNITS = (39, 48)
UNITS = 48


def head_back(head, q_ref, k_ref, v_ref, do_ref, lse_ref, dq_ref, dkv_ref, bases, acc_k, acc_v, causal):
    pair, half = lax.div(head, 2), lax.rem(head, 2)
    cols = pl.ds(pl.multiple_of(pair * 128, 128), 128)
    lanes = [pl.ds(pl.multiple_of(pair * 128 + base, 128), 128) for base in bases]
    mine = head_lanes(half)
    length = k_ref.shape[0]
    acc_k[pl.ds(0, length), :] = jnp.zeros((length, 128), F32)
    acc_v[pl.ds(0, length), :] = jnp.zeros((length, 128), F32)
    block = 256 if causal else q_ref.shape[0]
    if causal:
        keep = lax.broadcasted_iota(jnp.int32, (block, block), 0) <= lax.broadcasted_iota(
            jnp.int32, (block, block), 1
        )

    def merged(ref, rows, lane, value):
        before = jnp.where(half == 0, 0.0, ref[rows, lane].astype(F32))
        ref[rows, lane] = (before + value).astype(BF16)

    for i in range(q_ref.shape[0] // block):
        rows = pl.ds(i * block, block)
        q = only(mine, q_ref[rows, cols])
        do = only(mine, do_ref[rows, cols])
        lse = lse_ref[pl.ds(head, 1), rows]
        parts = [(0, length, False)]
        if causal:
            parts = [(0, i * block, False)] * (i > 0) + [(i * block, block, True)]
        held, inner = [], 0.0
        for first, count, diagonal in parts:
            keys = pl.ds(first, count)
            soft = jnp.exp(dot_nt(k_ref[keys, cols], q) * score_scale - lse)
            if diagonal:
                soft = jnp.where(keep, soft, 0.0)
            slope = dot_nt(v_ref[keys, cols], do)
            inner = inner + jnp.sum(soft * slope, axis=0, keepdims=True)
            held.append((keys, soft, slope))
        grad_q = 0.0
        for keys, soft, slope in held:
            ds = (soft * (slope - inner)).astype(BF16)
            acc_v[keys, :] += dot_nn(soft.astype(BF16), do)
            acc_k[keys, :] += dot_nn(ds, q)
            grad_q = grad_q + dot_tn(ds, k_ref[keys, cols])
        merged(dq_ref, rows, lanes[0], jnp.where(mine, grad_q * score_scale, 0.0))
    everything = pl.ds(0, length)
    merged(dkv_ref, everything, lanes[1], acc_k[everything, :] * score_scale)
    merged(dkv_ref, everything, lanes[2], acc_v[everything, :])


def backward_kernel(*refs):
    (e3_h, h3_h, h2_h, h1_h, a_h, slope_h, o2_h, o1_h, text_h), refs = refs[:9], refs[9:]
    (q2_h, k2_h, v2_h, q1_h, k1_h, v1_h, x3_h, x2_h, x1_h), refs = refs[:9], refs[9:]
    (w_q, w_k, w_v, w_o, w_ck, w_cv, w_cq, w_co, w_up, w_down), refs = refs[:10], refs[10:]
    (lse2_ref, lse1_ref, norms), refs = refs[:3], refs[3:]
    (out, layer_out, grad_input, grad_text, norm_out), refs = refs[:5], refs[5:]
    (du_h, dq2_h, e2_h, e1_h), refs = refs[:4], refs[4:]
    (gz, ga, xdz, ydz, xaz, yaz, xbz, ybz, lnz), refs = refs[:9], refs[9:]
    (xda, yda, xaa, yaa, xba, yba, lna, oz, oa), refs = refs[:9], refs[9:]
    (lbuf, rbuf, text_v, dkv_v, k2_v, v2_v, pool, dqkv, acc_k, acc_v), refs = refs[:10], refs[10:]
    (acc, grad, theirs, arrived, weights, text_part, text_send, text_got), refs = refs[:8], refs[8:]
    (norm_grads, got), refs = refs[:2], refs[2:]
    (first_sem, l_sem, r_sem, out_sem, send_z, send_a, recv_z, recv_a), refs = refs[:8], refs[8:]
    (pool_sem, slope_sem, weight_sem, x_sem, keep_sem, share_send, share_recv, norm_send), refs = refs[:8], refs[8:]
    norm_recv, credit = refs
    lefts = (e3_h, h3_h, e2_h, h2_h, e1_h, h1_h)
    rights = (a_h, du_h, o2_h, dq2_h, o1_h)
    width_z, width_a, slots = WIDTH_Z, WIDTH_A, SLOTS
    total, width = UNITS // 2, WIDTH_Z + WIDTH_A
    x, y, z, core = my_place()
    xn, yn = 1 - x, 1 - y
    near = neighbours(x, y, z, core)
    right, across, up, down = near
    has_up, has_down = z < 3, z > 0
    degree = 2 + has_up.astype(jnp.int32) + has_down.astype(jnp.int32)
    chip = lax.axis_index("dp")
    other = (chip, 1 - core)
    partners = [other]
    for bit in (1, 2, 4, 8):
        partners.append((chip + bit * (1 - 2 * lax.rem(lax.div(chip, bit), 2)), core))
    barrier = pltpu.get_barrier_semaphore()
    signal_neighbours([barrier] * 4, near, has_up, has_down)
    for device in (other, partners[4]):
        pl.semaphore_signal(barrier, inc=1, device_id=device, device_id_type=MESH_IDS)
    pl.semaphore_wait(barrier, degree + 2)
    rows = gz.shape[4]
    low, high = pl.ds(0, rows // 2), pl.ds(rows // 2, rows // 2)

    def remote(src, dst, send_sem, recv_sem, device):
        return pltpu.make_async_remote_copy(
            src_ref=src,
            dst_ref=dst,
            send_sem=send_sem,
            recv_sem=recv_sem,
            device_id=device,
            device_id_type=MESH_IDS,
        )

    def arrived_at(ref, sem):
        remote(ref, ref, send_z.at[0], sem, right).wait_recv()

    def sent(ref, sem):
        remote(ref, ref, sem, recv_z.at[0, 0], right).wait_send()

    firsts = [
        pltpu.make_async_copy(src, dst, first_sem.at[n])
        for n, (src, dst) in enumerate(((text_h, text_v), (k2_h, k2_v), (v2_h, v2_v)))
    ]

    def left_copy(n):
        return pltpu.make_async_copy(lefts[n], lbuf.at[n % 2], l_sem.at[n % 2])

    def right_copies(c, which):
        unit = 2 * c + which
        place, sem = rbuf.at[lax.rem(c, 2), which], r_sem.at[lax.rem(c, 2), which]
        for source, (lo, hi) in zip((*rights, dqkv), (*FIRST_R, SELF_UNITS), strict=True):
            first = pl.multiple_of((unit - lo) * UNIT, UNIT)
            yield (
                (unit >= lo) & (unit < hi),
                pltpu.make_async_copy(source.at[:, pl.ds(first, UNIT)], place, sem),
            )

    def start_rights(c):
        for which in range(2):
            for cond, copy in right_copies(c, which):
                pl.when(cond)(copy.start)

    def store_unit(which, k, i, value):
        for yy in range(2):
            for xx in range(2):
                first = (yy * 2 + xx) * rows
                block = value[first : first + rows, :].astype(BF16)
                if which == 0:
                    gz[k, i, yy, xx, :, pl.ds(0, UNIT)] = block
                else:
                    gz[k, i, yy, xx, :, pl.ds(UNIT, width_z - UNIT)] = block[:, : width_z - UNIT]
                    ga[k, i, yy, xx] = block[:, width_z - UNIT :]

    def compute(c, k):
        for n in range(1, ROWS_L):
            pl.when(c == FIRST_L[n] // 2)(left_copy(n).wait)
        for which in range(2):
            unit = 2 * c + which
            text = (unit >= TEXT_UNITS[0]) & (unit < TEXT_UNITS[1])
            slot = lax.rem(sum((unit >= first).astype(jnp.int32) for first in FIRST_L) + 1, 2)

            @pl.when(text)
            def _():
                first = pl.multiple_of((unit - TEXT_UNITS[0]) * UNIT, UNIT)
                right_part = dkv_v[:, pl.ds(first, UNIT)]
                for i in range(4):
                    store_unit(which, k, i, dot_tn(text_v[:, pl.ds(i * 4 * rows, 4 * rows)], right_part))

            @pl.when(jnp.logical_not(text))
            def _():
                par = lax.rem(c, 2)
                pltpu.make_async_copy(rbuf.at[par, which], rbuf.at[par, which], r_sem.at[par, which]).wait()
                right_part = rbuf[par, which]
                for i in range(4):
                    left_part = lbuf[slot, :, pl.ds(i * 4 * rows, 4 * rows)]
                    store_unit(which, k, i, dot_tn(left_part, right_part))

        for n, at in LOAD_L:
            pl.when(c == at)(left_copy(n).start)
        pl.when(c + 1 < total)(lambda: start_rights(c + 1))

    def out_copies(c):
        o = lax.rem(c, 2)
        first = pl.multiple_of(c * width, 128)
        return (
            pltpu.make_async_copy(oz.at[o], out.at[:, pl.ds(first, width_z)], out_sem.at[o, 0]),
            pltpu.make_async_copy(
                oa.at[o], out.at[:, pl.ds(first + width_z, width_a)], out_sem.at[o, 1]
            ),
        )

    def plane_first(own, k, bufs, send_sem, recv):
        xd, yd, xa, ya = bufs
        remote(own(yn, xn, low), xd.at[k], send_sem.at[k], recv.at[k, XD], right).start()
        remote(own(yn, xn, high), yd.at[k], send_sem.at[k], recv.at[k, YD], across).start()
        remote(own(y, xn, low), xa.at[k], send_sem.at[k], recv.at[k, XA], right).start()
        remote(own(yn, x, high), ya.at[k], send_sem.at[k], recv.at[k, YA], across).start()

    def plane_second(add, k, bufs, send_sem, recv):
        xd, yd, xb, yb = bufs
        arrived_at(xd.at[k], recv.at[k, XD])
        add(xd, yn, x, low)
        remote(xd.at[k], yb.at[k], send_sem.at[k], recv.at[k, YB], across).start()
        arrived_at(yd.at[k], recv.at[k, YD])
        add(yd, y, xn, high)
        remote(yd.at[k], xb.at[k], send_sem.at[k], recv.at[k, XB], right).start()

    def above(buf, k, first, blocks):
        return buf.at[k, pl.ds(first + 1, blocks)]

    def below(buf, k, blocks):
        return buf.at[k, pl.ds(0, blocks)]

    def line_up(first, buf, add, k, send_sem, recv):
        blocks = 4 - first
        arrived_at(above(buf, k, first, blocks), recv.at[k, UP])
        if blocks > 1:
            for block in range(first + 1, 4):
                add(buf, block, block + 1)
            ref = above(buf, k, first + 1, blocks - 1)
            remote(ref, ref, send_sem.at[k], recv.at[k, UP], up).start()

    def line_down(last, buf, add, k, send_sem, recv):
        arrived_at(below(buf, k, last + 1), recv.at[k, DOWN])
        if last > 0:
            for block in range(last):
                add(buf, block, block)
            ref = below(buf, k, last)
            remote(ref, ref, send_sem.at[k], recv.at[k, DOWN], down).start()

    def add_a(k):
        def add(buf, block, at):
            for yy in range(2):
                for xx in range(2):
                    buf[k, at, yy, xx] = total_of(
                        buf[k, at, yy, xx], ga[k, block, yy, xx]
                    ).astype(BF16)

        return add

    def add_z(k):
        def add(buf, block, at):
            buf[k, at] = total_of(buf[k, at], gz[k, block, y, x]).astype(BF16)

        return add

    def begin(c, k):
        @pl.when(c >= slots)
        def _():
            pl.semaphore_wait(credit.at[0], 1)
            pl.semaphore_wait(credit.at[1], 1)
            pl.when(has_up)(lambda: pl.semaphore_wait(credit.at[2], 1))
            pl.when(has_down)(lambda: pl.semaphore_wait(credit.at[3], 1))

        plane_first(
            lambda yy, xx, half: gz.at[k, :, yy, xx, half, :], k, (xdz, ydz, xaz, yaz), send_z, recv_z
        )

        @pl.when(z == 0)
        def _():
            ref = pl.ds(1, 3)
            remote(ga.at[k, ref], above(lna, k, 1, 3), send_a.at[k], recv_a.at[k, UP], up).start()

        @pl.when(z == 3)
        def _():
            ref = pl.ds(0, 3)
            remote(ga.at[k, ref], below(lna, k, 3), send_a.at[k], recv_a.at[k, DOWN], down).start()

    def second(c, k):
        def add(buf, yy, xx, half):
            for block in range(4):
                buf[k, block] = total_of(buf[k, block], gz[k, block, yy, xx, half, :]).astype(BF16)

        plane_second(add, k, (xdz, ydz, xbz, ybz), send_z, recv_z)
        pl.when(z == 1)(lambda: line_up(1, lna, add_a(k), k, send_a, recv_a))
        pl.when(z == 2)(lambda: line_down(2, lna, add_a(k), k, send_a, recv_a))

    def third(c, k):
        for buf, kind in ((xaz, XA), (yaz, YA), (xbz, XB), (ybz, YB)):
            arrived_at(buf.at[k], recv_z.at[k, kind])
        for block in range(4):
            for half, one, two in ((low, xaz, ybz), (high, yaz, xbz)):
                gz[k, block, y, x, half, :] = total_of(
                    gz[k, block, y, x, half, :], one[k, block], two[k, block]
                ).astype(BF16)

        @pl.when(z == 0)
        def _():
            ref = pl.ds(1, 3)
            remote(
                gz.at[k, ref, y, x], above(lnz, k, 1, 3), send_z.at[k], recv_z.at[k, UP], up
            ).start()

        @pl.when(z == 3)
        def _():
            ref = pl.ds(0, 3)
            remote(
                gz.at[k, ref, y, x], below(lnz, k, 3), send_z.at[k], recv_z.at[k, DOWN], down
            ).start()

        pl.when(z == 2)(lambda: line_up(2, lna, add_a(k), k, send_a, recv_a))
        pl.when(z == 1)(lambda: line_down(1, lna, add_a(k), k, send_a, recv_a))

    def fourth(c, k):
        pl.when(z == 1)(lambda: line_up(1, lnz, add_z(k), k, send_z, recv_z))
        pl.when(z == 2)(lambda: line_down(2, lnz, add_z(k), k, send_z, recv_z))
        pl.when(z == 3)(lambda: line_up(3, lna, None, k, send_a, recv_a))
        pl.when(z == 0)(lambda: line_down(0, lna, None, k, send_a, recv_a))
        for shift, exists in ((1, has_down), (0, has_up)):

            @pl.when(exists)
            def _():
                for yy in range(2):
                    for xx in range(2):
                        ga[k, z, yy, xx] = total_of(
                            ga[k, z, yy, xx], lna[k, z + shift, yy, xx]
                        ).astype(BF16)

        plane_first(
            lambda yy, xx, half: ga.at[k, z, yy, xx, half, :], k, (xda, yda, xaa, yaa), send_a, recv_a
        )

    def fifth(c, k):
        pl.when(z == 2)(lambda: line_up(2, lnz, add_z(k), k, send_z, recv_z))
        pl.when(z == 1)(lambda: line_down(1, lnz, add_z(k), k, send_z, recv_z))

        def add(buf, yy, xx, half):
            buf[k] = total_of(buf[k], ga[k, z, yy, xx, half, :]).astype(BF16)

        plane_second(add, k, (xda, yda, xba, yba), send_a, recv_a)

    def finish(c, k):
        pl.when(z == 3)(lambda: line_up(3, lnz, None, k, send_z, recv_z))
        pl.when(z == 0)(lambda: line_down(0, lnz, None, k, send_z, recv_z))
        o = lax.rem(c, 2)

        @pl.when(c >= 2)
        def _():
            for copy in out_copies(c - 2):
                copy.wait()

        oz[o] = gz[k, z, y, x].astype(F32)
        for shift, exists in ((1, has_down), (0, has_up)):

            @pl.when(exists)
            def _():
                oz[o] = oz[o] + lnz[k, z + shift].astype(F32)

        for buf, kind in ((xaa, XA), (yaa, YA), (xba, XB), (yba, YB)):
            arrived_at(buf.at[k], recv_a.at[k, kind])
        oa[o, low, :] = total_of(ga[k, z, y, x, low, :], xaa[k], yba[k])
        oa[o, high, :] = total_of(ga[k, z, y, x, high, :], yaa[k], xba[k])
        for copy in out_copies(c):
            copy.start()
        for buf in (xdz, ydz, xaz, yaz, xbz, ybz):
            sent(buf.at[k], send_z.at[k])
        for buf in (xda, yda, xaa, yaa, xba, yba):
            sent(buf.at[k], send_a.at[k])
        for step in range(3):

            @pl.when(z == step)
            def _():
                sent(above(lnz, k, step + 1, 3 - step), send_z.at[k])
                sent(above(lna, k, step + 1, 3 - step), send_a.at[k])

            @pl.when(z == 3 - step)
            def _():
                sent(below(lnz, k, 3 - step), send_z.at[k])
                sent(below(lna, k, 3 - step), send_a.at[k])

        @pl.when(c < total - slots)
        def _():
            signal_neighbours([credit.at[i] for i in (0, 1, 3, 2)], near, has_up, has_down)

    frames, features = e3_h.shape
    part, half_rows = pool.shape[2], frames // 2
    heads = part // HEAD_DIM
    own_rows = pl.ds(pl.multiple_of(core * half_rows, half_rows), half_rows)
    wide = pl.ds(0, features)
    slope = dqkv.at[:, pl.ds(features, part)]
    block = 256

    def columns(n):
        return pl.ds(pl.multiple_of(n * part, part), part)

    def weight_copy(slot, ref, n=0):
        return pltpu.make_async_copy(ref.at[:, columns(n)], weights.at[slot], weight_sem.at[slot])

    def use(slot):
        weight_copy(slot, w_q).wait()

    def pool_copy(n, ref, m=0):
        return pltpu.make_async_copy(ref.at[:, columns(m)], pool.at[n], pool_sem.at[n])

    def slope_copy(n):
        return pltpu.make_async_copy(slope_h.at[:, columns(n)], slope, slope_sem)

    def keep_copy(n, src, dst):
        return pltpu.make_async_copy(src, dst, keep_sem.at[n])

    def du_copy(n):
        return keep_copy(0, pool.at[n], du_h.at[:, columns(n)])

    def to_other(n, src, dst):
        return remote(src, dst, share_send.at[n], share_recv.at[n], other)

    def active_copy(whose, n):
        lines = pl.ds(pl.multiple_of(whose * half_rows, half_rows), half_rows)
        return keep_copy(0, a_h.at[lines, pl.ds(n * 2 * part, 2 * part)], theirs)

    def share_sum(n):
        return to_other(n, theirs, arrived.at[n % 2])

    def share_branch(n):
        ref = dqkv.at[own_rows, wide]
        return to_other(4 + n, ref, ref)

    def multiply(whose, source, slot, fresh):
        for first in range(0, half_rows, block):
            rows_of = pl.ds(pl.multiple_of(whose * half_rows + first, block), block)
            value = dot_nt(source(rows_of), weights[slot])
            lines = pl.ds(first, block)
            acc[lines, :] = value if fresh else acc[lines, :] + value

    def pooled(n):
        return lambda rows_of: pool[n, rows_of, :]

    def headed(n):
        return lambda rows_of: dqkv[rows_of, pl.ds(n * part, part)]

    def send_sum(n):
        for first in range(0, half_rows, block):
            lines = pl.ds(first, block)
            theirs[lines, :] = acc[lines, :].astype(BF16)
        share_sum(n).start()

    def norm_back(kind, n, load, before, store):
        step = 64
        gain = norms[2 * kind : 2 * kind + 1, :]

        def body(i, sums):
            first = pl.multiple_of(i * step, step)
            lines = pl.ds(first, step)
            value = load(i, lines)
            offset = value - jnp.mean(value, axis=-1, keepdims=True)
            scale = lax.rsqrt(jnp.mean(offset * offset, axis=-1, keepdims=True) + norm_eps)
            unit = offset * scale
            slope_in = acc[lines, :] + arrived[n % 2, lines, :].astype(F32)
            scaled = slope_in * gain
            inner = jnp.mean(scaled * unit, axis=-1, keepdims=True)
            change = scale * (scaled - jnp.mean(scaled, axis=-1, keepdims=True) - unit * inner)
            store(first, lines, before(first, lines) + change)
            return (
                sums[0] + jnp.sum(slope_in * unit, axis=0, keepdims=True),
                sums[1] + jnp.sum(slope_in, axis=0, keepdims=True),
            )

        zero = jnp.zeros((1, features), F32)
        gains, shifts = lax.fori_loop(0, half_rows // step, body, (zero, zero))
        norm_grads[2 * kind : 2 * kind + 1, :] = gains
        norm_grads[2 * kind + 1 : 2 * kind + 2, :] = shifts

    x2_copy = pltpu.make_async_copy(x2_h, lbuf.at[0], x_sem)

    def store_branch(first, lines, value):
        grad[lines, :] = value
        dqkv[pl.ds(pl.multiple_of(core * half_rows + first, 64), 64), wide] = value.astype(BF16)

    def project_to(n, slot):
        for first in range(0, frames, block):
            lines = pl.ds(first, block)
            pool[n, lines, :] = dot_nn(dqkv[lines, wide], weights[slot]).astype(BF16)

    def feed_forward(j):
        use(0)
        slope_copy(j).wait()
        for first in range(0, frames, block):
            lines = pl.ds(first, block)
            value = dot_nn(lbuf[0, lines, :], weights[0])
            pool[j, lines, :] = (
                value * dqkv[lines, pl.ds(features, part)].astype(F32)
            ).astype(BF16)

        @pl.when(j > 0)
        def _():
            du_copy(j - 1).wait()

        du_copy(j).start()

        @pl.when(j < 3)
        def _():
            weight_copy(0, w_down, j + 1).start()
            slope_copy(j + 1).start()

        pl.when(j == 3)(lambda: weight_copy(0, w_up, 0).start())
        use(1)
        multiply(1 - core, pooled(j), 1, False)
        pl.when(j < 3)(lambda: weight_copy(1, w_up, j + 1).start())
        pl.when(j == 3)(lambda: send_sum(0))

    def turn_4():
        du_copy(3).wait()
        keep_copy(3, x3_h, grad).start()
        multiply(core, pooled(3), 1, True)
        weight_copy(1, w_up, 1).start()
        use(0)
        multiply(core, pooled(0), 0, False)
        weight_copy(0, w_up, 2).start()

    def turn_5():
        use(1)
        multiply(core, pooled(1), 1, False)
        weight_copy(1, w_cq).start()
        use(0)
        multiply(core, pooled(2), 0, False)
        weight_copy(0, w_co).start()

    def turn_6():
        pool_copy(0, q2_h).start()
        share_sum(0).wait()
        keep_copy(3, x3_h, grad).wait()
        norm_back(
            2,
            0,
            lambda i, lines: grad[lines, :],
            lambda first, lines: lbuf[
                0, pl.ds(pl.multiple_of(core * half_rows + first, 64), 64), :
            ].astype(F32),
            store_branch,
        )
        share_branch(0).start()

    def turn_7():
        share_branch(0).wait()
        x2_copy.start()
        keep_copy(1, dqkv.at[:, wide], e2_h).start()
        use(0)
        project_to(1, 0)
        weight_copy(0, w_ck).start()

    def turn_8():
        pool_copy(0, q2_h).wait()
        for copy in firsts:
            copy.wait()

        def body(head, carry):
            head_back(
                head,
                pool.at[0],
                k2_v,
                v2_v,
                pool.at[1],
                lse2_ref,
                pool.at[2],
                dkv_v,
                (0, 0, part),
                acc_k,
                acc_v,
                False,
            )
            return carry

        lax.fori_loop(0, heads, body, 0, unroll=2)
        keep_copy(1, dqkv.at[:, wide], e2_h).wait()
        keep_copy(0, pool.at[2], dq2_h).start()
        use(0)
        text_part[...] = dot_nt(dkv_v[:, pl.ds(0, part)], weights[0])
        weight_copy(0, w_cv).start()

    def text_columns(whose):
        count = features // 2
        return pl.ds(pl.multiple_of(whose * count, count), count)

    def text_share():
        return to_other(6, text_send, text_got)

    def turn_9():
        keep_copy(0, pool.at[2], dq2_h).wait()
        use(0)
        text_part[...] += dot_nt(dkv_v[:, pl.ds(part, part)], weights[0])
        text_send[...] = text_part[:, text_columns(1 - core)].astype(BF16)
        text_share().start()
        weight_copy(0, w_o).start()
        use(1)
        multiply(1 - core, pooled(2), 1, True)
        send_sum(1)

    def turn_10():
        multiply(core, pooled(2), 1, True)
        for n, ref in enumerate((q1_h, k1_h, v1_h)):
            pool_copy(n, ref).start()
        share_sum(1).wait()
        x2_copy.wait()
        norm_back(
            1,
            1,
            lambda i, lines: lbuf[0, lines, :].astype(F32)
            + lbuf[0, pl.ds(pl.multiple_of(half_rows + i * 64, 64), 64), :].astype(F32),
            lambda first, lines: grad[lines, :],
            store_branch,
        )
        share_branch(1).start()
        text_share().wait()
        text_part[:, pl.ds(0, features // 2)] = text_part[:, text_columns(core)] + text_got[
            ...
        ].astype(F32)
        keep_copy(2, text_part.at[:, pl.ds(0, features // 2)], grad_text).start()

    def turn_11():
        share_branch(1).wait()
        keep_copy(1, dqkv.at[:, wide], e1_h).start()
        use(0)
        project_to(3, 0)
        weight_copy(0, w_down, 0).start()
        weight_copy(1, w_down, 1).start()
        active_copy(1 - core, 0).start()

    def turn_12():
        keep_copy(1, dqkv.at[:, wide], e1_h).wait()
        for n, ref in enumerate((q1_h, k1_h, v1_h)):
            pool_copy(n, ref).wait()

    def self_head(head):
        head_back(
            head,
            pool.at[0],
            pool.at[1],
            pool.at[2],
            pool.at[3],
            lse1_ref,
            dqkv,
            dqkv,
            (0, part, 2 * part),
            acc_k,
            acc_v,
            True,
        )

    def held(n):
        return lambda rows_of: theirs[rows_of, pl.ds(n * part, part)]

    def turn_13():
        active_copy(core, 0).wait()
        use(0)
        multiply(0, held(0), 0, True)
        weight_copy(0, w_down, 2).start()
        use(1)
        multiply(0, held(1), 1, False)
        weight_copy(1, w_down, 3).start()
        active_copy(1 - core, 1).start()

    def turn_14():
        active_copy(core, 0).wait()
        use(0)
        multiply(0, held(0), 0, False)
        use(1)
        multiply(0, held(1), 1, False)
        send_sum(3)

    def turn_15():
        share_sum(3).wait()
        keep_copy(3, x3_h, acc).start()
        active_copy(core, 1).start()

    def turn_16():
        active_copy(core, 0).wait()
        keep_copy(3, x3_h, acc).wait()
        multiply(0, held(0), 0, False)
        weight_copy(0, w_down, 0).start()
        multiply(0, held(1), 1, False)
        weight_copy(1, w_down, 1).start()
        active_copy(core, 0).start()

    def turn_17():
        active_copy(core, 0).wait()
        use(0)
        multiply(0, held(0), 0, False)
        weight_copy(0, w_q).start()
        use(1)
        multiply(0, held(1), 1, False)
        weight_copy(1, w_k).start()

        def body(i, carry):
            lines = pl.ds(pl.multiple_of(i * 64, 64), 64)
            theirs[lines, :] = (acc[lines, :] + arrived[1, lines, :].astype(F32)).astype(BF16)
            return carry

        lax.fori_loop(0, half_rows // 64, body, 0)
        keep_copy(0, theirs, layer_out).start()

    def turn_18():
        keep_copy(0, theirs, layer_out).wait()
        use(0)
        multiply(1 - core, headed(0), 0, True)
        weight_copy(0, w_v).start()
        use(1)
        multiply(1 - core, headed(1), 1, False)

    def turn_19():
        use(0)
        multiply(1 - core, headed(2), 0, False)
        send_sum(2)
        multiply(core, headed(2), 0, True)
        multiply(core, headed(1), 1, False)
        weight_copy(1, w_q).start()

    def turn_20():
        use(1)
        multiply(core, headed(0), 1, False)
        share_sum(2).wait()
        keep_copy(1, x1_h, theirs).start()

    def turn_21():
        keep_copy(1, x1_h, theirs).wait()

        def store(first, lines, value):
            grad[lines, :] = value

        norm_back(
            0,
            2,
            lambda i, lines: theirs[lines, :].astype(F32),
            lambda first, lines: grad[lines, :],
            store,
        )
        keep_copy(3, grad, grad_input).start()

    def norm_copy(step):
        return remote(
            got.at[2 * step],
            got.at[2 * step + 1],
            norm_send.at[step],
            norm_recv.at[step],
            partners[step],
        )

    def norm_sum(step):
        if step == 0:
            got[0] = norm_grads[...]
        else:
            norm_copy(step - 1).wait()
            got[2 * step] = got[2 * step - 2] + got[2 * step - 1]
        if step < len(partners):
            norm_copy(step).start()
        else:
            keep_copy(1, got.at[2 * step], norm_out).start()

    chain = {
        4: turn_4,
        5: turn_5,
        6: turn_6,
        7: turn_7,
        8: turn_8,
        9: turn_9,
        10: turn_10,
        11: turn_11,
        13: turn_13,
        14: turn_14,
        15: turn_15,
        16: turn_16,
        17: turn_17,
        18: turn_18,
        19: turn_19,
        20: turn_20,
        21: turn_21,
    }
    stages = (begin, second, third, fourth, fifth, finish)
    left_copy(0).start()
    weight_copy(0, w_down, 0).start()
    slope_copy(0).start()
    start_rights(jnp.int32(0))
    weight_copy(1, w_up, 0).start()
    left_copy(1).start()
    for copy in firsts:
        copy.start()
    for first in range(0, half_rows, block):
        acc[pl.ds(first, block), :] = jnp.zeros((block, features), F32)
    norm_grads[...] = jnp.zeros_like(norm_grads)
    left_copy(0).wait()

    def body(turn, carry):
        for step, stage in enumerate(stages):
            c = turn - step - 1

            @pl.when((c >= 0) & (c < total))
            def _():
                stage(c, lax.rem(c, slots))

        pl.when(turn < total)(lambda: compute(turn, lax.rem(turn, slots)))
        pl.when(turn < 4)(lambda: feed_forward(turn))
        for number, fn in chain.items():
            pl.when(turn == number)(fn)
        pl.when(turn == 12)(turn_12)

        @pl.when((turn >= 12) & (turn < 18))
        def _():
            def both(head, carry):
                self_head(head)
                return carry

            first = lax.div(heads, 6) * (turn - 12)
            lax.fori_loop(first, first + heads // 6, both, 0)

        for step in range(len(partners) + 1):
            pl.when(turn == 22 + step)(functools.partial(norm_sum, step))
        return carry

    lax.fori_loop(0, total + len(stages), body, 0)
    for c in (total - 2, total - 1):
        for copy in out_copies(jnp.int32(c)):
            copy.wait()
    keep_copy(3, grad, grad_input).wait()
    keep_copy(1, got.at[2 * len(partners)], norm_out).wait()
    keep_copy(2, text_part.at[:, pl.ds(0, features // 2)], grad_text).wait()


def backward_all(arrays, small):
    frames, width = arrays[0].shape
    text = arrays[8]
    rows, half, part = width // 16, frames // 2, arrays[9].shape[1]
    dma, vmem, shape = pltpu.SemaphoreType.DMA, pltpu.VMEM, jax.ShapeDtypeStruct

    def buffer(*dims):
        return vmem((SLOTS,) + dims, BF16)

    anywhere = pl.BlockSpec(memory_space=pl.ANY)
    return pl.pallas_call(
        backward_kernel,
        out_shape=[
            shape((rows, UNITS * UNIT), F32),
            shape((half, width), BF16),
            shape((half, width), F32),
            shape((text.shape[0], width // 2), F32),
            shape((8, width), F32),
            shape((frames, 4 * part), BF16),
            shape((frames, part), BF16),
            shape((frames, width), BF16),
            shape((frames, width), BF16),
        ],
        in_specs=[anywhere] * len(arrays) + [pl.BlockSpec(memory_space=vmem)] * len(small),
        out_specs=[anywhere] * 9,
        scratch_shapes=[
            buffer(4, 2, 2, rows, WIDTH_Z),
            buffer(4, 2, 2, rows, WIDTH_A),
            *[buffer(4, rows // 2, WIDTH_Z)] * 6,
            buffer(5, rows, WIDTH_Z),
            *[buffer(rows // 2, WIDTH_A)] * 6,
            buffer(5, 2, 2, rows, WIDTH_A),
            vmem((2, rows, WIDTH_Z), F32),
            vmem((2, rows, WIDTH_A), F32),
            vmem((2, frames, width), BF16),
            vmem((2, 2, frames, UNIT), BF16),
            vmem(text.shape, BF16),
            vmem((text.shape[0], 2 * part), BF16),
            *[vmem((text.shape[0], part), BF16)] * 2,
            vmem((4, frames, part), BF16),
            vmem((frames, 3 * part), BF16),
            *[vmem((frames, 128), F32)] * 2,
            *[vmem((half, width), F32)] * 2,
            vmem((half, width), BF16),
            vmem((2, half, width), BF16),
            vmem((2, width, part), BF16),
            vmem((text.shape[0], width), F32),
            *[vmem((text.shape[0], width // 2), BF16)] * 2,
            vmem((8, width), F32),
            vmem((11, 8, width), F32),
            dma((3,)),
            dma((2,)),
            dma((2, 2)),
            dma((2, 2)),
            dma((SLOTS,)),
            dma((SLOTS,)),
            dma((SLOTS, 8)),
            dma((SLOTS, 8)),
            dma((4,)),
            dma,
            dma((2,)),
            dma,
            dma((4,)),
            dma((7,)),
            dma((7,)),
            dma((5,)),
            dma((5,)),
            pltpu.SemaphoreType.REGULAR((4,)),
        ],
        compiler_params=pltpu.CompilerParams(
            collective_id=1, has_side_effects=True, vmem_limit_bytes=VMEM_LIMIT
        ),
        name="backward",
    )(*arrays, *small)


def gather_plan(columns):
    chunks, since = [], 0
    for array, width in enumerate(columns):
        size = 768 if width % 768 == 0 else width
        for first in range(0, width, size):
            since += 1
            family = "A" if since % 5 == 3 and size == 768 else "Z"
            chunks.append((array, first, size, family))
    return tuple(chunks)


def local_fast(
    hidden_in,
    text_states,
    norm1_gain,
    norm1_bias,
    self_query,
    self_key,
    self_value,
    self_out,
    norm2_gain,
    norm2_bias,
    cross_query,
    cross_key,
    cross_value,
    cross_out,
    norm3_gain,
    norm3_bias,
    hidden_up,
    hidden_down,
    cotangent,
):
    width = norm1_gain.shape[0] * 16
    norms = jnp.stack([norm1_gain, norm1_bias, norm2_gain, norm2_bias, norm3_gain, norm3_bias])
    norms = jnp.pad(norms, ((0, 26), (0, 128 - norms.shape[1])))
    shards = (
        norms,
        self_query.T,
        self_key.T,
        self_value.T,
        self_out,
        cross_key.T,
        cross_value.T,
        cross_query.T,
        cross_out,
        hidden_up.T,
        hidden_down,
    )
    gathered, kept = forward_all(
        shards,
        gather_plan([s.shape[1] for s in shards]),
        hidden_in[0],
        text_states[0],
        cotangent[0],
    )
    w_q, w_k, w_v, w_o, w_ck, w_cv, w_cq, w_co, w_up, w_down = [
        g.reshape(width, g.shape[-1]) for g in gathered[1:]
    ]
    normed_one, normed_two, normed_three = kept[:3]
    query_one, key_one, value_one, attended_one = kept[3:7]
    query_two, key_two, value_two, attended_two = kept[7:11]
    logsum_one, logsum_two, norms, stream_two, stream_three, branch, active, slope = kept[11:]
    summed, layer_out, grad_input, grad_text, norm_sums, *_ = backward_all(
        (
            *(branch, normed_three, normed_two, normed_one),
            *(active, slope, attended_two, attended_one, text_states[0]),
            *(query_two, key_two, value_two, query_one, key_one, value_one),
            *(stream_three, stream_two, hidden_in[0]),
            *(w_q, w_k, w_v, w_o, w_ck, w_cv, w_cq, w_co, w_up, w_down),
        ),
        (logsum_two, logsum_one, norms),
    )
    rows, part = width // 16, query_one.shape[1]
    norm_sums = lax.dynamic_slice_in_dim(norm_sums, lax.axis_index("dp") * rows, rows, 1)
    columns = [hidden_down.shape[1]] * 2 + [part] * 8
    pieces, first = [], 0
    for count in columns:
        pieces.append(summed[:, first : first + count])
        first += count
    down, up, out_cross, query_cross, key_cross, value_cross, out_self, query, key, value = pieces
    return (
        layer_out[None],
        grad_input[None],
        grad_text[None],
        norm_sums[0],
        norm_sums[1],
        query.T,
        key.T,
        value.T,
        out_self,
        norm_sums[2],
        norm_sums[3],
        query_cross.T,
        key_cross.T,
        value_cross.T,
        out_cross,
        norm_sums[4],
        norm_sums[5],
        up.T,
        down,
    )


def solution(mesh):
    placed = (
        P("dp", "tensor", None),
        P("dp", None, None),
        P("dp"),
        P("dp"),
        P("tensor", "dp"),
        P("tensor", "dp"),
        P("tensor", "dp"),
        P("dp", "tensor"),
        P("dp"),
        P("dp"),
        P("tensor", "dp"),
        P("tensor", "dp"),
        P("tensor", "dp"),
        P("dp", "tensor"),
        P("dp"),
        P("dp"),
        P("tensor", "dp"),
        P("dp", "tensor"),
        P("dp", "tensor", None),
    )
    fast = dict(mesh.shape) == {"dp": 16, "tensor": 2}
    return jax.shard_map(
        local_fast if fast else local_generic,
        mesh=mesh,
        in_specs=placed,
        out_specs=(
            P("dp", "tensor", None),
            P("dp", "tensor", None),
            P("dp", None, "tensor"),
            P("dp"),
            P("dp"),
            P("tensor", "dp"),
            P("tensor", "dp"),
            P("tensor", "dp"),
            P("dp", "tensor"),
            P("dp"),
            P("dp"),
            P("tensor", "dp"),
            P("tensor", "dp"),
            P("tensor", "dp"),
            P("dp", "tensor"),
            P("dp"),
            P("dp"),
            P("tensor", "dp"),
            P("dp", "tensor"),
        ),
        check_vma=False,
    )
```

```python
import functools

import jax
import jax.numpy as jnp
from jax import lax
from jax.experimental import pallas as pl
from jax.experimental.pallas import tpu as pltpu
from jax.sharding import PartitionSpec as P

HEAD_DIM = 64


norm_eps = 1e-05
score_scale = 0.125


def layer_norm(values, gain, shift):
    centre = jnp.mean(values, axis=-1, keepdims=True)
    offset = values - centre
    spread = jnp.mean(offset * offset, axis=-1, keepdims=True)
    return offset * lax.rsqrt(spread + norm_eps) * gain + shift


def gelu_exact(values):
    return jax.nn.gelu(values, approximate=False)


def project(row_data, weight):
    return jnp.einsum("cli,oi->clo", row_data, weight, preferred_element_type=jnp.float32)


def split_heads(values):
    return values.reshape(values.shape[0], values.shape[1], -1, HEAD_DIM)


def flatten_heads(values):
    return values.reshape(values.shape[0], values.shape[1], -1)


def causal_keep(first_row, count, length):
    row_ids = first_row + lax.broadcasted_iota(jnp.int32, (count, length), 0)
    col_ids = lax.broadcasted_iota(jnp.int32, (count, length), 1)
    return col_ids <= row_ids


def block_scores(queries, key_rows, first_row, block_rows, key_end, causal):
    scores = (
        jnp.einsum(
            "cqhe,ckhe->chqk",
            queries[:, first_row : first_row + block_rows],
            key_rows[:, :key_end],
            preferred_element_type=jnp.float32,
        )
        * score_scale
    )
    if causal:
        scores = jnp.where(causal_keep(first_row, block_rows, key_end), scores, -1e30)
    return scores


def attend(queries, key_rows, val_rows, causal):
    length = queries.shape[1]
    block_rows = min(512, length)
    outputs = []
    log_sums = []
    for block_num in range(length // block_rows):
        first_row = block_num * block_rows
        key_end = first_row + block_rows if causal else key_rows.shape[1]
        scores = block_scores(queries, key_rows, first_row, block_rows, key_end, causal)
        row_peak = jnp.max(scores, axis=-1, keepdims=True)
        exp_scores = jnp.exp(scores - row_peak)
        row_total = jnp.sum(exp_scores, axis=-1, keepdims=True)
        soft_weights = (exp_scores / row_total).astype(jnp.bfloat16)
        outputs.append(
            jnp.einsum(
                "chqk,ckhe->cqhe",
                soft_weights,
                val_rows[:, :key_end],
                preferred_element_type=jnp.float32,
            ).astype(jnp.bfloat16)
        )
        log_sums.append((row_peak + jnp.log(row_total))[..., 0])
    return (jnp.concatenate(outputs, axis=1), jnp.concatenate(log_sums, axis=2))


def attend_back(queries, key_rows, val_rows, grad_out, log_sums, causal):
    length = queries.shape[1]
    block_rows = min(512, length)
    grad_keys = jnp.zeros(key_rows.shape, jnp.float32)
    grad_vals = jnp.zeros(val_rows.shape, jnp.float32)
    grad_queries = []
    for block_num in range(length // block_rows):
        first_row = block_num * block_rows
        key_end = first_row + block_rows if causal else key_rows.shape[1]
        query_blk = queries[:, first_row : first_row + block_rows]
        grad_blk = grad_out[:, first_row : first_row + block_rows]
        scores = block_scores(queries, key_rows, first_row, block_rows, key_end, causal)
        soft = jnp.exp(scores - log_sums[:, :, first_row : first_row + block_rows, None])
        grad_soft = jnp.einsum(
            "cqhe,ckhe->chqk", grad_blk, val_rows[:, :key_end], preferred_element_type=jnp.float32
        )
        grad_vals = grad_vals.at[:, :key_end].add(
            jnp.einsum(
                "chqk,cqhe->ckhe",
                soft.astype(jnp.bfloat16),
                grad_blk,
                preferred_element_type=jnp.float32,
            )
        )
        inner = jnp.sum(soft * grad_soft, axis=-1, keepdims=True)
        grad_scores = (soft * (grad_soft - inner)).astype(jnp.bfloat16)
        grad_queries.append(
            jnp.einsum(
                "chqk,ckhe->cqhe",
                grad_scores,
                key_rows[:, :key_end],
                preferred_element_type=jnp.float32,
            )
            * score_scale
        )
        grad_keys = grad_keys.at[:, :key_end].add(
            jnp.einsum(
                "chqk,cqhe->ckhe", grad_scores, query_blk, preferred_element_type=jnp.float32
            )
            * score_scale
        )
    return (jnp.concatenate(grad_queries, axis=1), grad_keys, grad_vals)


def gather_rows(values):
    return lax.all_gather(values, "tensor", axis=1, tiled=True)


def scatter_rows(values):
    return lax.psum_scatter(values, "tensor", scatter_dimension=1, tiled=True)


def gather_grads(values):
    return lax.all_gather(values, "tensor", axis=1, tiled=True)


def scatter_grads(values):
    return lax.psum_scatter(
        values.astype(jnp.bfloat16), "tensor", scatter_dimension=1, tiled=True
    ).astype(jnp.float32)


def heads_grads(grad_branch, attended, out_weight):
    grad_out_proj = jnp.einsum(
        "clo,cla->oa", grad_branch, flatten_heads(attended), preferred_element_type=jnp.float32
    )
    grad_attended = split_heads(
        jnp.einsum(
            "clo,oa->cla", grad_branch, out_weight, preferred_element_type=jnp.float32
        ).astype(jnp.bfloat16)
    )
    return (grad_out_proj, grad_attended)


def weight_grad(grad_rows, source_rows):
    return jnp.einsum("cla,cli->ai", grad_rows, source_rows, preferred_element_type=jnp.float32)


def input_grad(grad_rows, weight):
    return jnp.einsum("cla,ai->cli", grad_rows, weight, preferred_element_type=jnp.float32)


def local_generic(
    hidden_in,
    text_states,
    norm1_gain,
    norm1_bias,
    self_query,
    self_key,
    self_value,
    self_out,
    norm2_gain,
    norm2_bias,
    cross_query,
    cross_key,
    cross_value,
    cross_out,
    norm3_gain,
    norm3_bias,
    hidden_up,
    hidden_down,
    cotangent,
):
    full_weights = (
        lax.all_gather(norm1_gain, "dp", axis=0, tiled=True),
        lax.all_gather(norm1_bias, "dp", axis=0, tiled=True),
        lax.all_gather(self_query, "dp", axis=1, tiled=True),
        lax.all_gather(self_key, "dp", axis=1, tiled=True),
        lax.all_gather(self_value, "dp", axis=1, tiled=True),
        lax.all_gather(self_out, "dp", axis=0, tiled=True),
        lax.all_gather(norm2_gain, "dp", axis=0, tiled=True),
        lax.all_gather(norm2_bias, "dp", axis=0, tiled=True),
        lax.all_gather(cross_query, "dp", axis=1, tiled=True),
        lax.all_gather(cross_key, "dp", axis=1, tiled=True),
        lax.all_gather(cross_value, "dp", axis=1, tiled=True),
        lax.all_gather(cross_out, "dp", axis=0, tiled=True),
        lax.all_gather(norm3_gain, "dp", axis=0, tiled=True),
        lax.all_gather(norm3_bias, "dp", axis=0, tiled=True),
        lax.all_gather(hidden_up, "dp", axis=1, tiled=True),
        lax.all_gather(hidden_down, "dp", axis=0, tiled=True),
    )
    gain_self = full_weights[0].astype(jnp.float32)
    bias_self = full_weights[1].astype(jnp.float32)
    gain_cross = full_weights[6].astype(jnp.float32)
    bias_cross = full_weights[7].astype(jnp.float32)
    gain_ffn = full_weights[12].astype(jnp.float32)
    bias_ffn = full_weights[13].astype(jnp.float32)
    stream_one = hidden_in.astype(jnp.float32)
    key_two = split_heads(project(text_states, full_weights[9]).astype(jnp.bfloat16))
    value_two = split_heads(project(text_states, full_weights[10]).astype(jnp.bfloat16))
    normed_one = gather_rows(layer_norm(stream_one, gain_self, bias_self).astype(jnp.bfloat16))
    query_one = split_heads(project(normed_one, full_weights[2]).astype(jnp.bfloat16))
    key_one = split_heads(project(normed_one, full_weights[3]).astype(jnp.bfloat16))
    value_one = split_heads(project(normed_one, full_weights[4]).astype(jnp.bfloat16))
    attended_one, logsum_one = attend(query_one, key_one, value_one, True)
    stream_two = stream_one + scatter_rows(project(flatten_heads(attended_one), full_weights[5]))
    normed_two = gather_rows(layer_norm(stream_two, gain_cross, bias_cross).astype(jnp.bfloat16))
    query_two = split_heads(project(normed_two, full_weights[8]).astype(jnp.bfloat16))
    attended_two, logsum_two = attend(query_two, key_two, value_two, False)
    stream_three = stream_two + scatter_rows(project(flatten_heads(attended_two), full_weights[11]))
    normed_three = gather_rows(layer_norm(stream_three, gain_ffn, bias_ffn).astype(jnp.bfloat16))
    upper = project(normed_three, full_weights[14])
    active = gelu_exact(upper).astype(jnp.bfloat16)
    layer_out = (stream_three + scatter_rows(project(active, full_weights[15]))).astype(
        jnp.bfloat16
    )
    grad_three = cotangent.astype(jnp.float32)
    grad_branch = gather_grads(grad_three.astype(jnp.bfloat16))
    grad_down = jnp.einsum("clo,clf->of", grad_branch, active, preferred_element_type=jnp.float32)
    grad_active = jnp.einsum(
        "clo,of->clf", grad_branch, full_weights[15], preferred_element_type=jnp.float32
    )
    grad_upper = jax.vjp(gelu_exact, upper)[1](grad_active)[0].astype(jnp.bfloat16)
    grad_up = weight_grad(grad_upper, normed_three)
    norm_back = jax.vjp(layer_norm, stream_three, gain_ffn, bias_ffn)[1]
    grad_stream, grad_gain_ffn, grad_bias_ffn = norm_back(
        scatter_grads(input_grad(grad_upper, full_weights[14]))
    )
    grad_two = grad_three + grad_stream
    grad_branch = gather_grads(grad_two.astype(jnp.bfloat16))
    grad_out_cross, grad_attended = heads_grads(grad_branch, attended_two, full_weights[11])
    grad_query, grad_key, grad_value = attend_back(
        query_two, key_two, value_two, grad_attended, logsum_two, False
    )
    grad_query = flatten_heads(grad_query).astype(jnp.bfloat16)
    grad_key = flatten_heads(grad_key).astype(jnp.bfloat16)
    grad_value = flatten_heads(grad_value).astype(jnp.bfloat16)
    grad_query_cross = weight_grad(grad_query, normed_two)
    grad_key_cross = weight_grad(grad_key, text_states)
    grad_value_cross = weight_grad(grad_value, text_states)
    text_part = input_grad(grad_key, full_weights[9]) + input_grad(grad_value, full_weights[10])
    grad_text = lax.psum_scatter(
        text_part.astype(jnp.bfloat16), "tensor", scatter_dimension=2, tiled=True
    ).astype(jnp.float32)
    norm_back = jax.vjp(layer_norm, stream_two, gain_cross, bias_cross)[1]
    grad_stream, grad_gain_cross, grad_bias_cross = norm_back(
        scatter_grads(input_grad(grad_query, full_weights[8]))
    )
    grad_one = grad_two + grad_stream
    grad_branch = gather_grads(grad_one.astype(jnp.bfloat16))
    grad_out_self, grad_attended = heads_grads(grad_branch, attended_one, full_weights[5])
    grad_query, grad_key, grad_value = attend_back(
        query_one, key_one, value_one, grad_attended, logsum_one, True
    )
    grad_query = flatten_heads(grad_query).astype(jnp.bfloat16)
    grad_key = flatten_heads(grad_key).astype(jnp.bfloat16)
    grad_value = flatten_heads(grad_value).astype(jnp.bfloat16)
    grad_query_self = weight_grad(grad_query, normed_one)
    grad_key_self = weight_grad(grad_key, normed_one)
    grad_value_self = weight_grad(grad_value, normed_one)
    grad_normed = (
        input_grad(grad_query, full_weights[2])
        + input_grad(grad_key, full_weights[3])
        + input_grad(grad_value, full_weights[4])
    )
    norm_back = jax.vjp(layer_norm, stream_one, gain_self, bias_self)[1]
    grad_stream, grad_gain_self, grad_bias_self = norm_back(scatter_grads(grad_normed))
    grad_input = grad_one + grad_stream
    summed = (
        lax.psum_scatter(
            grad_gain_self.astype(jnp.bfloat16), "dp", scatter_dimension=0, tiled=True
        ).astype(jnp.float32),
        lax.psum_scatter(
            grad_bias_self.astype(jnp.bfloat16), "dp", scatter_dimension=0, tiled=True
        ).astype(jnp.float32),
        lax.psum_scatter(
            grad_query_self.astype(jnp.bfloat16), "dp", scatter_dimension=1, tiled=True
        ).astype(jnp.float32),
        lax.psum_scatter(
            grad_key_self.astype(jnp.bfloat16), "dp", scatter_dimension=1, tiled=True
        ).astype(jnp.float32),
        lax.psum_scatter(
            grad_value_self.astype(jnp.bfloat16), "dp", scatter_dimension=1, tiled=True
        ).astype(jnp.float32),
        lax.psum_scatter(
            grad_out_self.astype(jnp.bfloat16), "dp", scatter_dimension=0, tiled=True
        ).astype(jnp.float32),
        lax.psum_scatter(
            grad_gain_cross.astype(jnp.bfloat16), "dp", scatter_dimension=0, tiled=True
        ).astype(jnp.float32),
        lax.psum_scatter(
            grad_bias_cross.astype(jnp.bfloat16), "dp", scatter_dimension=0, tiled=True
        ).astype(jnp.float32),
        lax.psum_scatter(
            grad_query_cross.astype(jnp.bfloat16), "dp", scatter_dimension=1, tiled=True
        ).astype(jnp.float32),
        lax.psum_scatter(
            grad_key_cross.astype(jnp.bfloat16), "dp", scatter_dimension=1, tiled=True
        ).astype(jnp.float32),
        lax.psum_scatter(
            grad_value_cross.astype(jnp.bfloat16), "dp", scatter_dimension=1, tiled=True
        ).astype(jnp.float32),
        lax.psum_scatter(
            grad_out_cross.astype(jnp.bfloat16), "dp", scatter_dimension=0, tiled=True
        ).astype(jnp.float32),
        lax.psum_scatter(
            grad_gain_ffn.astype(jnp.bfloat16), "dp", scatter_dimension=0, tiled=True
        ).astype(jnp.float32),
        lax.psum_scatter(
            grad_bias_ffn.astype(jnp.bfloat16), "dp", scatter_dimension=0, tiled=True
        ).astype(jnp.float32),
        lax.psum_scatter(
            grad_up.astype(jnp.bfloat16), "dp", scatter_dimension=1, tiled=True
        ).astype(jnp.float32),
        lax.psum_scatter(
            grad_down.astype(jnp.bfloat16), "dp", scatter_dimension=0, tiled=True
        ).astype(jnp.float32),
    )
    norm_sums = lax.psum(
        (summed[0], summed[1], summed[6], summed[7], summed[12], summed[13]), "tensor"
    )
    return (
        layer_out,
        grad_input,
        grad_text,
        norm_sums[0],
        norm_sums[1],
        summed[2],
        summed[3],
        summed[4],
        summed[5],
        norm_sums[2],
        norm_sums[3],
        summed[8],
        summed[9],
        summed[10],
        summed[11],
        norm_sums[4],
        norm_sums[5],
        summed[14],
        summed[15],
    )


MESH_IDS = pl.DeviceIdType.MESH
BF16 = jnp.bfloat16
F32 = jnp.float32
VMEM_LIMIT = 63 * 2**20


def my_place():
    chip = lax.axis_index("dp")
    core = lax.axis_index("tensor")
    return (lax.rem(chip, 2), lax.rem(lax.div(chip, 2), 2), lax.div(chip, 4), core)


def neighbours(x, y, z, core):
    def device(zz, yy, xx):
        return (zz * 4 + yy * 2 + xx, core)

    return (device(z, y, 1 - x), device(z, 1 - y, x), device(z + 1, y, x), device(z - 1, y, x))


def when(cond, fn):
    if cond is None:
        fn()
    else:
        pl.when(cond)(fn)


def signal_neighbours(sems, near, has_up, has_down):
    for sem, device, cond in zip(sems, near, (None, None, has_up, has_down), strict=True):
        when(
            cond,
            functools.partial(
                pl.semaphore_signal, sem, inc=1, device_id=device, device_id_type=MESH_IDS
            ),
        )


def gather_engine(chunks, shards, outs, sems):
    local_sem, send_sem, zs, xs, ys, ds = sems
    x, y, z, core = my_place()
    xn, yn = 1 - x, 1 - y
    near = neighbours(x, y, z, core)
    right, across, up, down = near
    has_up, has_down = z < 3, z > 0
    barrier = pltpu.get_barrier_semaphore()
    signal_neighbours([barrier] * 4, near, has_up, has_down)
    pl.semaphore_signal(barrier, inc=1, device_id=(lax.axis_index("dp"), 1 - core), device_id_type=MESH_IDS)
    pl.semaphore_wait(barrier, 3 + has_up.astype(jnp.int32) + has_down.astype(jnp.int32))
    total = len(chunks)
    pending = []


    def span(c):
        _, first, width, _ = chunks[c]
        return pl.ds(first, width)

    def at(zz, yy, xx, c, half=None):
        ref = outs[chunks[c][0]]
        half_rows = ref.shape[3] // 2
        lines = slice(None) if half is None else pl.ds(half * half_rows, half_rows)
        return ref.at[zz, yy, xx, lines, span(c)]

    def plane(zz, c):
        return outs[chunks[c][0]].at[zz, :, :, :, span(c)]

    def own(c):
        return shards[chunks[c][0]].at[:, span(c)]

    local = [pltpu.make_async_copy(own(c), at(z, y, x, c), local_sem.at[c]) for c in range(total)]

    def remote(src, dst, sem, device):
        return pltpu.make_async_remote_copy(
            src_ref=src,
            dst_ref=dst,
            send_sem=send_sem,
            recv_sem=sem,
            device_id=device,
            device_id_type=MESH_IDS,
        )

    def send(src, dst, sem, device, cond=None):
        copy = remote(src, dst, sem, device)
        when(cond, copy.start)
        pending.append((cond, copy))

    def wait(ref, sem, cond=None):
        when(cond, remote(ref, ref, sem, right).wait_recv)

    def lines(step):
        for sign, device, more in ((-1, up, has_up), (1, down, has_down)):
            block = z + sign * step
            yield block, (block >= 0) if sign < 0 else (block <= 3), device, more

    def stage_z(c, step):
        if step == 0:
            send(own(c), at(z, y, x, c), zs.at[c, z], up, has_up)
            send(own(c), at(z, y, x, c), zs.at[c, z], down, has_down)
            send(own(c), at(z, y, x, c), xs.at[c, z], right)
            send(own(c), at(z, y, x, c), ys.at[c, z], across)
            local[c].start()
        if 1 <= step <= 3:
            for block, exists, device, more in lines(step):
                ref = at(block, y, x, c)
                wait(ref, zs.at[c, block], exists)
                if step < 3:
                    send(ref, ref, zs.at[c, block], device, exists & more)
                send(ref, ref, xs.at[c, block], right, exists)
                send(ref, ref, ys.at[c, block], across, exists)
        if 1 <= step <= 4:
            for block, exists, _, _ in [(z, None, None, None)] if step == 1 else lines(step - 1):
                wait(at(block, y, xn, c), xs.at[c, block], exists)
                ref = at(block, y, xn, c, 0)
                send(ref, ref, ds.at[c, block, 0], across, exists)
                wait(at(block, yn, x, c), ys.at[c, block], exists)
                ref = at(block, yn, x, c, 1)
                send(ref, ref, ds.at[c, block, 1], right, exists)
        if step == 5:
            for block in range(4):
                for half in range(2):
                    wait(at(block, yn, xn, c, half), ds.at[c, block, half])
            local[c].wait()

    def stage_a(c, step):
        if step == 0:
            send(own(c), at(z, y, x, c), xs.at[c, z], right)
            send(own(c), at(z, y, x, c), ys.at[c, z], across)
            local[c].start()
        if step == 1:
            wait(at(z, y, xn, c), xs.at[c, z])
            ref = at(z, y, xn, c, 0)
            send(ref, ref, ds.at[c, z, 0], across)
            wait(at(z, yn, x, c), ys.at[c, z])
            ref = at(z, yn, x, c, 1)
            send(ref, ref, ds.at[c, z, 1], right)
        if step == 2:
            for half in range(2):
                wait(at(z, yn, xn, c, half), ds.at[c, z, half])
            local[c].wait()
            send(plane(z, c), plane(z, c), zs.at[c, z], up, has_up)
            send(plane(z, c), plane(z, c), zs.at[c, z], down, has_down)
        if step >= 3:
            for block, exists, device, more in lines(step - 2):
                wait(plane(block, c), zs.at[c, block], exists)
                if step < 5:
                    send(plane(block, c), plane(block, c), zs.at[c, block], device, exists & more)

    stages = 6

    def turn(number):
        for step in range(stages):
            c = number - step
            if 0 <= c < total:
                (stage_z if chunks[c][3] == "Z" else stage_a)(c, step)

    def finish():
        for cond, copy in pending:
            when(cond, copy.wait_send)

    return turn, finish


def total_of(*parts):
    value = parts[0].astype(F32)
    for part in parts[1:]:
        value = value + part.astype(F32)
    return value


def dot_nt(left, right):
    return lax.dot_general(left, right, (((1,), (1,)), ((), ())), preferred_element_type=F32)


def dot_tn(left, right):
    return lax.dot_general(left, right, (((0,), (0,)), ((), ())), preferred_element_type=F32)


def dot_nn(left, right):
    return jnp.dot(left, right, preferred_element_type=F32)


def project_rows(source, weight, store, rows=256, transposed=False):
    def body(n, carry):
        first = pl.multiple_of(n * rows, rows)
        part = source[pl.ds(first, rows), :]
        store(first, dot_nt(part, weight[...]) if transposed else dot_nn(part, weight[...]))
        return carry

    lax.fori_loop(0, source.shape[0] // rows, body, 0)


def normalize(values, gain, shift):
    offset = values - jnp.mean(values, axis=-1, keepdims=True)
    spread = jnp.mean(offset * offset, axis=-1, keepdims=True)
    return offset * lax.rsqrt(spread + norm_eps) * gain + shift


def head_lanes(half):
    return lax.div(lax.broadcasted_iota(jnp.int32, (1, 128), 1), 64) == half


def only(mask, value):
    return jnp.where(mask, value.astype(F32), 0.0).astype(BF16)


def pair_forward(pair, q_ref, k_ref, v_ref, o_ref, lse_ref, causal):
    cols = pl.ds(pl.multiple_of(pair * 128, 128), 128)
    block = 256
    keep = lax.broadcasted_iota(jnp.int32, (block, block), 0) <= lax.broadcasted_iota(
        jnp.int32, (block, block), 1
    )
    for i in range(q_ref.shape[0] // block):
        rows = pl.ds(i * block, block)
        parts = [(0, k_ref.shape[0], False)]
        if causal:
            parts = [(0, i * block, False)] * (i > 0) + [(i * block, block, True)]
        total = 0.0
        for half in range(2):
            mine = head_lanes(half)
            q = only(mine, q_ref[rows, cols])
            scores = []
            for first, count, diagonal in parts:
                part = dot_nt(k_ref[pl.ds(first, count), cols], q) * score_scale
                scores.append(jnp.where(keep, part, -1e30) if diagonal else part)
            peak = functools.reduce(
                jnp.maximum, [jnp.max(part, axis=0, keepdims=True) for part in scores]
            )
            scores = [jnp.exp(part - peak) for part in scores]
            weight = sum(jnp.sum(part, axis=0, keepdims=True) for part in scores)
            lse_ref[pl.ds(2 * pair + half, 1), rows] = peak + jnp.log(weight)
            share = 1.0 / weight
            for (first, count, _), part in zip(parts, scores, strict=True):
                v = only(mine, v_ref[pl.ds(first, count), cols])
                total = total + dot_tn((part * share).astype(BF16), v)
        o_ref[rows, cols] = total.astype(BF16)


def forward_kernel(chunks, count, *refs):
    shards, refs = refs[:count], refs[count:]
    hidden_h, text_h, cotangent_h, refs = refs[0], refs[1], refs[2], refs[3:]
    outs, refs = refs[:count], refs[count:]
    results, refs = refs[:19], refs[19:]
    sems, refs = refs[:6], refs[6:]
    (h1, h2, h3, q1, k1, v1, o1, q2, k2, v2, o2, lse1, lse2, x2, x3), refs = refs[:15], refs[15:]
    gathered_norms, norms, weights, hidden, text, mine, theirs, arrived, active, slopes, x2_parts = refs[:11]
    norm_sem, weight_sem, load_sem, share_send, share_recv, result_sem = refs[11:]
    names = dict(norms=0, q=1, k=2, v=3, o=4, ck=5, cv=6, cq=7, co=8, up=9, down=10)
    turn, finish = gather_engine(chunks, shards, outs, sems)
    chip, core = lax.axis_index("dp"), lax.axis_index("tensor")
    frames, width = h1.shape
    half = frames // 2
    own = pl.ds(pl.multiple_of(core * half, half), half)
    loads = [
        pltpu.make_async_copy(hidden_h, hidden, load_sem.at[0]),
        pltpu.make_async_copy(text_h, text, load_sem.at[1]),
        pltpu.make_async_copy(cotangent_h, theirs.at[1], load_sem.at[2]),
    ]
    for copy in loads:
        copy.start()
    pending = []

    def weight_copy(name, slot, first=0):
        return [
            pltpu.make_async_copy(
                outs[names[name]].at[zz, yy, xx, :, pl.ds(first, weights.shape[2])],
                weights.at[slot, pl.ds(((zz * 2 + yy) * 2 + xx) * rows, rows), :],
                weight_sem.at[slot, (zz * 2 + yy) * 2 + xx],
            )
            for zz in range(4)
            for yy in range(2)
            for xx in range(2)
        ]

    rows = width // 16

    def load_weight(name, slot, first=0):
        for copy in weight_copy(name, slot, first):
            copy.start()

    def wait_weight(slot):
        for copy in weight_copy("q", slot):
            copy.wait()

    def share(n, src, dst):
        return pltpu.make_async_remote_copy(
            src_ref=src,
            dst_ref=dst,
            send_sem=share_send.at[n],
            recv_sem=share_recv.at[n],
            device_id=(chip, 1 - core),
            device_id_type=MESH_IDS,
        )

    def give(n, ref):
        copy = pltpu.make_async_copy(ref, results[n], result_sem.at[n])
        copy.start()
        pending.append(copy)

    def norm_share(n, values, kind, h):
        step = 64

        def body(i, carry):
            first = pl.multiple_of(i * step, step)
            h[pl.ds(pl.multiple_of(core * half + first, step), step), :] = normalize(
                values(first, step), norms[2 * kind : 2 * kind + 1], norms[2 * kind + 1 : 2 * kind + 2]
            ).astype(BF16)
            return carry

        lax.fori_loop(0, half // step, body, 0)
        share(n, h.at[own], h.at[own]).start()

    def get_share(n, h):
        share(n, h.at[own], h.at[own]).wait()

    def to(ref):
        def store(first, value):
            ref[pl.ds(first, value.shape[0]), :] = value.astype(BF16)

        return store

    def out_project(n, o, slot):
        step = 256
        for whose, ref in ((1 - core, theirs.at[n]), (core, mine)):
            for first in range(0, half, step):
                part = o[pl.ds(pl.multiple_of(whose * half + first, step), step), :]
                ref[pl.ds(first, step), :] = dot_nt(part, weights[slot]).astype(ref.dtype)
            if whose is not core:
                share(3 + n, theirs.at[n], arrived.at[n]).start()

    def add_stream(n, before, after, parts=None):
        def values(first, step):
            lines = pl.ds(first, step)
            total = before[lines, :].astype(F32) + (mine[lines, :] + arrived[n, lines, :].astype(F32))
            after[lines, :] = total
            if parts is not None:
                high = total.astype(BF16)
                parts[lines, :] = high
                low = total - high.astype(F32)
                parts[pl.ds(pl.multiple_of(half + first, step), step), :] = low.astype(BF16)
            return total

        return values

    branch = results[16].at[own]
    branch_copy = pltpu.make_async_copy(theirs.at[1], branch, result_sem.at[16])

    def active_copies(j):
        lanes = pl.ds(j * active.shape[1], active.shape[1])
        return (
            pltpu.make_async_copy(active, results[17].at[:, lanes], result_sem.at[17]),
            pltpu.make_async_copy(slopes, results[18].at[:, lanes], result_sem.at[18]),
        )

    def hidden_units(j):
        wait_weight(j % 2)
        if j < 3:
            load_weight("up", (j + 1) % 2, (j + 1) * active.shape[1])
        if j:
            for copy in active_copies(j - 1):
                copy.wait()

        def store(first, value):
            lines = pl.ds(first, value.shape[0])
            below = 0.5 * (1.0 + lax.erf(value * (0.5**0.5)))
            density = jnp.exp(-0.5 * value * value) * 0.3989422804014327
            active[lines, :] = (value * below).astype(BF16)
            slopes[lines, :] = (below + value * density).astype(BF16)

        project_rows(h3, weights.at[j % 2], store)
        for copy in active_copies(j):
            copy.start()

    def work(number):
        if number == 5:
            copy = pltpu.make_async_copy(outs[0], gathered_norms, norm_sem)
            copy.start()
            copy.wait()
            for copy in loads:
                copy.wait()
            share(5, theirs.at[1], branch).start()
            branch_copy.start()
            total = 0.0
            lane = lax.broadcasted_iota(jnp.int32, (128, width), 0)
            place = lax.broadcasted_iota(jnp.int32, (128, width), 1)
            for n in range(16):
                pick = (place == lane + n * rows) & (lane < rows)
                total = total + dot_nn(
                    gathered_norms[n // 4, n // 2 % 2, n % 2],
                    jnp.where(pick, 1.0, 0.0).astype(BF16),
                )
            norms[...] = total
            give(13, norms)
            norm_share(0, lambda first, step: hidden[pl.ds(first, step), :].astype(F32), 0, h1)
        if number == 6:
            load_weight("q", 0)
            get_share(0, h1)
            give(0, h1)
            wait_weight(0)
            project_rows(h1, weights.at[0], to(q1))
            give(3, q1)
        if number == 7:
            load_weight("k", 1)
            wait_weight(1)
            project_rows(h1, weights.at[1], to(k1))
            give(4, k1)
        if number == 8:
            load_weight("v", 0)
            wait_weight(0)
            project_rows(h1, weights.at[0], to(v1))
            give(5, v1)
        if number in (9, 10, 11):
            if number == 9:
                load_weight("o", 1)
            pairs = q1.shape[1] // 128
            first = pairs * (number - 9) // 3
            last = pairs * (number - 8) // 3

            def body(pair, carry):
                pair_forward(pair, q1, k1, v1, o1, lse1, True)
                return carry

            lax.fori_loop(first, last, body, 0)
            if number == 11:
                load_weight("cv", 0)
        if number == 12:
            share(5, theirs.at[1], branch).wait()
            branch_copy.wait()
            give(6, o1)
            give(11, lse1)
            wait_weight(1)
            out_project(0, o1, 1)
            load_weight("ck", 1)
            wait_weight(0)
            v2[...] = dot_nn(text[...], weights[0]).astype(BF16)
            give(9, v2)
            load_weight("cq", 0)
        if number == 13:
            share(3, theirs.at[0], arrived.at[0]).wait()
            norm_share(1, add_stream(0, hidden, x2, x2_parts), 1, h2)
            give(14, x2_parts)
            wait_weight(1)
            k2[...] = dot_nn(text[...], weights[1]).astype(BF16)
            give(8, k2)
            load_weight("co", 1)
        if number == 14:
            get_share(1, h2)
            give(1, h2)
            wait_weight(0)
            project_rows(h2, weights.at[0], to(q2))
            give(7, q2)

            def body(pair, carry):
                pair_forward(pair, q2, k2, v2, o2, lse2, False)
                return carry

            lax.fori_loop(0, q2.shape[1] // 128, body, 0)
            give(10, o2)
            give(12, lse2)
        if number == 15:
            wait_weight(1)
            out_project(1, o2, 1)
        if number == 16:
            share(4, theirs.at[1], arrived.at[1]).wait()
            norm_share(2, add_stream(1, x2, x3), 2, h3)
            give(15, x3)
            load_weight("up", 0)
        if number == 17:
            get_share(2, h3)
            give(2, h3)
        for j in {17: (0,), 18: (1, 2), 19: (3,)}.get(number, ()):
            hidden_units(j)

    for number in range(len(chunks) + 5):
        turn(number)
        work(number)
    finish()
    for copy in (*pending, *active_copies(3)):
        copy.wait()


def forward_all(shards, chunks, hidden, text, cotangent):
    total, count = len(chunks), len(shards)
    dma, vmem = pltpu.SemaphoreType.DMA, pltpu.VMEM
    half, width = hidden.shape
    frames, part = 2 * half, shards[1].shape[1]
    anywhere = pl.BlockSpec(memory_space=pl.ANY)
    shape = jax.ShapeDtypeStruct
    kept = [
        *[((frames, width), BF16)] * 3,
        *[((frames, part), BF16)] * 4,
        ((frames, part), BF16),
        *[((text.shape[0], part), BF16)] * 2,
        ((frames, part), BF16),
        *[((16, frames), F32)] * 2,
    ]
    given = [*kept, ((shards[0].shape[0], width), F32), ((frames, width), BF16), ((half, width), F32)]
    given += [((frames, width), BF16), ((frames, 4 * part), BF16), ((frames, 4 * part), BF16)]
    held = [*kept, ((half, width), F32), ((half, width), F32)]
    outs = pl.pallas_call(
        functools.partial(forward_kernel, chunks, count),
        out_shape=[shape((4, 2, 2) + s.shape, s.dtype) for s in shards] + [shape(*g) for g in given],
        in_specs=[pl.BlockSpec(memory_space=vmem)] * count + [anywhere] * 3,
        out_specs=[anywhere] * (count + len(given)),
        scratch_shapes=[
            dma((total,)),
            dma,
            dma((total, 4)),
            dma((total, 4)),
            dma((total, 4)),
            dma((total, 4, 2)),
            *[vmem(*h) for h in held],
            vmem((4, 2, 2) + shards[0].shape, BF16),
            vmem((shards[0].shape[0], width), F32),
            vmem((2, width, part), BF16),
            vmem((half, width), BF16),
            vmem(text.shape, BF16),
            vmem((half, width), F32),
            vmem((2, half, width), BF16),
            vmem((2, half, width), BF16),
            vmem((frames, part), BF16),
            vmem((frames, part), BF16),
            vmem((frames, width), BF16),
            dma,
            dma((2, 16)),
            dma((3,)),
            dma((6,)),
            dma((6,)),
            dma((19,)),
        ],
        compiler_params=pltpu.CompilerParams(
            collective_id=0, has_side_effects=True, vmem_limit_bytes=VMEM_LIMIT
        ),
        name="forward",
    )(*shards, hidden, text, cotangent)
    return outs[:count], outs[count:]


XD, YD, XA, YA, XB, YB, UP, DOWN = range(8)


UNIT = 256
WIDTH_Z, WIDTH_A, SLOTS = 384, 128, 7
ROWS_L = 6
FIRST_L = (0, 12, 24, 27, 36, 39)
LOAD_L = ((2, 11), (3, 11), (4, 14), (5, 15))
FIRST_R = ((0, 12), (12, 24), (24, 27), (27, 30), (36, 39))
TEXT_UNITS = (30, 36)
SELF_UNITS = (39, 48)
UNITS = 48


def head_back(head, q_ref, k_ref, v_ref, do_ref, lse_ref, dq_ref, dkv_ref, bases, acc_k, acc_v, causal):
    pair, half = lax.div(head, 2), lax.rem(head, 2)
    cols = pl.ds(pl.multiple_of(pair * 128, 128), 128)
    lanes = [pl.ds(pl.multiple_of(pair * 128 + base, 128), 128) for base in bases]
    mine = head_lanes(half)
    length = k_ref.shape[0]
    acc_k[pl.ds(0, length), :] = jnp.zeros((length, 128), F32)
    acc_v[pl.ds(0, length), :] = jnp.zeros((length, 128), F32)
    block = 256 if causal else q_ref.shape[0]
    if causal:
        keep = lax.broadcasted_iota(jnp.int32, (block, block), 0) <= lax.broadcasted_iota(
            jnp.int32, (block, block), 1
        )

    def merged(ref, rows, lane, value):
        before = jnp.where(half == 0, 0.0, ref[rows, lane].astype(F32))
        ref[rows, lane] = (before + value).astype(BF16)

    for i in range(q_ref.shape[0] // block):
        rows = pl.ds(i * block, block)
        q = only(mine, q_ref[rows, cols])
        do = only(mine, do_ref[rows, cols])
        lse = lse_ref[pl.ds(head, 1), rows]
        parts = [(0, length, False)]
        if causal:
            parts = [(0, i * block, False)] * (i > 0) + [(i * block, block, True)]
        held, inner = [], 0.0
        for first, count, diagonal in parts:
            keys = pl.ds(first, count)
            soft = jnp.exp(dot_nt(k_ref[keys, cols], q) * score_scale - lse)
            if diagonal:
                soft = jnp.where(keep, soft, 0.0)
            slope = dot_nt(v_ref[keys, cols], do)
            inner = inner + jnp.sum(soft * slope, axis=0, keepdims=True)
            held.append((keys, soft, slope))
        grad_q = 0.0
        for keys, soft, slope in held:
            ds = (soft * (slope - inner)).astype(BF16)
            acc_v[keys, :] += dot_nn(soft.astype(BF16), do)
            acc_k[keys, :] += dot_nn(ds, q)
            grad_q = grad_q + dot_tn(ds, k_ref[keys, cols])
        merged(dq_ref, rows, lanes[0], jnp.where(mine, grad_q * score_scale, 0.0))
    everything = pl.ds(0, length)
    merged(dkv_ref, everything, lanes[1], acc_k[everything, :] * score_scale)
    merged(dkv_ref, everything, lanes[2], acc_v[everything, :])


def backward_kernel(*refs):
    (e3_h, h3_h, h2_h, h1_h, a_h, slope_h, o2_h, o1_h, text_h), refs = refs[:9], refs[9:]
    (q2_h, k2_h, v2_h, q1_h, k1_h, v1_h, x3_h, x2_h, x1_h), refs = refs[:9], refs[9:]
    (w_q, w_k, w_v, w_o, w_ck, w_cv, w_cq, w_co, w_up, w_down), refs = refs[:10], refs[10:]
    (lse2_ref, lse1_ref, norms), refs = refs[:3], refs[3:]
    (out, layer_out, grad_input, grad_text, norm_out), refs = refs[:5], refs[5:]
    (du_h, dq2_h, e2_h, e1_h), refs = refs[:4], refs[4:]
    (gz, ga, xdz, ydz, xaz, yaz, xbz, ybz, lnz), refs = refs[:9], refs[9:]
    (xda, yda, xaa, yaa, xba, yba, lna, oz, oa), refs = refs[:9], refs[9:]
    (lbuf, rbuf, text_v, dkv_v, k2_v, v2_v, pool, dqkv, acc_k, acc_v), refs = refs[:10], refs[10:]
    (acc, grad, theirs, arrived, weights, text_part, text_send, text_got), refs = refs[:8], refs[8:]
    (norm_grads, got), refs = refs[:2], refs[2:]
    (first_sem, l_sem, r_sem, out_sem, send_z, send_a, recv_z, recv_a), refs = refs[:8], refs[8:]
    (pool_sem, slope_sem, weight_sem, x_sem, keep_sem, share_send, share_recv, norm_send), refs = refs[:8], refs[8:]
    norm_recv, credit = refs
    lefts = (e3_h, h3_h, e2_h, h2_h, e1_h, h1_h)
    rights = (a_h, du_h, o2_h, dq2_h, o1_h)
    width_z, width_a, slots = WIDTH_Z, WIDTH_A, SLOTS
    total, width = UNITS // 2, WIDTH_Z + WIDTH_A
    x, y, z, core = my_place()
    xn, yn = 1 - x, 1 - y
    near = neighbours(x, y, z, core)
    right, across, up, down = near
    has_up, has_down = z < 3, z > 0
    degree = 2 + has_up.astype(jnp.int32) + has_down.astype(jnp.int32)
    chip = lax.axis_index("dp")
    other = (chip, 1 - core)
    partners = [other]
    for bit in (1, 2, 4, 8):
        partners.append((chip + bit * (1 - 2 * lax.rem(lax.div(chip, bit), 2)), core))
    barrier = pltpu.get_barrier_semaphore()
    signal_neighbours([barrier] * 4, near, has_up, has_down)
    for device in (other, partners[4]):
        pl.semaphore_signal(barrier, inc=1, device_id=device, device_id_type=MESH_IDS)
    pl.semaphore_wait(barrier, degree + 2)
    rows = gz.shape[4]
    low, high = pl.ds(0, rows // 2), pl.ds(rows // 2, rows // 2)

    def remote(src, dst, send_sem, recv_sem, device):
        return pltpu.make_async_remote_copy(
            src_ref=src,
            dst_ref=dst,
            send_sem=send_sem,
            recv_sem=recv_sem,
            device_id=device,
            device_id_type=MESH_IDS,
        )

    def arrived_at(ref, sem):
        remote(ref, ref, send_z.at[0], sem, right).wait_recv()

    def sent(ref, sem):
        remote(ref, ref, sem, recv_z.at[0, 0], right).wait_send()

    firsts = [
        pltpu.make_async_copy(src, dst, first_sem.at[n])
        for n, (src, dst) in enumerate(((text_h, text_v), (k2_h, k2_v), (v2_h, v2_v)))
    ]

    def left_copy(n):
        return pltpu.make_async_copy(lefts[n], lbuf.at[n % 2], l_sem.at[n % 2])

    def right_copies(c, which):
        unit = 2 * c + which
        place, sem = rbuf.at[lax.rem(c, 2), which], r_sem.at[lax.rem(c, 2), which]
        for source, (lo, hi) in zip((*rights, dqkv), (*FIRST_R, SELF_UNITS), strict=True):
            first = pl.multiple_of((unit - lo) * UNIT, UNIT)
            yield (
                (unit >= lo) & (unit < hi),
                pltpu.make_async_copy(source.at[:, pl.ds(first, UNIT)], place, sem),
            )

    def start_rights(c):
        for which in range(2):
            for cond, copy in right_copies(c, which):
                pl.when(cond)(copy.start)

    def store_unit(which, k, i, value):
        for yy in range(2):
            for xx in range(2):
                first = (yy * 2 + xx) * rows
                block = value[first : first + rows, :].astype(BF16)
                if which == 0:
                    gz[k, i, yy, xx, :, pl.ds(0, UNIT)] = block
                else:
                    gz[k, i, yy, xx, :, pl.ds(UNIT, width_z - UNIT)] = block[:, : width_z - UNIT]
                    ga[k, i, yy, xx] = block[:, width_z - UNIT :]

    def compute(c, k):
        for n in range(1, ROWS_L):
            pl.when(c == FIRST_L[n] // 2)(left_copy(n).wait)
        for which in range(2):
            unit = 2 * c + which
            text = (unit >= TEXT_UNITS[0]) & (unit < TEXT_UNITS[1])
            slot = lax.rem(sum((unit >= first).astype(jnp.int32) for first in FIRST_L) + 1, 2)

            @pl.when(text)
            def _():
                first = pl.multiple_of((unit - TEXT_UNITS[0]) * UNIT, UNIT)
                right_part = dkv_v[:, pl.ds(first, UNIT)]
                for i in range(4):
                    store_unit(which, k, i, dot_tn(text_v[:, pl.ds(i * 4 * rows, 4 * rows)], right_part))

            @pl.when(jnp.logical_not(text))
            def _():
                par = lax.rem(c, 2)
                pltpu.make_async_copy(rbuf.at[par, which], rbuf.at[par, which], r_sem.at[par, which]).wait()
                right_part = rbuf[par, which]
                for i in range(4):
                    left_part = lbuf[slot, :, pl.ds(i * 4 * rows, 4 * rows)]
                    store_unit(which, k, i, dot_tn(left_part, right_part))

        for n, at in LOAD_L:
            pl.when(c == at)(left_copy(n).start)
        pl.when(c + 1 < total)(lambda: start_rights(c + 1))

    def out_copies(c):
        o = lax.rem(c, 2)
        first = pl.multiple_of(c * width, 128)
        return (
            pltpu.make_async_copy(oz.at[o], out.at[:, pl.ds(first, width_z)], out_sem.at[o, 0]),
            pltpu.make_async_copy(
                oa.at[o], out.at[:, pl.ds(first + width_z, width_a)], out_sem.at[o, 1]
            ),
        )

    def plane_first(own, k, bufs, send_sem, recv):
        xd, yd, xa, ya = bufs
        remote(own(yn, xn, low), xd.at[k], send_sem.at[k], recv.at[k, XD], right).start()
        remote(own(yn, xn, high), yd.at[k], send_sem.at[k], recv.at[k, YD], across).start()
        remote(own(y, xn, low), xa.at[k], send_sem.at[k], recv.at[k, XA], right).start()
        remote(own(yn, x, high), ya.at[k], send_sem.at[k], recv.at[k, YA], across).start()

    def plane_second(add, k, bufs, send_sem, recv):
        xd, yd, xb, yb = bufs
        arrived_at(xd.at[k], recv.at[k, XD])
        add(xd, yn, x, low)
        remote(xd.at[k], yb.at[k], send_sem.at[k], recv.at[k, YB], across).start()
        arrived_at(yd.at[k], recv.at[k, YD])
        add(yd, y, xn, high)
        remote(yd.at[k], xb.at[k], send_sem.at[k], recv.at[k, XB], right).start()

    def above(buf, k, first, blocks):
        return buf.at[k, pl.ds(first + 1, blocks)]

    def below(buf, k, blocks):
        return buf.at[k, pl.ds(0, blocks)]

    def line_up(first, buf, add, k, send_sem, recv):
        blocks = 4 - first
        arrived_at(above(buf, k, first, blocks), recv.at[k, UP])
        if blocks > 1:
            for block in range(first + 1, 4):
                add(buf, block, block + 1)
            ref = above(buf, k, first + 1, blocks - 1)
            remote(ref, ref, send_sem.at[k], recv.at[k, UP], up).start()

    def line_down(last, buf, add, k, send_sem, recv):
        arrived_at(below(buf, k, last + 1), recv.at[k, DOWN])
        if last > 0:
            for block in range(last):
                add(buf, block, block)
            ref = below(buf, k, last)
            remote(ref, ref, send_sem.at[k], recv.at[k, DOWN], down).start()

    def add_a(k):
        def add(buf, block, at):
            for yy in range(2):
                for xx in range(2):
                    buf[k, at, yy, xx] = total_of(
                        buf[k, at, yy, xx], ga[k, block, yy, xx]
                    ).astype(BF16)

        return add

    def add_z(k):
        def add(buf, block, at):
            buf[k, at] = total_of(buf[k, at], gz[k, block, y, x]).astype(BF16)

        return add

    def begin(c, k):
        @pl.when(c >= slots)
        def _():
            pl.semaphore_wait(credit.at[0], 1)
            pl.semaphore_wait(credit.at[1], 1)
            pl.when(has_up)(lambda: pl.semaphore_wait(credit.at[2], 1))
            pl.when(has_down)(lambda: pl.semaphore_wait(credit.at[3], 1))

        plane_first(
            lambda yy, xx, half: gz.at[k, :, yy, xx, half, :], k, (xdz, ydz, xaz, yaz), send_z, recv_z
        )

        @pl.when(z == 0)
        def _():
            ref = pl.ds(1, 3)
            remote(ga.at[k, ref], above(lna, k, 1, 3), send_a.at[k], recv_a.at[k, UP], up).start()

        @pl.when(z == 3)
        def _():
            ref = pl.ds(0, 3)
            remote(ga.at[k, ref], below(lna, k, 3), send_a.at[k], recv_a.at[k, DOWN], down).start()

    def second(c, k):
        def add(buf, yy, xx, half):
            for block in range(4):
                buf[k, block] = total_of(buf[k, block], gz[k, block, yy, xx, half, :]).astype(BF16)

        plane_second(add, k, (xdz, ydz, xbz, ybz), send_z, recv_z)
        pl.when(z == 1)(lambda: line_up(1, lna, add_a(k), k, send_a, recv_a))
        pl.when(z == 2)(lambda: line_down(2, lna, add_a(k), k, send_a, recv_a))

    def third(c, k):
        for buf, kind in ((xaz, XA), (yaz, YA), (xbz, XB), (ybz, YB)):
            arrived_at(buf.at[k], recv_z.at[k, kind])
        for block in range(4):
            for half, one, two in ((low, xaz, ybz), (high, yaz, xbz)):
                gz[k, block, y, x, half, :] = total_of(
                    gz[k, block, y, x, half, :], one[k, block], two[k, block]
                ).astype(BF16)

        @pl.when(z == 0)
        def _():
            ref = pl.ds(1, 3)
            remote(
                gz.at[k, ref, y, x], above(lnz, k, 1, 3), send_z.at[k], recv_z.at[k, UP], up
            ).start()

        @pl.when(z == 3)
        def _():
            ref = pl.ds(0, 3)
            remote(
                gz.at[k, ref, y, x], below(lnz, k, 3), send_z.at[k], recv_z.at[k, DOWN], down
            ).start()

        pl.when(z == 2)(lambda: line_up(2, lna, add_a(k), k, send_a, recv_a))
        pl.when(z == 1)(lambda: line_down(1, lna, add_a(k), k, send_a, recv_a))

    def fourth(c, k):
        pl.when(z == 1)(lambda: line_up(1, lnz, add_z(k), k, send_z, recv_z))
        pl.when(z == 2)(lambda: line_down(2, lnz, add_z(k), k, send_z, recv_z))
        pl.when(z == 3)(lambda: line_up(3, lna, None, k, send_a, recv_a))
        pl.when(z == 0)(lambda: line_down(0, lna, None, k, send_a, recv_a))
        for shift, exists in ((1, has_down), (0, has_up)):

            @pl.when(exists)
            def _():
                for yy in range(2):
                    for xx in range(2):
                        ga[k, z, yy, xx] = total_of(
                            ga[k, z, yy, xx], lna[k, z + shift, yy, xx]
                        ).astype(BF16)

        plane_first(
            lambda yy, xx, half: ga.at[k, z, yy, xx, half, :], k, (xda, yda, xaa, yaa), send_a, recv_a
        )

    def fifth(c, k):
        pl.when(z == 2)(lambda: line_up(2, lnz, add_z(k), k, send_z, recv_z))
        pl.when(z == 1)(lambda: line_down(1, lnz, add_z(k), k, send_z, recv_z))

        def add(buf, yy, xx, half):
            buf[k] = total_of(buf[k], ga[k, z, yy, xx, half, :]).astype(BF16)

        plane_second(add, k, (xda, yda, xba, yba), send_a, recv_a)

    def finish(c, k):
        pl.when(z == 3)(lambda: line_up(3, lnz, None, k, send_z, recv_z))
        pl.when(z == 0)(lambda: line_down(0, lnz, None, k, send_z, recv_z))
        o = lax.rem(c, 2)

        @pl.when(c >= 2)
        def _():
            for copy in out_copies(c - 2):
                copy.wait()

        oz[o] = gz[k, z, y, x].astype(F32)
        for shift, exists in ((1, has_down), (0, has_up)):

            @pl.when(exists)
            def _():
                oz[o] = oz[o] + lnz[k, z + shift].astype(F32)

        for buf, kind in ((xaa, XA), (yaa, YA), (xba, XB), (yba, YB)):
            arrived_at(buf.at[k], recv_a.at[k, kind])
        oa[o, low, :] = total_of(ga[k, z, y, x, low, :], xaa[k], yba[k])
        oa[o, high, :] = total_of(ga[k, z, y, x, high, :], yaa[k], xba[k])
        for copy in out_copies(c):
            copy.start()
        for buf in (xdz, ydz, xaz, yaz, xbz, ybz):
            sent(buf.at[k], send_z.at[k])
        for buf in (xda, yda, xaa, yaa, xba, yba):
            sent(buf.at[k], send_a.at[k])
        for step in range(3):

            @pl.when(z == step)
            def _():
                sent(above(lnz, k, step + 1, 3 - step), send_z.at[k])
                sent(above(lna, k, step + 1, 3 - step), send_a.at[k])

            @pl.when(z == 3 - step)
            def _():
                sent(below(lnz, k, 3 - step), send_z.at[k])
                sent(below(lna, k, 3 - step), send_a.at[k])

        @pl.when(c < total - slots)
        def _():
            signal_neighbours([credit.at[i] for i in (0, 1, 3, 2)], near, has_up, has_down)

    frames, features = e3_h.shape
    part, half_rows = pool.shape[2], frames // 2
    heads = part // HEAD_DIM
    own_rows = pl.ds(pl.multiple_of(core * half_rows, half_rows), half_rows)
    wide = pl.ds(0, features)
    slope = dqkv.at[:, pl.ds(features, part)]
    block = 256

    def columns(n):
        return pl.ds(pl.multiple_of(n * part, part), part)

    def weight_copy(slot, ref, n=0):
        return pltpu.make_async_copy(ref.at[:, columns(n)], weights.at[slot], weight_sem.at[slot])

    def use(slot):
        weight_copy(slot, w_q).wait()

    def pool_copy(n, ref, m=0):
        return pltpu.make_async_copy(ref.at[:, columns(m)], pool.at[n], pool_sem.at[n])

    def slope_copy(n):
        return pltpu.make_async_copy(slope_h.at[:, columns(n)], slope, slope_sem)

    def keep_copy(n, src, dst):
        return pltpu.make_async_copy(src, dst, keep_sem.at[n])

    def du_copy(n):
        return keep_copy(0, pool.at[n], du_h.at[:, columns(n)])

    def to_other(n, src, dst):
        return remote(src, dst, share_send.at[n], share_recv.at[n], other)

    def active_copy(whose, n):
        lines = pl.ds(pl.multiple_of(whose * half_rows, half_rows), half_rows)
        return keep_copy(0, a_h.at[lines, pl.ds(n * 2 * part, 2 * part)], theirs)

    def share_sum(n):
        return to_other(n, theirs, arrived.at[n % 2])

    def share_branch(n):
        ref = dqkv.at[own_rows, wide]
        return to_other(4 + n, ref, ref)

    def multiply(whose, source, slot, fresh):
        for first in range(0, half_rows, block):
            rows_of = pl.ds(pl.multiple_of(whose * half_rows + first, block), block)
            value = dot_nt(source(rows_of), weights[slot])
            lines = pl.ds(first, block)
            acc[lines, :] = value if fresh else acc[lines, :] + value

    def pooled(n):
        return lambda rows_of: pool[n, rows_of, :]

    def headed(n):
        return lambda rows_of: dqkv[rows_of, pl.ds(n * part, part)]

    def send_sum(n):
        for first in range(0, half_rows, block):
            lines = pl.ds(first, block)
            theirs[lines, :] = acc[lines, :].astype(BF16)
        share_sum(n).start()

    def norm_back(kind, n, load, before, store):
        step = 64
        gain = norms[2 * kind : 2 * kind + 1, :]

        def body(i, sums):
            first = pl.multiple_of(i * step, step)
            lines = pl.ds(first, step)
            value = load(i, lines)
            offset = value - jnp.mean(value, axis=-1, keepdims=True)
            scale = lax.rsqrt(jnp.mean(offset * offset, axis=-1, keepdims=True) + norm_eps)
            unit = offset * scale
            slope_in = acc[lines, :] + arrived[n % 2, lines, :].astype(F32)
            scaled = slope_in * gain
            inner = jnp.mean(scaled * unit, axis=-1, keepdims=True)
            change = scale * (scaled - jnp.mean(scaled, axis=-1, keepdims=True) - unit * inner)
            store(first, lines, before(first, lines) + change)
            return (
                sums[0] + jnp.sum(slope_in * unit, axis=0, keepdims=True),
                sums[1] + jnp.sum(slope_in, axis=0, keepdims=True),
            )

        zero = jnp.zeros((1, features), F32)
        gains, shifts = lax.fori_loop(0, half_rows // step, body, (zero, zero))
        norm_grads[2 * kind : 2 * kind + 1, :] = gains
        norm_grads[2 * kind + 1 : 2 * kind + 2, :] = shifts

    x2_copy = pltpu.make_async_copy(x2_h, lbuf.at[0], x_sem)

    def store_branch(first, lines, value):
        grad[lines, :] = value
        dqkv[pl.ds(pl.multiple_of(core * half_rows + first, 64), 64), wide] = value.astype(BF16)

    def project_to(n, slot):
        for first in range(0, frames, block):
            lines = pl.ds(first, block)
            pool[n, lines, :] = dot_nn(dqkv[lines, wide], weights[slot]).astype(BF16)

    def feed_forward(j):
        use(0)
        slope_copy(j).wait()
        for first in range(0, frames, block):
            lines = pl.ds(first, block)
            value = dot_nn(lbuf[0, lines, :], weights[0])
            pool[j, lines, :] = (
                value * dqkv[lines, pl.ds(features, part)].astype(F32)
            ).astype(BF16)

        @pl.when(j > 0)
        def _():
            du_copy(j - 1).wait()

        du_copy(j).start()

        @pl.when(j < 3)
        def _():
            weight_copy(0, w_down, j + 1).start()
            slope_copy(j + 1).start()

        pl.when(j == 3)(lambda: weight_copy(0, w_up, 0).start())
        use(1)
        multiply(1 - core, pooled(j), 1, False)
        pl.when(j < 3)(lambda: weight_copy(1, w_up, j + 1).start())
        pl.when(j == 3)(lambda: send_sum(0))

    def turn_4():
        du_copy(3).wait()
        keep_copy(3, x3_h, grad).start()
        multiply(core, pooled(3), 1, True)
        weight_copy(1, w_up, 1).start()
        use(0)
        multiply(core, pooled(0), 0, False)
        weight_copy(0, w_up, 2).start()

    def turn_5():
        use(1)
        multiply(core, pooled(1), 1, False)
        weight_copy(1, w_cq).start()
        use(0)
        multiply(core, pooled(2), 0, False)
        weight_copy(0, w_co).start()

    def turn_6():
        pool_copy(0, q2_h).start()
        share_sum(0).wait()
        keep_copy(3, x3_h, grad).wait()
        norm_back(
            2,
            0,
            lambda i, lines: grad[lines, :],
            lambda first, lines: lbuf[
                0, pl.ds(pl.multiple_of(core * half_rows + first, 64), 64), :
            ].astype(F32),
            store_branch,
        )
        share_branch(0).start()

    def turn_7():
        share_branch(0).wait()
        x2_copy.start()
        keep_copy(1, dqkv.at[:, wide], e2_h).start()
        use(0)
        project_to(1, 0)
        weight_copy(0, w_ck).start()

    def turn_8():
        pool_copy(0, q2_h).wait()
        for copy in firsts:
            copy.wait()

        def body(head, carry):
            head_back(
                head,
                pool.at[0],
                k2_v,
                v2_v,
                pool.at[1],
                lse2_ref,
                pool.at[2],
                dkv_v,
                (0, 0, part),
                acc_k,
                acc_v,
                False,
            )
            return carry

        lax.fori_loop(0, heads, body, 0, unroll=2)
        keep_copy(1, dqkv.at[:, wide], e2_h).wait()
        keep_copy(0, pool.at[2], dq2_h).start()
        use(0)
        text_part[...] = dot_nt(dkv_v[:, pl.ds(0, part)], weights[0])
        weight_copy(0, w_cv).start()

    def text_columns(whose):
        count = features // 2
        return pl.ds(pl.multiple_of(whose * count, count), count)

    def text_share():
        return to_other(6, text_send, text_got)

    def turn_9():
        keep_copy(0, pool.at[2], dq2_h).wait()
        use(0)
        text_part[...] += dot_nt(dkv_v[:, pl.ds(part, part)], weights[0])
        text_send[...] = text_part[:, text_columns(1 - core)].astype(BF16)
        text_share().start()
        weight_copy(0, w_o).start()
        use(1)
        multiply(1 - core, pooled(2), 1, True)
        send_sum(1)

    def turn_10():
        multiply(core, pooled(2), 1, True)
        for n, ref in enumerate((q1_h, k1_h, v1_h)):
            pool_copy(n, ref).start()
        share_sum(1).wait()
        x2_copy.wait()
        norm_back(
            1,
            1,
            lambda i, lines: lbuf[0, lines, :].astype(F32)
            + lbuf[0, pl.ds(pl.multiple_of(half_rows + i * 64, 64), 64), :].astype(F32),
            lambda first, lines: grad[lines, :],
            store_branch,
        )
        share_branch(1).start()
        text_share().wait()
        text_part[:, pl.ds(0, features // 2)] = text_part[:, text_columns(core)] + text_got[
            ...
        ].astype(F32)
        keep_copy(2, text_part.at[:, pl.ds(0, features // 2)], grad_text).start()

    def turn_11():
        share_branch(1).wait()
        keep_copy(1, dqkv.at[:, wide], e1_h).start()
        use(0)
        project_to(3, 0)
        weight_copy(0, w_down, 0).start()
        weight_copy(1, w_down, 1).start()
        active_copy(1 - core, 0).start()

    def turn_12():
        keep_copy(1, dqkv.at[:, wide], e1_h).wait()
        for n, ref in enumerate((q1_h, k1_h, v1_h)):
            pool_copy(n, ref).wait()

    def self_head(head):
        head_back(
            head,
            pool.at[0],
            pool.at[1],
            pool.at[2],
            pool.at[3],
            lse1_ref,
            dqkv,
            dqkv,
            (0, part, 2 * part),
            acc_k,
            acc_v,
            True,
        )

    def held(n):
        return lambda rows_of: theirs[rows_of, pl.ds(n * part, part)]

    def turn_13():
        active_copy(core, 0).wait()
        use(0)
        multiply(0, held(0), 0, True)
        weight_copy(0, w_down, 2).start()
        use(1)
        multiply(0, held(1), 1, False)
        weight_copy(1, w_down, 3).start()
        active_copy(1 - core, 1).start()

    def turn_14():
        active_copy(core, 0).wait()
        use(0)
        multiply(0, held(0), 0, False)
        use(1)
        multiply(0, held(1), 1, False)
        send_sum(3)

    def turn_15():
        share_sum(3).wait()
        keep_copy(3, x3_h, acc).start()
        active_copy(core, 1).start()

    def turn_16():
        active_copy(core, 0).wait()
        keep_copy(3, x3_h, acc).wait()
        multiply(0, held(0), 0, False)
        weight_copy(0, w_down, 0).start()
        multiply(0, held(1), 1, False)
        weight_copy(1, w_down, 1).start()
        active_copy(core, 0).start()

    def turn_17():
        active_copy(core, 0).wait()
        use(0)
        multiply(0, held(0), 0, False)
        weight_copy(0, w_q).start()
        use(1)
        multiply(0, held(1), 1, False)
        weight_copy(1, w_k).start()

        def body(i, carry):
            lines = pl.ds(pl.multiple_of(i * 64, 64), 64)
            theirs[lines, :] = (acc[lines, :] + arrived[1, lines, :].astype(F32)).astype(BF16)
            return carry

        lax.fori_loop(0, half_rows // 64, body, 0)
        keep_copy(0, theirs, layer_out).start()

    def turn_18():
        keep_copy(0, theirs, layer_out).wait()
        use(0)
        multiply(1 - core, headed(0), 0, True)
        weight_copy(0, w_v).start()
        use(1)
        multiply(1 - core, headed(1), 1, False)

    def turn_19():
        use(0)
        multiply(1 - core, headed(2), 0, False)
        send_sum(2)
        multiply(core, headed(2), 0, True)
        multiply(core, headed(1), 1, False)
        weight_copy(1, w_q).start()

    def turn_20():
        use(1)
        multiply(core, headed(0), 1, False)
        share_sum(2).wait()
        keep_copy(1, x1_h, theirs).start()

    def turn_21():
        keep_copy(1, x1_h, theirs).wait()

        def store(first, lines, value):
            grad[lines, :] = value

        norm_back(
            0,
            2,
            lambda i, lines: theirs[lines, :].astype(F32),
            lambda first, lines: grad[lines, :],
            store,
        )
        keep_copy(3, grad, grad_input).start()

    def norm_copy(step):
        return remote(
            got.at[2 * step],
            got.at[2 * step + 1],
            norm_send.at[step],
            norm_recv.at[step],
            partners[step],
        )

    def norm_sum(step):
        if step == 0:
            got[0] = norm_grads[...]
        else:
            norm_copy(step - 1).wait()
            got[2 * step] = got[2 * step - 2] + got[2 * step - 1]
        if step < len(partners):
            norm_copy(step).start()
        else:
            keep_copy(1, got.at[2 * step], norm_out).start()

    chain = {
        4: turn_4,
        5: turn_5,
        6: turn_6,
        7: turn_7,
        8: turn_8,
        9: turn_9,
        10: turn_10,
        11: turn_11,
        13: turn_13,
        14: turn_14,
        15: turn_15,
        16: turn_16,
        17: turn_17,
        18: turn_18,
        19: turn_19,
        20: turn_20,
        21: turn_21,
    }
    stages = (begin, second, third, fourth, fifth, finish)
    left_copy(0).start()
    weight_copy(0, w_down, 0).start()
    slope_copy(0).start()
    start_rights(jnp.int32(0))
    weight_copy(1, w_up, 0).start()
    left_copy(1).start()
    for copy in firsts:
        copy.start()
    for first in range(0, half_rows, block):
        acc[pl.ds(first, block), :] = jnp.zeros((block, features), F32)
    norm_grads[...] = jnp.zeros_like(norm_grads)
    left_copy(0).wait()

    def body(turn, carry):
        for step, stage in enumerate(stages):
            c = turn - step - 1

            @pl.when((c >= 0) & (c < total))
            def _():
                stage(c, lax.rem(c, slots))

        pl.when(turn < total)(lambda: compute(turn, lax.rem(turn, slots)))
        pl.when(turn < 4)(lambda: feed_forward(turn))
        for number, fn in chain.items():
            pl.when(turn == number)(fn)
        pl.when(turn == 12)(turn_12)

        @pl.when((turn >= 12) & (turn < 18))
        def _():
            def both(head, carry):
                self_head(head)
                return carry

            first = lax.div(heads, 6) * (turn - 12)
            lax.fori_loop(first, first + heads // 6, both, 0)

        for step in range(len(partners) + 1):
            pl.when(turn == 22 + step)(functools.partial(norm_sum, step))
        return carry

    lax.fori_loop(0, total + len(stages), body, 0)
    for c in (total - 2, total - 1):
        for copy in out_copies(jnp.int32(c)):
            copy.wait()
    keep_copy(3, grad, grad_input).wait()
    keep_copy(1, got.at[2 * len(partners)], norm_out).wait()
    keep_copy(2, text_part.at[:, pl.ds(0, features // 2)], grad_text).wait()


def backward_all(arrays, small):
    frames, width = arrays[0].shape
    text = arrays[8]
    rows, half, part = width // 16, frames // 2, arrays[9].shape[1]
    dma, vmem, shape = pltpu.SemaphoreType.DMA, pltpu.VMEM, jax.ShapeDtypeStruct

    def buffer(*dims):
        return vmem((SLOTS,) + dims, BF16)

    anywhere = pl.BlockSpec(memory_space=pl.ANY)
    return pl.pallas_call(
        backward_kernel,
        out_shape=[
            shape((rows, UNITS * UNIT), F32),
            shape((half, width), BF16),
            shape((half, width), F32),
            shape((text.shape[0], width // 2), F32),
            shape((8, width), F32),
            shape((frames, 4 * part), BF16),
            shape((frames, part), BF16),
            shape((frames, width), BF16),
            shape((frames, width), BF16),
        ],
        in_specs=[anywhere] * len(arrays) + [pl.BlockSpec(memory_space=vmem)] * len(small),
        out_specs=[anywhere] * 9,
        scratch_shapes=[
            buffer(4, 2, 2, rows, WIDTH_Z),
            buffer(4, 2, 2, rows, WIDTH_A),
            *[buffer(4, rows // 2, WIDTH_Z)] * 6,
            buffer(5, rows, WIDTH_Z),
            *[buffer(rows // 2, WIDTH_A)] * 6,
            buffer(5, 2, 2, rows, WIDTH_A),
            vmem((2, rows, WIDTH_Z), F32),
            vmem((2, rows, WIDTH_A), F32),
            vmem((2, frames, width), BF16),
            vmem((2, 2, frames, UNIT), BF16),
            vmem(text.shape, BF16),
            vmem((text.shape[0], 2 * part), BF16),
            *[vmem((text.shape[0], part), BF16)] * 2,
            vmem((4, frames, part), BF16),
            vmem((frames, 3 * part), BF16),
            *[vmem((frames, 128), F32)] * 2,
            *[vmem((half, width), F32)] * 2,
            vmem((half, width), BF16),
            vmem((2, half, width), BF16),
            vmem((2, width, part), BF16),
            vmem((text.shape[0], width), F32),
            *[vmem((text.shape[0], width // 2), BF16)] * 2,
            vmem((8, width), F32),
            vmem((11, 8, width), F32),
            dma((3,)),
            dma((2,)),
            dma((2, 2)),
            dma((2, 2)),
            dma((SLOTS,)),
            dma((SLOTS,)),
            dma((SLOTS, 8)),
            dma((SLOTS, 8)),
            dma((4,)),
            dma,
            dma((2,)),
            dma,
            dma((4,)),
            dma((7,)),
            dma((7,)),
            dma((5,)),
            dma((5,)),
            pltpu.SemaphoreType.REGULAR((4,)),
        ],
        compiler_params=pltpu.CompilerParams(
            collective_id=1, has_side_effects=True, vmem_limit_bytes=VMEM_LIMIT
        ),
        name="backward",
    )(*arrays, *small)


def gather_plan(columns):
    chunks, since = [], 0
    for array, width in enumerate(columns):
        size = 768 if width % 768 == 0 else width
        for first in range(0, width, size):
            since += 1
            family = "A" if since % 5 == 3 and size == 768 else "Z"
            chunks.append((array, first, size, family))
    return tuple(chunks)


def local_fast(
    hidden_in,
    text_states,
    norm1_gain,
    norm1_bias,
    self_query,
    self_key,
    self_value,
    self_out,
    norm2_gain,
    norm2_bias,
    cross_query,
    cross_key,
    cross_value,
    cross_out,
    norm3_gain,
    norm3_bias,
    hidden_up,
    hidden_down,
    cotangent,
):
    width = norm1_gain.shape[0] * 16
    norms = jnp.stack([norm1_gain, norm1_bias, norm2_gain, norm2_bias, norm3_gain, norm3_bias])
    norms = jnp.pad(norms, ((0, 26), (0, 128 - norms.shape[1])))
    shards = (
        norms,
        self_query.T,
        self_key.T,
        self_value.T,
        self_out,
        cross_key.T,
        cross_value.T,
        cross_query.T,
        cross_out,
        hidden_up.T,
        hidden_down,
    )
    gathered, kept = forward_all(
        shards,
        gather_plan([s.shape[1] for s in shards]),
        hidden_in[0],
        text_states[0],
        cotangent[0],
    )
    w_q, w_k, w_v, w_o, w_ck, w_cv, w_cq, w_co, w_up, w_down = [
        g.reshape(width, g.shape[-1]) for g in gathered[1:]
    ]
    normed_one, normed_two, normed_three = kept[:3]
    query_one, key_one, value_one, attended_one = kept[3:7]
    query_two, key_two, value_two, attended_two = kept[7:11]
    logsum_one, logsum_two, norms, stream_two, stream_three, branch, active, slope = kept[11:]
    summed, layer_out, grad_input, grad_text, norm_sums, *_ = backward_all(
        (
            *(branch, normed_three, normed_two, normed_one),
            *(active, slope, attended_two, attended_one, text_states[0]),
            *(query_two, key_two, value_two, query_one, key_one, value_one),
            *(stream_three, stream_two, hidden_in[0]),
            *(w_q, w_k, w_v, w_o, w_ck, w_cv, w_cq, w_co, w_up, w_down),
        ),
        (logsum_two, logsum_one, norms),
    )
    rows, part = width // 16, query_one.shape[1]
    norm_sums = lax.dynamic_slice_in_dim(norm_sums, lax.axis_index("dp") * rows, rows, 1)
    columns = [hidden_down.shape[1]] * 2 + [part] * 8
    pieces, first = [], 0
    for count in columns:
        pieces.append(summed[:, first : first + count])
        first += count
    down, up, out_cross, query_cross, key_cross, value_cross, out_self, query, key, value = pieces
    return (
        layer_out[None],
        grad_input[None],
        grad_text[None],
        norm_sums[0],
        norm_sums[1],
        query.T,
        key.T,
        value.T,
        out_self,
        norm_sums[2],
        norm_sums[3],
        query_cross.T,
        key_cross.T,
        value_cross.T,
        out_cross,
        norm_sums[4],
        norm_sums[5],
        up.T,
        down,
    )


def solution(mesh):
    placed = (
        P("dp", "tensor", None),
        P("dp", None, None),
        P("dp"),
        P("dp"),
        P("tensor", "dp"),
        P("tensor", "dp"),
        P("tensor", "dp"),
        P("dp", "tensor"),
        P("dp"),
        P("dp"),
        P("tensor", "dp"),
        P("tensor", "dp"),
        P("tensor", "dp"),
        P("dp", "tensor"),
        P("dp"),
        P("dp"),
        P("tensor", "dp"),
        P("dp", "tensor"),
        P("dp", "tensor", None),
    )
    fast = dict(mesh.shape) == {"dp": 16, "tensor": 2}
    return jax.shard_map(
        local_fast if fast else local_generic,
        mesh=mesh,
        in_specs=placed,
        out_specs=(
            P("dp", "tensor", None),
            P("dp", "tensor", None),
            P("dp", None, "tensor"),
            P("dp"),
            P("dp"),
            P("tensor", "dp"),
            P("tensor", "dp"),
            P("tensor", "dp"),
            P("dp", "tensor"),
            P("dp"),
            P("dp"),
            P("tensor", "dp"),
            P("tensor", "dp"),
            P("tensor", "dp"),
            P("dp", "tensor"),
            P("dp"),
            P("dp"),
            P("tensor", "dp"),
            P("dp", "tensor"),
        ),
        check_vma=False,
    )
```

```python
import functools

import jax
import jax.numpy as jnp
from jax import lax
from jax.experimental import pallas as pl
from jax.experimental.pallas import tpu as pltpu
from jax.sharding import PartitionSpec as P

HEAD_DIM = 64


norm_eps = 1e-05
score_scale = 0.125


def layer_norm(values, gain, shift):
    centre = jnp.mean(values, axis=-1, keepdims=True)
    offset = values - centre
    spread = jnp.mean(offset * offset, axis=-1, keepdims=True)
    return offset * lax.rsqrt(spread + norm_eps) * gain + shift


def gelu_exact(values):
    return jax.nn.gelu(values, approximate=False)


def project(row_data, weight):
    return jnp.einsum("cli,oi->clo", row_data, weight, preferred_element_type=jnp.float32)


def split_heads(values):
    return values.reshape(values.shape[0], values.shape[1], -1, HEAD_DIM)


def flatten_heads(values):
    return values.reshape(values.shape[0], values.shape[1], -1)


def causal_keep(first_row, count, length):
    row_ids = first_row + lax.broadcasted_iota(jnp.int32, (count, length), 0)
    col_ids = lax.broadcasted_iota(jnp.int32, (count, length), 1)
    return col_ids <= row_ids


def block_scores(queries, key_rows, first_row, block_rows, key_end, causal):
    scores = (
        jnp.einsum(
            "cqhe,ckhe->chqk",
            queries[:, first_row : first_row + block_rows],
            key_rows[:, :key_end],
            preferred_element_type=jnp.float32,
        )
        * score_scale
    )
    if causal:
        scores = jnp.where(causal_keep(first_row, block_rows, key_end), scores, -1e30)
    return scores


def attend(queries, key_rows, val_rows, causal):
    length = queries.shape[1]
    block_rows = min(512, length)
    outputs = []
    log_sums = []
    for block_num in range(length // block_rows):
        first_row = block_num * block_rows
        key_end = first_row + block_rows if causal else key_rows.shape[1]
        scores = block_scores(queries, key_rows, first_row, block_rows, key_end, causal)
        row_peak = jnp.max(scores, axis=-1, keepdims=True)
        exp_scores = jnp.exp(scores - row_peak)
        row_total = jnp.sum(exp_scores, axis=-1, keepdims=True)
        soft_weights = (exp_scores / row_total).astype(jnp.bfloat16)
        outputs.append(
            jnp.einsum(
                "chqk,ckhe->cqhe",
                soft_weights,
                val_rows[:, :key_end],
                preferred_element_type=jnp.float32,
            ).astype(jnp.bfloat16)
        )
        log_sums.append((row_peak + jnp.log(row_total))[..., 0])
    return (jnp.concatenate(outputs, axis=1), jnp.concatenate(log_sums, axis=2))


def attend_back(queries, key_rows, val_rows, grad_out, log_sums, causal):
    length = queries.shape[1]
    block_rows = min(512, length)
    grad_keys = jnp.zeros(key_rows.shape, jnp.float32)
    grad_vals = jnp.zeros(val_rows.shape, jnp.float32)
    grad_queries = []
    for block_num in range(length // block_rows):
        first_row = block_num * block_rows
        key_end = first_row + block_rows if causal else key_rows.shape[1]
        query_blk = queries[:, first_row : first_row + block_rows]
        grad_blk = grad_out[:, first_row : first_row + block_rows]
        scores = block_scores(queries, key_rows, first_row, block_rows, key_end, causal)
        soft = jnp.exp(scores - log_sums[:, :, first_row : first_row + block_rows, None])
        grad_soft = jnp.einsum(
            "cqhe,ckhe->chqk", grad_blk, val_rows[:, :key_end], preferred_element_type=jnp.float32
        )
        grad_vals = grad_vals.at[:, :key_end].add(
            jnp.einsum(
                "chqk,cqhe->ckhe",
                soft.astype(jnp.bfloat16),
                grad_blk,
                preferred_element_type=jnp.float32,
            )
        )
        inner = jnp.sum(soft * grad_soft, axis=-1, keepdims=True)
        grad_scores = (soft * (grad_soft - inner)).astype(jnp.bfloat16)
        grad_queries.append(
            jnp.einsum(
                "chqk,ckhe->cqhe",
                grad_scores,
                key_rows[:, :key_end],
                preferred_element_type=jnp.float32,
            )
            * score_scale
        )
        grad_keys = grad_keys.at[:, :key_end].add(
            jnp.einsum(
                "chqk,cqhe->ckhe", grad_scores, query_blk, preferred_element_type=jnp.float32
            )
            * score_scale
        )
    return (jnp.concatenate(grad_queries, axis=1), grad_keys, grad_vals)


def gather_rows(values):
    return lax.all_gather(values, "tensor", axis=1, tiled=True)


def scatter_rows(values):
    return lax.psum_scatter(values, "tensor", scatter_dimension=1, tiled=True)


def gather_grads(values):
    return lax.all_gather(values, "tensor", axis=1, tiled=True)


def scatter_grads(values):
    return lax.psum_scatter(
        values.astype(jnp.bfloat16), "tensor", scatter_dimension=1, tiled=True
    ).astype(jnp.float32)


def heads_grads(grad_branch, attended, out_weight):
    grad_out_proj = jnp.einsum(
        "clo,cla->oa", grad_branch, flatten_heads(attended), preferred_element_type=jnp.float32
    )
    grad_attended = split_heads(
        jnp.einsum(
            "clo,oa->cla", grad_branch, out_weight, preferred_element_type=jnp.float32
        ).astype(jnp.bfloat16)
    )
    return (grad_out_proj, grad_attended)


def weight_grad(grad_rows, source_rows):
    return jnp.einsum("cla,cli->ai", grad_rows, source_rows, preferred_element_type=jnp.float32)


def input_grad(grad_rows, weight):
    return jnp.einsum("cla,ai->cli", grad_rows, weight, preferred_element_type=jnp.float32)


def local_generic(
    hidden_in,
    text_states,
    norm1_gain,
    norm1_bias,
    self_query,
    self_key,
    self_value,
    self_out,
    norm2_gain,
    norm2_bias,
    cross_query,
    cross_key,
    cross_value,
    cross_out,
    norm3_gain,
    norm3_bias,
    hidden_up,
    hidden_down,
    cotangent,
):
    full_weights = (
        lax.all_gather(norm1_gain, "dp", axis=0, tiled=True),
        lax.all_gather(norm1_bias, "dp", axis=0, tiled=True),
        lax.all_gather(self_query, "dp", axis=1, tiled=True),
        lax.all_gather(self_key, "dp", axis=1, tiled=True),
        lax.all_gather(self_value, "dp", axis=1, tiled=True),
        lax.all_gather(self_out, "dp", axis=0, tiled=True),
        lax.all_gather(norm2_gain, "dp", axis=0, tiled=True),
        lax.all_gather(norm2_bias, "dp", axis=0, tiled=True),
        lax.all_gather(cross_query, "dp", axis=1, tiled=True),
        lax.all_gather(cross_key, "dp", axis=1, tiled=True),
        lax.all_gather(cross_value, "dp", axis=1, tiled=True),
        lax.all_gather(cross_out, "dp", axis=0, tiled=True),
        lax.all_gather(norm3_gain, "dp", axis=0, tiled=True),
        lax.all_gather(norm3_bias, "dp", axis=0, tiled=True),
        lax.all_gather(hidden_up, "dp", axis=1, tiled=True),
        lax.all_gather(hidden_down, "dp", axis=0, tiled=True),
    )
    gain_self = full_weights[0].astype(jnp.float32)
    bias_self = full_weights[1].astype(jnp.float32)
    gain_cross = full_weights[6].astype(jnp.float32)
    bias_cross = full_weights[7].astype(jnp.float32)
    gain_ffn = full_weights[12].astype(jnp.float32)
    bias_ffn = full_weights[13].astype(jnp.float32)
    stream_one = hidden_in.astype(jnp.float32)
    key_two = split_heads(project(text_states, full_weights[9]).astype(jnp.bfloat16))
    value_two = split_heads(project(text_states, full_weights[10]).astype(jnp.bfloat16))
    normed_one = gather_rows(layer_norm(stream_one, gain_self, bias_self).astype(jnp.bfloat16))
    query_one = split_heads(project(normed_one, full_weights[2]).astype(jnp.bfloat16))
    key_one = split_heads(project(normed_one, full_weights[3]).astype(jnp.bfloat16))
    value_one = split_heads(project(normed_one, full_weights[4]).astype(jnp.bfloat16))
    attended_one, logsum_one = attend(query_one, key_one, value_one, True)
    stream_two = stream_one + scatter_rows(project(flatten_heads(attended_one), full_weights[5]))
    normed_two = gather_rows(layer_norm(stream_two, gain_cross, bias_cross).astype(jnp.bfloat16))
    query_two = split_heads(project(normed_two, full_weights[8]).astype(jnp.bfloat16))
    attended_two, logsum_two = attend(query_two, key_two, value_two, False)
    stream_three = stream_two + scatter_rows(project(flatten_heads(attended_two), full_weights[11]))
    normed_three = gather_rows(layer_norm(stream_three, gain_ffn, bias_ffn).astype(jnp.bfloat16))
    upper = project(normed_three, full_weights[14])
    active = gelu_exact(upper).astype(jnp.bfloat16)
    layer_out = (stream_three + scatter_rows(project(active, full_weights[15]))).astype(
        jnp.bfloat16
    )
    grad_three = cotangent.astype(jnp.float32)
    grad_branch = gather_grads(grad_three.astype(jnp.bfloat16))
    grad_down = jnp.einsum("clo,clf->of", grad_branch, active, preferred_element_type=jnp.float32)
    grad_active = jnp.einsum(
        "clo,of->clf", grad_branch, full_weights[15], preferred_element_type=jnp.float32
    )
    grad_upper = jax.vjp(gelu_exact, upper)[1](grad_active)[0].astype(jnp.bfloat16)
    grad_up = weight_grad(grad_upper, normed_three)
    norm_back = jax.vjp(layer_norm, stream_three, gain_ffn, bias_ffn)[1]
    grad_stream, grad_gain_ffn, grad_bias_ffn = norm_back(
        scatter_grads(input_grad(grad_upper, full_weights[14]))
    )
    grad_two = grad_three + grad_stream
    grad_branch = gather_grads(grad_two.astype(jnp.bfloat16))
    grad_out_cross, grad_attended = heads_grads(grad_branch, attended_two, full_weights[11])
    grad_query, grad_key, grad_value = attend_back(
        query_two, key_two, value_two, grad_attended, logsum_two, False
    )
    grad_query = flatten_heads(grad_query).astype(jnp.bfloat16)
    grad_key = flatten_heads(grad_key).astype(jnp.bfloat16)
    grad_value = flatten_heads(grad_value).astype(jnp.bfloat16)
    grad_query_cross = weight_grad(grad_query, normed_two)
    grad_key_cross = weight_grad(grad_key, text_states)
    grad_value_cross = weight_grad(grad_value, text_states)
    text_part = input_grad(grad_key, full_weights[9]) + input_grad(grad_value, full_weights[10])
    grad_text = lax.psum_scatter(
        text_part.astype(jnp.bfloat16), "tensor", scatter_dimension=2, tiled=True
    ).astype(jnp.float32)
    norm_back = jax.vjp(layer_norm, stream_two, gain_cross, bias_cross)[1]
    grad_stream, grad_gain_cross, grad_bias_cross = norm_back(
        scatter_grads(input_grad(grad_query, full_weights[8]))
    )
    grad_one = grad_two + grad_stream
    grad_branch = gather_grads(grad_one.astype(jnp.bfloat16))
    grad_out_self, grad_attended = heads_grads(grad_branch, attended_one, full_weights[5])
    grad_query, grad_key, grad_value = attend_back(
        query_one, key_one, value_one, grad_attended, logsum_one, True
    )
    grad_query = flatten_heads(grad_query).astype(jnp.bfloat16)
    grad_key = flatten_heads(grad_key).astype(jnp.bfloat16)
    grad_value = flatten_heads(grad_value).astype(jnp.bfloat16)
    grad_query_self = weight_grad(grad_query, normed_one)
    grad_key_self = weight_grad(grad_key, normed_one)
    grad_value_self = weight_grad(grad_value, normed_one)
    grad_normed = (
        input_grad(grad_query, full_weights[2])
        + input_grad(grad_key, full_weights[3])
        + input_grad(grad_value, full_weights[4])
    )
    norm_back = jax.vjp(layer_norm, stream_one, gain_self, bias_self)[1]
    grad_stream, grad_gain_self, grad_bias_self = norm_back(scatter_grads(grad_normed))
    grad_input = grad_one + grad_stream
    summed = (
        lax.psum_scatter(
            grad_gain_self.astype(jnp.bfloat16), "dp", scatter_dimension=0, tiled=True
        ).astype(jnp.float32),
        lax.psum_scatter(
            grad_bias_self.astype(jnp.bfloat16), "dp", scatter_dimension=0, tiled=True
        ).astype(jnp.float32),
        lax.psum_scatter(
            grad_query_self.astype(jnp.bfloat16), "dp", scatter_dimension=1, tiled=True
        ).astype(jnp.float32),
        lax.psum_scatter(
            grad_key_self.astype(jnp.bfloat16), "dp", scatter_dimension=1, tiled=True
        ).astype(jnp.float32),
        lax.psum_scatter(
            grad_value_self.astype(jnp.bfloat16), "dp", scatter_dimension=1, tiled=True
        ).astype(jnp.float32),
        lax.psum_scatter(
            grad_out_self.astype(jnp.bfloat16), "dp", scatter_dimension=0, tiled=True
        ).astype(jnp.float32),
        lax.psum_scatter(
            grad_gain_cross.astype(jnp.bfloat16), "dp", scatter_dimension=0, tiled=True
        ).astype(jnp.float32),
        lax.psum_scatter(
            grad_bias_cross.astype(jnp.bfloat16), "dp", scatter_dimension=0, tiled=True
        ).astype(jnp.float32),
        lax.psum_scatter(
            grad_query_cross.astype(jnp.bfloat16), "dp", scatter_dimension=1, tiled=True
        ).astype(jnp.float32),
        lax.psum_scatter(
            grad_key_cross.astype(jnp.bfloat16), "dp", scatter_dimension=1, tiled=True
        ).astype(jnp.float32),
        lax.psum_scatter(
            grad_value_cross.astype(jnp.bfloat16), "dp", scatter_dimension=1, tiled=True
        ).astype(jnp.float32),
        lax.psum_scatter(
            grad_out_cross.astype(jnp.bfloat16), "dp", scatter_dimension=0, tiled=True
        ).astype(jnp.float32),
        lax.psum_scatter(
            grad_gain_ffn.astype(jnp.bfloat16), "dp", scatter_dimension=0, tiled=True
        ).astype(jnp.float32),
        lax.psum_scatter(
            grad_bias_ffn.astype(jnp.bfloat16), "dp", scatter_dimension=0, tiled=True
        ).astype(jnp.float32),
        lax.psum_scatter(
            grad_up.astype(jnp.bfloat16), "dp", scatter_dimension=1, tiled=True
        ).astype(jnp.float32),
        lax.psum_scatter(
            grad_down.astype(jnp.bfloat16), "dp", scatter_dimension=0, tiled=True
        ).astype(jnp.float32),
    )
    norm_sums = lax.psum(
        (summed[0], summed[1], summed[6], summed[7], summed[12], summed[13]), "tensor"
    )
    return (
        layer_out,
        grad_input,
        grad_text,
        norm_sums[0],
        norm_sums[1],
        summed[2],
        summed[3],
        summed[4],
        summed[5],
        norm_sums[2],
        norm_sums[3],
        summed[8],
        summed[9],
        summed[10],
        summed[11],
        norm_sums[4],
        norm_sums[5],
        summed[14],
        summed[15],
    )


MESH_IDS = pl.DeviceIdType.MESH
BF16 = jnp.bfloat16
F32 = jnp.float32
VMEM_LIMIT = 63 * 2**20


def my_place():
    chip = lax.axis_index("dp")
    core = lax.axis_index("tensor")
    return (lax.rem(chip, 2), lax.rem(lax.div(chip, 2), 2), lax.div(chip, 4), core)


def neighbours(x, y, z, core):
    def device(zz, yy, xx):
        return (zz * 4 + yy * 2 + xx, core)

    return (device(z, y, 1 - x), device(z, 1 - y, x), device(z + 1, y, x), device(z - 1, y, x))


def when(cond, fn):
    if cond is None:
        fn()
    else:
        pl.when(cond)(fn)


def signal_neighbours(sems, near, has_up, has_down):
    for sem, device, cond in zip(sems, near, (None, None, has_up, has_down), strict=True):
        when(
            cond,
            functools.partial(
                pl.semaphore_signal, sem, inc=1, device_id=device, device_id_type=MESH_IDS
            ),
        )


def gather_engine(chunks, shards, outs, sems):
    local_sem, send_sem, zs, xs, ys, ds = sems
    x, y, z, core = my_place()
    xn, yn = 1 - x, 1 - y
    near = neighbours(x, y, z, core)
    right, across, up, down = near
    has_up, has_down = z < 3, z > 0
    barrier = pltpu.get_barrier_semaphore()
    signal_neighbours([barrier] * 4, near, has_up, has_down)
    pl.semaphore_signal(barrier, inc=1, device_id=(lax.axis_index("dp"), 1 - core), device_id_type=MESH_IDS)
    pl.semaphore_wait(barrier, 3 + has_up.astype(jnp.int32) + has_down.astype(jnp.int32))
    total = len(chunks)
    pending = []


    def span(c):
        _, first, width, _ = chunks[c]
        return pl.ds(first, width)

    def at(zz, yy, xx, c, half=None):
        ref = outs[chunks[c][0]]
        half_rows = ref.shape[3] // 2
        lines = slice(None) if half is None else pl.ds(half * half_rows, half_rows)
        return ref.at[zz, yy, xx, lines, span(c)]

    def plane(zz, c):
        return outs[chunks[c][0]].at[zz, :, :, :, span(c)]

    def own(c):
        return shards[chunks[c][0]].at[:, span(c)]

    local = [pltpu.make_async_copy(own(c), at(z, y, x, c), local_sem.at[c]) for c in range(total)]

    def remote(src, dst, sem, device):
        return pltpu.make_async_remote_copy(
            src_ref=src,
            dst_ref=dst,
            send_sem=send_sem,
            recv_sem=sem,
            device_id=device,
            device_id_type=MESH_IDS,
        )

    def send(src, dst, sem, device, cond=None):
        copy = remote(src, dst, sem, device)
        when(cond, copy.start)
        pending.append((cond, copy))

    def wait(ref, sem, cond=None):
        when(cond, remote(ref, ref, sem, right).wait_recv)

    def lines(step):
        for sign, device, more in ((-1, up, has_up), (1, down, has_down)):
            block = z + sign * step
            yield block, (block >= 0) if sign < 0 else (block <= 3), device, more

    def stage_z(c, step):
        if step == 0:
            send(own(c), at(z, y, x, c), zs.at[c, z], up, has_up)
            send(own(c), at(z, y, x, c), zs.at[c, z], down, has_down)
            send(own(c), at(z, y, x, c), xs.at[c, z], right)
            send(own(c), at(z, y, x, c), ys.at[c, z], across)
            local[c].start()
        if 1 <= step <= 3:
            for block, exists, device, more in lines(step):
                ref = at(block, y, x, c)
                wait(ref, zs.at[c, block], exists)
                if step < 3:
                    send(ref, ref, zs.at[c, block], device, exists & more)
                send(ref, ref, xs.at[c, block], right, exists)
                send(ref, ref, ys.at[c, block], across, exists)
        if 1 <= step <= 4:
            for block, exists, _, _ in [(z, None, None, None)] if step == 1 else lines(step - 1):
                wait(at(block, y, xn, c), xs.at[c, block], exists)
                ref = at(block, y, xn, c, 0)
                send(ref, ref, ds.at[c, block, 0], across, exists)
                wait(at(block, yn, x, c), ys.at[c, block], exists)
                ref = at(block, yn, x, c, 1)
                send(ref, ref, ds.at[c, block, 1], right, exists)
        if step == 5:
            for block in range(4):
                for half in range(2):
                    wait(at(block, yn, xn, c, half), ds.at[c, block, half])
            local[c].wait()

    def stage_a(c, step):
        if step == 0:
            send(own(c), at(z, y, x, c), xs.at[c, z], right)
            send(own(c), at(z, y, x, c), ys.at[c, z], across)
            local[c].start()
        if step == 1:
            wait(at(z, y, xn, c), xs.at[c, z])
            ref = at(z, y, xn, c, 0)
            send(ref, ref, ds.at[c, z, 0], across)
            wait(at(z, yn, x, c), ys.at[c, z])
            ref = at(z, yn, x, c, 1)
            send(ref, ref, ds.at[c, z, 1], right)
        if step == 2:
            for half in range(2):
                wait(at(z, yn, xn, c, half), ds.at[c, z, half])
            local[c].wait()
            send(plane(z, c), plane(z, c), zs.at[c, z], up, has_up)
            send(plane(z, c), plane(z, c), zs.at[c, z], down, has_down)
        if step >= 3:
            for block, exists, device, more in lines(step - 2):
                wait(plane(block, c), zs.at[c, block], exists)
                if step < 5:
                    send(plane(block, c), plane(block, c), zs.at[c, block], device, exists & more)

    stages = 6

    def turn(number):
        for step in range(stages):
            c = number - step
            if 0 <= c < total:
                (stage_z if chunks[c][3] == "Z" else stage_a)(c, step)

    def finish():
        for cond, copy in pending:
            when(cond, copy.wait_send)

    return turn, finish


def total_of(*parts):
    value = parts[0].astype(F32)
    for part in parts[1:]:
        value = value + part.astype(F32)
    return value


def dot_nt(left, right):
    return lax.dot_general(left, right, (((1,), (1,)), ((), ())), preferred_element_type=F32)


def dot_tn(left, right):
    return lax.dot_general(left, right, (((0,), (0,)), ((), ())), preferred_element_type=F32)


def dot_nn(left, right):
    return jnp.dot(left, right, preferred_element_type=F32)


def project_rows(source, weight, store, rows=256, transposed=False):
    def body(n, carry):
        first = pl.multiple_of(n * rows, rows)
        part = source[pl.ds(first, rows), :]
        store(first, dot_nt(part, weight[...]) if transposed else dot_nn(part, weight[...]))
        return carry

    lax.fori_loop(0, source.shape[0] // rows, body, 0)


def normalize(values, gain, shift):
    offset = values - jnp.mean(values, axis=-1, keepdims=True)
    spread = jnp.mean(offset * offset, axis=-1, keepdims=True)
    return offset * lax.rsqrt(spread + norm_eps) * gain + shift


def head_lanes(half):
    return lax.div(lax.broadcasted_iota(jnp.int32, (1, 128), 1), 64) == half


def only(mask, value):
    return jnp.where(mask, value.astype(F32), 0.0).astype(BF16)


def pair_forward(pair, q_ref, k_ref, v_ref, o_ref, lse_ref, causal):
    cols = pl.ds(pl.multiple_of(pair * 128, 128), 128)
    block = 256
    keep = lax.broadcasted_iota(jnp.int32, (block, block), 0) <= lax.broadcasted_iota(
        jnp.int32, (block, block), 1
    )
    for i in range(q_ref.shape[0] // block):
        rows = pl.ds(i * block, block)
        parts = [(0, k_ref.shape[0], False)]
        if causal:
            parts = [(0, i * block, False)] * (i > 0) + [(i * block, block, True)]
        total = 0.0
        for half in range(2):
            mine = head_lanes(half)
            q = only(mine, q_ref[rows, cols])
            scores = []
            for first, count, diagonal in parts:
                part = dot_nt(k_ref[pl.ds(first, count), cols], q) * score_scale
                scores.append(jnp.where(keep, part, -1e30) if diagonal else part)
            peak = functools.reduce(
                jnp.maximum, [jnp.max(part, axis=0, keepdims=True) for part in scores]
            )
            scores = [jnp.exp(part - peak) for part in scores]
            weight = sum(jnp.sum(part, axis=0, keepdims=True) for part in scores)
            lse_ref[pl.ds(2 * pair + half, 1), rows] = peak + jnp.log(weight)
            share = 1.0 / weight
            for (first, count, _), part in zip(parts, scores, strict=True):
                v = only(mine, v_ref[pl.ds(first, count), cols])
                total = total + dot_tn((part * share).astype(BF16), v)
        o_ref[rows, cols] = total.astype(BF16)


def forward_kernel(chunks, count, *refs):
    shards, refs = refs[:count], refs[count:]
    hidden_h, text_h, cotangent_h, refs = refs[0], refs[1], refs[2], refs[3:]
    outs, refs = refs[:count], refs[count:]
    results, refs = refs[:19], refs[19:]
    sems, refs = refs[:6], refs[6:]
    (h1, h2, h3, q1, k1, v1, o1, q2, k2, v2, o2, lse1, lse2, x2, x3), refs = refs[:15], refs[15:]
    gathered_norms, norms, weights, hidden, text, mine, theirs, arrived, active, slopes, x2_parts = refs[:11]
    norm_sem, weight_sem, load_sem, share_send, share_recv, result_sem = refs[11:]
    names = dict(norms=0, q=1, k=2, v=3, o=4, ck=5, cv=6, cq=7, co=8, up=9, down=10)
    turn, finish = gather_engine(chunks, shards, outs, sems)
    chip, core = lax.axis_index("dp"), lax.axis_index("tensor")
    frames, width = h1.shape
    half = frames // 2
    own = pl.ds(pl.multiple_of(core * half, half), half)
    loads = [
        pltpu.make_async_copy(hidden_h, hidden, load_sem.at[0]),
        pltpu.make_async_copy(text_h, text, load_sem.at[1]),
        pltpu.make_async_copy(cotangent_h, theirs.at[1], load_sem.at[2]),
    ]
    for copy in loads:
        copy.start()
    pending = []

    def weight_copy(name, slot, first=0):
        return [
            pltpu.make_async_copy(
                outs[names[name]].at[zz, yy, xx, :, pl.ds(first, weights.shape[2])],
                weights.at[slot, pl.ds(((zz * 2 + yy) * 2 + xx) * rows, rows), :],
                weight_sem.at[slot, (zz * 2 + yy) * 2 + xx],
            )
            for zz in range(4)
            for yy in range(2)
            for xx in range(2)
        ]

    rows = width // 16

    def load_weight(name, slot, first=0):
        for copy in weight_copy(name, slot, first):
            copy.start()

    def wait_weight(slot):
        for copy in weight_copy("q", slot):
            copy.wait()

    def share(n, src, dst):
        return pltpu.make_async_remote_copy(
            src_ref=src,
            dst_ref=dst,
            send_sem=share_send.at[n],
            recv_sem=share_recv.at[n],
            device_id=(chip, 1 - core),
            device_id_type=MESH_IDS,
        )

    def give(n, ref):
        copy = pltpu.make_async_copy(ref, results[n], result_sem.at[n])
        copy.start()
        pending.append(copy)

    def norm_share(n, values, kind, h):
        step = 64

        def body(i, carry):
            first = pl.multiple_of(i * step, step)
            h[pl.ds(pl.multiple_of(core * half + first, step), step), :] = normalize(
                values(first, step), norms[2 * kind : 2 * kind + 1], norms[2 * kind + 1 : 2 * kind + 2]
            ).astype(BF16)
            return carry

        lax.fori_loop(0, half // step, body, 0)
        share(n, h.at[own], h.at[own]).start()

    def get_share(n, h):
        share(n, h.at[own], h.at[own]).wait()

    def to(ref):
        def store(first, value):
            ref[pl.ds(first, value.shape[0]), :] = value.astype(BF16)

        return store

    def out_project(n, o, slot):
        step = 256
        for whose, ref in ((1 - core, theirs.at[n]), (core, mine)):
            for first in range(0, half, step):
                part = o[pl.ds(pl.multiple_of(whose * half + first, step), step), :]
                ref[pl.ds(first, step), :] = dot_nt(part, weights[slot]).astype(ref.dtype)
            if whose is not core:
                share(3 + n, theirs.at[n], arrived.at[n]).start()

    def add_stream(n, before, after, parts=None):
        def values(first, step):
            lines = pl.ds(first, step)
            total = before[lines, :].astype(F32) + (mine[lines, :] + arrived[n, lines, :].astype(F32))
            after[lines, :] = total
            if parts is not None:
                high = total.astype(BF16)
                parts[lines, :] = high
                low = total - high.astype(F32)
                parts[pl.ds(pl.multiple_of(half + first, step), step), :] = low.astype(BF16)
            return total

        return values

    branch = results[16].at[own]
    branch_copy = pltpu.make_async_copy(theirs.at[1], branch, result_sem.at[16])

    def active_copies(j):
        lanes = pl.ds(j * active.shape[1], active.shape[1])
        return (
            pltpu.make_async_copy(active, results[17].at[:, lanes], result_sem.at[17]),
            pltpu.make_async_copy(slopes, results[18].at[:, lanes], result_sem.at[18]),
        )

    def hidden_units(j):
        wait_weight(j % 2)
        if j < 3:
            load_weight("up", (j + 1) % 2, (j + 1) * active.shape[1])
        if j:
            for copy in active_copies(j - 1):
                copy.wait()

        def store(first, value):
            lines = pl.ds(first, value.shape[0])
            below = 0.5 * (1.0 + lax.erf(value * (0.5**0.5)))
            density = jnp.exp(-0.5 * value * value) * 0.3989422804014327
            active[lines, :] = (value * below).astype(BF16)
            slopes[lines, :] = (below + value * density).astype(BF16)

        project_rows(h3, weights.at[j % 2], store)
        for copy in active_copies(j):
            copy.start()

    def work(number):
        if number == 5:
            copy = pltpu.make_async_copy(outs[0], gathered_norms, norm_sem)
            copy.start()
            copy.wait()
            for copy in loads:
                copy.wait()
            share(5, theirs.at[1], branch).start()
            branch_copy.start()
            total = 0.0
            lane = lax.broadcasted_iota(jnp.int32, (128, width), 0)
            place = lax.broadcasted_iota(jnp.int32, (128, width), 1)
            for n in range(16):
                pick = (place == lane + n * rows) & (lane < rows)
                total = total + dot_nn(
                    gathered_norms[n // 4, n // 2 % 2, n % 2],
                    jnp.where(pick, 1.0, 0.0).astype(BF16),
                )
            norms[...] = total
            give(13, norms)
            norm_share(0, lambda first, step: hidden[pl.ds(first, step), :].astype(F32), 0, h1)
        if number == 6:
            load_weight("q", 0)
            get_share(0, h1)
            give(0, h1)
            wait_weight(0)
            project_rows(h1, weights.at[0], to(q1))
            give(3, q1)
        if number == 7:
            load_weight("k", 1)
            wait_weight(1)
            project_rows(h1, weights.at[1], to(k1))
            give(4, k1)
        if number == 8:
            load_weight("v", 0)
            wait_weight(0)
            project_rows(h1, weights.at[0], to(v1))
            give(5, v1)
        if number in (9, 10, 11):
            if number == 9:
                load_weight("o", 1)
            pairs = q1.shape[1] // 128
            first = pairs * (number - 9) // 3
            last = pairs * (number - 8) // 3

            def body(pair, carry):
                pair_forward(pair, q1, k1, v1, o1, lse1, True)
                return carry

            lax.fori_loop(first, last, body, 0)
            if number == 11:
                load_weight("cv", 0)
        if number == 12:
            share(5, theirs.at[1], branch).wait()
            branch_copy.wait()
            give(6, o1)
            give(11, lse1)
            wait_weight(1)
            out_project(0, o1, 1)
            load_weight("ck", 1)
            wait_weight(0)
            v2[...] = dot_nn(text[...], weights[0]).astype(BF16)
            give(9, v2)
            load_weight("cq", 0)
        if number == 13:
            share(3, theirs.at[0], arrived.at[0]).wait()
            norm_share(1, add_stream(0, hidden, x2, x2_parts), 1, h2)
            give(14, x2_parts)
            wait_weight(1)
            k2[...] = dot_nn(text[...], weights[1]).astype(BF16)
            give(8, k2)
            load_weight("co", 1)
        if number == 14:
            get_share(1, h2)
            give(1, h2)
            wait_weight(0)
            project_rows(h2, weights.at[0], to(q2))
            give(7, q2)

            def body(pair, carry):
                pair_forward(pair, q2, k2, v2, o2, lse2, False)
                return carry

            lax.fori_loop(0, q2.shape[1] // 128, body, 0)
            give(10, o2)
            give(12, lse2)
        if number == 15:
            wait_weight(1)
            out_project(1, o2, 1)
        if number == 16:
            share(4, theirs.at[1], arrived.at[1]).wait()
            norm_share(2, add_stream(1, x2, x3), 2, h3)
            give(15, x3)
            load_weight("up", 0)
        if number == 17:
            get_share(2, h3)
            give(2, h3)
        for j in {17: (0,), 18: (1, 2), 19: (3,)}.get(number, ()):
            hidden_units(j)

    for number in range(len(chunks) + 5):
        turn(number)
        work(number)
    finish()
    for copy in (*pending, *active_copies(3)):
        copy.wait()


def forward_all(shards, chunks, hidden, text, cotangent):
    total, count = len(chunks), len(shards)
    dma, vmem = pltpu.SemaphoreType.DMA, pltpu.VMEM
    half, width = hidden.shape
    frames, part = 2 * half, shards[1].shape[1]
    anywhere = pl.BlockSpec(memory_space=pl.ANY)
    shape = jax.ShapeDtypeStruct
    kept = [
        *[((frames, width), BF16)] * 3,
        *[((frames, part), BF16)] * 4,
        ((frames, part), BF16),
        *[((text.shape[0], part), BF16)] * 2,
        ((frames, part), BF16),
        *[((16, frames), F32)] * 2,
    ]
    given = [*kept, ((shards[0].shape[0], width), F32), ((frames, width), BF16), ((half, width), F32)]
    given += [((frames, width), BF16), ((frames, 4 * part), BF16), ((frames, 4 * part), BF16)]
    held = [*kept, ((half, width), F32), ((half, width), F32)]
    outs = pl.pallas_call(
        functools.partial(forward_kernel, chunks, count),
        out_shape=[shape((4, 2, 2) + s.shape, s.dtype) for s in shards] + [shape(*g) for g in given],
        in_specs=[pl.BlockSpec(memory_space=vmem)] * count + [anywhere] * 3,
        out_specs=[anywhere] * (count + len(given)),
        scratch_shapes=[
            dma((total,)),
            dma,
            dma((total, 4)),
            dma((total, 4)),
            dma((total, 4)),
            dma((total, 4, 2)),
            *[vmem(*h) for h in held],
            vmem((4, 2, 2) + shards[0].shape, BF16),
            vmem((shards[0].shape[0], width), F32),
            vmem((2, width, part), BF16),
            vmem((half, width), BF16),
            vmem(text.shape, BF16),
            vmem((half, width), F32),
            vmem((2, half, width), BF16),
            vmem((2, half, width), BF16),
            vmem((frames, part), BF16),
            vmem((frames, part), BF16),
            vmem((frames, width), BF16),
            dma,
            dma((2, 16)),
            dma((3,)),
            dma((6,)),
            dma((6,)),
            dma((19,)),
        ],
        compiler_params=pltpu.CompilerParams(
            collective_id=0, has_side_effects=True, vmem_limit_bytes=VMEM_LIMIT
        ),
        name="forward",
    )(*shards, hidden, text, cotangent)
    return outs[:count], outs[count:]


XD, YD, XA, YA, XB, YB, UP, DOWN = range(8)


UNIT = 256
WIDTH_Z, WIDTH_A, SLOTS = 384, 128, 7
ROWS_L = 6
FIRST_L = (0, 12, 24, 27, 36, 39)
LOAD_L = ((2, 11), (3, 11), (4, 14), (5, 15))
FIRST_R = ((0, 12), (12, 24), (24, 27), (27, 30), (36, 39))
TEXT_UNITS = (30, 36)
SELF_UNITS = (39, 48)
UNITS = 48


def head_back(head, q_ref, k_ref, v_ref, do_ref, lse_ref, dq_ref, dkv_ref, bases, acc_k, acc_v, causal):
    pair, half = lax.div(head, 2), lax.rem(head, 2)
    cols = pl.ds(pl.multiple_of(pair * 128, 128), 128)
    lanes = [pl.ds(pl.multiple_of(pair * 128 + base, 128), 128) for base in bases]
    mine = head_lanes(half)
    length = k_ref.shape[0]
    acc_k[pl.ds(0, length), :] = jnp.zeros((length, 128), F32)
    acc_v[pl.ds(0, length), :] = jnp.zeros((length, 128), F32)
    block = 256 if causal else q_ref.shape[0]
    if causal:
        keep = lax.broadcasted_iota(jnp.int32, (block, block), 0) <= lax.broadcasted_iota(
            jnp.int32, (block, block), 1
        )

    def merged(ref, rows, lane, value):
        before = jnp.where(half == 0, 0.0, ref[rows, lane].astype(F32))
        ref[rows, lane] = (before + value).astype(BF16)

    for i in range(q_ref.shape[0] // block):
        rows = pl.ds(i * block, block)
        q = only(mine, q_ref[rows, cols])
        do = only(mine, do_ref[rows, cols])
        lse = lse_ref[pl.ds(head, 1), rows]
        parts = [(0, length, False)]
        if causal:
            parts = [(0, i * block, False)] * (i > 0) + [(i * block, block, True)]
        held, inner = [], 0.0
        for first, count, diagonal in parts:
            keys = pl.ds(first, count)
            soft = jnp.exp(dot_nt(k_ref[keys, cols], q) * score_scale - lse)
            if diagonal:
                soft = jnp.where(keep, soft, 0.0)
            slope = dot_nt(v_ref[keys, cols], do)
            inner = inner + jnp.sum(soft * slope, axis=0, keepdims=True)
            held.append((keys, soft, slope))
        grad_q = 0.0
        for keys, soft, slope in held:
            ds = (soft * (slope - inner)).astype(BF16)
            acc_v[keys, :] += dot_nn(soft.astype(BF16), do)
            acc_k[keys, :] += dot_nn(ds, q)
            grad_q = grad_q + dot_tn(ds, k_ref[keys, cols])
        merged(dq_ref, rows, lanes[0], jnp.where(mine, grad_q * score_scale, 0.0))
    everything = pl.ds(0, length)
    merged(dkv_ref, everything, lanes[1], acc_k[everything, :] * score_scale)
    merged(dkv_ref, everything, lanes[2], acc_v[everything, :])


def backward_kernel(*refs):
    (e3_h, h3_h, h2_h, h1_h, a_h, slope_h, o2_h, o1_h, text_h), refs = refs[:9], refs[9:]
    (q2_h, k2_h, v2_h, q1_h, k1_h, v1_h, x3_h, x2_h, x1_h), refs = refs[:9], refs[9:]
    (w_q, w_k, w_v, w_o, w_ck, w_cv, w_cq, w_co, w_up, w_down), refs = refs[:10], refs[10:]
    (lse2_ref, lse1_ref, norms), refs = refs[:3], refs[3:]
    (out, layer_out, grad_input, grad_text, norm_out), refs = refs[:5], refs[5:]
    (du_h, dq2_h, e2_h, e1_h), refs = refs[:4], refs[4:]
    (gz, ga, xdz, ydz, xaz, yaz, xbz, ybz, lnz), refs = refs[:9], refs[9:]
    (xda, yda, xaa, yaa, xba, yba, lna, oz, oa), refs = refs[:9], refs[9:]
    (lbuf, rbuf, text_v, dkv_v, k2_v, v2_v, pool, dqkv, acc_k, acc_v), refs = refs[:10], refs[10:]
    (acc, grad, theirs, arrived, weights, text_part, text_send, text_got), refs = refs[:8], refs[8:]
    (norm_grads, got), refs = refs[:2], refs[2:]
    (first_sem, l_sem, r_sem, out_sem, send_z, send_a, recv_z, recv_a), refs = refs[:8], refs[8:]
    (pool_sem, slope_sem, weight_sem, x_sem, keep_sem, share_send, share_recv, norm_send), refs = refs[:8], refs[8:]
    norm_recv, credit = refs
    lefts = (e3_h, h3_h, e2_h, h2_h, e1_h, h1_h)
    rights = (a_h, du_h, o2_h, dq2_h, o1_h)
    width_z, width_a, slots = WIDTH_Z, WIDTH_A, SLOTS
    total, width = UNITS // 2, WIDTH_Z + WIDTH_A
    x, y, z, core = my_place()
    xn, yn = 1 - x, 1 - y
    near = neighbours(x, y, z, core)
    right, across, up, down = near
    has_up, has_down = z < 3, z > 0
    degree = 2 + has_up.astype(jnp.int32) + has_down.astype(jnp.int32)
    chip = lax.axis_index("dp")
    other = (chip, 1 - core)
    partners = [other]
    for bit in (1, 2, 4, 8):
        partners.append((chip + bit * (1 - 2 * lax.rem(lax.div(chip, bit), 2)), core))
    barrier = pltpu.get_barrier_semaphore()
    signal_neighbours([barrier] * 4, near, has_up, has_down)
    for device in (other, partners[4]):
        pl.semaphore_signal(barrier, inc=1, device_id=device, device_id_type=MESH_IDS)
    pl.semaphore_wait(barrier, degree + 2)
    rows = gz.shape[4]
    low, high = pl.ds(0, rows // 2), pl.ds(rows // 2, rows // 2)

    def remote(src, dst, send_sem, recv_sem, device):
        return pltpu.make_async_remote_copy(
            src_ref=src,
            dst_ref=dst,
            send_sem=send_sem,
            recv_sem=recv_sem,
            device_id=device,
            device_id_type=MESH_IDS,
        )

    def arrived_at(ref, sem):
        remote(ref, ref, send_z.at[0], sem, right).wait_recv()

    def sent(ref, sem):
        remote(ref, ref, sem, recv_z.at[0, 0], right).wait_send()

    firsts = [
        pltpu.make_async_copy(src, dst, first_sem.at[n])
        for n, (src, dst) in enumerate(((text_h, text_v), (k2_h, k2_v), (v2_h, v2_v)))
    ]

    def left_copy(n):
        return pltpu.make_async_copy(lefts[n], lbuf.at[n % 2], l_sem.at[n % 2])

    def right_copies(c, which):
        unit = 2 * c + which
        place, sem = rbuf.at[lax.rem(c, 2), which], r_sem.at[lax.rem(c, 2), which]
        for source, (lo, hi) in zip((*rights, dqkv), (*FIRST_R, SELF_UNITS), strict=True):
            first = pl.multiple_of((unit - lo) * UNIT, UNIT)
            yield (
                (unit >= lo) & (unit < hi),
                pltpu.make_async_copy(source.at[:, pl.ds(first, UNIT)], place, sem),
            )

    def start_rights(c):
        for which in range(2):
            for cond, copy in right_copies(c, which):
                pl.when(cond)(copy.start)

    def store_unit(which, k, i, value):
        for yy in range(2):
            for xx in range(2):
                first = (yy * 2 + xx) * rows
                block = value[first : first + rows, :].astype(BF16)
                if which == 0:
                    gz[k, i, yy, xx, :, pl.ds(0, UNIT)] = block
                else:
                    gz[k, i, yy, xx, :, pl.ds(UNIT, width_z - UNIT)] = block[:, : width_z - UNIT]
                    ga[k, i, yy, xx] = block[:, width_z - UNIT :]

    def compute(c, k):
        for n in range(1, ROWS_L):
            pl.when(c == FIRST_L[n] // 2)(left_copy(n).wait)
        for which in range(2):
            unit = 2 * c + which
            text = (unit >= TEXT_UNITS[0]) & (unit < TEXT_UNITS[1])
            slot = lax.rem(sum((unit >= first).astype(jnp.int32) for first in FIRST_L) + 1, 2)

            @pl.when(text)
            def _():
                first = pl.multiple_of((unit - TEXT_UNITS[0]) * UNIT, UNIT)
                right_part = dkv_v[:, pl.ds(first, UNIT)]
                for i in range(4):
                    store_unit(which, k, i, dot_tn(text_v[:, pl.ds(i * 4 * rows, 4 * rows)], right_part))

            @pl.when(jnp.logical_not(text))
            def _():
                par = lax.rem(c, 2)
                pltpu.make_async_copy(rbuf.at[par, which], rbuf.at[par, which], r_sem.at[par, which]).wait()
                right_part = rbuf[par, which]
                for i in range(4):
                    left_part = lbuf[slot, :, pl.ds(i * 4 * rows, 4 * rows)]
                    store_unit(which, k, i, dot_tn(left_part, right_part))

        for n, at in LOAD_L:
            pl.when(c == at)(left_copy(n).start)
        pl.when(c + 1 < total)(lambda: start_rights(c + 1))

    def out_copies(c):
        o = lax.rem(c, 2)
        first = pl.multiple_of(c * width, 128)
        return (
            pltpu.make_async_copy(oz.at[o], out.at[:, pl.ds(first, width_z)], out_sem.at[o, 0]),
            pltpu.make_async_copy(
                oa.at[o], out.at[:, pl.ds(first + width_z, width_a)], out_sem.at[o, 1]
            ),
        )

    def plane_first(own, k, bufs, send_sem, recv):
        xd, yd, xa, ya = bufs
        remote(own(yn, xn, low), xd.at[k], send_sem.at[k], recv.at[k, XD], right).start()
        remote(own(yn, xn, high), yd.at[k], send_sem.at[k], recv.at[k, YD], across).start()
        remote(own(y, xn, low), xa.at[k], send_sem.at[k], recv.at[k, XA], right).start()
        remote(own(yn, x, high), ya.at[k], send_sem.at[k], recv.at[k, YA], across).start()

    def plane_second(add, k, bufs, send_sem, recv):
        xd, yd, xb, yb = bufs
        arrived_at(xd.at[k], recv.at[k, XD])
        add(xd, yn, x, low)
        remote(xd.at[k], yb.at[k], send_sem.at[k], recv.at[k, YB], across).start()
        arrived_at(yd.at[k], recv.at[k, YD])
        add(yd, y, xn, high)
        remote(yd.at[k], xb.at[k], send_sem.at[k], recv.at[k, XB], right).start()

    def above(buf, k, first, blocks):
        return buf.at[k, pl.ds(first + 1, blocks)]

    def below(buf, k, blocks):
        return buf.at[k, pl.ds(0, blocks)]

    def line_up(first, buf, add, k, send_sem, recv):
        blocks = 4 - first
        arrived_at(above(buf, k, first, blocks), recv.at[k, UP])
        if blocks > 1:
            for block in range(first + 1, 4):
                add(buf, block, block + 1)
            ref = above(buf, k, first + 1, blocks - 1)
            remote(ref, ref, send_sem.at[k], recv.at[k, UP], up).start()

    def line_down(last, buf, add, k, send_sem, recv):
        arrived_at(below(buf, k, last + 1), recv.at[k, DOWN])
        if last > 0:
            for block in range(last):
                add(buf, block, block)
            ref = below(buf, k, last)
            remote(ref, ref, send_sem.at[k], recv.at[k, DOWN], down).start()

    def add_a(k):
        def add(buf, block, at):
            for yy in range(2):
                for xx in range(2):
                    buf[k, at, yy, xx] = total_of(
                        buf[k, at, yy, xx], ga[k, block, yy, xx]
                    ).astype(BF16)

        return add

    def add_z(k):
        def add(buf, block, at):
            buf[k, at] = total_of(buf[k, at], gz[k, block, y, x]).astype(BF16)

        return add

    def begin(c, k):
        @pl.when(c >= slots)
        def _():
            pl.semaphore_wait(credit.at[0], 1)
            pl.semaphore_wait(credit.at[1], 1)
            pl.when(has_up)(lambda: pl.semaphore_wait(credit.at[2], 1))
            pl.when(has_down)(lambda: pl.semaphore_wait(credit.at[3], 1))

        plane_first(
            lambda yy, xx, half: gz.at[k, :, yy, xx, half, :], k, (xdz, ydz, xaz, yaz), send_z, recv_z
        )

        @pl.when(z == 0)
        def _():
            ref = pl.ds(1, 3)
            remote(ga.at[k, ref], above(lna, k, 1, 3), send_a.at[k], recv_a.at[k, UP], up).start()

        @pl.when(z == 3)
        def _():
            ref = pl.ds(0, 3)
            remote(ga.at[k, ref], below(lna, k, 3), send_a.at[k], recv_a.at[k, DOWN], down).start()

    def second(c, k):
        def add(buf, yy, xx, half):
            for block in range(4):
                buf[k, block] = total_of(buf[k, block], gz[k, block, yy, xx, half, :]).astype(BF16)

        plane_second(add, k, (xdz, ydz, xbz, ybz), send_z, recv_z)
        pl.when(z == 1)(lambda: line_up(1, lna, add_a(k), k, send_a, recv_a))
        pl.when(z == 2)(lambda: line_down(2, lna, add_a(k), k, send_a, recv_a))

    def third(c, k):
        for buf, kind in ((xaz, XA), (yaz, YA), (xbz, XB), (ybz, YB)):
            arrived_at(buf.at[k], recv_z.at[k, kind])
        for block in range(4):
            for half, one, two in ((low, xaz, ybz), (high, yaz, xbz)):
                gz[k, block, y, x, half, :] = total_of(
                    gz[k, block, y, x, half, :], one[k, block], two[k, block]
                ).astype(BF16)

        @pl.when(z == 0)
        def _():
            ref = pl.ds(1, 3)
            remote(
                gz.at[k, ref, y, x], above(lnz, k, 1, 3), send_z.at[k], recv_z.at[k, UP], up
            ).start()

        @pl.when(z == 3)
        def _():
            ref = pl.ds(0, 3)
            remote(
                gz.at[k, ref, y, x], below(lnz, k, 3), send_z.at[k], recv_z.at[k, DOWN], down
            ).start()

        pl.when(z == 2)(lambda: line_up(2, lna, add_a(k), k, send_a, recv_a))
        pl.when(z == 1)(lambda: line_down(1, lna, add_a(k), k, send_a, recv_a))

    def fourth(c, k):
        pl.when(z == 1)(lambda: line_up(1, lnz, add_z(k), k, send_z, recv_z))
        pl.when(z == 2)(lambda: line_down(2, lnz, add_z(k), k, send_z, recv_z))
        pl.when(z == 3)(lambda: line_up(3, lna, None, k, send_a, recv_a))
        pl.when(z == 0)(lambda: line_down(0, lna, None, k, send_a, recv_a))
        for shift, exists in ((1, has_down), (0, has_up)):

            @pl.when(exists)
            def _():
                for yy in range(2):
                    for xx in range(2):
                        ga[k, z, yy, xx] = total_of(
                            ga[k, z, yy, xx], lna[k, z + shift, yy, xx]
                        ).astype(BF16)

        plane_first(
            lambda yy, xx, half: ga.at[k, z, yy, xx, half, :], k, (xda, yda, xaa, yaa), send_a, recv_a
        )

    def fifth(c, k):
        pl.when(z == 2)(lambda: line_up(2, lnz, add_z(k), k, send_z, recv_z))
        pl.when(z == 1)(lambda: line_down(1, lnz, add_z(k), k, send_z, recv_z))

        def add(buf, yy, xx, half):
            buf[k] = total_of(buf[k], ga[k, z, yy, xx, half, :]).astype(BF16)

        plane_second(add, k, (xda, yda, xba, yba), send_a, recv_a)

    def finish(c, k):
        pl.when(z == 3)(lambda: line_up(3, lnz, None, k, send_z, recv_z))
        pl.when(z == 0)(lambda: line_down(0, lnz, None, k, send_z, recv_z))
        o = lax.rem(c, 2)

        @pl.when(c >= 2)
        def _():
            for copy in out_copies(c - 2):
                copy.wait()

        oz[o] = gz[k, z, y, x].astype(F32)
        for shift, exists in ((1, has_down), (0, has_up)):

            @pl.when(exists)
            def _():
                oz[o] = oz[o] + lnz[k, z + shift].astype(F32)

        for buf, kind in ((xaa, XA), (yaa, YA), (xba, XB), (yba, YB)):
            arrived_at(buf.at[k], recv_a.at[k, kind])
        oa[o, low, :] = total_of(ga[k, z, y, x, low, :], xaa[k], yba[k])
        oa[o, high, :] = total_of(ga[k, z, y, x, high, :], yaa[k], xba[k])
        for copy in out_copies(c):
            copy.start()
        for buf in (xdz, ydz, xaz, yaz, xbz, ybz):
            sent(buf.at[k], send_z.at[k])
        for buf in (xda, yda, xaa, yaa, xba, yba):
            sent(buf.at[k], send_a.at[k])
        for step in range(3):

            @pl.when(z == step)
            def _():
                sent(above(lnz, k, step + 1, 3 - step), send_z.at[k])
                sent(above(lna, k, step + 1, 3 - step), send_a.at[k])

            @pl.when(z == 3 - step)
            def _():
                sent(below(lnz, k, 3 - step), send_z.at[k])
                sent(below(lna, k, 3 - step), send_a.at[k])

        @pl.when(c < total - slots)
        def _():
            signal_neighbours([credit.at[i] for i in (0, 1, 3, 2)], near, has_up, has_down)

    frames, features = e3_h.shape
    part, half_rows = pool.shape[2], frames // 2
    heads = part // HEAD_DIM
    own_rows = pl.ds(pl.multiple_of(core * half_rows, half_rows), half_rows)
    wide = pl.ds(0, features)
    slope = dqkv.at[:, pl.ds(features, part)]
    block = 256

    def columns(n):
        return pl.ds(pl.multiple_of(n * part, part), part)

    def weight_copy(slot, ref, n=0):
        return pltpu.make_async_copy(ref.at[:, columns(n)], weights.at[slot], weight_sem.at[slot])

    def use(slot):
        weight_copy(slot, w_q).wait()

    def pool_copy(n, ref, m=0):
        return pltpu.make_async_copy(ref.at[:, columns(m)], pool.at[n], pool_sem.at[n])

    def slope_copy(n):
        return pltpu.make_async_copy(slope_h.at[:, columns(n)], slope, slope_sem)

    def keep_copy(n, src, dst):
        return pltpu.make_async_copy(src, dst, keep_sem.at[n])

    def du_copy(n):
        return keep_copy(0, pool.at[n], du_h.at[:, columns(n)])

    def to_other(n, src, dst):
        return remote(src, dst, share_send.at[n], share_recv.at[n], other)

    def active_copy(whose, n):
        lines = pl.ds(pl.multiple_of(whose * half_rows, half_rows), half_rows)
        return keep_copy(0, a_h.at[lines, pl.ds(n * 2 * part, 2 * part)], theirs)

    def share_sum(n):
        return to_other(n, theirs, arrived.at[n % 2])

    def share_branch(n):
        ref = dqkv.at[own_rows, wide]
        return to_other(4 + n, ref, ref)

    def multiply(whose, source, slot, fresh):
        for first in range(0, half_rows, block):
            rows_of = pl.ds(pl.multiple_of(whose * half_rows + first, block), block)
            value = dot_nt(source(rows_of), weights[slot])
            lines = pl.ds(first, block)
            acc[lines, :] = value if fresh else acc[lines, :] + value

    def pooled(n):
        return lambda rows_of: pool[n, rows_of, :]

    def headed(n):
        return lambda rows_of: dqkv[rows_of, pl.ds(n * part, part)]

    def send_sum(n):
        for first in range(0, half_rows, block):
            lines = pl.ds(first, block)
            theirs[lines, :] = acc[lines, :].astype(BF16)
        share_sum(n).start()

    def norm_back(kind, n, load, before, store):
        step = 64
        gain = norms[2 * kind : 2 * kind + 1, :]

        def body(i, sums):
            first = pl.multiple_of(i * step, step)
            lines = pl.ds(first, step)
            value = load(i, lines)
            offset = value - jnp.mean(value, axis=-1, keepdims=True)
            scale = lax.rsqrt(jnp.mean(offset * offset, axis=-1, keepdims=True) + norm_eps)
            unit = offset * scale
            slope_in = acc[lines, :] + arrived[n % 2, lines, :].astype(F32)
            scaled = slope_in * gain
            inner = jnp.mean(scaled * unit, axis=-1, keepdims=True)
            change = scale * (scaled - jnp.mean(scaled, axis=-1, keepdims=True) - unit * inner)
            store(first, lines, before(first, lines) + change)
            return (
                sums[0] + jnp.sum(slope_in * unit, axis=0, keepdims=True),
                sums[1] + jnp.sum(slope_in, axis=0, keepdims=True),
            )

        zero = jnp.zeros((1, features), F32)
        gains, shifts = lax.fori_loop(0, half_rows // step, body, (zero, zero))
        norm_grads[2 * kind : 2 * kind + 1, :] = gains
        norm_grads[2 * kind + 1 : 2 * kind + 2, :] = shifts

    x2_copy = pltpu.make_async_copy(x2_h, lbuf.at[0], x_sem)

    def store_branch(first, lines, value):
        grad[lines, :] = value
        dqkv[pl.ds(pl.multiple_of(core * half_rows + first, 64), 64), wide] = value.astype(BF16)

    def project_to(n, slot):
        for first in range(0, frames, block):
            lines = pl.ds(first, block)
            pool[n, lines, :] = dot_nn(dqkv[lines, wide], weights[slot]).astype(BF16)

    def feed_forward(j):
        use(0)
        slope_copy(j).wait()
        for first in range(0, frames, block):
            lines = pl.ds(first, block)
            value = dot_nn(lbuf[0, lines, :], weights[0])
            pool[j, lines, :] = (
                value * dqkv[lines, pl.ds(features, part)].astype(F32)
            ).astype(BF16)

        @pl.when(j > 0)
        def _():
            du_copy(j - 1).wait()

        du_copy(j).start()

        @pl.when(j < 3)
        def _():
            weight_copy(0, w_down, j + 1).start()
            slope_copy(j + 1).start()

        pl.when(j == 3)(lambda: weight_copy(0, w_up, 0).start())
        use(1)
        multiply(1 - core, pooled(j), 1, False)
        pl.when(j < 3)(lambda: weight_copy(1, w_up, j + 1).start())
        pl.when(j == 3)(lambda: send_sum(0))

    def turn_4():
        du_copy(3).wait()
        keep_copy(3, x3_h, grad).start()
        multiply(core, pooled(3), 1, True)
        weight_copy(1, w_up, 1).start()
        use(0)
        multiply(core, pooled(0), 0, False)
        weight_copy(0, w_up, 2).start()

    def turn_5():
        use(1)
        multiply(core, pooled(1), 1, False)
        weight_copy(1, w_cq).start()
        use(0)
        multiply(core, pooled(2), 0, False)
        weight_copy(0, w_co).start()

    def turn_6():
        pool_copy(0, q2_h).start()
        share_sum(0).wait()
        keep_copy(3, x3_h, grad).wait()
        norm_back(
            2,
            0,
            lambda i, lines: grad[lines, :],
            lambda first, lines: lbuf[
                0, pl.ds(pl.multiple_of(core * half_rows + first, 64), 64), :
            ].astype(F32),
            store_branch,
        )
        share_branch(0).start()

    def turn_7():
        share_branch(0).wait()
        x2_copy.start()
        keep_copy(1, dqkv.at[:, wide], e2_h).start()
        use(0)
        project_to(1, 0)
        weight_copy(0, w_ck).start()

    def turn_8():
        pool_copy(0, q2_h).wait()
        for copy in firsts:
            copy.wait()

        def body(head, carry):
            head_back(
                head,
                pool.at[0],
                k2_v,
                v2_v,
                pool.at[1],
                lse2_ref,
                pool.at[2],
                dkv_v,
                (0, 0, part),
                acc_k,
                acc_v,
                False,
            )
            return carry

        lax.fori_loop(0, heads, body, 0, unroll=2)
        keep_copy(1, dqkv.at[:, wide], e2_h).wait()
        keep_copy(0, pool.at[2], dq2_h).start()
        use(0)
        text_part[...] = dot_nt(dkv_v[:, pl.ds(0, part)], weights[0])
        weight_copy(0, w_cv).start()

    def text_columns(whose):
        count = features // 2
        return pl.ds(pl.multiple_of(whose * count, count), count)

    def text_share():
        return to_other(6, text_send, text_got)

    def turn_9():
        keep_copy(0, pool.at[2], dq2_h).wait()
        use(0)
        text_part[...] += dot_nt(dkv_v[:, pl.ds(part, part)], weights[0])
        text_send[...] = text_part[:, text_columns(1 - core)].astype(BF16)
        text_share().start()
        weight_copy(0, w_o).start()
        use(1)
        multiply(1 - core, pooled(2), 1, True)
        send_sum(1)

    def turn_10():
        multiply(core, pooled(2), 1, True)
        for n, ref in enumerate((q1_h, k1_h, v1_h)):
            pool_copy(n, ref).start()
        share_sum(1).wait()
        x2_copy.wait()
        norm_back(
            1,
            1,
            lambda i, lines: lbuf[0, lines, :].astype(F32)
            + lbuf[0, pl.ds(pl.multiple_of(half_rows + i * 64, 64), 64), :].astype(F32),
            lambda first, lines: grad[lines, :],
            store_branch,
        )
        share_branch(1).start()
        text_share().wait()
        text_part[:, pl.ds(0, features // 2)] = text_part[:, text_columns(core)] + text_got[
            ...
        ].astype(F32)
        keep_copy(2, text_part.at[:, pl.ds(0, features // 2)], grad_text).start()

    def turn_11():
        share_branch(1).wait()
        keep_copy(1, dqkv.at[:, wide], e1_h).start()
        use(0)
        project_to(3, 0)
        weight_copy(0, w_down, 0).start()
        weight_copy(1, w_down, 1).start()
        active_copy(1 - core, 0).start()

    def turn_12():
        keep_copy(1, dqkv.at[:, wide], e1_h).wait()
        for n, ref in enumerate((q1_h, k1_h, v1_h)):
            pool_copy(n, ref).wait()

    def self_head(head):
        head_back(
            head,
            pool.at[0],
            pool.at[1],
            pool.at[2],
            pool.at[3],
            lse1_ref,
            dqkv,
            dqkv,
            (0, part, 2 * part),
            acc_k,
            acc_v,
            True,
        )

    def held(n):
        return lambda rows_of: theirs[rows_of, pl.ds(n * part, part)]

    def turn_13():
        active_copy(core, 0).wait()
        use(0)
        multiply(0, held(0), 0, True)
        weight_copy(0, w_down, 2).start()
        use(1)
        multiply(0, held(1), 1, False)
        weight_copy(1, w_down, 3).start()
        active_copy(1 - core, 1).start()

    def turn_14():
        active_copy(core, 0).wait()
        use(0)
        multiply(0, held(0), 0, False)
        use(1)
        multiply(0, held(1), 1, False)
        send_sum(3)

    def turn_15():
        share_sum(3).wait()
        keep_copy(3, x3_h, acc).start()
        active_copy(core, 1).start()

    def turn_16():
        active_copy(core, 0).wait()
        keep_copy(3, x3_h, acc).wait()
        multiply(0, held(0), 0, False)
        weight_copy(0, w_down, 0).start()
        multiply(0, held(1), 1, False)
        weight_copy(1, w_down, 1).start()
        active_copy(core, 0).start()

    def turn_17():
        active_copy(core, 0).wait()
        use(0)
        multiply(0, held(0), 0, False)
        weight_copy(0, w_q).start()
        use(1)
        multiply(0, held(1), 1, False)
        weight_copy(1, w_k).start()

        def body(i, carry):
            lines = pl.ds(pl.multiple_of(i * 64, 64), 64)
            theirs[lines, :] = (acc[lines, :] + arrived[1, lines, :].astype(F32)).astype(BF16)
            return carry

        lax.fori_loop(0, half_rows // 64, body, 0)
        keep_copy(0, theirs, layer_out).start()

    def turn_18():
        keep_copy(0, theirs, layer_out).wait()
        use(0)
        multiply(1 - core, headed(0), 0, True)
        weight_copy(0, w_v).start()
        use(1)
        multiply(1 - core, headed(1), 1, False)

    def turn_19():
        use(0)
        multiply(1 - core, headed(2), 0, False)
        send_sum(2)
        multiply(core, headed(2), 0, True)
        multiply(core, headed(1), 1, False)
        weight_copy(1, w_q).start()

    def turn_20():
        use(1)
        multiply(core, headed(0), 1, False)
        share_sum(2).wait()
        keep_copy(1, x1_h, theirs).start()

    def turn_21():
        keep_copy(1, x1_h, theirs).wait()

        def store(first, lines, value):
            grad[lines, :] = value

        norm_back(
            0,
            2,
            lambda i, lines: theirs[lines, :].astype(F32),
            lambda first, lines: grad[lines, :],
            store,
        )
        keep_copy(3, grad, grad_input).start()

    def norm_copy(step):
        return remote(
            got.at[2 * step],
            got.at[2 * step + 1],
            norm_send.at[step],
            norm_recv.at[step],
            partners[step],
        )

    def norm_sum(step):
        if step == 0:
            got[0] = norm_grads[...]
        else:
            norm_copy(step - 1).wait()
            got[2 * step] = got[2 * step - 2] + got[2 * step - 1]
        if step < len(partners):
            norm_copy(step).start()
        else:
            keep_copy(1, got.at[2 * step], norm_out).start()

    chain = {
        4: turn_4,
        5: turn_5,
        6: turn_6,
        7: turn_7,
        8: turn_8,
        9: turn_9,
        10: turn_10,
        11: turn_11,
        13: turn_13,
        14: turn_14,
        15: turn_15,
        16: turn_16,
        17: turn_17,
        18: turn_18,
        19: turn_19,
        20: turn_20,
        21: turn_21,
    }
    stages = (begin, second, third, fourth, fifth, finish)
    left_copy(0).start()
    weight_copy(0, w_down, 0).start()
    slope_copy(0).start()
    start_rights(jnp.int32(0))
    weight_copy(1, w_up, 0).start()
    left_copy(1).start()
    for copy in firsts:
        copy.start()
    for first in range(0, half_rows, block):
        acc[pl.ds(first, block), :] = jnp.zeros((block, features), F32)
    norm_grads[...] = jnp.zeros_like(norm_grads)
    left_copy(0).wait()

    def body(turn, carry):
        pl.when(turn < total)(lambda: compute(turn, lax.rem(turn, slots)))
        for step, stage in enumerate(stages):
            c = turn - step

            @pl.when((c >= 0) & (c < total))
            def _():
                stage(c, lax.rem(c, slots))

        pl.when(turn < 4)(lambda: feed_forward(turn))
        for number, fn in chain.items():
            pl.when(turn == number)(fn)
        pl.when(turn == 12)(turn_12)

        @pl.when((turn >= 12) & (turn < 18))
        def _():
            def both(head, carry):
                self_head(head)
                return carry

            first = lax.div(heads, 6) * (turn - 12)
            lax.fori_loop(first, first + heads // 6, both, 0)

        for step in range(len(partners) + 1):
            pl.when(turn == 22 + step)(functools.partial(norm_sum, step))
        return carry

    lax.fori_loop(0, total + len(stages) - 1, body, 0)
    for c in (total - 2, total - 1):
        for copy in out_copies(jnp.int32(c)):
            copy.wait()
    keep_copy(3, grad, grad_input).wait()
    keep_copy(1, got.at[2 * len(partners)], norm_out).wait()
    keep_copy(2, text_part.at[:, pl.ds(0, features // 2)], grad_text).wait()


def backward_all(arrays, small):
    frames, width = arrays[0].shape
    text = arrays[8]
    rows, half, part = width // 16, frames // 2, arrays[9].shape[1]
    dma, vmem, shape = pltpu.SemaphoreType.DMA, pltpu.VMEM, jax.ShapeDtypeStruct

    def buffer(*dims):
        return vmem((SLOTS,) + dims, BF16)

    anywhere = pl.BlockSpec(memory_space=pl.ANY)
    return pl.pallas_call(
        backward_kernel,
        out_shape=[
            shape((rows, UNITS * UNIT), F32),
            shape((half, width), BF16),
            shape((half, width), F32),
            shape((text.shape[0], width // 2), F32),
            shape((8, width), F32),
            shape((frames, 4 * part), BF16),
            shape((frames, part), BF16),
            shape((frames, width), BF16),
            shape((frames, width), BF16),
        ],
        in_specs=[anywhere] * len(arrays) + [pl.BlockSpec(memory_space=vmem)] * len(small),
        out_specs=[anywhere] * 9,
        scratch_shapes=[
            buffer(4, 2, 2, rows, WIDTH_Z),
            buffer(4, 2, 2, rows, WIDTH_A),
            *[buffer(4, rows // 2, WIDTH_Z)] * 6,
            buffer(5, rows, WIDTH_Z),
            *[buffer(rows // 2, WIDTH_A)] * 6,
            buffer(5, 2, 2, rows, WIDTH_A),
            vmem((2, rows, WIDTH_Z), F32),
            vmem((2, rows, WIDTH_A), F32),
            vmem((2, frames, width), BF16),
            vmem((2, 2, frames, UNIT), BF16),
            vmem(text.shape, BF16),
            vmem((text.shape[0], 2 * part), BF16),
            *[vmem((text.shape[0], part), BF16)] * 2,
            vmem((4, frames, part), BF16),
            vmem((frames, 3 * part), BF16),
            *[vmem((frames, 128), F32)] * 2,
            *[vmem((half, width), F32)] * 2,
            vmem((half, width), BF16),
            vmem((2, half, width), BF16),
            vmem((2, width, part), BF16),
            vmem((text.shape[0], width), F32),
            *[vmem((text.shape[0], width // 2), BF16)] * 2,
            vmem((8, width), F32),
            vmem((11, 8, width), F32),
            dma((3,)),
            dma((2,)),
            dma((2, 2)),
            dma((2, 2)),
            dma((SLOTS,)),
            dma((SLOTS,)),
            dma((SLOTS, 8)),
            dma((SLOTS, 8)),
            dma((4,)),
            dma,
            dma((2,)),
            dma,
            dma((4,)),
            dma((7,)),
            dma((7,)),
            dma((5,)),
            dma((5,)),
            pltpu.SemaphoreType.REGULAR((4,)),
        ],
        compiler_params=pltpu.CompilerParams(
            collective_id=1, has_side_effects=True, vmem_limit_bytes=VMEM_LIMIT
        ),
        name="backward",
    )(*arrays, *small)


def gather_plan(columns):
    chunks, since = [], 0
    for array, width in enumerate(columns):
        size = 768 if width % 768 == 0 else width
        for first in range(0, width, size):
            since += 1
            family = "A" if since % 5 == 3 and size == 768 else "Z"
            chunks.append((array, first, size, family))
    return tuple(chunks)


def local_fast(
    hidden_in,
    text_states,
    norm1_gain,
    norm1_bias,
    self_query,
    self_key,
    self_value,
    self_out,
    norm2_gain,
    norm2_bias,
    cross_query,
    cross_key,
    cross_value,
    cross_out,
    norm3_gain,
    norm3_bias,
    hidden_up,
    hidden_down,
    cotangent,
):
    width = norm1_gain.shape[0] * 16
    norms = jnp.stack([norm1_gain, norm1_bias, norm2_gain, norm2_bias, norm3_gain, norm3_bias])
    norms = jnp.pad(norms, ((0, 26), (0, 128 - norms.shape[1])))
    shards = (
        norms,
        self_query.T,
        self_key.T,
        self_value.T,
        self_out,
        cross_key.T,
        cross_value.T,
        cross_query.T,
        cross_out,
        hidden_up.T,
        hidden_down,
    )
    gathered, kept = forward_all(
        shards,
        gather_plan([s.shape[1] for s in shards]),
        hidden_in[0],
        text_states[0],
        cotangent[0],
    )
    w_q, w_k, w_v, w_o, w_ck, w_cv, w_cq, w_co, w_up, w_down = [
        g.reshape(width, g.shape[-1]) for g in gathered[1:]
    ]
    normed_one, normed_two, normed_three = kept[:3]
    query_one, key_one, value_one, attended_one = kept[3:7]
    query_two, key_two, value_two, attended_two = kept[7:11]
    logsum_one, logsum_two, norms, stream_two, stream_three, branch, active, slope = kept[11:]
    summed, layer_out, grad_input, grad_text, norm_sums, *_ = backward_all(
        (
            *(branch, normed_three, normed_two, normed_one),
            *(active, slope, attended_two, attended_one, text_states[0]),
            *(query_two, key_two, value_two, query_one, key_one, value_one),
            *(stream_three, stream_two, hidden_in[0]),
            *(w_q, w_k, w_v, w_o, w_ck, w_cv, w_cq, w_co, w_up, w_down),
        ),
        (logsum_two, logsum_one, norms),
    )
    rows, part = width // 16, query_one.shape[1]
    norm_sums = lax.dynamic_slice_in_dim(norm_sums, lax.axis_index("dp") * rows, rows, 1)
    columns = [hidden_down.shape[1]] * 2 + [part] * 8
    pieces, first = [], 0
    for count in columns:
        pieces.append(summed[:, first : first + count])
        first += count
    down, up, out_cross, query_cross, key_cross, value_cross, out_self, query, key, value = pieces
    return (
        layer_out[None],
        grad_input[None],
        grad_text[None],
        norm_sums[0],
        norm_sums[1],
        query.T,
        key.T,
        value.T,
        out_self,
        norm_sums[2],
        norm_sums[3],
        query_cross.T,
        key_cross.T,
        value_cross.T,
        out_cross,
        norm_sums[4],
        norm_sums[5],
        up.T,
        down,
    )


def solution(mesh):
    placed = (
        P("dp", "tensor", None),
        P("dp", None, None),
        P("dp"),
        P("dp"),
        P("tensor", "dp"),
        P("tensor", "dp"),
        P("tensor", "dp"),
        P("dp", "tensor"),
        P("dp"),
        P("dp"),
        P("tensor", "dp"),
        P("tensor", "dp"),
        P("tensor", "dp"),
        P("dp", "tensor"),
        P("dp"),
        P("dp"),
        P("tensor", "dp"),
        P("dp", "tensor"),
        P("dp", "tensor", None),
    )
    fast = dict(mesh.shape) == {"dp": 16, "tensor": 2}
    return jax.shard_map(
        local_fast if fast else local_generic,
        mesh=mesh,
        in_specs=placed,
        out_specs=(
            P("dp", "tensor", None),
            P("dp", "tensor", None),
            P("dp", None, "tensor"),
            P("dp"),
            P("dp"),
            P("tensor", "dp"),
            P("tensor", "dp"),
            P("tensor", "dp"),
            P("dp", "tensor"),
            P("dp"),
            P("dp"),
            P("tensor", "dp"),
            P("tensor", "dp"),
            P("tensor", "dp"),
            P("dp", "tensor"),
            P("dp"),
            P("dp"),
            P("tensor", "dp"),
            P("dp", "tensor"),
        ),
        check_vma=False,
    )
```
